32 devices in a mesh: row: 8 (over z, core), col: 4 (over y, x).
Axes of the slice: x: 2, y: 2, z: 4, core: 2. Of those that a mesh axis runs over, the one named last changes fastest.
Arguments:
- specimen: float32 [2, 1024, 512], P(None, 'row', 'col'), may hold values from -4 to 4
- probe_mode_stack: float32 [4, 2, 256, 256], replicated, may hold values from -4 to 4
- measured: float32 [8, 4, 1, 256, 256], P('row', 'col'), may hold values from 0.3 to 3
- centers: int32 [8, 4, 2, 2], P('row', 'col'), may hold values from 1 to 127
- frame_counts: int32 [8, 4], P('row', 'col'), may hold values from 0 to 2, as said below
- helper_cols: int32 [8, 4, 2], P('row', 'col'), may hold values from 0 to 3, as said below
Outputs:
- gradient: float32 [2, 1024, 512], P(None, 'row', 'col')
The draws below stay inside these ranges and needn't reach their ends.
Inputs may be any that keep to these rules, and one draw needn't show every extreme that they name: `frame_counts`: in every row of tiles the counts sum to 1 times the number of tiles in the row, and some tile of every row holds 2 frames. `helper_cols`: among a tile's live slots the helper columns are distinct; in every row of tiles each column is named by exactly one live slot; slots past a tile's count hold arbitrary columns.
All inputs are finite; a program needn't handle non-finite values.
Results may differ from the reference program's by a relative error of at most 0.007.
Values may be sent and summed in bfloat16 or wider, within the bound.
No kernel may reach another device: no remote copies, remote signals or barrier semaphores. Data moves between devices by JAX's collectives and lax.ppermute only.
A program may use at most 64 MiB of HBM per device.

```python
import math
import jax
import jax.numpy as jnp
from jax import lax

FRAME_PIXELS = 256
MODES = 4
CAP = 2
HELPER_FRAMES = 1
TILE = 128
TILE_ROWS = 8
TILE_COLUMNS = 4
OBJ_R = 1024
OBJ_C = 512


def plan_rows(key):
    folded = jax.random.fold_in(key, 4242)
    row_keys = jax.random.split(folded, TILE_ROWS)

    def one_row(row_key):
        key_order, key_extra, key_offset, key_helpers = jax.random.split(row_key, 4)
        ranking = jnp.argsort(jax.random.permutation(key_order, TILE_COLUMNS)).astype(jnp.int32)
        extra_move = jax.random.randint(key_extra, (), 0, 2, dtype=jnp.int32)
        counts_row = 1 + (ranking == 0).astype(jnp.int32) - (ranking == 1).astype(jnp.int32)
        counts_row = counts_row + extra_move * ((ranking == 2).astype(jnp.int32) - (ranking == 3).astype(jnp.int32))
        starts = jnp.cumsum(counts_row) - counts_row
        offset = jax.random.randint(key_offset, (), 0, TILE_COLUMNS, dtype=jnp.int32)
        helpers = jax.random.permutation(key_helpers, TILE_COLUMNS).astype(jnp.int32)
        slot_range = jnp.arange(CAP, dtype=jnp.int32)
        targets_row = helpers[(starts[:, None] + slot_range[None, :] + offset) % TILE_COLUMNS]
        return (counts_row.astype(jnp.int32), targets_row.astype(jnp.int32))
    return jax.vmap(one_row)(row_keys)


def draw_frame_counts(key, part):
    return plan_rows(key)[0]


def draw_helper_cols(key, part):
    return plan_rows(key)[1]


def place_ends(result, stream_key, low, largest):
    longest = result.shape.index(max(result.shape))
    spots = []
    for shift in (0, 1):
        where = [jax.random.randint(jax.random.fold_in(stream_key, axis), (), 0, length) for axis, length in enumerate(result.shape)]
        where[longest] = (where[longest] + shift) % result.shape[longest]
        spots.append(tuple(where))
    return result.at[spots[0]].set(low).at[spots[1]].set(largest)


def block_scale(rng, shape, cuts, smallest, high):
    def one(dim, parts):
        steps = jax.random.uniform(jax.random.fold_in(jax.random.fold_in(rng, 6), dim), (parts,), jnp.float32, smallest / len(cuts), high / len(cuts))
        return jnp.repeat(jnp.exp(steps), shape[dim] // parts).reshape((-1,) + (1,) * (len(shape) - dim - 1))

    loudness = one(*cuts[0])
    for cut in cuts[1:]:
        loudness = loudness * one(*cut)
    return loudness


def gaussian(own_key, dims, deviation, limit, cuts=(), kind=jnp.bfloat16):
    array = jax.random.normal(own_key, dims, jnp.float32) * deviation
    if len(cuts) > 0:
        array = block_scale(own_key, dims, cuts, -0.22, 0.18) * array
    return jnp.clip(array, min=-limit, max=limit).astype(kind)


def setup_inputs(seed: int = 0) -> dict:
    streams_of = jax.random.split(jax.random.key(seed), 7)
    return {
        "specimen": gaussian(streams_of[0], (2, OBJ_R, OBJ_C), 0.5, 4.0, ((1, 8), (2, 4)), jnp.float32),
        "probe_mode_stack": gaussian(streams_of[1], (MODES, 2, FRAME_PIXELS, FRAME_PIXELS), 0.5, 4.0, (), jnp.float32),
        "measured": jnp.clip(jnp.exp(math.log(3.0) - 2.3025851 * jax.random.uniform(streams_of[2], (TILE_ROWS, TILE_COLUMNS, HELPER_FRAMES, FRAME_PIXELS, FRAME_PIXELS), jnp.float32) ** block_scale(streams_of[2], (TILE_ROWS, TILE_COLUMNS, HELPER_FRAMES, FRAME_PIXELS, FRAME_PIXELS), ((0, 8), (1, 4)), -0.2, 0.2)), 0.3, 3.0),
        "centers": place_ends(jax.random.randint(streams_of[3], (TILE_ROWS, TILE_COLUMNS, CAP, 2), 1, TILE), jax.random.fold_in(streams_of[3], 1), 1, TILE - 1).astype(jnp.int32),
        "frame_counts": draw_frame_counts(jax.random.fold_in(streams_of[6], 71), 0),
        "helper_cols": draw_helper_cols(jax.random.fold_in(streams_of[6], 71), 0),
    }


def dft_tables(extent):
    steps_idx = jnp.arange(extent, dtype=jnp.int32)
    product = steps_idx[:, None] * steps_idx[None, :] % extent
    angles = product.astype(jnp.float32) * (2.0 * math.pi / extent)
    scaling = 1.0 / math.sqrt(extent)
    return ((jnp.cos(angles) * scaling).astype(jnp.bfloat16), (-jnp.sin(angles) * scaling).astype(jnp.bfloat16))

def widen_exact(values):
    return lax.optimization_barrier(values).astype(jnp.float32)

def right_apply(operand, fourier_real_table, fourier_imaginary_table, conj_sign):
    extent = fourier_real_table.shape[0]
    joined = widen_exact(jnp.concatenate([fourier_real_table, fourier_imaginary_table], axis=1))
    products = jnp.einsum('bxy,yv->bxv', widen_exact(operand), joined, precision=lax.Precision.HIGHEST)
    real_part = products[:, :extent, :extent] - conj_sign * products[:, extent:, extent:]
    imag_part = products[:, extent:, :extent] + conj_sign * products[:, :extent, extent:]
    return jnp.concatenate([real_part, imag_part], axis=1)

def left_apply(operand, fourier_real_table, fourier_imaginary_table, conj_sign):
    upper_rows = jnp.concatenate([fourier_real_table, -conj_sign * fourier_imaginary_table], axis=1)
    lower_rows = jnp.concatenate([conj_sign * fourier_imaginary_table, fourier_real_table], axis=1)
    mixer_matrix = widen_exact(jnp.concatenate([upper_rows, lower_rows], axis=0))
    return jnp.einsum('uv,bvc->buc', mixer_matrix, widen_exact(operand), precision=lax.Precision.HIGHEST)

def per_frame_gradients(object_patches, probe_mode_stack, measured, fourier_real_table, fourier_imaginary_table):
    helper_slot_count = object_patches.shape[0]
    extent = object_patches.shape[2]
    mode_count = probe_mode_stack.shape[0]
    wide_patch = widen_exact(object_patches)
    patch_re = wide_patch[:, None, :extent]
    patch_im = wide_patch[:, None, extent:]
    probe_re = probe_mode_stack[None, :, 0]
    probe_im = probe_mode_stack[None, :, 1]
    exit_wave = jnp.concatenate([probe_re * patch_re - probe_im * patch_im, probe_re * patch_im + probe_im * patch_re], axis=2)
    exit_wave = exit_wave.astype(jnp.bfloat16).reshape(helper_slot_count * mode_count, 2 * extent, extent)
    half_wave = right_apply(exit_wave, fourier_real_table, fourier_imaginary_table, 1.0).astype(jnp.bfloat16)
    far_field = left_apply(half_wave, fourier_real_table, fourier_imaginary_table, 1.0).reshape(helper_slot_count, mode_count, 2 * extent, extent)
    far_re = far_field[:, :, :extent]
    far_im = far_field[:, :, extent:]
    intensity = lax.optimization_barrier(jnp.sum(far_re * far_re + far_im * far_im, axis=1))
    factor = 1.0 - measured / jnp.sqrt(jnp.maximum(intensity, 0.25))
    doubled = jnp.concatenate([factor, factor], axis=1)[:, None]
    corrected = (far_field * doubled).astype(jnp.bfloat16).reshape(helper_slot_count * mode_count, 2 * extent, extent)
    back_half = right_apply(corrected, fourier_real_table, fourier_imaginary_table, -1.0).astype(jnp.bfloat16)
    inverse = left_apply(back_half, fourier_real_table, fourier_imaginary_table, -1.0).reshape(helper_slot_count, mode_count, 2 * extent, extent)
    chi_re = inverse[:, :, :extent]
    chi_im = inverse[:, :, extent:]
    grad_re = lax.optimization_barrier(jnp.sum(probe_re * chi_re + probe_im * chi_im, axis=1))
    grad_im = lax.optimization_barrier(jnp.sum(probe_re * chi_im - probe_im * chi_re, axis=1))
    return jnp.concatenate([grad_re, grad_im], axis=1).astype(jnp.bfloat16)

def reference(specimen, probe_mode_stack, measured, centers, frame_counts, helper_cols):
    half_size = FRAME_PIXELS // 2
    fourier_real_table, fourier_imaginary_table = dft_tables(FRAME_PIXELS)
    slots_range = jnp.arange(CAP, dtype=jnp.int32)
    is_live = slots_range[None, None, :] < frame_counts[:, :, None]
    helper_range = jnp.arange(TILE_COLUMNS, dtype=jnp.int32)
    hit_table = is_live[:, :, None, :] & (helper_cols[:, :, None, :] == helper_range[None, None, :, None])
    has_frame = jnp.any(hit_table, axis=3).astype(jnp.int32)
    before = (jnp.cumsum(has_frame, axis=1) - has_frame).astype(jnp.int32)
    select = has_frame[..., None] * (before[..., None] == jnp.arange(HELPER_FRAMES, dtype=jnp.int32)[None, None, None, :]).astype(jnp.int32)
    src_col = lax.optimization_barrier(jnp.sum(select * helper_range[None, :, None, None], axis=1)).astype(jnp.int32)
    frame_slot = lax.optimization_barrier(jnp.sum(hit_table.astype(jnp.int32) * slots_range[None, None, None, :], axis=3)).astype(jnp.int32)
    src_slot = lax.optimization_barrier(jnp.sum(select * frame_slot[..., None], axis=1)).astype(jnp.int32)
    row_range = jnp.arange(TILE_ROWS, dtype=jnp.int32)[:, None, None]
    picked = centers[row_range, src_col, src_slot]
    first_row = (row_range * TILE + picked[..., 0]).reshape(TILE_ROWS * TILE_COLUMNS, HELPER_FRAMES).astype(jnp.int32)
    first_column = (src_col * TILE + picked[..., 1]).reshape(TILE_ROWS * TILE_COLUMNS, HELPER_FRAMES).astype(jnp.int32)
    padded = jnp.pad(specimen, ((0, 0), (half_size, half_size), (half_size, half_size)))
    flat_measurements = measured.reshape(TILE_ROWS * TILE_COLUMNS, HELPER_FRAMES, FRAME_PIXELS, FRAME_PIXELS)

    def process_helper_frame(summed_gradient, input_arrays):
        row_positions, column_positions, current_measurements = input_arrays
        pieces = []
        for slot_idx in range(HELPER_FRAMES):
            corner = (jnp.int32(0), row_positions[slot_idx], column_positions[slot_idx])
            pieces.append(lax.dynamic_slice(padded, corner, (2, FRAME_PIXELS, FRAME_PIXELS)).reshape(2 * FRAME_PIXELS, FRAME_PIXELS))
        object_patches = jnp.stack(pieces).astype(jnp.bfloat16)
        patch_gradients = per_frame_gradients(object_patches, probe_mode_stack, current_measurements, fourier_real_table, fourier_imaginary_table)
        for slot_idx in range(HELPER_FRAMES):
            corner = (jnp.int32(0), row_positions[slot_idx], column_positions[slot_idx])
            current = lax.dynamic_slice(summed_gradient, corner, (2, FRAME_PIXELS, FRAME_PIXELS))
            added = current + widen_exact(patch_gradients[slot_idx]).reshape(2, FRAME_PIXELS, FRAME_PIXELS)
            summed_gradient = lax.dynamic_update_slice(summed_gradient, added, corner)
        return (summed_gradient, None)
    summed_gradient = jnp.zeros(padded.shape, jnp.float32)
    summed_gradient, ignored_value = lax.scan(process_helper_frame, summed_gradient, (first_row, first_column, flat_measurements))
    return summed_gradient[:, half_size:half_size + OBJ_R, half_size:half_size + OBJ_C]
```

```python
import functools
import math

import jax
import jax.numpy as jnp
import numpy as np
from jax import lax
from jax.experimental import pallas as pl
from jax.experimental.pallas import tpu as pltpu
from jax.sharding import PartitionSpec as P

F32 = jnp.float32
BF16 = jnp.bfloat16


def dft_tables(extent):
    half = extent // 2
    steps = np.arange(extent, dtype=np.int32)
    angles = (steps[:, None] * steps[None, :] % extent).astype(np.float32)
    angles = angles * np.float32(2.0 * math.pi / extent)
    scaling = np.float32(1.0 / math.sqrt(extent))
    real = (np.cos(angles) * scaling).astype(BF16)
    imag = (-np.sin(angles) * scaling).astype(BF16)
    tables = []
    for parity in (0, 1):
        re, im = real[:half, parity::2], imag[:half, parity::2]
        right = np.concatenate(
            [np.concatenate([re, im], 1), np.concatenate([-im, re], 1)], 0
        )
        tables += [right, np.ascontiguousarray(right.T)]
    return jnp.asarray(np.stack(tables))


def dot(a, b):
    return jnp.dot(a, b, preferred_element_type=F32)


def quarters(tl, tr, bl, br):
    return jnp.concatenate(
        [jnp.concatenate([tl, tr], 1), jnp.concatenate([bl, br], 1)], 0
    )


def one_hot(shape, hit):
    rows = lax.broadcasted_iota(jnp.int32, shape, 0)
    cols = lax.broadcasted_iota(jnp.int32, shape, 1)
    return jnp.where(hit(rows, cols), 1.0, 0.0).astype(BF16)


def frames_kernel(
    centers, count, helpers, top, mid, bottom, probe, measured, tables,
    up, down, centre, wide, far, corrected, acc,
):
    extent = probe.shape[-1]
    half = extent // 2
    tile = mid.shape[1]
    modes = probe.shape[0]
    span = tile + 2 * half
    planes = 2
    for p in range(planes):
        wide[p, :half] = top[p]
        wide[p, half : half + tile] = mid[p]
        wide[p, half + tile :] = bottom[p]
    acc[...] = jnp.zeros_like(acc)

    def one_frame(slot, carry):
        row, col = centers[slot, 0], centers[slot, 1]
        pick_rows = one_hot((extent, span), lambda i, k: k == i + row)
        pick_cols = one_hot((span, extent), lambda k, i: k == i + col)
        patch = [
            dot(dot(pick_rows, wide[p]).astype(BF16), pick_cols) for p in range(planes)
        ]
        sort = one_hot(
            (extent, extent),
            lambda i, k: k == jnp.where(i < half, 2 * i, 2 * (i - half) + 1),
        )
        sort_t = one_hot(
            (extent, extent),
            lambda k, i: k == jnp.where(i < half, 2 * i, 2 * (i - half) + 1),
        )
        amplitude = dot(dot(sort, measured[helpers[slot]]).astype(BF16), sort_t)
        right = (tables[0], tables[2])
        left = (tables[1], tables[3])
        intensity = [jnp.zeros((half, extent), F32) for _ in range(2)]
        for k in range(modes):
            pr, pi = probe[k, 0], probe[k, 1]
            wr = pr * patch[0] - pi * patch[1]
            wi = pr * patch[1] + pi * patch[0]
            spectra = []
            for parity, sign in ((0, 1), (1, -1)):
                folded = jnp.concatenate(
                    [wr[:, :half] + sign * wr[:, half:], wi[:, :half] + sign * wi[:, half:]], 1
                ).astype(BF16)
                spectra.append(dot(folded, right[parity]))
            even, odd = spectra
            for parity, sign in ((0, 1), (1, -1)):
                e = even[:half] + sign * even[half:]
                o = odd[:half] + sign * odd[half:]
                folded = quarters(e[:, :half], o[:, :half], e[:, half:], o[:, half:])
                f = dot(left[parity], folded.astype(BF16))
                far[k, parity] = f
                intensity[parity] += f[:half] * f[:half] + f[half:] * f[half:]
        factor = [
            1.0
            - amplitude[i * half : (i + 1) * half]
            * lax.rsqrt(jnp.maximum(intensity[i], 0.25))
            for i in range(2)
        ]
        grad = [[jnp.zeros((half, extent), F32) for _ in range(2)] for _ in range(2)]
        for k in range(modes):
            c = []
            for parity in range(2):
                f = far[k, parity]
                c.append(
                    (f * jnp.concatenate([factor[parity], factor[parity]], 0)).astype(BF16)
                )
            a = dot(
                quarters(c[0][:half, :half], c[0][half:, :half], c[1][:half, :half], c[1][half:, :half]),
                left[0],
            )
            b = dot(
                quarters(c[0][:half, half:], c[0][half:, half:], c[1][:half, half:], c[1][half:, half:]),
                left[1],
            )
            lo, hi = (a + b).astype(BF16), (a - b).astype(BF16)
            turned = []
            for parity in range(2):
                l = lo[parity * half : (parity + 1) * half]
                h = hi[parity * half : (parity + 1) * half]
                turned.append(
                    dot(
                        right[parity],
                        quarters(l[:, :half], h[:, :half], l[:, half:], h[:, half:]),
                    )
                )
            for i, chi in enumerate((turned[0] + turned[1], turned[0] - turned[1])):
                cr, ci = chi[:half], chi[half:]
                pr = probe[k, 0, i * half : (i + 1) * half]
                pi = probe[k, 1, i * half : (i + 1) * half]
                grad[0][i] += pr * cr + pi * ci
                grad[1][i] += pr * ci - pi * cr
        put_rows = one_hot((span, extent), lambda k, i: k == i + row)
        put_cols = one_hot((extent, span), lambda i, k: k == i + col)
        for p in range(planes):
            g = jnp.concatenate(grad[p], 0).astype(BF16)
            acc[p] += dot(put_rows, dot(g, put_cols).astype(BF16))
        return carry

    lax.fori_loop(0, count[0], one_frame, 0)
    for p in range(planes):
        up[p] = acc[p, :half].astype(BF16)
        centre[p] = acc[p, half : half + tile]
        down[p] = acc[p, half + tile :].astype(BF16)


def shifts(axis):
    count = lax.axis_size(axis)
    forward = [(i, i + 1) for i in range(count - 1)]
    return forward, [(b, a) for a, b in forward]


def per_device(specimen, probe, measured, centers, frame_counts, helper_cols):
    extent = probe.shape[-1]
    half = extent // 2
    tile = specimen.shape[1]
    modes = probe.shape[0]
    cap = centers.shape[2]
    span = tile + 2 * half
    right_of, left_of = shifts("col")
    below, above = shifts("row")
    amplitudes = lax.all_gather(measured[0, 0, 0].astype(BF16), "col")
    own = specimen.astype(BF16)
    west = lax.ppermute(own[:, :, tile - half :], "col", right_of)
    east = lax.ppermute(own[:, :, :half], "col", left_of)
    mid = jnp.concatenate([west, own, east], 2)
    top = lax.ppermute(mid[:, tile - half :], "row", below)
    bottom = lax.ppermute(mid[:, :half], "row", above)
    vmem = pl.BlockSpec(memory_space=pltpu.VMEM)
    smem = pl.BlockSpec(memory_space=pltpu.SMEM)
    up, down, centre = pl.pallas_call(
        frames_kernel,
        out_shape=(
            jax.ShapeDtypeStruct((2, half, span), BF16),
            jax.ShapeDtypeStruct((2, half, span), BF16),
            jax.ShapeDtypeStruct((2, tile, span), F32),
        ),
        in_specs=[smem] * 3 + [vmem] * 6,
        out_specs=(vmem,) * 3,
        scratch_shapes=[
            pltpu.VMEM((2, span, span), BF16),
            pltpu.VMEM((modes, 2, extent, extent), F32),
            pltpu.VMEM((8, 128), F32),
            pltpu.VMEM((2, span, span), F32),
        ],
        compiler_params=pltpu.CompilerParams(vmem_limit_bytes=40 * 2**20),
        cost_estimate=pl.CostEstimate(
            flops=2 * 10**9, bytes_accessed=4 * 2**20, transcendentals=extent * extent
        ),
        name="frames",
    )(
        centers.reshape(cap, 2), frame_counts.reshape(1), helper_cols.reshape(cap),
        top, mid, bottom, probe, amplitudes, dft_tables(extent),
    )
    from_above = lax.ppermute(down, "row", below)
    from_below = lax.ppermute(up, "row", above)
    band = centre.at[:, :half].add(from_above.astype(F32)).at[:, tile - half :].add(from_below.astype(F32))
    from_west = lax.ppermute(band[:, :, half + tile :].astype(BF16), "col", right_of)
    from_east = lax.ppermute(band[:, :, :half].astype(BF16), "col", left_of)
    result = band[:, :, half : half + tile]
    return result.at[:, :, :half].add(from_west.astype(F32)).at[:, :, tile - half :].add(from_east.astype(F32))


def solution(mesh):
    return jax.shard_map(
        per_device,
        mesh=mesh,
        in_specs=(
            P(None, "row", "col"),
            P(),
            P("row", "col", None, None, None),
            P("row", "col", None, None),
            P("row", "col"),
            P("row", "col", None),
        ),
        out_specs=P(None, "row", "col"),
        check_vma=False,
    )
```

```python
import functools
import math

import jax
import jax.numpy as jnp
import numpy as np
from jax import lax
from jax.experimental import pallas as pl
from jax.experimental.pallas import tpu as pltpu
from jax.sharding import PartitionSpec as P

F32 = jnp.float32
BF16 = jnp.bfloat16
INFO = 16
VMEM = pl.BlockSpec(memory_space=pltpu.VMEM)
ANY = pl.BlockSpec(memory_space=pl.ANY)


def dft_tables(extent):
    half = extent // 2
    steps = np.arange(extent, dtype=np.int32)
    angles = (steps[:, None] * steps[None, :] % extent).astype(np.float32)
    angles = angles * np.float32(2.0 * math.pi / extent)
    scaling = np.float32(1.0 / math.sqrt(extent))
    real = (np.cos(angles) * scaling).astype(BF16)
    imag = (-np.sin(angles) * scaling).astype(BF16)
    tables = []
    for parity in (0, 1):
        re, im = real[:half, parity::2], imag[:half, parity::2]
        right = np.concatenate(
            [np.concatenate([re, im], 1), np.concatenate([-im, re], 1)], 0
        )
        tables += [right, np.ascontiguousarray(right.T)]
    return jnp.asarray(np.stack(tables))


def dot(a, b):
    return jnp.dot(a, b, preferred_element_type=F32)


def quarters(tl, tr, bl, br):
    return jnp.concatenate(
        [jnp.concatenate([tl, tr], 1), jnp.concatenate([bl, br], 1)], 0
    )


def iota(shape, dim):
    return lax.broadcasted_iota(jnp.int32, shape, dim)


def fetch(pairs, sems):
    copies = [
        pltpu.make_async_copy(source, target, sems.at[i])
        for i, (source, target) in enumerate(pairs)
    ]
    for copy in copies:
        copy.start()
    return copies


def pack_kernel(specimen, centers, counts, helpers, out, tile_v, cen, cnt, hlp, sems):
    copies = fetch(
        ((specimen, tile_v), (centers, cen), (counts, cnt), (helpers, hlp)), sems
    )
    for copy in copies:
        copy.wait()
    tile = tile_v.shape[1]
    lanes = tile_v.shape[2]
    rows, cols = iota((INFO, lanes), 0), iota((INFO, lanes), 1)
    info = jnp.where(rows == 0, -1.0, 0.0)
    for j in range(centers.shape[2]):
        helper = jnp.where(j < cnt[0, 0], hlp[0, 0, j], -1)
        for r, value in enumerate((helper, cen[0, 0, j, 0], cen[0, 0, j, 1])):
            info = jnp.where((rows == r) & (cols == j), value.astype(F32), info)
    info = info.astype(BF16)
    for c in range(out.shape[0]):
        for p in range(2):
            out[c, p * tile : (p + 1) * tile] = tile_v[p].astype(BF16)
        out[c, 2 * tile :] = info


def load_kernel(probe, measured, tables, probe_out, amplitude, tables_out, raw, sems):
    copies = fetch(
        ((measured, raw), (probe, probe_out), (tables, tables_out)), sems
    )
    copies[0].wait()
    extent = raw.shape[-1]
    half = extent // 2
    shape = (extent, extent)

    def source(i):
        return jnp.where(i < half, 2 * i, 2 * (i - half) + 1)

    sort = (iota(shape, 1) == source(iota(shape, 0))).astype(F32).astype(BF16)
    sort_t = (iota(shape, 0) == source(iota(shape, 1))).astype(F32).astype(BF16)
    value = raw[0, 0, 0]
    coarse = value.astype(BF16)
    fine = (value - coarse.astype(F32)).astype(BF16)
    amplitude[...] = sum(
        dot(dot(sort, part).astype(BF16), sort_t) for part in (coarse, fine)
    )
    for copy in copies[1:]:
        copy.wait()


def frame_kernel(
    band, first, second, probe, amplitude, tables,
    to_first, to_second, centre, wide, far, spread,
):
    columns = band.shape[0]
    lanes = band.shape[2]
    tile = (band.shape[1] - INFO) // 2
    extent = probe.shape[-1]
    half = extent // 2
    modes = probe.shape[0]
    odd = lax.axis_index("row") % 2 == 1
    me = lax.axis_index("col").astype(F32)

    code = jnp.zeros((1, lanes), F32)
    for c in range(columns):
        info = band[c, 2 * tile :].astype(F32)
        hit = info[0:1] == me
        code += jnp.where(hit, c * 128.0 * 128.0 + info[1:2] * 128.0 + info[2:3], 0.0)
    code = jnp.sum(code).astype(jnp.int32)
    source = code // (128 * 128)
    row = code // 128 % 128
    col = code % 128

    for d in range(3):
        c = source + d - 1
        inside = (c >= 0) & (c < columns)
        c = jnp.clip(c, 0, columns - 1)
        for p in range(2):
            part = pl.ds(p * tile, tile)
            above = jnp.where(odd, first[c, part], second[c, part])
            below = jnp.where(odd, second[c, part], first[c, part])
            for i, block in enumerate((above, band[c, part], below)):
                wide[p, i * tile : (i + 1) * tile, d * tile : (d + 1) * tile] = jnp.where(
                    inside, block.astype(F32), 0.0
                )
    groups = extent // 8 + 1
    base = pl.multiple_of(row // 8 * 8, 8)
    step = row % 8
    window = pl.ds(base, 8 * groups)
    lane = iota((8 * groups, tile), 1)
    sub = iota((groups - 1, 8, extent), 1)
    patch = []
    for p in range(2):
        turned = [
            pltpu.roll(wide[p, window, d * tile : (d + 1) * tile], tile - col, 1)
            for d in range(3)
        ]
        shifted = jnp.concatenate(
            [jnp.where(lane < tile - col, turned[d], turned[d + 1]) for d in range(2)], 1
        )
        turned = pltpu.roll(shifted.reshape(groups, 8, extent), (8 - step) % 8, 1)
        patch.append(
            jnp.where(sub < 8 - step, turned[:-1], turned[1:]).reshape(extent, extent)
        )

    right = (tables[0], tables[2])
    left = (tables[1], tables[3])
    intensity = [jnp.zeros((half, extent), F32) for _ in range(2)]
    for k in range(modes):
        pr, pi = probe[k, 0], probe[k, 1]
        wr = pr * patch[0] - pi * patch[1]
        wi = pr * patch[1] + pi * patch[0]
        spectra = []
        for parity, sign in ((0, 1), (1, -1)):
            folded = jnp.concatenate(
                [wr[:, :half] + sign * wr[:, half:], wi[:, :half] + sign * wi[:, half:]], 1
            ).astype(BF16)
            spectra.append(dot(folded, right[parity]))
        even, odds = spectra
        for parity, sign in ((0, 1), (1, -1)):
            e = even[:half] + sign * even[half:]
            o = odds[:half] + sign * odds[half:]
            folded = quarters(e[:, :half], o[:, :half], e[:, half:], o[:, half:])
            f = dot(left[parity], folded.astype(BF16))
            far[k, parity] = f
            intensity[parity] += f[:half] * f[:half] + f[half:] * f[half:]
    factor = [
        1.0
        - amplitude[i * half : (i + 1) * half]
        * lax.rsqrt(jnp.maximum(intensity[i], 0.25))
        for i in range(2)
    ]
    grad = [[jnp.zeros((half, extent), F32) for _ in range(2)] for _ in range(2)]
    for k in range(modes):
        c = []
        for parity in range(2):
            f = far[k, parity]
            c.append(
                (f * jnp.concatenate([factor[parity], factor[parity]], 0)).astype(BF16)
            )
        a = dot(
            quarters(c[0][:half, :half], c[0][half:, :half], c[1][:half, :half], c[1][half:, :half]),
            left[0],
        )
        b = dot(
            quarters(c[0][:half, half:], c[0][half:, half:], c[1][:half, half:], c[1][half:, half:]),
            left[1],
        )
        lo, hi = (a + b).astype(BF16), (a - b).astype(BF16)
        turned = []
        for parity in range(2):
            l = lo[parity * half : (parity + 1) * half]
            h = hi[parity * half : (parity + 1) * half]
            turned.append(
                dot(
                    right[parity],
                    quarters(l[:, :half], h[:, :half], l[:, half:], h[:, half:]),
                )
            )
        for i, chi in enumerate((turned[0] + turned[1], turned[0] - turned[1])):
            cr, ci = chi[:half], chi[half:]
            pr = probe[k, 0, i * half : (i + 1) * half]
            pi = probe[k, 1, i * half : (i + 1) * half]
            grad[0][i] += pr * cr + pi * ci
            grad[1][i] += pr * ci - pi * cr

    to_first[...] = jnp.zeros_like(to_first)
    to_second[...] = jnp.zeros_like(to_second)
    centre[...] = jnp.zeros_like(centre)
    spread[...] = jnp.zeros_like(spread)
    for p in range(2):
        g = jnp.concatenate(grad[p], 0).astype(BF16).astype(F32)
        turned = pltpu.roll(g.reshape(groups - 1, 8, extent), step, 1)
        none = jnp.zeros((1, 8, extent), F32)
        g = jnp.where(
            iota((groups, 8, extent), 1) >= step,
            jnp.concatenate([turned, none], 0),
            jnp.concatenate([none, turned], 0),
        ).reshape(8 * groups, extent)
        turned = [pltpu.roll(g[:, d * tile : (d + 1) * tile], col, 1) for d in range(2)]
        spread[p, window, 0:tile] = jnp.where(lane >= col, turned[0], 0.0)
        spread[p, window, tile : 2 * tile] = jnp.where(lane >= col, turned[1], turned[0])
        spread[p, window, 2 * tile :] = jnp.where(lane < col, turned[1], 0.0)
    for d in range(3):
        c = source + d - 1

        @pl.when((c >= 0) & (c < columns))
        def _():
            for p in range(2):
                part = pl.ds(p * tile, tile)
                above, own, below = (
                    spread[p, i * tile : (i + 1) * tile, d * tile : (d + 1) * tile].astype(BF16)
                    for i in range(3)
                )
                to_first[c, part] = jnp.where(odd, above, below)
                to_second[c, part] = jnp.where(odd, below, above)
                centre[c, part] = own


def call(kernel, name, out_shape, in_specs, scratch, flops, moved, *args):
    return pl.pallas_call(
        kernel,
        out_shape=out_shape,
        in_specs=in_specs,
        out_specs=jax.tree.map(lambda _: VMEM, out_shape),
        scratch_shapes=scratch,
        compiler_params=pltpu.CompilerParams(vmem_limit_bytes=24 * 2**20),
        cost_estimate=pl.CostEstimate(flops=flops, bytes_accessed=moved, transcendentals=0),
        name=name,
    )(*args)


def per_device(specimen, probe, measured, centers, frame_counts, helper_cols):
    extent = probe.shape[-1]
    half = extent // 2
    tile = specimen.shape[1]
    modes = probe.shape[0]
    columns = lax.axis_size("col")
    height = 2 * tile
    block = jax.ShapeDtypeStruct((columns, height, tile), BF16)
    dma = pltpu.SemaphoreType.DMA

    packed = call(
        pack_kernel, "pack",
        jax.ShapeDtypeStruct((columns, height + INFO, tile), BF16),
        [ANY] * 4,
        [
            pltpu.VMEM(specimen.shape, F32),
            pltpu.SMEM(centers.shape, jnp.int32),
            pltpu.SMEM(frame_counts.shape, jnp.int32),
            pltpu.SMEM(helper_cols.shape, jnp.int32),
            dma((4,)),
        ],
        10**5, 2**19,
        specimen, centers, frame_counts, helper_cols,
    )
    tables = dft_tables(extent)
    probe, amplitude, tables = call(
        load_kernel, "load",
        (
            jax.ShapeDtypeStruct(probe.shape, F32),
            jax.ShapeDtypeStruct((extent, extent), F32),
            jax.ShapeDtypeStruct(tables.shape, BF16),
        ),
        [ANY] * 3,
        [pltpu.VMEM(measured.shape, F32), dma((3,))],
        10**8, 2**22,
        probe, measured, tables,
    )
    band = lax.all_to_all(packed, "col", split_axis=0, concat_axis=0, tiled=True)

    rows = lax.axis_size("row")
    swaps = []
    for start in (0, 1):
        pairs = [(i, i + 1) for i in range(start, rows - 1, 2)]
        swaps.append(pairs + [(b, a) for a, b in pairs])
    second = lax.ppermute(band, "row", swaps[1])
    first = lax.ppermute(band, "row", swaps[0])
    to_first, to_second, centre = call(
        frame_kernel, "frame",
        (block, block, block),
        [VMEM] * 6,
        [
            pltpu.VMEM((2, tile + 2 * half, 3 * tile), F32),
            pltpu.VMEM((modes, 2, extent, extent), F32),
            pltpu.VMEM((2, tile + 2 * half, 3 * tile), F32),
        ],
        2 * 10**9, 2**22,
        band, first, second, probe, amplitude, tables,
    )
    from_second = lax.ppermute(to_second, "row", swaps[1])
    from_first = lax.ppermute(to_first, "row", swaps[0])
    summed = centre.astype(F32) + from_second.astype(F32) + from_first.astype(F32)
    shares = lax.all_to_all(
        summed.astype(BF16), "col", split_axis=0, concat_axis=0, tiled=True
    )
    return jnp.sum(shares.astype(F32), axis=0).reshape(2, tile, tile)


def solution(mesh):
    return jax.shard_map(
        per_device,
        mesh=mesh,
        in_specs=(
            P(None, "row", "col"),
            P(),
            P("row", "col", None, None, None),
            P("row", "col", None, None),
            P("row", "col"),
            P("row", "col", None),
        ),
        out_specs=P(None, "row", "col"),
        check_vma=False,
    )
```

```python
import functools
import math

import jax
import jax.numpy as jnp
import numpy as np
from jax import lax
from jax.experimental import pallas as pl
from jax.experimental.pallas import tpu as pltpu
from jax.sharding import PartitionSpec as P

F32 = jnp.float32
BF16 = jnp.bfloat16
INFO = 16
VMEM = pl.BlockSpec(memory_space=pltpu.VMEM)
SMEM = pl.BlockSpec(memory_space=pltpu.SMEM)
HBM = pl.BlockSpec(memory_space=pltpu.HBM)


def dft_tables(extent):
    half = extent // 2
    steps = np.arange(extent, dtype=np.int32)
    angles = (steps[:, None] * steps[None, :] % extent).astype(np.float32)
    angles = angles * np.float32(2.0 * math.pi / extent)
    scaling = np.float32(1.0 / math.sqrt(extent))
    real = (np.cos(angles) * scaling).astype(BF16)
    imag = (-np.sin(angles) * scaling).astype(BF16)
    tables = []
    for parity in (0, 1):
        re, im = real[:half, parity::2], imag[:half, parity::2]
        right = np.concatenate(
            [np.concatenate([re, im], 1), np.concatenate([-im, re], 1)], 0
        )
        tables += [right, np.ascontiguousarray(right.T)]
    return jnp.asarray(np.stack(tables))


def dot(a, b):
    return jnp.dot(a, b, preferred_element_type=F32)


def quarters(tl, tr, bl, br):
    return jnp.concatenate(
        [jnp.concatenate([tl, tr], 1), jnp.concatenate([bl, br], 1)], 0
    )


def iota(shape, dim):
    return lax.broadcasted_iota(jnp.int32, shape, dim)


def fetch(pairs, sems):
    copies = [
        pltpu.make_async_copy(source, target, sems.at[i])
        for i, (source, target) in enumerate(pairs)
    ]
    for copy in copies:
        copy.start()
    return copies


def pack_kernel(specimen, centers, cnt, helpers, out, tile_v, cen, hlp, sems):
    copies = fetch(((specimen, tile_v), (centers, cen), (helpers, hlp)), sems)
    for copy in copies:
        copy.wait()
    tile = tile_v.shape[1]
    lanes = tile_v.shape[2]
    rows, cols = iota((INFO, lanes), 0), iota((INFO, lanes), 1)
    info = jnp.where(rows == 0, -1.0, 0.0)
    for j in range(centers.shape[2]):
        helper = jnp.where(j < cnt[0, 0], hlp[0, 0, j], -1)
        for r, value in enumerate((helper, cen[0, 0, j, 0], cen[0, 0, j, 1])):
            info = jnp.where((rows == r) & (cols == j), value.astype(F32), info)
    info = info.astype(BF16)
    for c in range(out.shape[0]):
        for p in range(2):
            out[c, p * tile : (p + 1) * tile] = tile_v[p].astype(BF16)
        out[c, 2 * tile :] = info


def load_kernel(probe, measured, tables, probe_out, amplitude, tables_out, raw, sems):
    copies = fetch(
        ((measured, raw), (probe, probe_out), (tables, tables_out)), sems
    )
    copies[0].wait()
    extent = raw.shape[-1]
    half = extent // 2
    shape = (extent, extent)

    def source(i):
        return jnp.where(i < half, 2 * i, 2 * (i - half) + 1)

    sort = (iota(shape, 1) == source(iota(shape, 0))).astype(F32).astype(BF16)
    sort_t = (iota(shape, 0) == source(iota(shape, 1))).astype(F32).astype(BF16)
    value = raw[0, 0, 0]
    coarse = value.astype(BF16)
    fine = (value - coarse.astype(F32)).astype(BF16)
    amplitude[...] = sum(
        dot(dot(sort, part).astype(BF16), sort_t) for part in (coarse, fine)
    )
    for copy in copies[1:]:
        copy.wait()


def frame_kernel(
    band, first, second, probe, amplitude, tables,
    to_first, to_second, centre, wide, far, spread,
):
    columns = band.shape[0]
    lanes = band.shape[2]
    tile = (band.shape[1] - INFO) // 2
    extent = probe.shape[-1]
    half = extent // 2
    modes = probe.shape[0]
    odd = lax.axis_index("row") % 2 == 1
    me = lax.axis_index("col").astype(F32)

    code = jnp.zeros((1, lanes), F32)
    for c in range(columns):
        info = band[c, 2 * tile :].astype(F32)
        hit = info[0:1] == me
        code += jnp.where(hit, c * 128.0 * 128.0 + info[1:2] * 128.0 + info[2:3], 0.0)
    code = jnp.sum(code).astype(jnp.int32)
    source = code // (128 * 128)
    row = code // 128 % 128
    col = code % 128

    for d in range(3):
        c = source + d - 1
        inside = (c >= 0) & (c < columns)
        c = jnp.clip(c, 0, columns - 1)
        for p in range(2):
            part = pl.ds(p * tile, tile)
            above = jnp.where(odd, first[c, part], second[c, part])
            below = jnp.where(odd, second[c, part], first[c, part])
            for i, block in enumerate((above, band[c, part], below)):
                wide[p, i * tile : (i + 1) * tile, d * tile : (d + 1) * tile] = jnp.where(
                    inside, block.astype(F32), 0.0
                )
    groups = extent // 8 + 1
    base = pl.multiple_of(row // 8 * 8, 8)
    step = row % 8
    window = pl.ds(base, 8 * groups)
    lane = iota((8 * groups, tile), 1)
    sub = iota((groups - 1, 8, extent), 1)
    patch = []
    for p in range(2):
        turned = [
            pltpu.roll(wide[p, window, d * tile : (d + 1) * tile], tile - col, 1)
            for d in range(3)
        ]
        shifted = jnp.concatenate(
            [jnp.where(lane < tile - col, turned[d], turned[d + 1]) for d in range(2)], 1
        )
        turned = pltpu.roll(shifted.reshape(groups, 8, extent), (8 - step) % 8, 1)
        patch.append(
            jnp.where(sub < 8 - step, turned[:-1], turned[1:]).reshape(extent, extent)
        )

    right = (tables[0], tables[2])
    left = (tables[1], tables[3])
    intensity = [jnp.zeros((half, extent), F32) for _ in range(2)]
    for k in range(modes):
        pr, pi = probe[k, 0], probe[k, 1]
        wr = pr * patch[0] - pi * patch[1]
        wi = pr * patch[1] + pi * patch[0]
        spectra = []
        for parity, sign in ((0, 1), (1, -1)):
            folded = jnp.concatenate(
                [wr[:, :half] + sign * wr[:, half:], wi[:, :half] + sign * wi[:, half:]], 1
            ).astype(BF16)
            spectra.append(dot(folded, right[parity]))
        even, odds = spectra
        for parity, sign in ((0, 1), (1, -1)):
            e = even[:half] + sign * even[half:]
            o = odds[:half] + sign * odds[half:]
            folded = quarters(e[:, :half], o[:, :half], e[:, half:], o[:, half:])
            f = dot(left[parity], folded.astype(BF16))
            far[k, parity] = f
            intensity[parity] += f[:half] * f[:half] + f[half:] * f[half:]
    factor = [
        1.0
        - amplitude[i * half : (i + 1) * half]
        * lax.rsqrt(jnp.maximum(intensity[i], 0.25))
        for i in range(2)
    ]
    grad = [[jnp.zeros((half, extent), F32) for _ in range(2)] for _ in range(2)]
    for k in range(modes):
        c = []
        for parity in range(2):
            f = far[k, parity]
            c.append(
                (f * jnp.concatenate([factor[parity], factor[parity]], 0)).astype(BF16)
            )
        a = dot(
            quarters(c[0][:half, :half], c[0][half:, :half], c[1][:half, :half], c[1][half:, :half]),
            left[0],
        )
        b = dot(
            quarters(c[0][:half, half:], c[0][half:, half:], c[1][:half, half:], c[1][half:, half:]),
            left[1],
        )
        lo, hi = (a + b).astype(BF16), (a - b).astype(BF16)
        turned = []
        for parity in range(2):
            l = lo[parity * half : (parity + 1) * half]
            h = hi[parity * half : (parity + 1) * half]
            turned.append(
                dot(
                    right[parity],
                    quarters(l[:, :half], h[:, :half], l[:, half:], h[:, half:]),
                )
            )
        for i, chi in enumerate((turned[0] + turned[1], turned[0] - turned[1])):
            cr, ci = chi[:half], chi[half:]
            pr = probe[k, 0, i * half : (i + 1) * half]
            pi = probe[k, 1, i * half : (i + 1) * half]
            grad[0][i] += pr * cr + pi * ci
            grad[1][i] += pr * ci - pi * cr

    spread[...] = jnp.zeros_like(spread)
    for p in range(2):
        g = jnp.concatenate(grad[p], 0).astype(BF16).astype(F32)
        turned = pltpu.roll(g.reshape(groups - 1, 8, extent), step, 1)
        none = jnp.zeros((1, 8, extent), F32)
        spread[p, window, :] = jnp.where(
            iota((groups, 8, extent), 1) >= step,
            jnp.concatenate([turned, none], 0),
            jnp.concatenate([none, turned], 0),
        ).reshape(8 * groups, extent)
    which = iota((INFO, extent), 0)
    info = jnp.where(which == 0, source, col).astype(F32).astype(BF16)
    for p in range(2):
        part = pl.ds(p * tile, tile)
        above, own, below = (
            spread[p, i * tile : (i + 1) * tile].astype(BF16) for i in range(3)
        )
        to_first[part] = jnp.where(odd, above, below)
        to_second[part] = jnp.where(odd, below, above)
        centre[part] = own
    for out in (to_first, to_second, centre):
        out[2 * tile :] = info


def fold_kernel(centre, first, second, out):
    columns, height, tile = out.shape
    extent = centre.shape[1]
    half = extent // 2
    gradients, places = [], []
    for part in (centre, first, second):
        source = part[height : height + 1, :].astype(F32).astype(jnp.int32)
        col = part[height + 1 : height + 2, :].astype(F32).astype(jnp.int32)
        start = jnp.concatenate([source * tile + col - half] * (columns * tile // extent), 1)
        shape = (extent, columns * tile)
        places.append((iota(shape, 1) - iota(shape, 0) == start).astype(F32).astype(BF16))
        gradients.append(part[:height])
    total = dot(jnp.concatenate(gradients, 1), jnp.concatenate(places, 0))
    for c in range(columns):
        out[c] = total[:, c * tile : (c + 1) * tile].astype(BF16)


def call(kernel, name, out_shape, in_specs, scratch, flops, moved, *args):
    args = [
        pltpu.with_memory_space_constraint(arg, pltpu.HBM) if spec is HBM else arg
        for arg, spec in zip(args, in_specs)
    ]
    return pl.pallas_call(
        kernel,
        out_shape=out_shape,
        in_specs=in_specs,
        out_specs=jax.tree.map(lambda _: VMEM, out_shape),
        scratch_shapes=scratch,
        compiler_params=pltpu.CompilerParams(vmem_limit_bytes=24 * 2**20),
        cost_estimate=pl.CostEstimate(flops=flops, bytes_accessed=moved, transcendentals=0),
        name=name,
    )(*args)


def per_device(specimen, probe, measured, centers, frame_counts, helper_cols):
    extent = probe.shape[-1]
    half = extent // 2
    tile = specimen.shape[1]
    modes = probe.shape[0]
    columns = lax.axis_size("col")
    height = 2 * tile
    part = jax.ShapeDtypeStruct((height + INFO, extent), BF16)
    dma = pltpu.SemaphoreType.DMA

    packed = call(
        pack_kernel, "pack",
        jax.ShapeDtypeStruct((columns, height + INFO, tile), BF16),
        [HBM, HBM, SMEM, HBM],
        [
            pltpu.VMEM(specimen.shape, F32),
            pltpu.SMEM(centers.shape, jnp.int32),
            pltpu.SMEM(helper_cols.shape, jnp.int32),
            dma((3,)),
        ],
        10**5, 2**19,
        specimen, centers, frame_counts, helper_cols,
    )
    tables = dft_tables(extent)
    probe, amplitude, tables = call(
        load_kernel, "load",
        (
            jax.ShapeDtypeStruct(probe.shape, F32),
            jax.ShapeDtypeStruct((extent, extent), F32),
            jax.ShapeDtypeStruct(tables.shape, BF16),
        ),
        [HBM] * 3,
        [pltpu.VMEM(measured.shape, F32), dma((3,))],
        10**8, 2**22,
        probe, measured, tables,
    )
    band = lax.all_to_all(packed, "col", split_axis=0, concat_axis=0, tiled=True)

    rows = lax.axis_size("row")
    swaps = []
    for start in (0, 1):
        pairs = [(i, i + 1) for i in range(start, rows - 1, 2)]
        swaps.append(pairs + [(b, a) for a, b in pairs])
    second = lax.ppermute(band, "row", swaps[1])
    first = lax.ppermute(band, "row", swaps[0])
    to_first, to_second, centre = call(
        frame_kernel, "frame",
        (part, part, part),
        [VMEM] * 6,
        [
            pltpu.VMEM((2, tile + 2 * half, 3 * tile), F32),
            pltpu.VMEM((modes, 2, extent, extent), F32),
            pltpu.VMEM((2, tile + 2 * half, extent), F32),
        ],
        2 * 10**9, 2**22,
        band, first, second, probe, amplitude, tables,
    )
    from_second = lax.ppermute(to_second, "row", swaps[1])
    from_first = lax.ppermute(to_first, "row", swaps[0])
    summed = call(
        fold_kernel, "fold",
        jax.ShapeDtypeStruct((columns, height, tile), BF16),
        [VMEM] * 3,
        [],
        10**9, 2**20,
        centre, from_first, from_second,
    )
    shares = lax.all_to_all(summed, "col", split_axis=0, concat_axis=0, tiled=True)
    return jnp.sum(shares.astype(F32), axis=0).reshape(2, tile, tile)


def solution(mesh):
    return jax.shard_map(
        per_device,
        mesh=mesh,
        in_specs=(
            P(None, "row", "col"),
            P(),
            P("row", "col", None, None, None),
            P("row", "col", None, None),
            P("row", "col"),
            P("row", "col", None),
        ),
        out_specs=P(None, "row", "col"),
        check_vma=False,
    )
```

```python
import functools
import math

import jax
import jax.numpy as jnp
import numpy as np
from jax import lax
from jax.experimental import pallas as pl
from jax.experimental.pallas import tpu as pltpu
from jax.sharding import PartitionSpec as P

F32 = jnp.float32
BF16 = jnp.bfloat16
INFO = 16
VMEM = pl.BlockSpec(memory_space=pltpu.VMEM)
SMEM = pl.BlockSpec(memory_space=pltpu.SMEM)
HBM = pl.BlockSpec(memory_space=pltpu.HBM)


def dft_tables(extent):
    half = extent // 2
    steps = np.arange(extent, dtype=np.int32)
    angles = (steps[:, None] * steps[None, :] % extent).astype(np.float32)
    angles = angles * np.float32(2.0 * math.pi / extent)
    scaling = np.float32(1.0 / math.sqrt(extent))
    real = (np.cos(angles) * scaling).astype(BF16)
    imag = (-np.sin(angles) * scaling).astype(BF16)
    tables = []
    for parity in (0, 1):
        re, im = real[:half, parity::2], imag[:half, parity::2]
        right = np.concatenate(
            [np.concatenate([re, im], 1), np.concatenate([-im, re], 1)], 0
        )
        tables += [right, np.ascontiguousarray(right.T)]
    return jnp.asarray(np.stack(tables))


def dot(a, b):
    return jnp.dot(a, b, preferred_element_type=F32)


def quarters(tl, tr, bl, br):
    return jnp.concatenate(
        [jnp.concatenate([tl, tr], 1), jnp.concatenate([bl, br], 1)], 0
    )


def iota(shape, dim):
    return lax.broadcasted_iota(jnp.int32, shape, dim)


def fetch(pairs, sems):
    copies = [
        pltpu.make_async_copy(source, target, sems.at[i])
        for i, (source, target) in enumerate(pairs)
    ]
    for copy in copies:
        copy.start()
    return copies


def pack_kernel(specimen, centers, cnt, helpers, out, tile_v, cen, hlp, sems):
    copies = fetch(((specimen, tile_v), (centers, cen), (helpers, hlp)), sems)
    for copy in copies:
        copy.wait()
    tile = tile_v.shape[1]
    lanes = tile_v.shape[2]
    rows, cols = iota((INFO, lanes), 0), iota((INFO, lanes), 1)
    info = jnp.where(rows == 0, -1.0, 0.0)
    for j in range(centers.shape[2]):
        helper = jnp.where(j < cnt[0, 0], hlp[0, 0, j], -1)
        for r, value in enumerate((helper, cen[0, 0, j, 0], cen[0, 0, j, 1])):
            info = jnp.where((rows == r) & (cols == j), value.astype(F32), info)
    info = info.astype(BF16)
    for p in range(2):
        out[p * tile : (p + 1) * tile] = tile_v[p].astype(BF16)
    out[2 * tile :] = info


def load_kernel(probe, measured, tables, probe_out, amplitude, tables_out, raw, sems):
    copies = fetch(
        ((measured, raw), (probe, probe_out), (tables, tables_out)), sems
    )
    copies[0].wait()
    extent = raw.shape[-1]
    half = extent // 2
    shape = (extent, extent)

    def source(i):
        return jnp.where(i < half, 2 * i, 2 * (i - half) + 1)

    sort = (iota(shape, 1) == source(iota(shape, 0))).astype(F32).astype(BF16)
    sort_t = (iota(shape, 0) == source(iota(shape, 1))).astype(F32).astype(BF16)
    value = raw[0, 0, 0]
    coarse = value.astype(BF16)
    fine = (value - coarse.astype(F32)).astype(BF16)
    amplitude[...] = sum(
        dot(dot(sort, part).astype(BF16), sort_t) for part in (coarse, fine)
    )
    for copy in copies[1:]:
        copy.wait()


def frame_kernel(
    band, first, second, probe, amplitude, tables,
    to_second, to_first, centre, wide, far, spread,
):
    columns = band.shape[0]
    lanes = band.shape[2]
    tile = (band.shape[1] - INFO) // 2
    extent = probe.shape[-1]
    half = extent // 2
    modes = probe.shape[0]
    odd = lax.axis_index("row") % 2 == 1
    me = lax.axis_index("col").astype(F32)

    code = jnp.zeros((1, lanes), F32)
    for c in range(columns):
        info = band[c, 2 * tile :].astype(F32)
        hit = info[0:1] == me
        code += jnp.where(hit, c * 128.0 * 128.0 + info[1:2] * 128.0 + info[2:3], 0.0)
    code = jnp.sum(code).astype(jnp.int32)
    source = code // (128 * 128)
    row = code // 128 % 128
    col = code % 128

    for d in range(3):
        c = source + d - 1
        inside = (c >= 0) & (c < columns)
        c = jnp.clip(c, 0, columns - 1)
        for p in range(2):
            part = pl.ds(p * tile, tile)
            above = jnp.where(odd, first[c, part], second[c, part])
            below = jnp.where(odd, second[c, part], first[c, part])
            for i, block in enumerate((above, band[c, part], below)):
                wide[p, i * tile : (i + 1) * tile, d * tile : (d + 1) * tile] = jnp.where(
                    inside, block.astype(F32), 0.0
                )
    groups = extent // 8 + 1
    base = pl.multiple_of(row // 8 * 8, 8)
    step = row % 8
    window = pl.ds(base, 8 * groups)
    lane = iota((8 * groups, tile), 1)
    sub = iota((groups - 1, 8, extent), 1)
    patch = []
    for p in range(2):
        turned = [
            pltpu.roll(wide[p, window, d * tile : (d + 1) * tile], tile - col, 1)
            for d in range(3)
        ]
        shifted = jnp.concatenate(
            [jnp.where(lane < tile - col, turned[d], turned[d + 1]) for d in range(2)], 1
        )
        turned = pltpu.roll(shifted.reshape(groups, 8, extent), (8 - step) % 8, 1)
        patch.append(
            jnp.where(sub < 8 - step, turned[:-1], turned[1:]).reshape(extent, extent)
        )

    right = (tables[0], tables[2])
    left = (tables[1], tables[3])
    intensity = [jnp.zeros((half, extent), F32) for _ in range(2)]
    for k in range(modes):
        pr, pi = probe[k, 0], probe[k, 1]
        wr = pr * patch[0] - pi * patch[1]
        wi = pr * patch[1] + pi * patch[0]
        spectra = []
        for parity, sign in ((0, 1), (1, -1)):
            folded = jnp.concatenate(
                [wr[:, :half] + sign * wr[:, half:], wi[:, :half] + sign * wi[:, half:]], 1
            ).astype(BF16)
            spectra.append(dot(folded, right[parity]))
        even, odds = spectra
        for parity, sign in ((0, 1), (1, -1)):
            e = even[:half] + sign * even[half:]
            o = odds[:half] + sign * odds[half:]
            folded = quarters(e[:, :half], o[:, :half], e[:, half:], o[:, half:])
            f = dot(left[parity], folded.astype(BF16))
            far[k, parity] = f
            intensity[parity] += f[:half] * f[:half] + f[half:] * f[half:]
    factor = [
        1.0
        - amplitude[i * half : (i + 1) * half]
        * lax.rsqrt(jnp.maximum(intensity[i], 0.25))
        for i in range(2)
    ]
    grad = [[jnp.zeros((half, extent), F32) for _ in range(2)] for _ in range(2)]
    for k in range(modes):
        c = []
        for parity in range(2):
            f = far[k, parity]
            c.append(
                (f * jnp.concatenate([factor[parity], factor[parity]], 0)).astype(BF16)
            )
        a = dot(
            quarters(c[0][:half, :half], c[0][half:, :half], c[1][:half, :half], c[1][half:, :half]),
            left[0],
        )
        b = dot(
            quarters(c[0][:half, half:], c[0][half:, half:], c[1][:half, half:], c[1][half:, half:]),
            left[1],
        )
        lo, hi = (a + b).astype(BF16), (a - b).astype(BF16)
        turned = []
        for parity in range(2):
            l = lo[parity * half : (parity + 1) * half]
            h = hi[parity * half : (parity + 1) * half]
            turned.append(
                dot(
                    right[parity],
                    quarters(l[:, :half], h[:, :half], l[:, half:], h[:, half:]),
                )
            )
        for i, chi in enumerate((turned[0] + turned[1], turned[0] - turned[1])):
            cr, ci = chi[:half], chi[half:]
            pr = probe[k, 0, i * half : (i + 1) * half]
            pi = probe[k, 1, i * half : (i + 1) * half]
            grad[0][i] += pr * cr + pi * ci
            grad[1][i] += pr * ci - pi * cr

    spread[...] = jnp.zeros_like(spread)
    for p in range(2):
        g = jnp.concatenate(grad[p], 0).astype(BF16).astype(F32)
        turned = pltpu.roll(g.reshape(groups - 1, 8, extent), step, 1)
        none = jnp.zeros((1, 8, extent), F32)
        spread[p, window, :] = jnp.where(
            iota((groups, 8, extent), 1) >= step,
            jnp.concatenate([turned, none], 0),
            jnp.concatenate([none, turned], 0),
        ).reshape(8 * groups, extent)
    which = iota((INFO, extent), 0)
    info = jnp.where(which == 0, source, col).astype(F32).astype(BF16)
    for p in range(2):
        part = pl.ds(p * tile, tile)
        above, own, below = (
            spread[p, i * tile : (i + 1) * tile].astype(BF16) for i in range(3)
        )
        to_first[part] = jnp.where(odd, above, below)
        to_second[part] = jnp.where(odd, below, above)
        centre[part] = own
    for out in (to_first, to_second, centre):
        out[2 * tile :] = info


def fold_kernel(centre, first, second, out):
    columns, height, tile = out.shape
    extent = centre.shape[1]
    half = extent // 2
    gradients, places = [], []
    for part in (centre, first, second):
        source = part[height : height + 1, :].astype(F32).astype(jnp.int32)
        col = part[height + 1 : height + 2, :].astype(F32).astype(jnp.int32)
        start = jnp.concatenate([source * tile + col - half] * (columns * tile // extent), 1)
        shape = (extent, columns * tile)
        places.append((iota(shape, 1) - iota(shape, 0) == start).astype(F32).astype(BF16))
        gradients.append(part[:height])
    total = dot(jnp.concatenate(gradients, 1), jnp.concatenate(places, 0))
    for c in range(columns):
        out[c] = total[:, c * tile : (c + 1) * tile].astype(BF16)


def call(kernel, name, out_shape, in_specs, scratch, flops, moved, *args):
    args = [
        pltpu.with_memory_space_constraint(arg, pltpu.HBM) if spec is HBM else arg
        for arg, spec in zip(args, in_specs)
    ]
    return pl.pallas_call(
        kernel,
        out_shape=out_shape,
        in_specs=in_specs,
        out_specs=jax.tree.map(lambda _: VMEM, out_shape),
        scratch_shapes=scratch,
        compiler_params=pltpu.CompilerParams(vmem_limit_bytes=24 * 2**20),
        cost_estimate=pl.CostEstimate(flops=flops, bytes_accessed=moved, transcendentals=0),
        name=name,
    )(*args)


def per_device(specimen, probe, measured, centers, frame_counts, helper_cols):
    extent = probe.shape[-1]
    half = extent // 2
    tile = specimen.shape[1]
    modes = probe.shape[0]
    columns = lax.axis_size("col")
    height = 2 * tile
    part = jax.ShapeDtypeStruct((height + INFO, extent), BF16)
    dma = pltpu.SemaphoreType.DMA

    packed = call(
        pack_kernel, "pack",
        jax.ShapeDtypeStruct((height + INFO, tile), BF16),
        [HBM, HBM, SMEM, HBM],
        [
            pltpu.VMEM(specimen.shape, F32),
            pltpu.SMEM(centers.shape, jnp.int32),
            pltpu.SMEM(helper_cols.shape, jnp.int32),
            dma((3,)),
        ],
        10**5, 2**19,
        specimen, centers, frame_counts, helper_cols,
    )
    tables = dft_tables(extent)
    probe, amplitude, tables = call(
        load_kernel, "load",
        (
            jax.ShapeDtypeStruct(probe.shape, F32),
            jax.ShapeDtypeStruct((extent, extent), F32),
            jax.ShapeDtypeStruct(tables.shape, BF16),
        ),
        [HBM] * 3,
        [pltpu.VMEM(measured.shape, F32), dma((3,))],
        10**8, 2**22,
        probe, measured, tables,
    )
    band = lax.all_gather(packed, "col")

    rows = lax.axis_size("row")
    swaps = []
    for start in (0, 1):
        pairs = [(i, i + 1) for i in range(start, rows - 1, 2)]
        swaps.append(pairs + [(b, a) for a, b in pairs])
    second = lax.ppermute(band, "row", swaps[1])
    first = lax.ppermute(band, "row", swaps[0])
    to_second, to_first, centre = call(
        frame_kernel, "frame",
        (part, part, part),
        [VMEM] * 6,
        [
            pltpu.VMEM((2, tile + 2 * half, 3 * tile), F32),
            pltpu.VMEM((modes, 2, extent, extent), F32),
            pltpu.VMEM((2, tile + 2 * half, extent), F32),
        ],
        2 * 10**9, 2**22,
        band, first, second, probe, amplitude, tables,
    )
    from_second = lax.ppermute(to_second, "row", swaps[1])
    from_first = lax.ppermute(to_first, "row", swaps[0])
    summed = call(
        fold_kernel, "fold",
        jax.ShapeDtypeStruct((columns, height, tile), BF16),
        [VMEM] * 3,
        [],
        10**9, 2**20,
        centre, from_first, from_second,
    )
    shares = lax.all_to_all(summed, "col", split_axis=0, concat_axis=0, tiled=True)
    return jnp.sum(shares.astype(F32), axis=0).reshape(2, tile, tile)


def solution(mesh):
    return jax.shard_map(
        per_device,
        mesh=mesh,
        in_specs=(
            P(None, "row", "col"),
            P(),
            P("row", "col", None, None, None),
            P("row", "col", None, None),
            P("row", "col"),
            P("row", "col", None),
        ),
        out_specs=P(None, "row", "col"),
        check_vma=False,
    )
```

```python
import functools
import math

import jax
import jax.numpy as jnp
import numpy as np
from jax import lax
from jax.experimental import pallas as pl
from jax.experimental.pallas import tpu as pltpu
from jax.sharding import PartitionSpec as P

F32 = jnp.float32
BF16 = jnp.bfloat16
INFO = 16
VMEM = pl.BlockSpec(memory_space=pltpu.VMEM)
SMEM = pl.BlockSpec(memory_space=pltpu.SMEM)
HBM = pl.BlockSpec(memory_space=pltpu.HBM)


def dft_tables(extent):
    half = extent // 2
    steps = np.arange(extent, dtype=np.int32)
    angles = (steps[:, None] * steps[None, :] % extent).astype(np.float32)
    angles = angles * np.float32(2.0 * math.pi / extent)
    scaling = np.float32(1.0 / math.sqrt(extent))
    real = (np.cos(angles) * scaling).astype(BF16)
    imag = (-np.sin(angles) * scaling).astype(BF16)
    tables = []
    for parity in (0, 1):
        re, im = real[:half, parity::2], imag[:half, parity::2]
        right = np.concatenate(
            [np.concatenate([re, im], 1), np.concatenate([-im, re], 1)], 0
        )
        tables += [right, np.ascontiguousarray(right.T)]
    return jnp.asarray(np.stack(tables))


def dot(a, b):
    return jnp.dot(a, b, preferred_element_type=F32)


def quarters(tl, tr, bl, br):
    return jnp.concatenate(
        [jnp.concatenate([tl, tr], 1), jnp.concatenate([bl, br], 1)], 0
    )


def iota(shape, dim):
    return lax.broadcasted_iota(jnp.int32, shape, dim)


def fetch(pairs, sems):
    copies = [
        pltpu.make_async_copy(source, target, sems.at[i])
        for i, (source, target) in enumerate(pairs)
    ]
    for copy in copies:
        copy.start()
    return copies


def pack_kernel(specimen, centers, cnt, helpers, out, tile_v, cen, hlp, sems):
    copies = fetch(((specimen, tile_v), (centers, cen), (helpers, hlp)), sems)
    for copy in copies:
        copy.wait()
    tile = tile_v.shape[1]
    lanes = tile_v.shape[2]
    rows, cols = iota((INFO, lanes), 0), iota((INFO, lanes), 1)
    info = jnp.where(rows == 0, -1.0, 0.0)
    for j in range(centers.shape[2]):
        helper = jnp.where(j < cnt[0, 0], hlp[0, 0, j], -1)
        for r, value in enumerate((helper, cen[0, 0, j, 0], cen[0, 0, j, 1])):
            info = jnp.where((rows == r) & (cols == j), value.astype(F32), info)
    info = info.astype(BF16)
    for p in range(2):
        out[p * tile : (p + 1) * tile] = tile_v[p].astype(BF16)
    out[2 * tile :] = info


def load_kernel(probe, measured, tables, probe_out, amplitude, tables_out, raw, sems):
    copies = fetch(
        ((measured, raw), (probe, probe_out), (tables, tables_out)), sems
    )
    copies[0].wait()
    extent = raw.shape[-1]
    half = extent // 2
    shape = (extent, extent)

    def source(i):
        return jnp.where(i < half, 2 * i, 2 * (i - half) + 1)

    sort = (iota(shape, 1) == source(iota(shape, 0))).astype(F32).astype(BF16)
    sort_t = (iota(shape, 0) == source(iota(shape, 1))).astype(F32).astype(BF16)
    value = raw[0, 0, 0]
    coarse = value.astype(BF16)
    fine = (value - coarse.astype(F32)).astype(BF16)
    amplitude[...] = sum(
        dot(dot(sort, part).astype(BF16), sort_t) for part in (coarse, fine)
    )
    for copy in copies[1:]:
        copy.wait()


def frame_kernel(
    band, first, second_lo, second_hi, probe, amplitude, tables,
    to_second, to_first, centre, wide, far, spread,
):
    columns = band.shape[0]
    lanes = band.shape[2]
    tile = (band.shape[1] - INFO) // 2
    extent = probe.shape[-1]
    half = extent // 2
    modes = probe.shape[0]
    odd = lax.axis_index("row") % 2 == 1
    me = lax.axis_index("col").astype(F32)

    code = jnp.zeros((1, lanes), F32)
    for c in range(columns):
        info = band[c, 2 * tile :].astype(F32)
        hit = info[0:1] == me
        code += jnp.where(hit, c * 128.0 * 128.0 + info[1:2] * 128.0 + info[2:3], 0.0)
    code = jnp.sum(code).astype(jnp.int32)
    source = code // (128 * 128)
    row = code // 128 % 128
    col = code % 128

    for d in range(3):
        c = source + d - 1
        inside = (c >= 0) & (c < columns)
        c = jnp.clip(c, 0, columns - 1)
        for p in range(2):
            part = pl.ds(p * tile, tile)
            pair = second_lo.shape[0]
            other = jnp.where(
                c < pair,
                second_lo[jnp.minimum(c, pair - 1), part],
                second_hi[jnp.maximum(c - pair, 0), part],
            )
            above = jnp.where(odd, first[c, part], other)
            below = jnp.where(odd, other, first[c, part])
            for i, block in enumerate((above, band[c, part], below)):
                wide[p, i * tile : (i + 1) * tile, d * tile : (d + 1) * tile] = jnp.where(
                    inside, block.astype(F32), 0.0
                )
    groups = extent // 8 + 1
    base = pl.multiple_of(row // 8 * 8, 8)
    step = row % 8
    window = pl.ds(base, 8 * groups)
    lane = iota((8 * groups, tile), 1)
    sub = iota((groups - 1, 8, extent), 1)
    patch = []
    for p in range(2):
        turned = [
            pltpu.roll(wide[p, window, d * tile : (d + 1) * tile], tile - col, 1)
            for d in range(3)
        ]
        shifted = jnp.concatenate(
            [jnp.where(lane < tile - col, turned[d], turned[d + 1]) for d in range(2)], 1
        )
        turned = pltpu.roll(shifted.reshape(groups, 8, extent), (8 - step) % 8, 1)
        patch.append(
            jnp.where(sub < 8 - step, turned[:-1], turned[1:]).reshape(extent, extent)
        )

    right = (tables[0], tables[2])
    left = (tables[1], tables[3])
    intensity = [jnp.zeros((half, extent), F32) for _ in range(2)]
    for k in range(modes):
        pr, pi = probe[k, 0], probe[k, 1]
        wr = pr * patch[0] - pi * patch[1]
        wi = pr * patch[1] + pi * patch[0]
        spectra = []
        for parity, sign in ((0, 1), (1, -1)):
            folded = jnp.concatenate(
                [wr[:, :half] + sign * wr[:, half:], wi[:, :half] + sign * wi[:, half:]], 1
            ).astype(BF16)
            spectra.append(dot(folded, right[parity]))
        even, odds = spectra
        for parity, sign in ((0, 1), (1, -1)):
            e = even[:half] + sign * even[half:]
            o = odds[:half] + sign * odds[half:]
            folded = quarters(e[:, :half], o[:, :half], e[:, half:], o[:, half:])
            f = dot(left[parity], folded.astype(BF16))
            far[k, parity] = f
            intensity[parity] += f[:half] * f[:half] + f[half:] * f[half:]
    factor = [
        1.0
        - amplitude[i * half : (i + 1) * half]
        * lax.rsqrt(jnp.maximum(intensity[i], 0.25))
        for i in range(2)
    ]
    grad = [[jnp.zeros((half, extent), F32) for _ in range(2)] for _ in range(2)]
    for k in range(modes):
        c = []
        for parity in range(2):
            f = far[k, parity]
            c.append(
                (f * jnp.concatenate([factor[parity], factor[parity]], 0)).astype(BF16)
            )
        a = dot(
            quarters(c[0][:half, :half], c[0][half:, :half], c[1][:half, :half], c[1][half:, :half]),
            left[0],
        )
        b = dot(
            quarters(c[0][:half, half:], c[0][half:, half:], c[1][:half, half:], c[1][half:, half:]),
            left[1],
        )
        lo, hi = (a + b).astype(BF16), (a - b).astype(BF16)
        turned = []
        for parity in range(2):
            l = lo[parity * half : (parity + 1) * half]
            h = hi[parity * half : (parity + 1) * half]
            turned.append(
                dot(
                    right[parity],
                    quarters(l[:, :half], h[:, :half], l[:, half:], h[:, half:]),
                )
            )
        for i, chi in enumerate((turned[0] + turned[1], turned[0] - turned[1])):
            cr, ci = chi[:half], chi[half:]
            pr = probe[k, 0, i * half : (i + 1) * half]
            pi = probe[k, 1, i * half : (i + 1) * half]
            grad[0][i] += pr * cr + pi * ci
            grad[1][i] += pr * ci - pi * cr

    spread[...] = jnp.zeros_like(spread)
    for p in range(2):
        g = jnp.concatenate(grad[p], 0).astype(BF16).astype(F32)
        turned = pltpu.roll(g.reshape(groups - 1, 8, extent), step, 1)
        none = jnp.zeros((1, 8, extent), F32)
        spread[p, window, :] = jnp.where(
            iota((groups, 8, extent), 1) >= step,
            jnp.concatenate([turned, none], 0),
            jnp.concatenate([none, turned], 0),
        ).reshape(8 * groups, extent)
    which = iota((INFO, extent), 0)
    info = jnp.where(which == 0, source, col).astype(F32).astype(BF16)
    for p in range(2):
        part = pl.ds(p * tile, tile)
        above, own, below = (
            spread[p, i * tile : (i + 1) * tile].astype(BF16) for i in range(3)
        )
        to_first[part] = jnp.where(odd, above, below)
        to_second[part] = jnp.where(odd, below, above)
        centre[part] = own
    for out in (to_first, to_second, centre):
        out[2 * tile :] = info


def fold_kernel(centre, second, first, out):
    columns, height, tile = out.shape
    extent = centre.shape[1]
    half = extent // 2
    gradients, places = [], []
    for part in (centre, first, second):
        source = part[height : height + 1, :].astype(F32).astype(jnp.int32)
        col = part[height + 1 : height + 2, :].astype(F32).astype(jnp.int32)
        start = jnp.concatenate([source * tile + col - half] * (columns * tile // extent), 1)
        shape = (extent, columns * tile)
        places.append((iota(shape, 1) - iota(shape, 0) == start).astype(F32).astype(BF16))
        gradients.append(part[:height])
    total = dot(jnp.concatenate(gradients, 1), jnp.concatenate(places, 0))
    for c in range(columns):
        out[c] = total[:, c * tile : (c + 1) * tile].astype(BF16)


def call(kernel, name, out_shape, in_specs, scratch, flops, moved, *args):
    args = [
        pltpu.with_memory_space_constraint(arg, pltpu.HBM) if spec is HBM else arg
        for arg, spec in zip(args, in_specs)
    ]
    return pl.pallas_call(
        kernel,
        out_shape=out_shape,
        in_specs=in_specs,
        out_specs=jax.tree.map(lambda _: VMEM, out_shape),
        scratch_shapes=scratch,
        compiler_params=pltpu.CompilerParams(vmem_limit_bytes=24 * 2**20),
        cost_estimate=pl.CostEstimate(flops=flops, bytes_accessed=moved, transcendentals=0),
        name=name,
    )(*args)


def per_device(specimen, probe, measured, centers, frame_counts, helper_cols):
    extent = probe.shape[-1]
    half = extent // 2
    tile = specimen.shape[1]
    modes = probe.shape[0]
    columns = lax.axis_size("col")
    height = 2 * tile
    part = jax.ShapeDtypeStruct((height + INFO, extent), BF16)
    dma = pltpu.SemaphoreType.DMA

    packed = call(
        pack_kernel, "pack",
        jax.ShapeDtypeStruct((height + INFO, tile), BF16),
        [HBM, HBM, SMEM, HBM],
        [
            pltpu.VMEM(specimen.shape, F32),
            pltpu.SMEM(centers.shape, jnp.int32),
            pltpu.SMEM(helper_cols.shape, jnp.int32),
            dma((3,)),
        ],
        10**5, 2**19,
        specimen, centers, frame_counts, helper_cols,
    )
    tables = dft_tables(extent)
    probe, amplitude, tables = call(
        load_kernel, "load",
        (
            jax.ShapeDtypeStruct(probe.shape, F32),
            jax.ShapeDtypeStruct((extent, extent), F32),
            jax.ShapeDtypeStruct(tables.shape, BF16),
        ),
        [HBM] * 3,
        [pltpu.VMEM(measured.shape, F32), dma((3,))],
        10**8, 2**22,
        probe, measured, tables,
    )
    band = lax.all_gather(packed, "col")

    rows = lax.axis_size("row")
    swaps = []
    for start in (0, 1):
        pairs = [(i, i + 1) for i in range(start, rows - 1, 2)]
        swaps.append(pairs + [(b, a) for a, b in pairs])
    pair = columns // 2
    second = [
        lax.ppermute(part, "row", swaps[1]) for part in (band[:pair], band[pair:])
    ]
    first = lax.ppermute(band, "row", swaps[0])
    to_second, to_first, centre = call(
        frame_kernel, "frame",
        (part, part, part),
        [VMEM] * 7,
        [
            pltpu.VMEM((2, tile + 2 * half, 3 * tile), F32),
            pltpu.VMEM((modes, 2, extent, extent), F32),
            pltpu.VMEM((2, tile + 2 * half, extent), F32),
        ],
        2 * 10**9, 2**22,
        band, first, *second, probe, amplitude, tables,
    )
    from_first = lax.ppermute(to_first, "row", swaps[0])
    from_second = lax.ppermute(to_second, "row", swaps[1])
    summed = call(
        fold_kernel, "fold",
        jax.ShapeDtypeStruct((columns, height, tile), BF16),
        [VMEM] * 3,
        [],
        10**9, 2**20,
        centre, from_second, from_first,
    )
    shares = lax.all_to_all(summed, "col", split_axis=0, concat_axis=0, tiled=True)
    return jnp.sum(shares.astype(F32), axis=0).reshape(2, tile, tile)


def solution(mesh):
    return jax.shard_map(
        per_device,
        mesh=mesh,
        in_specs=(
            P(None, "row", "col"),
            P(),
            P("row", "col", None, None, None),
            P("row", "col", None, None),
            P("row", "col"),
            P("row", "col", None),
        ),
        out_specs=P(None, "row", "col"),
        check_vma=False,
    )
```

```python
import functools
import math

import jax
import jax.numpy as jnp
import numpy as np
from jax import lax
from jax.experimental import pallas as pl
from jax.experimental.pallas import tpu as pltpu
from jax.sharding import PartitionSpec as P

F32 = jnp.float32
BF16 = jnp.bfloat16
INFO = 16
VMEM = pl.BlockSpec(memory_space=pltpu.VMEM)
SMEM = pl.BlockSpec(memory_space=pltpu.SMEM)
HBM = pl.BlockSpec(memory_space=pltpu.HBM)


def dft_tables(extent):
    half = extent // 2
    steps = np.arange(extent, dtype=np.int32)
    angles = (steps[:, None] * steps[None, :] % extent).astype(np.float32)
    angles = angles * np.float32(2.0 * math.pi / extent)
    scaling = np.float32(1.0 / math.sqrt(extent))
    real = (np.cos(angles) * scaling).astype(BF16)
    imag = (-np.sin(angles) * scaling).astype(BF16)
    tables = []
    for parity in (0, 1):
        re, im = real[:half, parity::2], imag[:half, parity::2]
        right = np.concatenate(
            [np.concatenate([re, im], 1), np.concatenate([-im, re], 1)], 0
        )
        tables += [right, np.ascontiguousarray(right.T)]
    return jnp.asarray(np.stack(tables))


def dot(a, b):
    return jnp.dot(a, b, preferred_element_type=F32)


def quarters(tl, tr, bl, br):
    return jnp.concatenate(
        [jnp.concatenate([tl, tr], 1), jnp.concatenate([bl, br], 1)], 0
    )


def iota(shape, dim):
    return lax.broadcasted_iota(jnp.int32, shape, dim)


def fetch(pairs, sems):
    copies = [
        pltpu.make_async_copy(source, target, sems.at[i])
        for i, (source, target) in enumerate(pairs)
    ]
    for copy in copies:
        copy.start()
    return copies


def pack_kernel(specimen, centers, cnt, helpers, out, tile_v, cen, hlp, sems):
    copies = fetch(((specimen, tile_v), (centers, cen), (helpers, hlp)), sems)
    for copy in copies:
        copy.wait()
    tile = tile_v.shape[1]
    lanes = tile_v.shape[2]
    rows, cols = iota((INFO, lanes), 0), iota((INFO, lanes), 1)
    info = jnp.where(rows == 0, -1.0, 0.0)
    for j in range(centers.shape[2]):
        helper = jnp.where(j < cnt[0, 0], hlp[0, 0, j], -1)
        for r, value in enumerate((helper, cen[0, 0, j, 0], cen[0, 0, j, 1])):
            info = jnp.where((rows == r) & (cols == j), value.astype(F32), info)
    info = info.astype(BF16)
    for p in range(2):
        out[p * tile : (p + 1) * tile] = tile_v[p].astype(BF16)
    out[2 * tile :] = info


def gather_columns(get, source, col, columns, shape):
    lane = iota(shape, 1)
    beside = own = jnp.zeros(shape, F32)
    for c in range(columns):
        block = get(c)
        near = ((source == c + 1) & (lane >= col)) | ((source == c - 1) & (lane < col))
        beside = jnp.where(near, block, beside)
        own = jnp.where(source == c, block, own)
    return jnp.concatenate([beside, own], 1)


def first_product(probe, patch, tables):
    half = patch[0].shape[1] // 2
    wr = probe[0] * patch[0] - probe[1] * patch[1]
    wi = probe[0] * patch[1] + probe[1] * patch[0]
    out = []
    for sign, table in zip((1, -1), tables):
        folded = jnp.concatenate(
            [wr[:, :half] + sign * wr[:, half:], wi[:, :half] + sign * wi[:, half:]], 1
        )
        out.append(dot(folded.astype(BF16), table))
    return out


def prepare_kernel(
    band, probe, measured, tables,
    info_out, amplitude, tables_out, probe_out, half_out, raw, raw_tables, raw_probe, groups, sems,
):
    copies = fetch(
        ((measured, raw), (tables, raw_tables), (probe, raw_probe)), sems
    )
    columns = band.shape[0]
    lanes = band.shape[2]
    tile = (band.shape[1] - INFO) // 2
    extent = raw.shape[-1]
    half = extent // 2
    modes = raw_probe.shape[0]
    me = lax.axis_index("col").astype(F32)

    code = jnp.zeros((1, lanes), F32)
    for c in range(columns):
        info = band[c, 2 * tile :].astype(F32)
        hit = info[0:1] == me
        code += jnp.where(hit, c * 128.0 * 128.0 + info[1:2] * 128.0 + info[2:3], 0.0)
    code = jnp.sum(code).astype(jnp.int32)
    source = code // (128 * 128)
    row = code // 128 % 128
    col = code % 128
    which = iota((INFO, extent), 0)
    info = jnp.where(which == 0, source, jnp.where(which == 1, col, row))
    info_out[...] = info.astype(F32).astype(BF16)

    shape = (extent, extent)

    def original(i):
        return jnp.where(i < half, 2 * i, 2 * (i - half) + 1)

    copies[0].wait()
    sort = (iota(shape, 1) == original(iota(shape, 0))).astype(F32).astype(BF16)
    sort_t = (iota(shape, 0) == original(iota(shape, 1))).astype(F32).astype(BF16)
    value = raw[0, 0, 0]
    coarse = value.astype(BF16)
    fine = (value - coarse.astype(F32)).astype(BF16)
    amplitude[...] = sum(
        dot(dot(sort, part).astype(BF16), sort_t) for part in (coarse, fine)
    )

    def roller(old, new, shift, parity):
        wrapped = new % half < shift
        hit = (old + shift - jnp.where(old % half + shift >= half, half, 0)) == new
        sign = jnp.where(wrapped, -1.0, 1.0) if parity else 1.0
        return jnp.where(hit, sign, 0.0).astype(BF16)

    copies[1].wait()
    i, j = iota(shape, 0), iota(shape, 1)
    for parity in range(2):
        right, left = raw_tables[2 * parity], raw_tables[2 * parity + 1]
        for axis, shift in enumerate((col, row)):
            rolled = dot(left, roller(i, j, shift, parity)).astype(BF16)
            rolled_t = dot(roller(j, i, shift, parity), right).astype(BF16)
            tables_out[4 * axis + parity] = rolled_t if axis == 0 else rolled
            tables_out[4 * axis + 2 + parity] = rolled if axis == 0 else rolled_t

    copies[2].wait()
    count = extent // 8
    base = row // 8
    step = row % 8
    lane = iota((extent, half), 1)
    sub = iota((count, 8, extent), 1)
    for k in range(modes):
        for p in range(2):
            lo = pltpu.roll(raw_probe[k, p, :, :half], col, 1)
            hi = pltpu.roll(raw_probe[k, p, :, half:], col, 1)
            turned = jnp.concatenate(
                [jnp.where(lane < col, hi, lo), jnp.where(lane < col, lo, hi)], 1
            )
            turned = pltpu.roll(turned.reshape(count, 8, extent), step, 1)
            turned = jnp.where(
                sub < step, jnp.concatenate([turned[-1:], turned[:-1]], 0), turned
            )
            groups[:count] = turned
            groups[count:] = turned
            probe_out[k, p] = groups[pl.ds(count - base, count)].reshape(extent, extent)

    patch = [
        gather_columns(
            lambda c: band[c, p * tile : (p + 1) * tile].astype(F32),
            source, col, columns, (tile, tile),
        )
        for p in range(2)
    ]
    for k in range(modes):
        products = first_product(
            [probe_out[k, p, half:] for p in range(2)], patch, (tables_out[0], tables_out[1])
        )
        for parity in range(2):
            half_out[k, parity] = products[parity]


def frame_kernel(
    first, second, info, amplitude, tables, probe, half_own,
    to_rows, centre, far,
):
    columns = first.shape[0]
    tile = (first.shape[1] - INFO) // 2
    extent = probe.shape[-1]
    half = extent // 2
    modes = probe.shape[0]
    odd = lax.axis_index("row") % 2
    source, col, row = (
        info[r : r + 1, :tile].astype(F32).astype(jnp.int32) for r in range(3)
    )
    from_above = (iota((tile, tile), 0) >= row).astype(jnp.int32)
    from_first = from_above == odd
    patch = []
    for p in range(2):
        part = slice(p * tile, (p + 1) * tile)
        patch.append(
            gather_columns(
                lambda c: jnp.where(
                    from_first, first[c, part].astype(F32), second[c, part].astype(F32)
                ),
                source, col, columns, (tile, tile),
            )
        )

    right, right_back = (tables[0], tables[1]), (tables[2], tables[3])
    left, left_back = (tables[4], tables[5]), (tables[6], tables[7])
    intensity = [jnp.zeros((half, extent), F32) for _ in range(2)]
    for k in range(modes):
        even, odds = first_product(
            [probe[k, p, :half] for p in range(2)], patch, right
        )
        for parity, sign in ((0, 1), (1, -1)):
            e = even + sign * half_own[k, 0]
            o = odds + sign * half_own[k, 1]
            folded = quarters(e[:, :half], o[:, :half], e[:, half:], o[:, half:])
            f = dot(left[parity], folded.astype(BF16))
            far[k, parity] = f
            intensity[parity] += f[:half] * f[:half] + f[half:] * f[half:]
    factor = [
        1.0
        - amplitude[i * half : (i + 1) * half]
        * lax.rsqrt(jnp.maximum(intensity[i], 0.25))
        for i in range(2)
    ]
    grad = [[jnp.zeros((half, extent), F32) for _ in range(2)] for _ in range(2)]
    for k in range(modes):
        c = []
        for parity in range(2):
            f = far[k, parity]
            c.append(
                (f * jnp.concatenate([factor[parity], factor[parity]], 0)).astype(BF16)
            )
        a = dot(
            quarters(c[0][:half, :half], c[0][half:, :half], c[1][:half, :half], c[1][half:, :half]),
            right_back[0],
        )
        b = dot(
            quarters(c[0][:half, half:], c[0][half:, half:], c[1][:half, half:], c[1][half:, half:]),
            right_back[1],
        )
        lo, hi = (a + b).astype(BF16), (a - b).astype(BF16)
        turned = []
        for parity in range(2):
            l = lo[parity * half : (parity + 1) * half]
            h = hi[parity * half : (parity + 1) * half]
            turned.append(
                dot(
                    left_back[parity],
                    quarters(l[:, :half], h[:, :half], l[:, half:], h[:, half:]),
                )
            )
        for i, chi in enumerate((turned[0] + turned[1], turned[0] - turned[1])):
            cr, ci = chi[:half], chi[half:]
            pr = probe[k, 0, i * half : (i + 1) * half]
            pi = probe[k, 1, i * half : (i + 1) * half]
            grad[0][i] += pr * cr + pi * ci
            grad[1][i] += pr * ci - pi * cr
    for p in range(2):
        to_rows[p * tile : (p + 1) * tile] = grad[p][0].astype(BF16)
        centre[p * tile : (p + 1) * tile] = grad[p][1].astype(BF16)
    for out in (to_rows, centre):
        out[2 * tile :] = info[...]


def fold_kernel(centre, second, first, out):
    columns, height, tile = out.shape
    odd = lax.axis_index("row") % 2
    shape = (tile, tile)
    lane = iota(shape, 1)
    totals = [[jnp.zeros(shape, F32) for _ in range(columns)] for _ in range(2)]
    for which, part in enumerate((centre, second, first)):
        source, col, row = (
            part[height + r : height + r + 1, :tile].astype(F32).astype(jnp.int32)
            for r in range(3)
        )
        before = (iota(shape, 0) < row).astype(jnp.int32)
        taken = before == (odd if which == 2 else 1 - odd)
        for p in range(2):
            block = part[p * tile : (p + 1) * tile].astype(F32)
            beside, own = block[:, :tile], block[:, tile:]
            if which:
                beside, own = jnp.where(taken, beside, 0.0), jnp.where(taken, own, 0.0)
            for c in range(columns):
                near = ((source == c + 1) & (lane >= col)) | ((source == c - 1) & (lane < col))
                totals[p][c] += jnp.where(near, beside, 0.0) + jnp.where(source == c, own, 0.0)
    for p in range(2):
        for c in range(columns):
            out[c, p * tile : (p + 1) * tile] = totals[p][c].astype(BF16)


def call(kernel, name, out_shape, in_specs, scratch, flops, moved, *args):
    args = [
        pltpu.with_memory_space_constraint(arg, pltpu.HBM) if spec is HBM else arg
        for arg, spec in zip(args, in_specs)
    ]
    return pl.pallas_call(
        kernel,
        out_shape=out_shape,
        in_specs=in_specs,
        out_specs=jax.tree.map(lambda _: VMEM, out_shape),
        scratch_shapes=scratch,
        compiler_params=pltpu.CompilerParams(vmem_limit_bytes=24 * 2**20),
        cost_estimate=pl.CostEstimate(flops=flops, bytes_accessed=moved, transcendentals=0),
        name=name,
    )(*args)


def per_device(specimen, probe, measured, centers, frame_counts, helper_cols):
    extent = probe.shape[-1]
    half = extent // 2
    tile = specimen.shape[1]
    modes = probe.shape[0]
    columns = lax.axis_size("col")
    height = 2 * tile
    part = jax.ShapeDtypeStruct((height + INFO, extent), BF16)
    dma = pltpu.SemaphoreType.DMA

    packed = call(
        pack_kernel, "pack",
        jax.ShapeDtypeStruct((height + INFO, tile), BF16),
        [HBM, HBM, SMEM, HBM],
        [
            pltpu.VMEM(specimen.shape, F32),
            pltpu.SMEM(centers.shape, jnp.int32),
            pltpu.SMEM(helper_cols.shape, jnp.int32),
            dma((3,)),
        ],
        10**5, 2**19,
        specimen, centers, frame_counts, helper_cols,
    )
    band = lax.all_gather(packed, "col")

    rows = lax.axis_size("row")
    swaps = []
    for start in (0, 1):
        pairs = [(i, i + 1) for i in range(start, rows - 1, 2)]
        swaps.append(pairs + [(b, a) for a, b in pairs])
    second = lax.ppermute(band, "row", swaps[1])
    first = lax.ppermute(band, "row", swaps[0])
    tables = dft_tables(extent)
    prepared = call(
        prepare_kernel, "prepare",
        (
            jax.ShapeDtypeStruct((INFO, extent), BF16),
            jax.ShapeDtypeStruct((extent, extent), F32),
            jax.ShapeDtypeStruct((8, extent, extent), BF16),
            jax.ShapeDtypeStruct(probe.shape, F32),
            jax.ShapeDtypeStruct((modes, 2, tile, extent), F32),
        ),
        [VMEM, HBM, HBM, HBM],
        [
            pltpu.VMEM(measured.shape, F32),
            pltpu.VMEM(tables.shape, BF16),
            pltpu.VMEM(probe.shape, F32),
            pltpu.VMEM((extent // 4, 8, extent), F32),
            dma((3,)),
        ],
        10**9, 2**22,
        band, probe, measured, tables,
    )
    to_rows, centre = call(
        frame_kernel, "frame",
        (part, part),
        [VMEM] * 7,
        [pltpu.VMEM((modes, 2, extent, extent), F32)],
        2 * 10**9, 2**22,
        first, second, *prepared,
    )
    from_first = lax.ppermute(to_rows, "row", swaps[0])
    from_second = lax.ppermute(to_rows, "row", swaps[1])
    summed = call(
        fold_kernel, "fold",
        jax.ShapeDtypeStruct((columns, height, tile), BF16),
        [VMEM] * 3,
        [],
        10**9, 2**20,
        centre, from_second, from_first,
    )
    shares = lax.all_to_all(summed, "col", split_axis=0, concat_axis=0, tiled=True)
    return jnp.sum(shares.astype(F32), axis=0).reshape(2, tile, tile)


def solution(mesh):
    return jax.shard_map(
        per_device,
        mesh=mesh,
        in_specs=(
            P(None, "row", "col"),
            P(),
            P("row", "col", None, None, None),
            P("row", "col", None, None),
            P("row", "col"),
            P("row", "col", None),
        ),
        out_specs=P(None, "row", "col"),
        check_vma=False,
    )
```

```python
import functools
import math

import jax
import jax.numpy as jnp
import numpy as np
from jax import lax
from jax.experimental import pallas as pl
from jax.experimental.pallas import tpu as pltpu
from jax.sharding import PartitionSpec as P

F32 = jnp.float32
BF16 = jnp.bfloat16
INFO = 16
VMEM = pl.BlockSpec(memory_space=pltpu.VMEM)
SMEM = pl.BlockSpec(memory_space=pltpu.SMEM)
HBM = pl.BlockSpec(memory_space=pltpu.HBM)


def dft_tables(extent):
    half = extent // 2
    steps = np.arange(extent, dtype=np.int32)
    angles = (steps[:, None] * steps[None, :] % extent).astype(np.float32)
    angles = angles * np.float32(2.0 * math.pi / extent)
    scaling = np.float32(1.0 / math.sqrt(extent))
    real = (np.cos(angles) * scaling).astype(BF16)
    imag = (-np.sin(angles) * scaling).astype(BF16)
    tables = []
    for parity in (0, 1):
        re, im = real[:half, parity::2], imag[:half, parity::2]
        right = np.concatenate(
            [np.concatenate([re, im], 1), np.concatenate([-im, re], 1)], 0
        )
        tables += [right, np.ascontiguousarray(right.T)]
    return jnp.asarray(np.stack(tables))


def dot(a, b):
    return jnp.dot(a, b, preferred_element_type=F32)


def quarters(tl, tr, bl, br):
    return jnp.concatenate(
        [jnp.concatenate([tl, tr], 1), jnp.concatenate([bl, br], 1)], 0
    )


def iota(shape, dim):
    return lax.broadcasted_iota(jnp.int32, shape, dim)


def fetch(pairs, sems):
    copies = [
        pltpu.make_async_copy(source, target, sems.at[i])
        for i, (source, target) in enumerate(pairs)
    ]
    for copy in copies:
        copy.start()
    return copies


def pack_kernel(specimen, centers, cnt, helpers, out, tile_v, cen, hlp, sems):
    copies = fetch(((specimen, tile_v), (centers, cen), (helpers, hlp)), sems)
    for copy in copies:
        copy.wait()
    tile = tile_v.shape[1]
    lanes = tile_v.shape[2]
    rows, cols = iota((INFO, lanes), 0), iota((INFO, lanes), 1)
    info = jnp.where(rows == 0, -1.0, 0.0)
    for j in range(centers.shape[2]):
        helper = jnp.where(j < cnt[0, 0], hlp[0, 0, j], -1)
        for r, value in enumerate((helper, cen[0, 0, j, 0], cen[0, 0, j, 1])):
            info = jnp.where((rows == r) & (cols == j), value.astype(F32), info)
    info = info.astype(BF16)
    for p in range(2):
        out[p * tile : (p + 1) * tile] = tile_v[p].astype(BF16)
    out[2 * tile :] = info


def gather_columns(get, source, col, columns, shape):
    lane = iota(shape, 1)
    beside = own = jnp.zeros(shape, F32)
    for c in range(columns):
        block = get(c)
        near = ((source == c + 1) & (lane >= col)) | ((source == c - 1) & (lane < col))
        beside = jnp.where(near, block, beside)
        own = jnp.where(source == c, block, own)
    return jnp.concatenate([beside, own], 1)


def first_product(probe, patch, tables):
    half = patch[0].shape[1] // 2
    wr = probe[0] * patch[0] - probe[1] * patch[1]
    wi = probe[0] * patch[1] + probe[1] * patch[0]
    out = []
    for sign, table in zip((1, -1), tables):
        folded = jnp.concatenate(
            [wr[:, :half] + sign * wr[:, half:], wi[:, :half] + sign * wi[:, half:]], 1
        )
        out.append(dot(folded.astype(BF16), table))
    return out


def prepare_kernel(
    band, probe, measured, tables,
    info_out, amplitude, tables_out, probe_out, half_out, raw, raw_tables, raw_probe, groups, sems,
):
    copies = fetch(
        ((measured, raw), (tables, raw_tables), (probe, raw_probe)), sems
    )
    columns = band.shape[0]
    lanes = band.shape[2]
    tile = (band.shape[1] - INFO) // 2
    extent = raw.shape[-1]
    half = extent // 2
    modes = raw_probe.shape[0]
    me = lax.axis_index("col").astype(F32)

    code = jnp.zeros((1, lanes), F32)
    for c in range(columns):
        info = band[c, 2 * tile :].astype(F32)
        hit = info[0:1] == me
        code += jnp.where(hit, c * 128.0 * 128.0 + info[1:2] * 128.0 + info[2:3], 0.0)
    code = jnp.sum(code).astype(jnp.int32)
    source = code // (128 * 128)
    row = code // 128 % 128
    col = code % 128
    which = iota((INFO, extent), 0)
    info = jnp.where(which == 0, source, jnp.where(which == 1, col, row))
    info_out[...] = info.astype(F32).astype(BF16)

    shape = (extent, extent)

    def original(i):
        return jnp.where(i < half, 2 * i, 2 * (i - half) + 1)

    copies[0].wait()
    sort = (iota(shape, 1) == original(iota(shape, 0))).astype(F32).astype(BF16)
    sort_t = (iota(shape, 0) == original(iota(shape, 1))).astype(F32).astype(BF16)
    value = raw[0, 0, 0]
    coarse = value.astype(BF16)
    fine = (value - coarse.astype(F32)).astype(BF16)
    amplitude[...] = sum(
        dot(dot(sort, part).astype(BF16), sort_t) for part in (coarse, fine)
    )

    def roller(old, new, shift, parity):
        wrapped = new % half < shift
        hit = (old + shift - jnp.where(old % half + shift >= half, half, 0)) == new
        sign = jnp.where(wrapped, -1.0, 1.0) if parity else 1.0
        return jnp.where(hit, sign, 0.0).astype(BF16)

    copies[1].wait()
    i, j = iota(shape, 0), iota(shape, 1)
    for parity in range(2):
        right, left = raw_tables[2 * parity], raw_tables[2 * parity + 1]
        for axis, shift in enumerate((col, row)):
            rolled = dot(left, roller(i, j, shift, parity)).astype(BF16)
            rolled_t = dot(roller(j, i, shift, parity), right).astype(BF16)
            tables_out[4 * axis + parity] = rolled_t if axis == 0 else rolled
            tables_out[4 * axis + 2 + parity] = rolled if axis == 0 else rolled_t

    copies[2].wait()
    count = extent // 8
    base = row // 8
    step = row % 8
    lane = iota((extent, half), 1)
    sub = iota((count, 8, extent), 1)
    for k in range(modes):
        for p in range(2):
            lo = pltpu.roll(raw_probe[k, p, :, :half], col, 1)
            hi = pltpu.roll(raw_probe[k, p, :, half:], col, 1)
            turned = jnp.concatenate(
                [jnp.where(lane < col, hi, lo), jnp.where(lane < col, lo, hi)], 1
            )
            turned = pltpu.roll(turned.reshape(count, 8, extent), step, 1)
            turned = jnp.where(
                sub < step, jnp.concatenate([turned[-1:], turned[:-1]], 0), turned
            )
            groups[:count] = turned
            groups[count:] = turned
            probe_out[k, p] = groups[pl.ds(count - base, count)].reshape(extent, extent)

    patch = [
        gather_columns(
            lambda c: band[c, p * tile : (p + 1) * tile].astype(F32),
            source, col, columns, (tile, tile),
        )
        for p in range(2)
    ]
    for k in range(modes):
        products = first_product(
            [probe_out[k, p, half:] for p in range(2)], patch, (tables_out[0], tables_out[1])
        )
        for parity in range(2):
            half_out[k, parity] = products[parity]


def frame_kernel(
    first, second, info, amplitude, tables, probe, half_own,
    to_rows, centre, far,
):
    columns = first.shape[0]
    tile = (first.shape[1] - INFO) // 2
    extent = probe.shape[-1]
    half = extent // 2
    modes = probe.shape[0]
    odd = lax.axis_index("row") % 2
    source, col, row = (
        info[r : r + 1, :tile].astype(F32).astype(jnp.int32) for r in range(3)
    )
    from_above = (iota((tile, tile), 0) >= row).astype(jnp.int32)
    from_first = from_above == odd
    patch = []
    for p in range(2):
        part = slice(p * tile, (p + 1) * tile)
        patch.append(
            gather_columns(
                lambda c: jnp.where(
                    from_first, first[c, part].astype(F32), second[c, part].astype(F32)
                ),
                source, col, columns, (tile, tile),
            )
        )

    right, right_back = (tables[0], tables[1]), (tables[2], tables[3])
    left, left_back = (tables[4], tables[5]), (tables[6], tables[7])
    intensity = [jnp.zeros((half, extent), F32) for _ in range(2)]
    for k in range(modes):
        even, odds = first_product(
            [probe[k, p, :half] for p in range(2)], patch, right
        )
        for parity, sign in ((0, 1), (1, -1)):
            e = even + sign * half_own[k, 0]
            o = odds + sign * half_own[k, 1]
            folded = quarters(e[:, :half], o[:, :half], e[:, half:], o[:, half:])
            f = dot(left[parity], folded.astype(BF16))
            far[k, parity] = f
            intensity[parity] += f[:half] * f[:half] + f[half:] * f[half:]
    factor = [
        1.0
        - amplitude[i * half : (i + 1) * half]
        * lax.rsqrt(jnp.maximum(intensity[i], 0.25))
        for i in range(2)
    ]
    grad = [[jnp.zeros((half, extent), F32) for _ in range(2)] for _ in range(2)]
    for k in range(modes):
        c = []
        for parity in range(2):
            f = far[k, parity]
            c.append(
                (f * jnp.concatenate([factor[parity], factor[parity]], 0)).astype(BF16)
            )
        a = dot(
            quarters(c[0][:half, :half], c[0][half:, :half], c[1][:half, :half], c[1][half:, :half]),
            right_back[0],
        )
        b = dot(
            quarters(c[0][:half, half:], c[0][half:, half:], c[1][:half, half:], c[1][half:, half:]),
            right_back[1],
        )
        lo, hi = (a + b).astype(BF16), (a - b).astype(BF16)
        turned = []
        for parity in range(2):
            l = lo[parity * half : (parity + 1) * half]
            h = hi[parity * half : (parity + 1) * half]
            turned.append(
                dot(
                    left_back[parity],
                    quarters(l[:, :half], h[:, :half], l[:, half:], h[:, half:]),
                )
            )
        for i, chi in enumerate((turned[0] + turned[1], turned[0] - turned[1])):
            cr, ci = chi[:half], chi[half:]
            pr = probe[k, 0, i * half : (i + 1) * half]
            pi = probe[k, 1, i * half : (i + 1) * half]
            grad[0][i] += pr * cr + pi * ci
            grad[1][i] += pr * ci - pi * cr
    for p in range(2):
        to_rows[p * tile : (p + 1) * tile] = grad[p][0].astype(BF16)
        centre[p * tile : (p + 1) * tile] = grad[p][1].astype(BF16)
    for out in (to_rows, centre):
        out[2 * tile :] = info[...]


def fold_kernel(centre, second, first, out):
    columns, height, tile = out.shape
    odd = lax.axis_index("row") % 2
    shape = (tile, tile)
    lane = iota(shape, 1)
    totals = [[jnp.zeros(shape, F32) for _ in range(columns)] for _ in range(2)]
    for which, part in enumerate((centre, second, first)):
        source, col, row = (
            part[height + r : height + r + 1, :tile].astype(F32).astype(jnp.int32)
            for r in range(3)
        )
        before = (iota(shape, 0) < row).astype(jnp.int32)
        taken = before == (odd if which == 2 else 1 - odd)
        for p in range(2):
            block = part[p * tile : (p + 1) * tile].astype(F32)
            beside, own = block[:, :tile], block[:, tile:]
            if which:
                beside, own = jnp.where(taken, beside, 0.0), jnp.where(taken, own, 0.0)
            for c in range(columns):
                near = ((source == c + 1) & (lane >= col)) | ((source == c - 1) & (lane < col))
                totals[p][c] += jnp.where(near, beside, 0.0) + jnp.where(source == c, own, 0.0)
    for p in range(2):
        for c in range(columns):
            out[c, p * tile : (p + 1) * tile] = totals[p][c].astype(BF16)


def call(kernel, name, out_shape, in_specs, scratch, flops, moved, *args):
    args = [
        pltpu.with_memory_space_constraint(arg, pltpu.HBM) if spec is HBM else arg
        for arg, spec in zip(args, in_specs)
    ]
    return pl.pallas_call(
        kernel,
        out_shape=out_shape,
        in_specs=in_specs,
        out_specs=jax.tree.map(lambda _: VMEM, out_shape),
        scratch_shapes=scratch,
        compiler_params=pltpu.CompilerParams(vmem_limit_bytes=24 * 2**20),
        cost_estimate=pl.CostEstimate(flops=flops, bytes_accessed=moved, transcendentals=0),
        name=name,
    )(*args)


def per_device(specimen, probe, measured, centers, frame_counts, helper_cols):
    extent = probe.shape[-1]
    half = extent // 2
    tile = specimen.shape[1]
    modes = probe.shape[0]
    columns = lax.axis_size("col")
    height = 2 * tile
    part = jax.ShapeDtypeStruct((height + INFO, extent), BF16)
    dma = pltpu.SemaphoreType.DMA

    packed = call(
        pack_kernel, "pack",
        jax.ShapeDtypeStruct((height + INFO, tile), BF16),
        [HBM, HBM, SMEM, HBM],
        [
            pltpu.VMEM(specimen.shape, F32),
            pltpu.SMEM(centers.shape, jnp.int32),
            pltpu.SMEM(helper_cols.shape, jnp.int32),
            dma((3,)),
        ],
        10**5, 2**19,
        specimen, centers, frame_counts, helper_cols,
    )
    band = lax.all_gather(packed, "col")

    rows = lax.axis_size("row")
    swaps = []
    for start in (0, 1):
        pairs = [(i, i + 1) for i in range(start, rows - 1, 2)]
        swaps.append(pairs + [(b, a) for a, b in pairs])
    second = lax.ppermute(band, "row", swaps[1])
    first = lax.ppermute(band, "row", swaps[0])
    tables = dft_tables(extent)
    prepared = call(
        prepare_kernel, "prepare",
        (
            jax.ShapeDtypeStruct((INFO, extent), BF16),
            jax.ShapeDtypeStruct((extent, extent), F32),
            jax.ShapeDtypeStruct((8, extent, extent), BF16),
            jax.ShapeDtypeStruct(probe.shape, F32),
            jax.ShapeDtypeStruct((modes, 2, tile, extent), F32),
        ),
        [VMEM, HBM, HBM, HBM],
        [
            pltpu.VMEM(measured.shape, F32),
            pltpu.VMEM(tables.shape, BF16),
            pltpu.VMEM(probe.shape, F32),
            pltpu.VMEM((extent // 4, 8, extent), F32),
            dma((3,)),
        ],
        10**9, 2**22,
        band, probe, measured, tables,
    )
    to_rows, centre = call(
        frame_kernel, "frame",
        (part, part),
        [VMEM] * 7,
        [pltpu.VMEM((modes, 2, extent, extent), F32)],
        2 * 10**9, 2**22,
        first, second, *prepared,
    )
    from_second = lax.ppermute(to_rows, "row", swaps[1])
    from_first = lax.ppermute(to_rows, "row", swaps[0])
    summed = call(
        fold_kernel, "fold",
        jax.ShapeDtypeStruct((columns, height, tile), BF16),
        [VMEM] * 3,
        [],
        10**9, 2**20,
        centre, from_second, from_first,
    )
    share = lax.psum_scatter(summed, "col", scatter_dimension=0)
    return share.astype(F32).reshape(2, tile, tile)


def solution(mesh):
    return jax.shard_map(
        per_device,
        mesh=mesh,
        in_specs=(
            P(None, "row", "col"),
            P(),
            P("row", "col", None, None, None),
            P("row", "col", None, None),
            P("row", "col"),
            P("row", "col", None),
        ),
        out_specs=P(None, "row", "col"),
        check_vma=False,
    )
```

```python
import functools
import math

import jax
import jax.numpy as jnp
import numpy as np
from jax import lax
from jax.experimental import pallas as pl
from jax.experimental.pallas import tpu as pltpu
from jax.sharding import PartitionSpec as P

F32 = jnp.float32
BF16 = jnp.bfloat16
INFO = 16
STRIP = 16
VMEM = pl.BlockSpec(memory_space=pltpu.VMEM)
SMEM = pl.BlockSpec(memory_space=pltpu.SMEM)
HBM = pl.BlockSpec(memory_space=pltpu.HBM)


def dft_tables(extent):
    half = extent // 2
    steps = np.arange(extent, dtype=np.int32)
    angles = (steps[:, None] * steps[None, :] % extent).astype(np.float32)
    angles = angles * np.float32(2.0 * math.pi / extent)
    scaling = np.float32(1.0 / math.sqrt(extent))
    real = (np.cos(angles) * scaling).astype(BF16)
    imag = (-np.sin(angles) * scaling).astype(BF16)
    tables = []
    for parity in (0, 1):
        re, im = real[:half, parity::2], imag[:half, parity::2]
        right = np.concatenate(
            [np.concatenate([re, im], 1), np.concatenate([-im, re], 1)], 0
        )
        tables += [right, np.ascontiguousarray(right.T)]
    return jnp.asarray(np.stack(tables))


def dot(a, b):
    return jnp.dot(a, b, preferred_element_type=F32)


def quarters(tl, tr, bl, br):
    return jnp.concatenate(
        [jnp.concatenate([tl, tr], 1), jnp.concatenate([bl, br], 1)], 0
    )


def iota(shape, dim):
    return lax.broadcasted_iota(jnp.int32, shape, dim)


def fetch(pairs, sems):
    copies = [
        pltpu.make_async_copy(source, target, sems.at[i])
        for i, (source, target) in enumerate(pairs)
    ]
    for copy in copies:
        copy.start()
    return copies


def pack_kernel(specimen, centers, cnt, helpers, out, tile_v, cen, hlp, sems):
    copies = fetch(((specimen, tile_v), (centers, cen), (helpers, hlp)), sems)
    for copy in copies:
        copy.wait()
    tile = tile_v.shape[1]
    lanes = tile_v.shape[2]
    rows, cols = iota((INFO, lanes), 0), iota((INFO, lanes), 1)
    info = jnp.where(rows == 0, -1.0, 0.0)
    for j in range(centers.shape[2]):
        helper = jnp.where(j < cnt[0, 0], hlp[0, 0, j], -1)
        for r, value in enumerate((helper, cen[0, 0, j, 0], cen[0, 0, j, 1])):
            info = jnp.where((rows == r) & (cols == j), value.astype(F32), info)
    info = info.astype(BF16)
    for p in range(2):
        out[p * tile : (p + 1) * tile] = tile_v[p].astype(BF16)
    out[2 * tile :] = info


def gather_columns(get, source, col, columns, shape):
    lane = iota(shape, 1)
    beside = own = jnp.zeros(shape, F32)
    for c in range(columns):
        block = get(c)
        near = ((source == c + 1) & (lane >= col)) | ((source == c - 1) & (lane < col))
        beside = jnp.where(near, block, beside)
        own = jnp.where(source == c, block, own)
    return jnp.concatenate([beside, own], 1)


def first_product(probe, patch, tables):
    half = patch[0].shape[1] // 2
    wr = probe[0] * patch[0] - probe[1] * patch[1]
    wi = probe[0] * patch[1] + probe[1] * patch[0]
    out = []
    for sign, table in zip((1, -1), tables):
        folded = jnp.concatenate(
            [wr[:, :half] + sign * wr[:, half:], wi[:, :half] + sign * wi[:, half:]], 1
        )
        out.append(dot(folded.astype(BF16), table))
    return out


def prepare_kernel(
    band, probe, measured, tables,
    info_out, amplitude, tables_out, probe_out, half_out, raw, raw_tables, raw_probe, groups, sems,
):
    copies = fetch(
        ((measured, raw), (tables, raw_tables), (probe, raw_probe)), sems
    )
    columns = band.shape[0]
    lanes = band.shape[2]
    tile = (band.shape[1] - INFO) // 2
    extent = raw.shape[-1]
    half = extent // 2
    modes = raw_probe.shape[0]
    me = lax.axis_index("col").astype(F32)

    code = jnp.zeros((1, lanes), F32)
    for c in range(columns):
        info = band[c, 2 * tile :].astype(F32)
        hit = info[0:1] == me
        code += jnp.where(hit, c * 128.0 * 128.0 + info[1:2] * 128.0 + info[2:3], 0.0)
    code = jnp.sum(code).astype(jnp.int32)
    source = code // (128 * 128)
    row = code // 128 % 128
    col = code % 128
    which = iota((INFO, extent), 0)
    info = jnp.where(which == 0, source, jnp.where(which == 1, col, row))
    info_out[...] = info.astype(F32).astype(BF16)

    shape = (extent, extent)

    def original(i):
        return jnp.where(i < half, 2 * i, 2 * (i - half) + 1)

    copies[0].wait()
    sort = (iota(shape, 1) == original(iota(shape, 0))).astype(F32).astype(BF16)
    sort_t = (iota(shape, 0) == original(iota(shape, 1))).astype(F32).astype(BF16)
    value = raw[0, 0, 0]
    coarse = value.astype(BF16)
    fine = (value - coarse.astype(F32)).astype(BF16)
    amplitude[...] = sum(
        dot(dot(sort, part).astype(BF16), sort_t) for part in (coarse, fine)
    )

    def roller(old, new, shift, parity):
        wrapped = new % half < shift
        hit = (old + shift - jnp.where(old % half + shift >= half, half, 0)) == new
        sign = jnp.where(wrapped, -1.0, 1.0) if parity else 1.0
        return jnp.where(hit, sign, 0.0).astype(BF16)

    copies[1].wait()
    i, j = iota(shape, 0), iota(shape, 1)
    for parity in range(2):
        right, left = raw_tables[2 * parity], raw_tables[2 * parity + 1]
        for axis, shift in enumerate((col, row)):
            rolled = dot(left, roller(i, j, shift, parity)).astype(BF16)
            rolled_t = dot(roller(j, i, shift, parity), right).astype(BF16)
            tables_out[4 * axis + parity] = rolled_t if axis == 0 else rolled
            tables_out[4 * axis + 2 + parity] = rolled if axis == 0 else rolled_t

    copies[2].wait()
    count = extent // 8
    base = row // 8
    step = row % 8
    lane = iota((extent, half), 1)
    sub = iota((count, 8, extent), 1)
    for k in range(modes):
        for p in range(2):
            lo = pltpu.roll(raw_probe[k, p, :, :half], col, 1)
            hi = pltpu.roll(raw_probe[k, p, :, half:], col, 1)
            turned = jnp.concatenate(
                [jnp.where(lane < col, hi, lo), jnp.where(lane < col, lo, hi)], 1
            )
            turned = pltpu.roll(turned.reshape(count, 8, extent), step, 1)
            turned = jnp.where(
                sub < step, jnp.concatenate([turned[-1:], turned[:-1]], 0), turned
            )
            groups[:count] = turned
            groups[count:] = turned
            probe_out[k, p] = groups[pl.ds(count - base, count)].reshape(extent, extent)

    patch = [
        gather_columns(
            lambda c: band[c, p * tile : (p + 1) * tile].astype(F32),
            source, col, columns, (tile, tile),
        )
        for p in range(2)
    ]
    for k in range(modes):
        products = first_product(
            [probe_out[k, p, half:] for p in range(2)], patch, (tables_out[0], tables_out[1])
        )
        for parity in range(2):
            half_out[k, parity] = products[parity]


def frame_kernel(
    first, second, info, amplitude, tables, probe, half_own,
    to_rows, centre, patch, folded, half_far, mixed, far, corrected, product, mixed_back, turned,
):
    columns = first.shape[0]
    tile = (first.shape[1] - INFO) // 2
    extent = probe.shape[-1]
    half = extent // 2
    modes = probe.shape[0]
    odd = lax.axis_index("row") % 2
    source, col, row = (
        info[r : r + 1, :tile].astype(F32).astype(jnp.int32) for r in range(3)
    )
    strips = [pl.ds(r, STRIP) for r in range(0, half, STRIP)]
    lower = [pl.ds(half + r, STRIP) for r in range(0, half, STRIP)]

    def split(x):
        return x[:, :half], x[:, half:]

    def join(x, y):
        return jnp.concatenate([x, y], 1).astype(BF16)

    def gather(s):
        rows = iota((STRIP, tile), 0) + s.start
        from_first = (rows >= row).astype(jnp.int32) == odd
        for p in range(2):
            part = pl.ds(p * tile + s.start, STRIP)
            patch[p, s] = gather_columns(
                lambda c: jnp.where(
                    from_first, first[c, part].astype(F32), second[c, part].astype(F32)
                ),
                source, col, columns, (STRIP, tile),
            )

    def wave(k):
        for s in strips:
            pr, pi, xr, xi = probe[k, 0, s], probe[k, 1, s], patch[0, s], patch[1, s]
            re = split(pr * xr - pi * xi)
            im = split(pr * xi + pi * xr)
            folded[k, 0, s] = join(re[0] + re[1], im[0] + im[1])
            folded[k, 1, s] = join(re[0] - re[1], im[0] - im[1])

    def along_rows(k):
        for q in range(2):
            half_far[k, q] = dot(folded[k, q], tables[q])

    def mix(k):
        for s, t in zip(strips, lower):
            even, odds = half_far[k, 0, s], half_far[k, 1, s]
            even_own, odds_own = half_own[k, 0, s], half_own[k, 1, s]
            for q, (e, o) in enumerate(
                ((even + even_own, odds + odds_own), (even - even_own, odds - odds_own))
            ):
                (er, ei), (our, oui) = split(e), split(o)
                mixed[k, q, s] = join(er, our)
                mixed[k, q, t] = join(ei, oui)

    def along_columns(k, q):
        far[k, q] = dot(tables[4 + q], mixed[k, q])

    def correct(q, which):
        for s, t in list(zip(strips, lower))[which]:
            re = [far[k, q, s] for k in range(modes)]
            im = [far[k, q, t] for k in range(modes)]
            intensity = sum(x * x for x in re + im)
            size = amplitude[pl.ds(q * half + s.start, STRIP)]
            factor = 1.0 - size * lax.rsqrt(jnp.maximum(intensity, 0.25))
            out = pl.ds(q * half + s.start, STRIP)
            for k in range(modes):
                (re_even, re_odd), (im_even, im_odd) = split(re[k] * factor), split(im[k] * factor)
                corrected[k, 0, out] = join(re_even, im_even)
                corrected[k, 1, out] = join(re_odd, im_odd)

    def back_along_rows(k, q):
        part = pl.ds(q * half, half)
        for c in range(2):
            product[k, c, part] = dot(corrected[k, c, part], tables[2 + c])

    def mix_back(k, q):
        for s, t in zip(strips, lower):
            part = pl.ds(q * half + s.start, STRIP)
            x, y = product[k, 0, part], product[k, 1, part]
            (lr, li), (hr, hi) = split(x + y), split(x - y)
            mixed_back[k, q, s] = join(lr, hr)
            mixed_back[k, q, t] = join(li, hi)

    def back_along_columns(k, q):
        turned[k, q] = dot(tables[6 + q], mixed_back[k, q])

    def accumulate(s, t):
        total = [[0.0, 0.0], [0.0, 0.0]]
        for k in range(modes):
            er, ei, our, oui = turned[k, 0, s], turned[k, 0, t], turned[k, 1, s], turned[k, 1, t]
            for i, (cr, ci, rows) in enumerate(
                ((er + our, ei + oui, s), (er - our, ei - oui, t))
            ):
                pr, pi = probe[k, 0, rows], probe[k, 1, rows]
                total[i][0] += pr * cr + pi * ci
                total[i][1] += pr * ci - pi * cr
        for out, parts in zip((to_rows, centre), total):
            for p in range(2):
                out[pl.ds(p * tile + s.start, STRIP)] = parts[p].astype(BF16)

    for s in strips:
        gather(s)
    for k in range(modes + 1):
        if k < modes:
            wave(k)
            along_rows(k)
        if k > 0:
            mix(k - 1)
            along_columns(k - 1, 0)
    share = -(-len(strips) // modes)
    for k in range(modes):
        along_columns(k, 1)
        correct(0, slice(k * share, (k + 1) * share))
    for k in range(modes):
        back_along_rows(k, 0)
        correct(1, slice(k * share, (k + 1) * share))
    for k in range(modes):
        mix_back(k, 0)
        back_along_columns(k, 0)
        back_along_rows(k, 1)
    for k in range(modes):
        mix_back(k, 1)
        back_along_columns(k, 1)
    for s, t in zip(strips, lower):
        accumulate(s, t)
    for out in (to_rows, centre):
        out[2 * tile :] = info[...]


def fold_kernel(centre, second, first, out):
    columns, height, tile = out.shape
    odd = lax.axis_index("row") % 2
    shape = (tile, tile)
    lane = iota(shape, 1)
    totals = [[jnp.zeros(shape, F32) for _ in range(columns)] for _ in range(2)]
    for which, part in enumerate((centre, second, first)):
        source, col, row = (
            part[height + r : height + r + 1, :tile].astype(F32).astype(jnp.int32)
            for r in range(3)
        )
        before = (iota(shape, 0) < row).astype(jnp.int32)
        taken = before == (odd if which == 2 else 1 - odd)
        for p in range(2):
            block = part[p * tile : (p + 1) * tile].astype(F32)
            beside, own = block[:, :tile], block[:, tile:]
            if which:
                beside, own = jnp.where(taken, beside, 0.0), jnp.where(taken, own, 0.0)
            for c in range(columns):
                near = ((source == c + 1) & (lane >= col)) | ((source == c - 1) & (lane < col))
                totals[p][c] += jnp.where(near, beside, 0.0) + jnp.where(source == c, own, 0.0)
    for p in range(2):
        for c in range(columns):
            out[c, p * tile : (p + 1) * tile] = totals[p][c].astype(BF16)


def call(kernel, name, out_shape, in_specs, scratch, flops, moved, *args):
    args = [
        pltpu.with_memory_space_constraint(arg, pltpu.HBM) if spec is HBM else arg
        for arg, spec in zip(args, in_specs)
    ]
    return pl.pallas_call(
        kernel,
        out_shape=out_shape,
        in_specs=in_specs,
        out_specs=jax.tree.map(lambda _: VMEM, out_shape),
        scratch_shapes=scratch,
        compiler_params=pltpu.CompilerParams(vmem_limit_bytes=32 * 2**20),
        cost_estimate=pl.CostEstimate(flops=flops, bytes_accessed=moved, transcendentals=0),
        name=name,
    )(*args)


def per_device(specimen, probe, measured, centers, frame_counts, helper_cols):
    extent = probe.shape[-1]
    half = extent // 2
    tile = specimen.shape[1]
    modes = probe.shape[0]
    columns = lax.axis_size("col")
    height = 2 * tile
    part = jax.ShapeDtypeStruct((height + INFO, extent), BF16)
    dma = pltpu.SemaphoreType.DMA

    packed = call(
        pack_kernel, "pack",
        jax.ShapeDtypeStruct((height + INFO, tile), BF16),
        [HBM, HBM, SMEM, HBM],
        [
            pltpu.VMEM(specimen.shape, F32),
            pltpu.SMEM(centers.shape, jnp.int32),
            pltpu.SMEM(helper_cols.shape, jnp.int32),
            dma((3,)),
        ],
        10**5, 2**19,
        specimen, centers, frame_counts, helper_cols,
    )
    band = lax.all_gather(packed, "col")

    rows = lax.axis_size("row")
    swaps = []
    for start in (0, 1):
        pairs = [(i, i + 1) for i in range(start, rows - 1, 2)]
        swaps.append(pairs + [(b, a) for a, b in pairs])
    second = lax.ppermute(band, "row", swaps[1])
    first = lax.ppermute(band, "row", swaps[0])
    tables = dft_tables(extent)
    prepared = call(
        prepare_kernel, "prepare",
        (
            jax.ShapeDtypeStruct((INFO, extent), BF16),
            jax.ShapeDtypeStruct((extent, extent), F32),
            jax.ShapeDtypeStruct((8, extent, extent), BF16),
            jax.ShapeDtypeStruct(probe.shape, F32),
            jax.ShapeDtypeStruct((modes, 2, tile, extent), F32),
        ),
        [VMEM, HBM, HBM, HBM],
        [
            pltpu.VMEM(measured.shape, F32),
            pltpu.VMEM(tables.shape, BF16),
            pltpu.VMEM(probe.shape, F32),
            pltpu.VMEM((extent // 4, 8, extent), F32),
            dma((3,)),
        ],
        10**9, 2**22,
        band, probe, measured, tables,
    )
    to_rows, centre = call(
        frame_kernel, "frame",
        (part, part),
        [VMEM] * 7,
        [
            pltpu.VMEM((2, tile, extent), F32),
            pltpu.VMEM((modes, 2, half, extent), BF16),
            pltpu.VMEM((modes, 2, half, extent), F32),
            pltpu.VMEM((modes, 2, extent, extent), BF16),
            pltpu.VMEM((modes, 2, extent, extent), F32),
            pltpu.VMEM((modes, 2, extent, extent), BF16),
            pltpu.VMEM((modes, 2, extent, extent), F32),
            pltpu.VMEM((modes, 2, extent, extent), BF16),
            pltpu.VMEM((modes, 2, extent, extent), F32),
        ],
        2 * 10**9, 2**22,
        first, second, *prepared,
    )
    from_first = lax.ppermute(to_rows, "row", swaps[0])
    from_second = lax.ppermute(to_rows, "row", swaps[1])
    summed = call(
        fold_kernel, "fold",
        jax.ShapeDtypeStruct((columns, height, tile), BF16),
        [VMEM] * 3,
        [],
        10**9, 2**20,
        centre, from_second, from_first,
    )
    shares = lax.all_to_all(summed, "col", split_axis=0, concat_axis=0, tiled=True)
    return jnp.sum(shares.astype(F32), axis=0).reshape(2, tile, tile)


def solution(mesh):
    return jax.shard_map(
        per_device,
        mesh=mesh,
        in_specs=(
            P(None, "row", "col"),
            P(),
            P("row", "col", None, None, None),
            P("row", "col", None, None),
            P("row", "col"),
            P("row", "col", None),
        ),
        out_specs=P(None, "row", "col"),
        check_vma=False,
    )
```

```python
import functools
import math

import jax
import jax.numpy as jnp
import numpy as np
from jax import lax
from jax.experimental import pallas as pl
from jax.experimental.pallas import tpu as pltpu
from jax.sharding import PartitionSpec as P

F32 = jnp.float32
BF16 = jnp.bfloat16
INFO = 16
STRIP = 16
VMEM = pl.BlockSpec(memory_space=pltpu.VMEM)
SMEM = pl.BlockSpec(memory_space=pltpu.SMEM)
HBM = pl.BlockSpec(memory_space=pltpu.HBM)


def dft_tables(extent):
    half = extent // 2
    steps = np.arange(extent, dtype=np.int32)
    angles = (steps[:, None] * steps[None, :] % extent).astype(np.float32)
    angles = angles * np.float32(2.0 * math.pi / extent)
    scaling = np.float32(1.0 / math.sqrt(extent))
    real = (np.cos(angles) * scaling).astype(BF16)
    imag = (-np.sin(angles) * scaling).astype(BF16)
    tables = []
    for parity in (0, 1):
        re, im = real[:half, parity::2], imag[:half, parity::2]
        right = np.concatenate(
            [np.concatenate([re, im], 1), np.concatenate([-im, re], 1)], 0
        )
        tables += [right, np.ascontiguousarray(right.T)]
    return jnp.asarray(np.stack(tables))


def dot(a, b):
    return jnp.dot(a, b, preferred_element_type=F32)


def quarters(tl, tr, bl, br):
    return jnp.concatenate(
        [jnp.concatenate([tl, tr], 1), jnp.concatenate([bl, br], 1)], 0
    )


def iota(shape, dim):
    return lax.broadcasted_iota(jnp.int32, shape, dim)


def fetch(pairs, sems):
    copies = [
        pltpu.make_async_copy(source, target, sems.at[i])
        for i, (source, target) in enumerate(pairs)
    ]
    for copy in copies:
        copy.start()
    return copies


def pack_kernel(specimen, centers, cnt, helpers, out, tile_v, cen, hlp, sems):
    copies = fetch(((specimen, tile_v), (centers, cen), (helpers, hlp)), sems)
    for copy in copies:
        copy.wait()
    tile = tile_v.shape[1]
    lanes = tile_v.shape[2]
    rows, cols = iota((INFO, lanes), 0), iota((INFO, lanes), 1)
    info = jnp.where(rows == 0, -1.0, 0.0)
    for j in range(centers.shape[2]):
        helper = jnp.where(j < cnt[0, 0], hlp[0, 0, j], -1)
        for r, value in enumerate((helper, cen[0, 0, j, 0], cen[0, 0, j, 1])):
            info = jnp.where((rows == r) & (cols == j), value.astype(F32), info)
    info = info.astype(BF16)
    for p in range(2):
        out[p * tile : (p + 1) * tile] = tile_v[p].astype(BF16)
    out[2 * tile :] = info


def gather_columns(get, source, col, columns, shape):
    lane = iota(shape, 1)
    beside = own = jnp.zeros(shape, F32)
    for c in range(columns):
        block = get(c)
        near = ((source == c + 1) & (lane >= col)) | ((source == c - 1) & (lane < col))
        beside = jnp.where(near, block, beside)
        own = jnp.where(source == c, block, own)
    return jnp.concatenate([beside, own], 1)


def first_product(probe, patch, tables):
    half = patch[0].shape[1] // 2
    wr = probe[0] * patch[0] - probe[1] * patch[1]
    wi = probe[0] * patch[1] + probe[1] * patch[0]
    out = []
    for sign, table in zip((1, -1), tables):
        folded = jnp.concatenate(
            [wr[:, :half] + sign * wr[:, half:], wi[:, :half] + sign * wi[:, half:]], 1
        )
        out.append(dot(folded.astype(BF16), table))
    return out


def prepare_kernel(
    band, probe, measured, tables,
    info_out, amplitude, tables_out, probe_out, half_out, raw, raw_tables, raw_probe, groups, sems,
):
    copies = fetch(
        ((measured, raw), (tables, raw_tables), (probe, raw_probe)), sems
    )
    columns = band.shape[0]
    lanes = band.shape[2]
    tile = (band.shape[1] - INFO) // 2
    extent = raw.shape[-1]
    half = extent // 2
    modes = raw_probe.shape[0]
    me = lax.axis_index("col").astype(F32)

    code = jnp.zeros((1, lanes), F32)
    for c in range(columns):
        info = band[c, 2 * tile :].astype(F32)
        hit = info[0:1] == me
        code += jnp.where(hit, c * 128.0 * 128.0 + info[1:2] * 128.0 + info[2:3], 0.0)
    code = jnp.sum(code).astype(jnp.int32)
    source = code // (128 * 128)
    row = code // 128 % 128
    col = code % 128
    which = iota((INFO, extent), 0)
    info = jnp.where(which == 0, source, jnp.where(which == 1, col, row))
    info_out[...] = info.astype(F32).astype(BF16)

    shape = (extent, extent)

    def original(i):
        return jnp.where(i < half, 2 * i, 2 * (i - half) + 1)

    copies[0].wait()
    sort = (iota(shape, 1) == original(iota(shape, 0))).astype(F32).astype(BF16)
    sort_t = (iota(shape, 0) == original(iota(shape, 1))).astype(F32).astype(BF16)
    value = raw[0, 0, 0]
    coarse = value.astype(BF16)
    fine = (value - coarse.astype(F32)).astype(BF16)
    amplitude[...] = sum(
        dot(dot(sort, part).astype(BF16), sort_t) for part in (coarse, fine)
    )

    def roller(old, new, shift, parity):
        wrapped = new % half < shift
        hit = (old + shift - jnp.where(old % half + shift >= half, half, 0)) == new
        sign = jnp.where(wrapped, -1.0, 1.0) if parity else 1.0
        return jnp.where(hit, sign, 0.0).astype(BF16)

    copies[1].wait()
    i, j = iota(shape, 0), iota(shape, 1)
    for parity in range(2):
        right, left = raw_tables[2 * parity], raw_tables[2 * parity + 1]
        for axis, shift in enumerate((col, row)):
            rolled = dot(left, roller(i, j, shift, parity)).astype(BF16)
            rolled_t = dot(roller(j, i, shift, parity), right).astype(BF16)
            tables_out[4 * axis + parity] = rolled_t if axis == 0 else rolled
            tables_out[4 * axis + 2 + parity] = rolled if axis == 0 else rolled_t

    copies[2].wait()
    count = extent // 8
    base = row // 8
    step = row % 8
    lane = iota((extent, half), 1)
    sub = iota((count, 8, extent), 1)
    for k in range(modes):
        for p in range(2):
            lo = pltpu.roll(raw_probe[k, p, :, :half], col, 1)
            hi = pltpu.roll(raw_probe[k, p, :, half:], col, 1)
            turned = jnp.concatenate(
                [jnp.where(lane < col, hi, lo), jnp.where(lane < col, lo, hi)], 1
            )
            turned = pltpu.roll(turned.reshape(count, 8, extent), step, 1)
            turned = jnp.where(
                sub < step, jnp.concatenate([turned[-1:], turned[:-1]], 0), turned
            )
            groups[:count] = turned
            groups[count:] = turned
            probe_out[k, p] = groups[pl.ds(count - base, count)].reshape(extent, extent)

    patch = [
        gather_columns(
            lambda c: band[c, p * tile : (p + 1) * tile].astype(F32),
            source, col, columns, (tile, tile),
        )
        for p in range(2)
    ]
    for k in range(modes):
        products = first_product(
            [probe_out[k, p, half:] for p in range(2)], patch, (tables_out[0], tables_out[1])
        )
        for parity in range(2):
            half_out[k, parity] = products[parity]


def frame_kernel(
    first, second, info, amplitude, tables, probe, half_own,
    to_rows, centre, patch, folded, half_far, mixed, far, corrected, product, mixed_back, turned,
):
    columns = first.shape[0]
    tile = (first.shape[1] - INFO) // 2
    extent = probe.shape[-1]
    half = extent // 2
    modes = probe.shape[0]
    odd = lax.axis_index("row") % 2
    source, col, row = (
        info[r : r + 1, :tile].astype(F32).astype(jnp.int32) for r in range(3)
    )
    strips = [pl.ds(r, STRIP) for r in range(0, half, STRIP)]
    lower = [pl.ds(half + r, STRIP) for r in range(0, half, STRIP)]

    def split(x):
        return x[:, :half], x[:, half:]

    def join(x, y):
        return jnp.concatenate([x, y], 1).astype(BF16)

    def gather(s):
        rows = iota((STRIP, tile), 0) + s.start
        from_first = (rows >= row).astype(jnp.int32) == odd
        for p in range(2):
            part = pl.ds(p * tile + s.start, STRIP)
            patch[p, s] = gather_columns(
                lambda c: jnp.where(
                    from_first, first[c, part].astype(F32), second[c, part].astype(F32)
                ),
                source, col, columns, (STRIP, tile),
            )

    def wave(k):
        for s in strips:
            pr, pi, xr, xi = probe[k, 0, s], probe[k, 1, s], patch[0, s], patch[1, s]
            re = split(pr * xr - pi * xi)
            im = split(pr * xi + pi * xr)
            folded[k, 0, s] = join(re[0] + re[1], im[0] + im[1])
            folded[k, 1, s] = join(re[0] - re[1], im[0] - im[1])

    def along_rows(k):
        for q in range(2):
            half_far[k, q] = dot(folded[k, q], tables[q])

    def mix(k):
        for s, t in zip(strips, lower):
            even, odds = half_far[k, 0, s], half_far[k, 1, s]
            even_own, odds_own = half_own[k, 0, s], half_own[k, 1, s]
            for q, (e, o) in enumerate(
                ((even + even_own, odds + odds_own), (even - even_own, odds - odds_own))
            ):
                (er, ei), (our, oui) = split(e), split(o)
                mixed[k, q, s] = join(er, our)
                mixed[k, q, t] = join(ei, oui)

    def along_columns(k, q):
        far[k, q] = dot(tables[4 + q], mixed[k, q])

    def correct(q, which):
        for s, t in list(zip(strips, lower))[which]:
            re = [far[k, q, s] for k in range(modes)]
            im = [far[k, q, t] for k in range(modes)]
            intensity = sum(x * x for x in re + im)
            size = amplitude[pl.ds(q * half + s.start, STRIP)]
            factor = 1.0 - size * lax.rsqrt(jnp.maximum(intensity, 0.25))
            out = pl.ds(q * half + s.start, STRIP)
            for k in range(modes):
                (re_even, re_odd), (im_even, im_odd) = split(re[k] * factor), split(im[k] * factor)
                corrected[k, 0, out] = join(re_even, im_even)
                corrected[k, 1, out] = join(re_odd, im_odd)

    def back_along_rows(k, q):
        part = pl.ds(q * half, half)
        for c in range(2):
            product[k, c, part] = dot(corrected[k, c, part], tables[2 + c])

    def mix_back(k, q):
        for s, t in zip(strips, lower):
            part = pl.ds(q * half + s.start, STRIP)
            x, y = product[k, 0, part], product[k, 1, part]
            (lr, li), (hr, hi) = split(x + y), split(x - y)
            mixed_back[k, q, s] = join(lr, hr)
            mixed_back[k, q, t] = join(li, hi)

    def back_along_columns(k, q):
        turned[k, q] = dot(tables[6 + q], mixed_back[k, q])

    def accumulate(s, t):
        total = [[0.0, 0.0], [0.0, 0.0]]
        for k in range(modes):
            er, ei, our, oui = turned[k, 0, s], turned[k, 0, t], turned[k, 1, s], turned[k, 1, t]
            for i, (cr, ci, rows) in enumerate(
                ((er + our, ei + oui, s), (er - our, ei - oui, t))
            ):
                pr, pi = probe[k, 0, rows], probe[k, 1, rows]
                total[i][0] += pr * cr + pi * ci
                total[i][1] += pr * ci - pi * cr
        for out, parts in zip((to_rows, centre), total):
            for p in range(2):
                out[pl.ds(p * tile + s.start, STRIP)] = parts[p].astype(BF16)

    for s in strips:
        gather(s)
    for k in range(modes + 1):
        if k < modes:
            wave(k)
            along_rows(k)
        if k > 0:
            mix(k - 1)
            along_columns(k - 1, 0)
    share = -(-len(strips) // modes)
    for k in range(modes):
        along_columns(k, 1)
        correct(0, slice(k * share, (k + 1) * share))
    for k in range(modes):
        back_along_rows(k, 0)
        correct(1, slice(k * share, (k + 1) * share))
    for k in range(modes):
        mix_back(k, 0)
        back_along_columns(k, 0)
        back_along_rows(k, 1)
    for k in range(modes):
        mix_back(k, 1)
        back_along_columns(k, 1)
    for s, t in zip(strips, lower):
        accumulate(s, t)
    for out in (to_rows, centre):
        out[2 * tile :] = info[...]


def fold_kernel(centre, to_rows, first, out):
    _, height, tile = out.shape
    columns = out.shape[0] // 2
    me = lax.axis_index("row")
    odd = me % 2
    shape = (tile, tile)
    lane = iota(shape, 1)
    outer = (me > 0) & (me < lax.axis_size("row") - 1)
    own_row = [[jnp.zeros(shape, F32) for _ in range(columns)] for _ in range(2)]
    other_row = [[jnp.zeros(shape, F32) for _ in range(columns)] for _ in range(2)]
    for part, totals, wanted in (
        (centre, own_row, None), (first, own_row, odd), (to_rows, other_row, odd)
    ):
        source, col, row = (
            part[height + r : height + r + 1, :tile].astype(F32).astype(jnp.int32)
            for r in range(3)
        )
        taken = (iota(shape, 0) < row).astype(jnp.int32) == odd
        if totals is other_row:
            taken = taken & outer
        for p in range(2):
            block = part[p * tile : (p + 1) * tile].astype(F32)
            beside, own = block[:, :tile], block[:, tile:]
            if wanted is not None:
                beside, own = jnp.where(taken, beside, 0.0), jnp.where(taken, own, 0.0)
            for c in range(columns):
                near = ((source == c + 1) & (lane >= col)) | ((source == c - 1) & (lane < col))
                totals[p][c] += jnp.where(near, beside, 0.0) + jnp.where(source == c, own, 0.0)
    for p in range(2):
        part = slice(p * tile, (p + 1) * tile)
        for c in range(columns):
            out[(1 - odd) * columns + c, part] = own_row[p][c].astype(BF16)
            out[odd * columns + c, part] = other_row[p][c].astype(BF16)


def call(kernel, name, out_shape, in_specs, scratch, flops, moved, *args):
    args = [
        pltpu.with_memory_space_constraint(arg, pltpu.HBM) if spec is HBM else arg
        for arg, spec in zip(args, in_specs)
    ]
    return pl.pallas_call(
        kernel,
        out_shape=out_shape,
        in_specs=in_specs,
        out_specs=jax.tree.map(lambda _: VMEM, out_shape),
        scratch_shapes=scratch,
        compiler_params=pltpu.CompilerParams(vmem_limit_bytes=32 * 2**20),
        cost_estimate=pl.CostEstimate(flops=flops, bytes_accessed=moved, transcendentals=0),
        name=name,
    )(*args)


def per_device(specimen, probe, measured, centers, frame_counts, helper_cols):
    extent = probe.shape[-1]
    half = extent // 2
    tile = specimen.shape[1]
    modes = probe.shape[0]
    columns = lax.axis_size("col")
    height = 2 * tile
    part = jax.ShapeDtypeStruct((height + INFO, extent), BF16)
    dma = pltpu.SemaphoreType.DMA

    packed = call(
        pack_kernel, "pack",
        jax.ShapeDtypeStruct((height + INFO, tile), BF16),
        [HBM, HBM, SMEM, HBM],
        [
            pltpu.VMEM(specimen.shape, F32),
            pltpu.SMEM(centers.shape, jnp.int32),
            pltpu.SMEM(helper_cols.shape, jnp.int32),
            dma((3,)),
        ],
        10**5, 2**19,
        specimen, centers, frame_counts, helper_cols,
    )
    band = lax.all_gather(packed, "col")

    rows = lax.axis_size("row")
    swaps = []
    for start in (0, 1):
        pairs = [(i, i + 1) for i in range(start, rows - 1, 2)]
        swaps.append(pairs + [(b, a) for a, b in pairs])
    second = lax.ppermute(band, "row", swaps[1])
    first = lax.ppermute(band, "row", swaps[0])
    tables = dft_tables(extent)
    prepared = call(
        prepare_kernel, "prepare",
        (
            jax.ShapeDtypeStruct((INFO, extent), BF16),
            jax.ShapeDtypeStruct((extent, extent), F32),
            jax.ShapeDtypeStruct((8, extent, extent), BF16),
            jax.ShapeDtypeStruct(probe.shape, F32),
            jax.ShapeDtypeStruct((modes, 2, tile, extent), F32),
        ),
        [VMEM, HBM, HBM, HBM],
        [
            pltpu.VMEM(measured.shape, F32),
            pltpu.VMEM(tables.shape, BF16),
            pltpu.VMEM(probe.shape, F32),
            pltpu.VMEM((extent // 4, 8, extent), F32),
            dma((3,)),
        ],
        10**9, 2**22,
        band, probe, measured, tables,
    )
    to_rows, centre = call(
        frame_kernel, "frame",
        (part, part),
        [VMEM] * 7,
        [
            pltpu.VMEM((2, tile, extent), F32),
            pltpu.VMEM((modes, 2, half, extent), BF16),
            pltpu.VMEM((modes, 2, half, extent), F32),
            pltpu.VMEM((modes, 2, extent, extent), BF16),
            pltpu.VMEM((modes, 2, extent, extent), F32),
            pltpu.VMEM((modes, 2, extent, extent), BF16),
            pltpu.VMEM((modes, 2, extent, extent), F32),
            pltpu.VMEM((modes, 2, extent, extent), BF16),
            pltpu.VMEM((modes, 2, extent, extent), F32),
        ],
        2 * 10**9, 2**22,
        first, second, *prepared,
    )
    from_first = lax.ppermute(to_rows, "row", swaps[0])
    summed = call(
        fold_kernel, "fold",
        jax.ShapeDtypeStruct((2 * columns, height, tile), BF16),
        [VMEM] * 3,
        [],
        10**7, 2**20,
        centre, to_rows, from_first,
    )
    groups = [
        [r * columns + c for r in (start, (start + 1) % rows) for c in range(columns)]
        for start in range(1, rows, 2)
    ]
    shares = lax.all_to_all(
        summed, ("row", "col"), split_axis=0, concat_axis=0, axis_index_groups=groups, tiled=True
    )
    return jnp.sum(shares.astype(F32), axis=0).reshape(2, tile, tile)


def solution(mesh):
    return jax.shard_map(
        per_device,
        mesh=mesh,
        in_specs=(
            P(None, "row", "col"),
            P(),
            P("row", "col", None, None, None),
            P("row", "col", None, None),
            P("row", "col"),
            P("row", "col", None),
        ),
        out_specs=P(None, "row", "col"),
        check_vma=False,
    )
```

```python
import functools
import math

import jax
import jax.numpy as jnp
import numpy as np
from jax import lax
from jax.experimental import pallas as pl
from jax.experimental.pallas import tpu as pltpu
from jax.sharding import PartitionSpec as P

F32 = jnp.float32
BF16 = jnp.bfloat16
INFO = 16
STRIP = 16
VMEM = pl.BlockSpec(memory_space=pltpu.VMEM)
SMEM = pl.BlockSpec(memory_space=pltpu.SMEM)
HBM = pl.BlockSpec(memory_space=pltpu.HBM)


def dft_tables(extent):
    half = extent // 2
    steps = np.arange(extent, dtype=np.int32)
    angles = (steps[:, None] * steps[None, :] % extent).astype(np.float32)
    angles = angles * np.float32(2.0 * math.pi / extent)
    scaling = np.float32(1.0 / math.sqrt(extent))
    real = (np.cos(angles) * scaling).astype(BF16)
    imag = (-np.sin(angles) * scaling).astype(BF16)
    tables = []
    for parity in (0, 1):
        re, im = real[:half, parity::2], imag[:half, parity::2]
        right = np.concatenate(
            [np.concatenate([re, im], 1), np.concatenate([-im, re], 1)], 0
        )
        tables += [right, np.ascontiguousarray(right.T)]
    return jnp.asarray(np.stack(tables))


def dot(a, b):
    return jnp.dot(a, b, preferred_element_type=F32)


def quarters(tl, tr, bl, br):
    return jnp.concatenate(
        [jnp.concatenate([tl, tr], 1), jnp.concatenate([bl, br], 1)], 0
    )


def iota(shape, dim):
    return lax.broadcasted_iota(jnp.int32, shape, dim)


def fetch(pairs, sems):
    copies = [
        pltpu.make_async_copy(source, target, sems.at[i])
        for i, (source, target) in enumerate(pairs)
    ]
    for copy in copies:
        copy.start()
    return copies


def pack_kernel(specimen, centers, cnt, helpers, out, tile_v, cen, hlp, sems):
    copies = fetch(((specimen, tile_v), (centers, cen), (helpers, hlp)), sems)
    for copy in copies:
        copy.wait()
    tile = tile_v.shape[1]
    lanes = tile_v.shape[2]
    rows, cols = iota((INFO, lanes), 0), iota((INFO, lanes), 1)
    info = jnp.where(rows == 0, -1.0, 0.0)
    for j in range(centers.shape[2]):
        helper = jnp.where(j < cnt[0, 0], hlp[0, 0, j], -1)
        for r, value in enumerate((helper, cen[0, 0, j, 0], cen[0, 0, j, 1])):
            info = jnp.where((rows == r) & (cols == j), value.astype(F32), info)
    info = info.astype(BF16)
    for p in range(2):
        out[p * tile : (p + 1) * tile] = tile_v[p].astype(BF16)
    out[2 * tile :] = info


def gather_columns(get, source, col, columns, shape):
    lane = iota(shape, 1)
    beside = own = jnp.zeros(shape, F32)
    for c in range(columns):
        block = get(c)
        near = ((source == c + 1) & (lane >= col)) | ((source == c - 1) & (lane < col))
        beside = jnp.where(near, block, beside)
        own = jnp.where(source == c, block, own)
    return jnp.concatenate([beside, own], 1)


def first_product(probe, patch, tables):
    half = patch[0].shape[1] // 2
    wr = probe[0] * patch[0] - probe[1] * patch[1]
    wi = probe[0] * patch[1] + probe[1] * patch[0]
    out = []
    for sign, table in zip((1, -1), tables):
        folded = jnp.concatenate(
            [wr[:, :half] + sign * wr[:, half:], wi[:, :half] + sign * wi[:, half:]], 1
        )
        out.append(dot(folded.astype(BF16), table))
    return out


def frame_of(band):
    columns, height, lanes = band.shape
    me = lax.axis_index("col").astype(F32)
    code = jnp.zeros((1, lanes), F32)
    for c in range(columns):
        info = band[c, height - INFO :].astype(F32)
        hit = info[0:1] == me
        code += jnp.where(hit, c * 128.0 * 128.0 + info[1:2] * 128.0 + info[2:3], 0.0)
    code = jnp.sum(code).astype(jnp.int32)
    return code // (128 * 128), code // 128 % 128, code % 128


def prepare_kernel(
    band, probe, measured, tables,
    info_out, amplitude, tables_out, probe_out, half_out, raw, raw_tables, raw_probe, groups, sems,
):
    copies = fetch(
        ((measured, raw), (tables, raw_tables), (probe, raw_probe)), sems
    )
    columns = band.shape[0]
    tile = (band.shape[1] - INFO) // 2
    extent = raw.shape[-1]
    half = extent // 2
    modes = raw_probe.shape[0]
    source, row, col = frame_of(band)
    which = iota((INFO, extent), 0)
    info = jnp.where(which == 0, source, jnp.where(which == 1, col, row))
    info_out[...] = info.astype(F32).astype(BF16)

    shape = (extent, extent)

    def original(i):
        return jnp.where(i < half, 2 * i, 2 * (i - half) + 1)

    copies[0].wait()
    sort = (iota(shape, 1) == original(iota(shape, 0))).astype(F32).astype(BF16)
    sort_t = (iota(shape, 0) == original(iota(shape, 1))).astype(F32).astype(BF16)
    value = raw[0, 0, 0]
    coarse = value.astype(BF16)
    fine = (value - coarse.astype(F32)).astype(BF16)
    amplitude[...] = sum(
        dot(dot(sort, part).astype(BF16), sort_t) for part in (coarse, fine)
    )

    def roller(old, new, shift, parity):
        wrapped = new % half < shift
        hit = (old + shift - jnp.where(old % half + shift >= half, half, 0)) == new
        sign = jnp.where(wrapped, -1.0, 1.0) if parity else 1.0
        return jnp.where(hit, sign, 0.0).astype(BF16)

    copies[1].wait()
    i, j = iota(shape, 0), iota(shape, 1)
    for parity in range(2):
        right, left = raw_tables[2 * parity], raw_tables[2 * parity + 1]
        for axis, shift in enumerate((col, row)):
            rolled = dot(left, roller(i, j, shift, parity)).astype(BF16)
            rolled_t = dot(roller(j, i, shift, parity), right).astype(BF16)
            tables_out[4 * axis + parity] = rolled_t if axis == 0 else rolled
            tables_out[4 * axis + 2 + parity] = rolled if axis == 0 else rolled_t

    copies[2].wait()
    count = extent // 8
    base = row // 8
    step = row % 8
    lane = iota((extent, half), 1)
    sub = iota((count, 8, extent), 1)
    for k in range(modes):
        for p in range(2):
            lo = pltpu.roll(raw_probe[k, p, :, :half], col, 1)
            hi = pltpu.roll(raw_probe[k, p, :, half:], col, 1)
            turned = jnp.concatenate(
                [jnp.where(lane < col, hi, lo), jnp.where(lane < col, lo, hi)], 1
            )
            turned = pltpu.roll(turned.reshape(count, 8, extent), step, 1)
            turned = jnp.where(
                sub < step, jnp.concatenate([turned[-1:], turned[:-1]], 0), turned
            )
            groups[:count] = turned
            groups[count:] = turned
            probe_out[k, p] = groups[pl.ds(count - base, count)].reshape(extent, extent)

    patch = [
        gather_columns(
            lambda c: band[c, p * tile : (p + 1) * tile].astype(F32),
            source, col, columns, (tile, tile),
        )
        for p in range(2)
    ]
    for k in range(modes):
        products = first_product(
            [probe_out[k, p, half:] for p in range(2)], patch, (tables_out[0], tables_out[1])
        )
        for parity in range(2):
            half_out[k, parity] = products[parity]


def frame_kernel(
    first, second, info, amplitude, tables, probe, half_own,
    to_rows, turned, patch, folded, half_far, mixed, far, corrected, product, mixed_back,
):
    columns = first.shape[0]
    tile = (first.shape[1] - INFO) // 2
    extent = probe.shape[-1]
    half = extent // 2
    modes = probe.shape[0]
    odd = lax.axis_index("row") % 2
    source, col, row = (
        info[r : r + 1, :tile].astype(F32).astype(jnp.int32) for r in range(3)
    )
    strips = [pl.ds(r, STRIP) for r in range(0, half, STRIP)]
    lower = [pl.ds(half + r, STRIP) for r in range(0, half, STRIP)]

    def split(x):
        return x[:, :half], x[:, half:]

    def join(x, y):
        return jnp.concatenate([x, y], 1).astype(BF16)

    def gather(s):
        rows = iota((STRIP, tile), 0) + s.start
        from_first = (rows >= row).astype(jnp.int32) == odd
        for p in range(2):
            part = pl.ds(p * tile + s.start, STRIP)
            patch[p, s] = gather_columns(
                lambda c: jnp.where(
                    from_first, first[c, part].astype(F32), second[c, part].astype(F32)
                ),
                source, col, columns, (STRIP, tile),
            )

    def wave(k):
        for s in strips:
            pr, pi, xr, xi = probe[k, 0, s], probe[k, 1, s], patch[0, s], patch[1, s]
            re = split(pr * xr - pi * xi)
            im = split(pr * xi + pi * xr)
            folded[k, 0, s] = join(re[0] + re[1], im[0] + im[1])
            folded[k, 1, s] = join(re[0] - re[1], im[0] - im[1])

    def along_rows(k):
        for q in range(2):
            half_far[k, q] = dot(folded[k, q], tables[q])

    def mix(k):
        for s, t in zip(strips, lower):
            even, odds = half_far[k, 0, s], half_far[k, 1, s]
            even_own, odds_own = half_own[k, 0, s], half_own[k, 1, s]
            for q, (e, o) in enumerate(
                ((even + even_own, odds + odds_own), (even - even_own, odds - odds_own))
            ):
                (er, ei), (our, oui) = split(e), split(o)
                mixed[k, q, s] = join(er, our)
                mixed[k, q, t] = join(ei, oui)

    def along_columns(k, q):
        far[k, q] = dot(tables[4 + q], mixed[k, q])

    def correct(q, which):
        for s, t in list(zip(strips, lower))[which]:
            re = [far[k, q, s] for k in range(modes)]
            im = [far[k, q, t] for k in range(modes)]
            intensity = sum(x * x for x in re + im)
            size = amplitude[pl.ds(q * half + s.start, STRIP)]
            factor = 1.0 - size * lax.rsqrt(jnp.maximum(intensity, 0.25))
            out = pl.ds(q * half + s.start, STRIP)
            for k in range(modes):
                (re_even, re_odd), (im_even, im_odd) = split(re[k] * factor), split(im[k] * factor)
                corrected[k, 0, out] = join(re_even, im_even)
                corrected[k, 1, out] = join(re_odd, im_odd)

    def back_along_rows(k, q):
        part = pl.ds(q * half, half)
        for c in range(2):
            product[k, c, part] = dot(corrected[k, c, part], tables[2 + c])

    def mix_back(k, q):
        for s, t in zip(strips, lower):
            part = pl.ds(q * half + s.start, STRIP)
            x, y = product[k, 0, part], product[k, 1, part]
            (lr, li), (hr, hi) = split(x + y), split(x - y)
            mixed_back[k, q, s] = join(lr, hr)
            mixed_back[k, q, t] = join(li, hi)

    def back_along_columns(k, q):
        turned[k, q] = dot(tables[6 + q], mixed_back[k, q])

    for s in strips:
        gather(s)
    for k in range(modes + 1):
        if k < modes:
            wave(k)
            along_rows(k)
        if k > 0:
            mix(k - 1)
            along_columns(k - 1, 0)
    share = -(-len(strips) // modes)
    for k in range(modes):
        along_columns(k, 1)
        correct(0, slice(k * share, (k + 1) * share))
    for k in range(modes):
        back_along_rows(k, 0)
        correct(1, slice(k * share, (k + 1) * share))
    for k in range(modes):
        mix_back(k, 0)
        back_along_columns(k, 0)
        back_along_rows(k, 1)
    for k in range(modes):
        mix_back(k, 1)
        back_along_columns(k, 1)
    for s, t in zip(strips, lower):
        accumulate(to_rows, turned, probe, s, t, s, 1)


def accumulate(out, turned, probe, s, t, rows, sign):
    tile = out.shape[0] // 2
    re = im = 0.0
    for k in range(probe.shape[0]):
        pr, pi = probe[k, 0, rows], probe[k, 1, rows]
        cr = turned[k, 0, s] + sign * turned[k, 1, s]
        ci = turned[k, 0, t] + sign * turned[k, 1, t]
        re += pr * cr + pi * ci
        im += pr * ci - pi * cr
    out[s] = re.astype(BF16)
    out[pl.ds(tile + s.start, STRIP)] = im.astype(BF16)


def place(block, columns, source, col, taken):
    tile = block.shape[1] // 2
    beside, own = block[:, :tile], block[:, tile:]
    lane = iota(own.shape, 1)
    if taken is not None:
        beside, own = jnp.where(taken, beside, 0.0), jnp.where(taken, own, 0.0)
    out = []
    for c in range(columns):
        near = ((source == c + 1) & (lane >= col)) | ((source == c - 1) & (lane < col))
        out.append(jnp.where(near, beside, 0.0) + jnp.where(source == c, own, 0.0))
    return out


def finish_kernel(
    band, first_band, second_band, turned, probe, first, partial, second_info, centre,
):
    columns = band.shape[0]
    tile = (band.shape[1] - INFO) // 2
    odd = lax.axis_index("row") % 2
    own_frame, first_frame, second_frame = (
        frame_of(b) for b in (band, first_band, second_band)
    )
    which = iota(second_info.shape, 0)
    second_info[...] = jnp.where(
        which == 0, second_frame[0], jnp.where(which == 1, second_frame[1], second_frame[2])
    )
    for r in range(0, tile, STRIP):
        s, t = pl.ds(r, STRIP), pl.ds(tile + r, STRIP)
        accumulate(centre, turned, probe, s, t, t, -1)
        before = (iota((STRIP, tile), 0) + r < first_frame[1]).astype(jnp.int32)
        for part in (s, t):
            mine = place(centre[part].astype(F32), columns, own_frame[0], own_frame[2], None)
            other = place(
                first[part].astype(F32), columns, first_frame[0], first_frame[2], before == odd
            )
            for c in range(columns):
                partial[c, part] = mine[c] + other[c]


def fold_kernel(partial, second, second_info, out):
    columns, height, tile = out.shape
    odd = lax.axis_index("row") % 2
    source, row, col = (second_info[r : r + 1] for r in range(3))
    for r in range(0, height, STRIP):
        s = pl.ds(r, STRIP)
        before = (iota((STRIP, tile), 0) + r % tile < row).astype(jnp.int32)
        other = place(second[s].astype(F32), columns, source, col, before == 1 - odd)
        for c in range(columns):
            out[c, s] = (partial[c, s] + other[c]).astype(BF16)


def call(kernel, name, out_shape, in_specs, scratch, flops, moved, *args):
    args = [
        pltpu.with_memory_space_constraint(arg, pltpu.HBM) if spec is HBM else arg
        for arg, spec in zip(args, in_specs)
    ]
    return pl.pallas_call(
        kernel,
        out_shape=out_shape,
        in_specs=in_specs,
        out_specs=jax.tree.map(lambda _: VMEM, out_shape),
        scratch_shapes=scratch,
        compiler_params=pltpu.CompilerParams(vmem_limit_bytes=32 * 2**20),
        cost_estimate=pl.CostEstimate(flops=flops, bytes_accessed=moved, transcendentals=0),
        name=name,
    )(*args)


def per_device(specimen, probe, measured, centers, frame_counts, helper_cols):
    extent = probe.shape[-1]
    half = extent // 2
    tile = specimen.shape[1]
    modes = probe.shape[0]
    columns = lax.axis_size("col")
    height = 2 * tile
    part = jax.ShapeDtypeStruct((height, extent), BF16)
    dma = pltpu.SemaphoreType.DMA

    packed = call(
        pack_kernel, "pack",
        jax.ShapeDtypeStruct((height + INFO, tile), BF16),
        [HBM, HBM, SMEM, HBM],
        [
            pltpu.VMEM(specimen.shape, F32),
            pltpu.SMEM(centers.shape, jnp.int32),
            pltpu.SMEM(helper_cols.shape, jnp.int32),
            dma((3,)),
        ],
        10**5, 2**19,
        specimen, centers, frame_counts, helper_cols,
    )
    band = lax.all_gather(packed, "col")

    rows = lax.axis_size("row")
    swaps = []
    for start in (0, 1):
        pairs = [(i, i + 1) for i in range(start, rows - 1, 2)]
        swaps.append(pairs + [(b, a) for a, b in pairs])
    second = lax.ppermute(band, "row", swaps[1])
    first = lax.ppermute(band, "row", swaps[0])
    tables = dft_tables(extent)
    prepared = call(
        prepare_kernel, "prepare",
        (
            jax.ShapeDtypeStruct((INFO, extent), BF16),
            jax.ShapeDtypeStruct((extent, extent), F32),
            jax.ShapeDtypeStruct((8, extent, extent), BF16),
            jax.ShapeDtypeStruct(probe.shape, F32),
            jax.ShapeDtypeStruct((modes, 2, tile, extent), F32),
        ),
        [VMEM, HBM, HBM, HBM],
        [
            pltpu.VMEM(measured.shape, F32),
            pltpu.VMEM(tables.shape, BF16),
            pltpu.VMEM(probe.shape, F32),
            pltpu.VMEM((extent // 4, 8, extent), F32),
            dma((3,)),
        ],
        10**9, 2**22,
        band, probe, measured, tables,
    )
    full = (modes, 2, extent, extent)
    to_rows, turned = call(
        frame_kernel, "frame",
        (part, jax.ShapeDtypeStruct(full, F32)),
        [VMEM] * 7,
        [
            pltpu.VMEM((2, tile, extent), F32),
            pltpu.VMEM((modes, 2, half, extent), BF16),
            pltpu.VMEM((modes, 2, half, extent), F32),
            pltpu.VMEM(full, BF16),
            pltpu.VMEM(full, F32),
            pltpu.VMEM(full, BF16),
            pltpu.VMEM(full, F32),
            pltpu.VMEM(full, BF16),
        ],
        2 * 10**9, 2**22,
        first, second, *prepared,
    )
    from_first = lax.ppermute(to_rows, "row", swaps[0])
    from_second = lax.ppermute(to_rows, "row", swaps[1])
    partial, second_info = call(
        finish_kernel, "finish",
        (
            jax.ShapeDtypeStruct((columns, height, tile), F32),
            jax.ShapeDtypeStruct((8, tile), jnp.int32),
        ),
        [VMEM] * 6,
        [pltpu.VMEM((height, extent), BF16)],
        10**7, 2**22,
        band, first, second, turned, prepared[3], from_first,
    )
    summed = call(
        fold_kernel, "fold",
        jax.ShapeDtypeStruct((columns, height, tile), BF16),
        [VMEM] * 3,
        [],
        10**7, 2**20,
        partial, from_second, second_info,
    )
    shares = lax.all_to_all(summed, "col", split_axis=0, concat_axis=0, tiled=True)
    return jnp.sum(shares.astype(F32), axis=0).reshape(2, tile, tile)


def solution(mesh):
    return jax.shard_map(
        per_device,
        mesh=mesh,
        in_specs=(
            P(None, "row", "col"),
            P(),
            P("row", "col", None, None, None),
            P("row", "col", None, None),
            P("row", "col"),
            P("row", "col", None),
        ),
        out_specs=P(None, "row", "col"),
        check_vma=False,
    )
```

```python
import functools
import math

import jax
import jax.numpy as jnp
import numpy as np
from jax import lax
from jax.experimental import pallas as pl
from jax.experimental.pallas import tpu as pltpu
from jax.sharding import PartitionSpec as P

F32 = jnp.float32
BF16 = jnp.bfloat16
INFO = 16
STRIP = 16
VMEM = pl.BlockSpec(memory_space=pltpu.VMEM)
SMEM = pl.BlockSpec(memory_space=pltpu.SMEM)
HBM = pl.BlockSpec(memory_space=pltpu.HBM)


def dft_tables(extent):
    half = extent // 2
    steps = np.arange(extent, dtype=np.int32)
    angles = (steps[:, None] * steps[None, :] % extent).astype(np.float32)
    angles = angles * np.float32(2.0 * math.pi / extent)
    scaling = np.float32(1.0 / math.sqrt(extent))
    real = (np.cos(angles) * scaling).astype(BF16)
    imag = (-np.sin(angles) * scaling).astype(BF16)
    tables = []
    for parity in (0, 1):
        re, im = real[:half, parity::2], imag[:half, parity::2]
        right = np.concatenate(
            [np.concatenate([re, im], 1), np.concatenate([-im, re], 1)], 0
        )
        tables += [right, np.ascontiguousarray(right.T)]
    return jnp.asarray(np.stack(tables))


def dot(a, b):
    return jnp.dot(a, b, preferred_element_type=F32)


def quarters(tl, tr, bl, br):
    return jnp.concatenate(
        [jnp.concatenate([tl, tr], 1), jnp.concatenate([bl, br], 1)], 0
    )


def iota(shape, dim):
    return lax.broadcasted_iota(jnp.int32, shape, dim)


def fetch(pairs, sems):
    copies = [
        pltpu.make_async_copy(source, target, sems.at[i])
        for i, (source, target) in enumerate(pairs)
    ]
    for copy in copies:
        copy.start()
    return copies


def pack_kernel(specimen, centers, cnt, helpers, out, tile_v, cen, hlp, sems):
    copies = fetch(((specimen, tile_v), (centers, cen), (helpers, hlp)), sems)
    for copy in copies:
        copy.wait()
    tile = tile_v.shape[1]
    lanes = tile_v.shape[2]
    rows, cols = iota((INFO, lanes), 0), iota((INFO, lanes), 1)
    info = jnp.where(rows == 0, -1.0, 0.0)
    for j in range(centers.shape[2]):
        helper = jnp.where(j < cnt[0, 0], hlp[0, 0, j], -1)
        for r, value in enumerate((helper, cen[0, 0, j, 0], cen[0, 0, j, 1])):
            info = jnp.where((rows == r) & (cols == j), value.astype(F32), info)
    info = info.astype(BF16)
    for p in range(2):
        out[p * tile : (p + 1) * tile] = tile_v[p].astype(BF16)
    out[2 * tile :] = info


def gather_columns(get, source, col, columns, shape):
    lane = iota(shape, 1)
    beside = own = jnp.zeros(shape, F32)
    for c in range(columns):
        block = get(c)
        near = ((source == c + 1) & (lane >= col)) | ((source == c - 1) & (lane < col))
        beside = jnp.where(near, block, beside)
        own = jnp.where(source == c, block, own)
    return jnp.concatenate([beside, own], 1)


def first_product(probe, patch, tables):
    half = patch[0].shape[1] // 2
    wr = probe[0] * patch[0] - probe[1] * patch[1]
    wi = probe[0] * patch[1] + probe[1] * patch[0]
    out = []
    for sign, table in zip((1, -1), tables):
        folded = jnp.concatenate(
            [wr[:, :half] + sign * wr[:, half:], wi[:, :half] + sign * wi[:, half:]], 1
        )
        out.append(dot(folded.astype(BF16), table))
    return out


def frame_of(band, base, columns):
    _, height, lanes = band.shape
    me = lax.axis_index("col").astype(F32)
    code = jnp.zeros((1, lanes), F32)
    for c in range(columns):
        info = band[base + c, height - INFO :].astype(F32)
        hit = info[0:1] == me
        code += jnp.where(hit, c * 128.0 * 128.0 + info[1:2] * 128.0 + info[2:3], 0.0)
    code = jnp.sum(code).astype(jnp.int32)
    return code // (128 * 128), code // 128 % 128, code % 128


def halves(bands):
    columns = bands.shape[0] // 2
    odd = lax.axis_index("row") % 2
    return odd * columns, (1 - odd) * columns, columns


def prepare_kernel(
    bands, probe, measured, tables,
    info_out, amplitude, tables_out, probe_out, half_out, raw, raw_tables, raw_probe, groups, sems,
):
    copies = fetch(
        ((measured, raw), (tables, raw_tables), (probe, raw_probe)), sems
    )
    mine, _, columns = halves(bands)
    tile = (bands.shape[1] - INFO) // 2
    extent = raw.shape[-1]
    half = extent // 2
    modes = raw_probe.shape[0]
    source, row, col = frame_of(bands, mine, columns)
    which = iota((INFO, extent), 0)
    info = jnp.where(which == 0, source, jnp.where(which == 1, col, row))
    info_out[...] = info.astype(F32).astype(BF16)

    shape = (extent, extent)

    def original(i):
        return jnp.where(i < half, 2 * i, 2 * (i - half) + 1)

    copies[0].wait()
    sort = (iota(shape, 1) == original(iota(shape, 0))).astype(F32).astype(BF16)
    sort_t = (iota(shape, 0) == original(iota(shape, 1))).astype(F32).astype(BF16)
    value = raw[0, 0, 0]
    coarse = value.astype(BF16)
    fine = (value - coarse.astype(F32)).astype(BF16)
    amplitude[...] = sum(
        dot(dot(sort, part).astype(BF16), sort_t) for part in (coarse, fine)
    )

    def roller(old, new, shift, parity):
        wrapped = new % half < shift
        hit = (old + shift - jnp.where(old % half + shift >= half, half, 0)) == new
        sign = jnp.where(wrapped, -1.0, 1.0) if parity else 1.0
        return jnp.where(hit, sign, 0.0).astype(BF16)

    copies[1].wait()
    i, j = iota(shape, 0), iota(shape, 1)
    for parity in range(2):
        right, left = raw_tables[2 * parity], raw_tables[2 * parity + 1]
        for axis, shift in enumerate((col, row)):
            rolled = dot(left, roller(i, j, shift, parity)).astype(BF16)
            rolled_t = dot(roller(j, i, shift, parity), right).astype(BF16)
            tables_out[4 * axis + parity] = rolled_t if axis == 0 else rolled
            tables_out[4 * axis + 2 + parity] = rolled if axis == 0 else rolled_t

    copies[2].wait()
    count = extent // 8
    base = row // 8
    step = row % 8
    lane = iota((extent, half), 1)
    sub = iota((count, 8, extent), 1)
    for k in range(modes):
        for p in range(2):
            lo = pltpu.roll(raw_probe[k, p, :, :half], col, 1)
            hi = pltpu.roll(raw_probe[k, p, :, half:], col, 1)
            turned = jnp.concatenate(
                [jnp.where(lane < col, hi, lo), jnp.where(lane < col, lo, hi)], 1
            )
            turned = pltpu.roll(turned.reshape(count, 8, extent), step, 1)
            turned = jnp.where(
                sub < step, jnp.concatenate([turned[-1:], turned[:-1]], 0), turned
            )
            groups[:count] = turned
            groups[count:] = turned
            probe_out[k, p] = groups[pl.ds(count - base, count)].reshape(extent, extent)

    patch = [
        gather_columns(
            lambda c: bands[mine + c, p * tile : (p + 1) * tile].astype(F32),
            source, col, columns, (tile, tile),
        )
        for p in range(2)
    ]
    for k in range(modes):
        products = first_product(
            [probe_out[k, p, half:] for p in range(2)], patch, (tables_out[0], tables_out[1])
        )
        for parity in range(2):
            half_out[k, parity] = products[parity]


def frame_kernel(
    bands, second, info, amplitude, tables, probe, half_own,
    to_rows, turned, patch, folded, half_far, mixed, far, corrected, product, mixed_back,
):
    _, theirs, columns = halves(bands)
    tile = (bands.shape[1] - INFO) // 2
    extent = probe.shape[-1]
    half = extent // 2
    modes = probe.shape[0]
    odd = lax.axis_index("row") % 2
    source, col, row = (
        info[r : r + 1, :tile].astype(F32).astype(jnp.int32) for r in range(3)
    )
    strips = [pl.ds(r, STRIP) for r in range(0, half, STRIP)]
    lower = [pl.ds(half + r, STRIP) for r in range(0, half, STRIP)]

    def split(x):
        return x[:, :half], x[:, half:]

    def join(x, y):
        return jnp.concatenate([x, y], 1).astype(BF16)

    def gather(s):
        rows = iota((STRIP, tile), 0) + s.start
        from_first = (rows >= row).astype(jnp.int32) == odd
        for p in range(2):
            part = pl.ds(p * tile + s.start, STRIP)
            patch[p, s] = gather_columns(
                lambda c: jnp.where(
                    from_first, bands[theirs + c, part].astype(F32), second[c, part].astype(F32)
                ),
                source, col, columns, (STRIP, tile),
            )

    def wave(k):
        for s in strips:
            pr, pi, xr, xi = probe[k, 0, s], probe[k, 1, s], patch[0, s], patch[1, s]
            re = split(pr * xr - pi * xi)
            im = split(pr * xi + pi * xr)
            folded[k, 0, s] = join(re[0] + re[1], im[0] + im[1])
            folded[k, 1, s] = join(re[0] - re[1], im[0] - im[1])

    def along_rows(k):
        for q in range(2):
            half_far[k, q] = dot(folded[k, q], tables[q])

    def mix(k):
        for s, t in zip(strips, lower):
            even, odds = half_far[k, 0, s], half_far[k, 1, s]
            even_own, odds_own = half_own[k, 0, s], half_own[k, 1, s]
            for q, (e, o) in enumerate(
                ((even + even_own, odds + odds_own), (even - even_own, odds - odds_own))
            ):
                (er, ei), (our, oui) = split(e), split(o)
                mixed[k, q, s] = join(er, our)
                mixed[k, q, t] = join(ei, oui)

    def along_columns(k, q):
        far[k, q] = dot(tables[4 + q], mixed[k, q])

    def correct(q, which):
        for s, t in list(zip(strips, lower))[which]:
            re = [far[k, q, s] for k in range(modes)]
            im = [far[k, q, t] for k in range(modes)]
            intensity = sum(x * x for x in re + im)
            size = amplitude[pl.ds(q * half + s.start, STRIP)]
            factor = 1.0 - size * lax.rsqrt(jnp.maximum(intensity, 0.25))
            out = pl.ds(q * half + s.start, STRIP)
            for k in range(modes):
                (re_even, re_odd), (im_even, im_odd) = split(re[k] * factor), split(im[k] * factor)
                corrected[k, 0, out] = join(re_even, im_even)
                corrected[k, 1, out] = join(re_odd, im_odd)

    def back_along_rows(k, q):
        part = pl.ds(q * half, half)
        for c in range(2):
            product[k, c, part] = dot(corrected[k, c, part], tables[2 + c])

    def mix_back(k, q):
        for s, t in zip(strips, lower):
            part = pl.ds(q * half + s.start, STRIP)
            x, y = product[k, 0, part], product[k, 1, part]
            (lr, li), (hr, hi) = split(x + y), split(x - y)
            mixed_back[k, q, s] = join(lr, hr)
            mixed_back[k, q, t] = join(li, hi)

    def back_along_columns(k, q):
        turned[k, q] = dot(tables[6 + q], mixed_back[k, q])

    for s in strips:
        gather(s)
    for k in range(modes + 1):
        if k < modes:
            wave(k)
            along_rows(k)
        if k > 0:
            mix(k - 1)
            along_columns(k - 1, 0)
    share = -(-len(strips) // modes)
    for k in range(modes):
        along_columns(k, 1)
        correct(0, slice(k * share, (k + 1) * share))
    for k in range(modes):
        back_along_rows(k, 0)
        correct(1, slice(k * share, (k + 1) * share))
    for k in range(modes):
        mix_back(k, 0)
        back_along_columns(k, 0)
        back_along_rows(k, 1)
    for k in range(modes):
        mix_back(k, 1)
        back_along_columns(k, 1)
    for s, t in zip(strips, lower):
        accumulate(to_rows, turned, probe, s, t, s, 1)


def accumulate(out, turned, probe, s, t, rows, sign):
    tile = out.shape[0] // 2
    re = im = 0.0
    for k in range(probe.shape[0]):
        pr, pi = probe[k, 0, rows], probe[k, 1, rows]
        cr = turned[k, 0, s] + sign * turned[k, 1, s]
        ci = turned[k, 0, t] + sign * turned[k, 1, t]
        re += pr * cr + pi * ci
        im += pr * ci - pi * cr
    out[s] = re.astype(BF16)
    out[pl.ds(tile + s.start, STRIP)] = im.astype(BF16)


def place(block, columns, source, col, taken):
    tile = block.shape[1] // 2
    beside, own = block[:, :tile], block[:, tile:]
    lane = iota(own.shape, 1)
    if taken is not None:
        beside, own = jnp.where(taken, beside, 0.0), jnp.where(taken, own, 0.0)
    out = []
    for c in range(columns):
        near = ((source == c + 1) & (lane >= col)) | ((source == c - 1) & (lane < col))
        out.append(jnp.where(near, beside, 0.0) + jnp.where(source == c, own, 0.0))
    return out


def finish_kernel(
    bands, second_band, turned, probe, first, partial, second_info, centre,
):
    mine, theirs, columns = halves(bands)
    tile = (bands.shape[1] - INFO) // 2
    odd = lax.axis_index("row") % 2
    own_frame, first_frame, second_frame = (
        frame_of(ref, base, columns)
        for ref, base in ((bands, mine), (bands, theirs), (second_band, 0))
    )
    which = iota(second_info.shape, 0)
    second_info[...] = jnp.where(
        which == 0, second_frame[0], jnp.where(which == 1, second_frame[1], second_frame[2])
    )
    for r in range(0, tile, STRIP):
        s, t = pl.ds(r, STRIP), pl.ds(tile + r, STRIP)
        accumulate(centre, turned, probe, s, t, t, -1)
        before = (iota((STRIP, tile), 0) + r < first_frame[1]).astype(jnp.int32)
        for part in (s, t):
            own = place(centre[part].astype(F32), columns, own_frame[0], own_frame[2], None)
            other = place(
                first[part].astype(F32), columns, first_frame[0], first_frame[2], before == odd
            )
            for c in range(columns):
                partial[c, part] = own[c] + other[c]


def fold_kernel(partial, second, second_info, out):
    columns, height, tile = out.shape
    odd = lax.axis_index("row") % 2
    source, row, col = (second_info[r : r + 1] for r in range(3))
    for r in range(0, height, STRIP):
        s = pl.ds(r, STRIP)
        before = (iota((STRIP, tile), 0) + r % tile < row).astype(jnp.int32)
        other = place(second[s].astype(F32), columns, source, col, before == 1 - odd)
        for c in range(columns):
            out[c, s] = (partial[c, s] + other[c]).astype(BF16)


def call(kernel, name, out_shape, in_specs, scratch, flops, moved, *args):
    args = [
        pltpu.with_memory_space_constraint(arg, pltpu.HBM) if spec is HBM else arg
        for arg, spec in zip(args, in_specs)
    ]
    return pl.pallas_call(
        kernel,
        out_shape=out_shape,
        in_specs=in_specs,
        out_specs=jax.tree.map(lambda _: VMEM, out_shape),
        scratch_shapes=scratch,
        compiler_params=pltpu.CompilerParams(vmem_limit_bytes=32 * 2**20),
        cost_estimate=pl.CostEstimate(flops=flops, bytes_accessed=moved, transcendentals=0),
        name=name,
    )(*args)


def per_device(specimen, probe, measured, centers, frame_counts, helper_cols):
    extent = probe.shape[-1]
    half = extent // 2
    tile = specimen.shape[1]
    modes = probe.shape[0]
    columns = lax.axis_size("col")
    height = 2 * tile
    part = jax.ShapeDtypeStruct((height, extent), BF16)
    dma = pltpu.SemaphoreType.DMA

    packed = call(
        pack_kernel, "pack",
        jax.ShapeDtypeStruct((height + INFO, tile), BF16),
        [HBM, HBM, SMEM, HBM],
        [
            pltpu.VMEM(specimen.shape, F32),
            pltpu.SMEM(centers.shape, jnp.int32),
            pltpu.SMEM(helper_cols.shape, jnp.int32),
            dma((3,)),
        ],
        10**5, 2**19,
        specimen, centers, frame_counts, helper_cols,
    )
    rows = lax.axis_size("row")
    swaps = []
    for start in (0, 1):
        pairs = [(i, i + 1) for i in range(start, rows - 1, 2)]
        swaps.append(pairs + [(b, a) for a, b in pairs])
    groups = [
        [r * columns + c for r in (start, start + 1) for c in range(columns)]
        for start in range(0, rows, 2)
    ]
    bands = lax.all_gather(packed, ("row", "col"), axis_index_groups=groups)
    band = lax.dynamic_slice_in_dim(bands, lax.axis_index("row") % 2 * columns, columns)
    second = lax.ppermute(band, "row", swaps[1])
    tables = dft_tables(extent)
    prepared = call(
        prepare_kernel, "prepare",
        (
            jax.ShapeDtypeStruct((INFO, extent), BF16),
            jax.ShapeDtypeStruct((extent, extent), F32),
            jax.ShapeDtypeStruct((8, extent, extent), BF16),
            jax.ShapeDtypeStruct(probe.shape, F32),
            jax.ShapeDtypeStruct((modes, 2, tile, extent), F32),
        ),
        [VMEM, HBM, HBM, HBM],
        [
            pltpu.VMEM(measured.shape, F32),
            pltpu.VMEM(tables.shape, BF16),
            pltpu.VMEM(probe.shape, F32),
            pltpu.VMEM((extent // 4, 8, extent), F32),
            dma((3,)),
        ],
        10**9, 2**22,
        bands, probe, measured, tables,
    )
    full = (modes, 2, extent, extent)
    to_rows, turned = call(
        frame_kernel, "frame",
        (part, jax.ShapeDtypeStruct(full, F32)),
        [VMEM] * 7,
        [
            pltpu.VMEM((2, tile, extent), F32),
            pltpu.VMEM((modes, 2, half, extent), BF16),
            pltpu.VMEM((modes, 2, half, extent), F32),
            pltpu.VMEM(full, BF16),
            pltpu.VMEM(full, F32),
            pltpu.VMEM(full, BF16),
            pltpu.VMEM(full, F32),
            pltpu.VMEM(full, BF16),
        ],
        2 * 10**9, 2**22,
        bands, second, *prepared,
    )
    from_first = lax.ppermute(to_rows, "row", swaps[0])
    from_second = lax.ppermute(to_rows, "row", swaps[1])
    partial, second_info = call(
        finish_kernel, "finish",
        (
            jax.ShapeDtypeStruct((columns, height, tile), F32),
            jax.ShapeDtypeStruct((8, tile), jnp.int32),
        ),
        [VMEM] * 5,
        [pltpu.VMEM((height, extent), BF16)],
        10**7, 2**22,
        bands, second, turned, prepared[3], from_first,
    )
    summed = call(
        fold_kernel, "fold",
        jax.ShapeDtypeStruct((columns, height, tile), BF16),
        [VMEM] * 3,
        [],
        10**7, 2**20,
        partial, from_second, second_info,
    )
    shares = lax.all_to_all(summed, "col", split_axis=0, concat_axis=0, tiled=True)
    return jnp.sum(shares.astype(F32), axis=0).reshape(2, tile, tile)


def solution(mesh):
    return jax.shard_map(
        per_device,
        mesh=mesh,
        in_specs=(
            P(None, "row", "col"),
            P(),
            P("row", "col", None, None, None),
            P("row", "col", None, None),
            P("row", "col"),
            P("row", "col", None),
        ),
        out_specs=P(None, "row", "col"),
        check_vma=False,
    )
```

```python
import functools
import math

import jax
import jax.numpy as jnp
import numpy as np
from jax import lax
from jax.experimental import pallas as pl
from jax.experimental.pallas import tpu as pltpu
from jax.sharding import PartitionSpec as P

F32 = jnp.float32
BF16 = jnp.bfloat16
INFO = 16
STRIP = 16
BATCH = 2
VMEM = pl.BlockSpec(memory_space=pltpu.VMEM)
SMEM = pl.BlockSpec(memory_space=pltpu.SMEM)
HBM = pl.BlockSpec(memory_space=pltpu.HBM)


def dft_tables(extent):
    half = extent // 2
    steps = np.arange(extent, dtype=np.int32)
    angles = (steps[:, None] * steps[None, :] % extent).astype(np.float32)
    angles = angles * np.float32(2.0 * math.pi / extent)
    scaling = np.float32(1.0 / math.sqrt(extent))
    real = (np.cos(angles) * scaling).astype(BF16)
    imag = (-np.sin(angles) * scaling).astype(BF16)
    tables = []
    for parity in (0, 1):
        re, im = real[:half, parity::2], imag[:half, parity::2]
        right = np.concatenate(
            [np.concatenate([re, im], 1), np.concatenate([-im, re], 1)], 0
        )
        tables += [right, np.ascontiguousarray(right.T)]
    return jnp.asarray(np.stack(tables))


def dot(a, b):
    return jnp.dot(a, b, preferred_element_type=F32)


def quarters(tl, tr, bl, br):
    return jnp.concatenate(
        [jnp.concatenate([tl, tr], 1), jnp.concatenate([bl, br], 1)], 0
    )


def iota(shape, dim):
    return lax.broadcasted_iota(jnp.int32, shape, dim)


def fetch(pairs, sems):
    copies = [
        pltpu.make_async_copy(source, target, sems.at[i])
        for i, (source, target) in enumerate(pairs)
    ]
    for copy in copies:
        copy.start()
    return copies


def pack_kernel(specimen, centers, cnt, helpers, out, tile_v, cen, hlp, sems):
    copies = fetch(((specimen, tile_v), (centers, cen), (helpers, hlp)), sems)
    for copy in copies:
        copy.wait()
    tile = tile_v.shape[1]
    lanes = tile_v.shape[2]
    rows, cols = iota((INFO, lanes), 0), iota((INFO, lanes), 1)
    info = jnp.where(rows == 0, -1.0, 0.0)
    for j in range(centers.shape[2]):
        helper = jnp.where(j < cnt[0, 0], hlp[0, 0, j], -1)
        for r, value in enumerate((helper, cen[0, 0, j, 0], cen[0, 0, j, 1])):
            info = jnp.where((rows == r) & (cols == j), value.astype(F32), info)
    info = info.astype(BF16)
    for p in range(2):
        out[p * tile : (p + 1) * tile] = tile_v[p].astype(BF16)
    out[2 * tile :] = info


def gather_columns(get, source, col, columns, shape):
    lane = iota(shape, 1)
    beside = own = jnp.zeros(shape, F32)
    for c in range(columns):
        block = get(c)
        near = ((source == c + 1) & (lane >= col)) | ((source == c - 1) & (lane < col))
        beside = jnp.where(near, block, beside)
        own = jnp.where(source == c, block, own)
    return jnp.concatenate([beside, own], 1)


def first_product(probe, patch, tables):
    half = patch[0].shape[1] // 2
    wr = probe[0] * patch[0] - probe[1] * patch[1]
    wi = probe[0] * patch[1] + probe[1] * patch[0]
    out = []
    for sign, table in zip((1, -1), tables):
        folded = jnp.concatenate(
            [wr[:, :half] + sign * wr[:, half:], wi[:, :half] + sign * wi[:, half:]], 1
        )
        out.append(dot(folded.astype(BF16), table))
    return out


def frame_of(band):
    columns, height, lanes = band.shape
    me = lax.axis_index("col").astype(F32)
    code = jnp.zeros((1, lanes), F32)
    for c in range(columns):
        info = band[c, height - INFO :].astype(F32)
        hit = info[0:1] == me
        code += jnp.where(hit, c * 128.0 * 128.0 + info[1:2] * 128.0 + info[2:3], 0.0)
    code = jnp.sum(code).astype(jnp.int32)
    return code // (128 * 128), code // 128 % 128, code % 128


def prepare_kernel(
    band, probe, measured, tables,
    info_out, amplitude, tables_out, probe_out, half_out, raw, raw_tables, raw_probe, groups, sems,
):
    copies = fetch(
        ((measured, raw), (tables, raw_tables), (probe, raw_probe)), sems
    )
    columns = band.shape[0]
    tile = (band.shape[1] - INFO) // 2
    extent = raw.shape[-1]
    half = extent // 2
    modes = raw_probe.shape[0]
    source, row, col = frame_of(band)
    which = iota((INFO, extent), 0)
    info = jnp.where(which == 0, source, jnp.where(which == 1, col, row))
    info_out[...] = info.astype(F32).astype(BF16)

    shape = (extent, extent)

    def original(i):
        return jnp.where(i < half, 2 * i, 2 * (i - half) + 1)

    copies[0].wait()
    sort = (iota(shape, 1) == original(iota(shape, 0))).astype(F32).astype(BF16)
    sort_t = (iota(shape, 0) == original(iota(shape, 1))).astype(F32).astype(BF16)
    value = raw[0, 0, 0]
    coarse = value.astype(BF16)
    fine = (value - coarse.astype(F32)).astype(BF16)
    amplitude[...] = sum(
        dot(dot(sort, part).astype(BF16), sort_t) for part in (coarse, fine)
    )

    def roller(old, new, shift, parity):
        wrapped = new % half < shift
        hit = (old + shift - jnp.where(old % half + shift >= half, half, 0)) == new
        sign = jnp.where(wrapped, -1.0, 1.0) if parity else 1.0
        return jnp.where(hit, sign, 0.0).astype(BF16)

    copies[1].wait()
    i, j = iota(shape, 0), iota(shape, 1)
    for parity in range(2):
        right, left = raw_tables[2 * parity], raw_tables[2 * parity + 1]
        for axis, shift in enumerate((col, row)):
            rolled = dot(left, roller(i, j, shift, parity)).astype(BF16)
            rolled_t = dot(roller(j, i, shift, parity), right).astype(BF16)
            tables_out[4 * axis + parity] = rolled_t if axis == 0 else rolled
            tables_out[4 * axis + 2 + parity] = rolled if axis == 0 else rolled_t

    copies[2].wait()
    count = extent // 8
    base = row // 8
    step = row % 8
    lane = iota((extent, half), 1)
    sub = iota((count, 8, extent), 1)
    for k in range(modes):
        for p in range(2):
            lo = pltpu.roll(raw_probe[k, p, :, :half], col, 1)
            hi = pltpu.roll(raw_probe[k, p, :, half:], col, 1)
            turned = jnp.concatenate(
                [jnp.where(lane < col, hi, lo), jnp.where(lane < col, lo, hi)], 1
            )
            turned = pltpu.roll(turned.reshape(count, 8, extent), step, 1)
            turned = jnp.where(
                sub < step, jnp.concatenate([turned[-1:], turned[:-1]], 0), turned
            )
            groups[:count] = turned
            groups[count:] = turned
            probe_out[k, p] = groups[pl.ds(count - base, count)].reshape(extent, extent)

    patch = [
        gather_columns(
            lambda c: band[c, p * tile : (p + 1) * tile].astype(F32),
            source, col, columns, (tile, tile),
        )
        for p in range(2)
    ]
    for k in range(modes):
        products = first_product(
            [probe_out[k, p, half:] for p in range(2)], patch, (tables_out[0], tables_out[1])
        )
        for parity in range(2):
            half_out[k, parity] = products[parity]


def frame_kernel(
    first, second, info, amplitude, tables, probe, half_own,
    to_rows, turned, patch, folded, half_far, mixed, far, corrected, product, mixed_back,
):
    columns = first.shape[0]
    tile = (first.shape[1] - INFO) // 2
    extent = probe.shape[-1]
    half = extent // 2
    modes = probe.shape[0]
    odd = lax.axis_index("row") % 2
    source, col, row = (
        info[r : r + 1, :tile].astype(F32).astype(jnp.int32) for r in range(3)
    )
    strips = [pl.ds(r, STRIP) for r in range(0, half, STRIP)]
    lower = [pl.ds(half + r, STRIP) for r in range(0, half, STRIP)]

    def split(x):
        return x[:, :half], x[:, half:]

    def join(x, y):
        return jnp.concatenate([x, y], 1).astype(BF16)

    def gather(s):
        rows = iota((STRIP, tile), 0) + s.start
        from_first = (rows >= row).astype(jnp.int32) == odd
        for p in range(2):
            part = pl.ds(p * tile + s.start, STRIP)
            patch[p, s] = gather_columns(
                lambda c: jnp.where(
                    from_first, first[c, part].astype(F32), second[c, part].astype(F32)
                ),
                source, col, columns, (STRIP, tile),
            )

    def wave(k):
        for s in strips:
            pr, pi, xr, xi = probe[k, 0, s], probe[k, 1, s], patch[0, s], patch[1, s]
            re = split(pr * xr - pi * xi)
            im = split(pr * xi + pi * xr)
            out = pl.ds(k * half + s.start, STRIP)
            folded[0, out] = join(re[0] + re[1], im[0] + im[1])
            folded[1, out] = join(re[0] - re[1], im[0] - im[1])

    def along_rows(k, count):
        part = pl.ds(k * half, count * half)
        for q in range(2):
            half_far[q, part] = dot(folded[q, part], tables[q])

    def mix(k):
        for s, t in zip(strips, lower):
            rows = pl.ds(k * half + s.start, STRIP)
            even, odds = half_far[0, rows], half_far[1, rows]
            even_own, odds_own = half_own[k, 0, s], half_own[k, 1, s]
            for q, (e, o) in enumerate(
                ((even + even_own, odds + odds_own), (even - even_own, odds - odds_own))
            ):
                (er, ei), (our, oui) = split(e), split(o)
                mixed[k, q, s] = join(er, our)
                mixed[k, q, t] = join(ei, oui)

    def along_columns(k, q):
        far[k, q] = dot(tables[4 + q], mixed[k, q])

    def correct(q, which):
        for s, t in list(zip(strips, lower))[which]:
            re = [far[k, q, s] for k in range(modes)]
            im = [far[k, q, t] for k in range(modes)]
            intensity = sum(x * x for x in re + im)
            size = amplitude[pl.ds(q * half + s.start, STRIP)]
            factor = 1.0 - size * lax.rsqrt(jnp.maximum(intensity, 0.25))
            for k in range(modes):
                out = pl.ds(k * half + s.start, STRIP)
                (re_even, re_odd), (im_even, im_odd) = split(re[k] * factor), split(im[k] * factor)
                corrected[q, 0, out] = join(re_even, im_even)
                corrected[q, 1, out] = join(re_odd, im_odd)

    def back_along_rows(q):
        for c in range(2):
            product[q, c] = dot(corrected[q, c], tables[2 + c])

    def mix_back(k, q):
        for s, t in zip(strips, lower):
            part = pl.ds(k * half + s.start, STRIP)
            x, y = product[q, 0, part], product[q, 1, part]
            (lr, li), (hr, hi) = split(x + y), split(x - y)
            mixed_back[k, q, s] = join(lr, hr)
            mixed_back[k, q, t] = join(li, hi)

    def back_along_columns(k, q):
        turned[k, q] = dot(tables[6 + q], mixed_back[k, q])

    for s in strips:
        gather(s)
    for k in range(0, modes, BATCH):
        batch = range(k, min(k + BATCH, modes))
        for m in batch:
            wave(m)
        along_rows(k, len(batch))
        for m in range(k - BATCH, k):
            if m >= 0:
                mix(m)
                along_columns(m, 0)
    for m in range(modes - len(batch), modes):
        mix(m)
        along_columns(m, 0)
    share = -(-len(strips) // modes)
    for k in range(modes):
        along_columns(k, 1)
        correct(0, slice(k * share, (k + 1) * share))
    back_along_rows(0)
    correct(1, slice(0, None))
    for k in range(modes):
        mix_back(k, 0)
        back_along_columns(k, 0)
    back_along_rows(1)
    for k in range(modes):
        mix_back(k, 1)
        back_along_columns(k, 1)
    for s, t in zip(strips, lower):
        accumulate(to_rows, turned, probe, s, t, s, 1)


def accumulate(out, turned, probe, s, t, rows, sign):
    tile = out.shape[0] // 2
    re = im = 0.0
    for k in range(probe.shape[0]):
        pr, pi = probe[k, 0, rows], probe[k, 1, rows]
        cr = turned[k, 0, s] + sign * turned[k, 1, s]
        ci = turned[k, 0, t] + sign * turned[k, 1, t]
        re += pr * cr + pi * ci
        im += pr * ci - pi * cr
    out[s] = re.astype(BF16)
    out[pl.ds(tile + s.start, STRIP)] = im.astype(BF16)


def place(block, columns, source, col, taken):
    tile = block.shape[1] // 2
    beside, own = block[:, :tile], block[:, tile:]
    lane = iota(own.shape, 1)
    if taken is not None:
        beside, own = jnp.where(taken, beside, 0.0), jnp.where(taken, own, 0.0)
    out = []
    for c in range(columns):
        near = ((source == c + 1) & (lane >= col)) | ((source == c - 1) & (lane < col))
        out.append(jnp.where(near, beside, 0.0) + jnp.where(source == c, own, 0.0))
    return out


def finish_kernel(
    band, first_band, second_band, turned, probe, first, partial, second_info, centre,
):
    columns = band.shape[0]
    tile = (band.shape[1] - INFO) // 2
    odd = lax.axis_index("row") % 2
    own_frame, first_frame, second_frame = (
        frame_of(b) for b in (band, first_band, second_band)
    )
    which = iota(second_info.shape, 0)
    second_info[...] = jnp.where(
        which == 0, second_frame[0], jnp.where(which == 1, second_frame[1], second_frame[2])
    )
    for r in range(0, tile, STRIP):
        s, t = pl.ds(r, STRIP), pl.ds(tile + r, STRIP)
        accumulate(centre, turned, probe, s, t, t, -1)
        before = (iota((STRIP, tile), 0) + r < first_frame[1]).astype(jnp.int32)
        for part in (s, t):
            mine = place(centre[part].astype(F32), columns, own_frame[0], own_frame[2], None)
            other = place(
                first[part].astype(F32), columns, first_frame[0], first_frame[2], before == odd
            )
            for c in range(columns):
                partial[c, part] = mine[c] + other[c]


def fold_kernel(partial, second, second_info, out):
    columns, height, tile = out.shape
    odd = lax.axis_index("row") % 2
    source, row, col = (second_info[r : r + 1] for r in range(3))
    for r in range(0, height, STRIP):
        s = pl.ds(r, STRIP)
        before = (iota((STRIP, tile), 0) + r % tile < row).astype(jnp.int32)
        other = place(second[s].astype(F32), columns, source, col, before == 1 - odd)
        for c in range(columns):
            out[c, s] = (partial[c, s] + other[c]).astype(BF16)


def call(kernel, name, out_shape, in_specs, scratch, flops, moved, *args):
    args = [
        pltpu.with_memory_space_constraint(arg, pltpu.HBM) if spec is HBM else arg
        for arg, spec in zip(args, in_specs)
    ]
    return pl.pallas_call(
        kernel,
        out_shape=out_shape,
        in_specs=in_specs,
        out_specs=jax.tree.map(lambda _: VMEM, out_shape),
        scratch_shapes=scratch,
        compiler_params=pltpu.CompilerParams(vmem_limit_bytes=32 * 2**20),
        cost_estimate=pl.CostEstimate(flops=flops, bytes_accessed=moved, transcendentals=0),
        name=name,
    )(*args)


def per_device(specimen, probe, measured, centers, frame_counts, helper_cols):
    extent = probe.shape[-1]
    half = extent // 2
    tile = specimen.shape[1]
    modes = probe.shape[0]
    columns = lax.axis_size("col")
    height = 2 * tile
    part = jax.ShapeDtypeStruct((height, extent), BF16)
    dma = pltpu.SemaphoreType.DMA

    packed = call(
        pack_kernel, "pack",
        jax.ShapeDtypeStruct((height + INFO, tile), BF16),
        [HBM, HBM, SMEM, HBM],
        [
            pltpu.VMEM(specimen.shape, F32),
            pltpu.SMEM(centers.shape, jnp.int32),
            pltpu.SMEM(helper_cols.shape, jnp.int32),
            dma((3,)),
        ],
        10**5, 2**19,
        specimen, centers, frame_counts, helper_cols,
    )
    band = lax.all_gather(packed, "col")

    rows = lax.axis_size("row")
    swaps = []
    for start in (0, 1):
        pairs = [(i, i + 1) for i in range(start, rows - 1, 2)]
        swaps.append(pairs + [(b, a) for a, b in pairs])
    second = lax.ppermute(band, "row", swaps[1])
    first = lax.ppermute(band, "row", swaps[0])
    tables = dft_tables(extent)
    prepared = call(
        prepare_kernel, "prepare",
        (
            jax.ShapeDtypeStruct((INFO, extent), BF16),
            jax.ShapeDtypeStruct((extent, extent), F32),
            jax.ShapeDtypeStruct((8, extent, extent), BF16),
            jax.ShapeDtypeStruct(probe.shape, F32),
            jax.ShapeDtypeStruct((modes, 2, tile, extent), F32),
        ),
        [VMEM, HBM, HBM, HBM],
        [
            pltpu.VMEM(measured.shape, F32),
            pltpu.VMEM(tables.shape, BF16),
            pltpu.VMEM(probe.shape, F32),
            pltpu.VMEM((extent // 4, 8, extent), F32),
            dma((3,)),
        ],
        10**9, 2**22,
        band, probe, measured, tables,
    )
    full = (modes, 2, extent, extent)
    to_rows, turned = call(
        frame_kernel, "frame",
        (part, jax.ShapeDtypeStruct(full, F32)),
        [VMEM] * 7,
        [
            pltpu.VMEM((2, tile, extent), F32),
            pltpu.VMEM((2, modes * half, extent), BF16),
            pltpu.VMEM((2, modes * half, extent), F32),
            pltpu.VMEM(full, BF16),
            pltpu.VMEM(full, F32),
            pltpu.VMEM((2, 2, modes * half, extent), BF16),
            pltpu.VMEM((2, 2, modes * half, extent), F32),
            pltpu.VMEM(full, BF16),
        ],
        2 * 10**9, 2**22,
        first, second, *prepared,
    )
    from_first = lax.ppermute(to_rows, "row", swaps[0])
    from_second = lax.ppermute(to_rows, "row", swaps[1])
    partial, second_info = call(
        finish_kernel, "finish",
        (
            jax.ShapeDtypeStruct((columns, height, tile), F32),
            jax.ShapeDtypeStruct((8, tile), jnp.int32),
        ),
        [VMEM] * 6,
        [pltpu.VMEM((height, extent), BF16)],
        10**7, 2**22,
        band, first, second, turned, prepared[3], from_first,
    )
    summed = call(
        fold_kernel, "fold",
        jax.ShapeDtypeStruct((columns, height, tile), BF16),
        [VMEM] * 3,
        [],
        10**7, 2**20,
        partial, from_second, second_info,
    )
    shares = lax.all_to_all(summed, "col", split_axis=0, concat_axis=0, tiled=True)
    return jnp.sum(shares.astype(F32), axis=0).reshape(2, tile, tile)


def solution(mesh):
    return jax.shard_map(
        per_device,
        mesh=mesh,
        in_specs=(
            P(None, "row", "col"),
            P(),
            P("row", "col", None, None, None),
            P("row", "col", None, None),
            P("row", "col"),
            P("row", "col", None),
        ),
        out_specs=P(None, "row", "col"),
        check_vma=False,
    )
```

```python
import functools
import math

import jax
import jax.numpy as jnp
import numpy as np
from jax import lax
from jax.experimental import pallas as pl
from jax.experimental.pallas import tpu as pltpu
from jax.sharding import PartitionSpec as P

F32 = jnp.float32
BF16 = jnp.bfloat16
INFO = 16
STRIP = 16
VMEM = pl.BlockSpec(memory_space=pltpu.VMEM)
SMEM = pl.BlockSpec(memory_space=pltpu.SMEM)
HBM = pl.BlockSpec(memory_space=pltpu.HBM)


def dft_tables(extent):
    half = extent // 2
    steps = np.arange(extent, dtype=np.int32)
    angles = (steps[:, None] * steps[None, :] % extent).astype(np.float32)
    angles = angles * np.float32(2.0 * math.pi / extent)
    scaling = np.float32(1.0 / math.sqrt(extent))
    real = (np.cos(angles) * scaling).astype(BF16)
    imag = (-np.sin(angles) * scaling).astype(BF16)
    tables = []
    for parity in (0, 1):
        re, im = real[:half, parity::2], imag[:half, parity::2]
        right = np.concatenate(
            [np.concatenate([re, im], 1), np.concatenate([-im, re], 1)], 0
        )
        tables += [right, np.ascontiguousarray(right.T)]
    return jnp.asarray(np.stack(tables))


def dot(a, b):
    return jnp.dot(a, b, preferred_element_type=F32)


def quarters(tl, tr, bl, br):
    return jnp.concatenate(
        [jnp.concatenate([tl, tr], 1), jnp.concatenate([bl, br], 1)], 0
    )


def iota(shape, dim):
    return lax.broadcasted_iota(jnp.int32, shape, dim)


def fetch(pairs, sems):
    copies = [
        pltpu.make_async_copy(source, target, sems.at[i])
        for i, (source, target) in enumerate(pairs)
    ]
    for copy in copies:
        copy.start()
    return copies


def pack_kernel(specimen, centers, cnt, helpers, out, tile_v, cen, hlp, sems):
    copies = fetch(((specimen, tile_v), (centers, cen), (helpers, hlp)), sems)
    for copy in copies:
        copy.wait()
    tile = tile_v.shape[1]
    lanes = tile_v.shape[2]
    rows, cols = iota((INFO, lanes), 0), iota((INFO, lanes), 1)
    info = jnp.where(rows == 0, -1.0, 0.0)
    for j in range(centers.shape[2]):
        helper = jnp.where(j < cnt[0, 0], hlp[0, 0, j], -1)
        for r, value in enumerate((helper, cen[0, 0, j, 0], cen[0, 0, j, 1])):
            info = jnp.where((rows == r) & (cols == j), value.astype(F32), info)
    info = info.astype(BF16)
    for p in range(2):
        out[p * tile : (p + 1) * tile] = tile_v[p].astype(BF16)
    out[2 * tile :] = info


def gather_columns(get, source, col, columns, shape):
    lane = iota(shape, 1)
    beside = own = jnp.zeros(shape, F32)
    for c in range(columns):
        block = get(c)
        near = ((source == c + 1) & (lane >= col)) | ((source == c - 1) & (lane < col))
        beside = jnp.where(near, block, beside)
        own = jnp.where(source == c, block, own)
    return jnp.concatenate([beside, own], 1)


def first_product(probe, patch, tables):
    half = patch[0].shape[1] // 2
    wr = probe[0] * patch[0] - probe[1] * patch[1]
    wi = probe[0] * patch[1] + probe[1] * patch[0]
    out = []
    for sign, table in zip((1, -1), tables):
        folded = jnp.concatenate(
            [wr[:, :half] + sign * wr[:, half:], wi[:, :half] + sign * wi[:, half:]], 1
        )
        out.append(dot(folded.astype(BF16), table))
    return out


def frame_of(band):
    columns, height, lanes = band.shape
    me = lax.axis_index("col").astype(F32)
    code = jnp.zeros((1, lanes), F32)
    for c in range(columns):
        info = band[c, height - INFO :].astype(F32)
        hit = info[0:1] == me
        code += jnp.where(hit, c * 128.0 * 128.0 + info[1:2] * 128.0 + info[2:3], 0.0)
    code = jnp.sum(code).astype(jnp.int32)
    return code // (128 * 128), code // 128 % 128, code % 128


def prepare_kernel(
    band, probe, measured, tables,
    info_out, amplitude, tables_out, probe_out, half_out, raw, raw_tables, raw_probe, groups, sems,
):
    copies = fetch(
        ((measured, raw), (tables, raw_tables), (probe, raw_probe)), sems
    )
    columns = band.shape[0]
    tile = (band.shape[1] - INFO) // 2
    extent = raw.shape[-1]
    half = extent // 2
    modes = raw_probe.shape[0]
    source, row, col = frame_of(band)
    which = iota((INFO, extent), 0)
    info = jnp.where(which == 0, source, jnp.where(which == 1, col, row))
    info_out[...] = info.astype(F32).astype(BF16)

    shape = (extent, extent)

    def original(i):
        return jnp.where(i < half, 2 * i, 2 * (i - half) + 1)

    copies[0].wait()
    sort = (iota(shape, 1) == original(iota(shape, 0))).astype(F32).astype(BF16)
    sort_t = (iota(shape, 0) == original(iota(shape, 1))).astype(F32).astype(BF16)
    value = raw[0, 0, 0]
    coarse = value.astype(BF16)
    fine = (value - coarse.astype(F32)).astype(BF16)
    amplitude[...] = sum(
        dot(dot(sort, part).astype(BF16), sort_t) for part in (coarse, fine)
    )

    def roller(old, new, shift, parity):
        wrapped = new % half < shift
        hit = (old + shift - jnp.where(old % half + shift >= half, half, 0)) == new
        sign = jnp.where(wrapped, -1.0, 1.0) if parity else 1.0
        return jnp.where(hit, sign, 0.0).astype(BF16)

    copies[1].wait()
    i, j = iota(shape, 0), iota(shape, 1)
    for parity in range(2):
        right, left = raw_tables[2 * parity], raw_tables[2 * parity + 1]
        for axis, shift in enumerate((col, row)):
            rolled = dot(left, roller(i, j, shift, parity)).astype(BF16)
            rolled_t = dot(roller(j, i, shift, parity), right).astype(BF16)
            tables_out[4 * axis + parity] = rolled_t if axis == 0 else rolled
            tables_out[4 * axis + 2 + parity] = rolled if axis == 0 else rolled_t

    copies[2].wait()
    count = extent // 8
    base = row // 8
    step = row % 8
    lane = iota((extent, half), 1)
    sub = iota((count, 8, extent), 1)
    for k in range(modes):
        for p in range(2):
            lo = pltpu.roll(raw_probe[k, p, :, :half], col, 1)
            hi = pltpu.roll(raw_probe[k, p, :, half:], col, 1)
            turned = jnp.concatenate(
                [jnp.where(lane < col, hi, lo), jnp.where(lane < col, lo, hi)], 1
            )
            turned = pltpu.roll(turned.reshape(count, 8, extent), step, 1)
            turned = jnp.where(
                sub < step, jnp.concatenate([turned[-1:], turned[:-1]], 0), turned
            )
            groups[:count] = turned
            groups[count:] = turned
            probe_out[k, p] = groups[pl.ds(count - base, count)].reshape(extent, extent)

    patch = [
        gather_columns(
            lambda c: band[c, p * tile : (p + 1) * tile].astype(F32),
            source, col, columns, (tile, tile),
        )
        for p in range(2)
    ]
    for k in range(modes):
        products = first_product(
            [probe_out[k, p, half:] for p in range(2)], patch, (tables_out[0], tables_out[1])
        )
        for parity in range(2):
            half_out[k, parity] = products[parity]


def frame_kernel(
    first, second, info, amplitude, tables, probe, half_own,
    to_rows, mixed_back, patch, folded, mixed, far, corrected, total,
):
    columns = first.shape[0]
    tile = (first.shape[1] - INFO) // 2
    extent = probe.shape[-1]
    half = extent // 2
    modes = probe.shape[0]
    odd = lax.axis_index("row") % 2
    source, col, row = (
        info[r : r + 1, :tile].astype(F32).astype(jnp.int32) for r in range(3)
    )
    strips = [pl.ds(r, STRIP) for r in range(0, half, STRIP)]
    lower = [pl.ds(half + r, STRIP) for r in range(0, half, STRIP)]

    def split(x):
        return x[:, :half], x[:, half:]

    def join(x, y):
        return jnp.concatenate([x, y], 1).astype(BF16)

    def gather(s):
        rows = iota((STRIP, tile), 0) + s.start
        from_first = (rows >= row).astype(jnp.int32) == odd
        for p in range(2):
            part = pl.ds(p * tile + s.start, STRIP)
            patch[p, s] = gather_columns(
                lambda c: jnp.where(
                    from_first, first[c, part].astype(F32), second[c, part].astype(F32)
                ),
                source, col, columns, (STRIP, tile),
            )

    def wave(k):
        for s in strips:
            pr, pi, xr, xi = probe[k, 0, s], probe[k, 1, s], patch[0, s], patch[1, s]
            re = split(pr * xr - pi * xi)
            im = split(pr * xi + pi * xr)
            folded[k, 0, s] = join(re[0] + re[1], im[0] + im[1])
            folded[k, 1, s] = join(re[0] - re[1], im[0] - im[1])

    def mix(k):
        both = [dot(folded[k, q], tables[q]) for q in range(2)]
        for s, t in zip(strips, lower):
            even, odds = (x[s.start : s.start + STRIP] for x in both)
            even_own, odds_own = half_own[k, 0, s], half_own[k, 1, s]
            for q, (e, o) in enumerate(
                ((even + even_own, odds + odds_own), (even - even_own, odds - odds_own))
            ):
                (er, ei), (our, oui) = split(e), split(o)
                mixed[k, q, s] = join(er, our)
                mixed[k, q, t] = join(ei, oui)

    def along_columns(k, q):
        far[k, q] = dot(tables[4 + q], mixed[k, q])

    def correct(q, which):
        for s, t in list(zip(strips, lower))[which]:
            re = [far[k, q, s] for k in range(modes)]
            im = [far[k, q, t] for k in range(modes)]
            intensity = sum(x * x for x in re + im)
            size = amplitude[pl.ds(q * half + s.start, STRIP)]
            factor = 1.0 - size * lax.rsqrt(jnp.maximum(intensity, 0.25))
            out = pl.ds(q * half + s.start, STRIP)
            for k in range(modes):
                (re_even, re_odd), (im_even, im_odd) = split(re[k] * factor), split(im[k] * factor)
                corrected[k, 0, out] = join(re_even, im_even)
                corrected[k, 1, out] = join(re_odd, im_odd)

    def mix_back(k, q):
        part = pl.ds(q * half, half)
        both = [dot(corrected[k, c, part], tables[2 + c]) for c in range(2)]
        for s, t in zip(strips, lower):
            x, y = (z[s.start : s.start + STRIP] for z in both)
            (lr, li), (hr, hi) = split(x + y), split(x - y)
            mixed_back[k, q, s] = join(lr, hr)
            mixed_back[k, q, t] = join(li, hi)

    both_back = jnp.concatenate([tables[6], tables[7]], 1)

    def accumulate(k):
        chi = dot(both_back, mixed_back[k].reshape(2 * extent, extent))
        for s in strips:
            pr, pi = probe[k, 0, s], probe[k, 1, s]
            cr, ci = (chi[r : r + STRIP] for r in (s.start, half + s.start))
            re, im = pr * cr + pi * ci, pr * ci - pi * cr
            if k > 0:
                re, im = re + total[0, s], im + total[1, s]
            if k < modes - 1:
                total[0, s], total[1, s] = re, im
            else:
                to_rows[s] = re.astype(BF16)
                to_rows[pl.ds(tile + s.start, STRIP)] = im.astype(BF16)

    for s in strips:
        gather(s)
    for k in range(modes + 1):
        if k < modes:
            wave(k)
        if k > 0:
            mix(k - 1)
            along_columns(k - 1, 0)
    share = -(-len(strips) // modes)
    for k in range(modes):
        along_columns(k, 1)
        correct(0, slice(k * share, (k + 1) * share))
    for k in range(modes):
        mix_back(k, 0)
        correct(1, slice(k * share, (k + 1) * share))
    for k in range(modes):
        mix_back(k, 1)
        if k > 0:
            accumulate(k - 1)
    accumulate(modes - 1)


def place(block, columns, source, col, taken):
    tile = block.shape[1] // 2
    beside, own = block[:, :tile], block[:, tile:]
    lane = iota(own.shape, 1)
    if taken is not None:
        beside, own = jnp.where(taken, beside, 0.0), jnp.where(taken, own, 0.0)
    out = []
    for c in range(columns):
        near = ((source == c + 1) & (lane >= col)) | ((source == c - 1) & (lane < col))
        out.append(jnp.where(near, beside, 0.0) + jnp.where(source == c, own, 0.0))
    return out


def finish_kernel(
    band, first_band, second_band, mixed_back, tables, probe, first,
    partial, second_info, total, centre,
):
    columns = band.shape[0]
    extent = probe.shape[-1]
    modes = probe.shape[0]
    tile = (band.shape[1] - INFO) // 2
    odd = lax.axis_index("row") % 2
    own_frame, first_frame, second_frame = (
        frame_of(b) for b in (band, first_band, second_band)
    )
    which = iota(second_info.shape, 0)
    second_info[...] = jnp.where(
        which == 0, second_frame[0], jnp.where(which == 1, second_frame[1], second_frame[2])
    )
    both_back = jnp.concatenate([tables[6], -tables[7]], 1)
    for k in range(modes):
        chi = dot(both_back, mixed_back[k].reshape(2 * extent, extent))
        for r in range(0, tile, STRIP):
            s, t = pl.ds(r, STRIP), pl.ds(tile + r, STRIP)
            pr, pi = probe[k, 0, t], probe[k, 1, t]
            cr, ci = (chi[i : i + STRIP] for i in (r, tile + r))
            re, im = pr * cr + pi * ci, pr * ci - pi * cr
            if k > 0:
                re, im = re + total[0, s], im + total[1, s]
            if k < modes - 1:
                total[0, s], total[1, s] = re, im
            else:
                centre[s], centre[t] = re.astype(BF16), im.astype(BF16)
    for r in range(0, tile, STRIP):
        s, t = pl.ds(r, STRIP), pl.ds(tile + r, STRIP)
        before = (iota((STRIP, tile), 0) + r < first_frame[1]).astype(jnp.int32)
        for part in (s, t):
            mine = place(centre[part].astype(F32), columns, own_frame[0], own_frame[2], None)
            other = place(
                first[part].astype(F32), columns, first_frame[0], first_frame[2], before == odd
            )
            for c in range(columns):
                partial[c, part] = mine[c] + other[c]


def fold_kernel(partial, second, second_info, out):
    columns, height, tile = out.shape
    odd = lax.axis_index("row") % 2
    source, row, col = (second_info[r : r + 1] for r in range(3))
    for r in range(0, height, STRIP):
        s = pl.ds(r, STRIP)
        before = (iota((STRIP, tile), 0) + r % tile < row).astype(jnp.int32)
        other = place(second[s].astype(F32), columns, source, col, before == 1 - odd)
        for c in range(columns):
            out[c, s] = (partial[c, s] + other[c]).astype(BF16)


def call(kernel, name, out_shape, in_specs, scratch, flops, moved, *args):
    args = [
        pltpu.with_memory_space_constraint(arg, pltpu.HBM) if spec is HBM else arg
        for arg, spec in zip(args, in_specs)
    ]
    return pl.pallas_call(
        kernel,
        out_shape=out_shape,
        in_specs=in_specs,
        out_specs=jax.tree.map(lambda _: VMEM, out_shape),
        scratch_shapes=scratch,
        compiler_params=pltpu.CompilerParams(vmem_limit_bytes=32 * 2**20),
        cost_estimate=pl.CostEstimate(flops=flops, bytes_accessed=moved, transcendentals=0),
        name=name,
    )(*args)


def per_device(specimen, probe, measured, centers, frame_counts, helper_cols):
    extent = probe.shape[-1]
    half = extent // 2
    tile = specimen.shape[1]
    modes = probe.shape[0]
    columns = lax.axis_size("col")
    height = 2 * tile
    part = jax.ShapeDtypeStruct((height, extent), BF16)
    dma = pltpu.SemaphoreType.DMA

    packed = call(
        pack_kernel, "pack",
        jax.ShapeDtypeStruct((height + INFO, tile), BF16),
        [HBM, HBM, SMEM, HBM],
        [
            pltpu.VMEM(specimen.shape, F32),
            pltpu.SMEM(centers.shape, jnp.int32),
            pltpu.SMEM(helper_cols.shape, jnp.int32),
            dma((3,)),
        ],
        10**5, 2**19,
        specimen, centers, frame_counts, helper_cols,
    )
    band = lax.all_gather(packed, "col")

    rows = lax.axis_size("row")
    swaps = []
    for start in (0, 1):
        pairs = [(i, i + 1) for i in range(start, rows - 1, 2)]
        swaps.append(pairs + [(b, a) for a, b in pairs])
    second = lax.ppermute(band, "row", swaps[1])
    first = lax.ppermute(band, "row", swaps[0])
    tables = dft_tables(extent)
    prepared = call(
        prepare_kernel, "prepare",
        (
            jax.ShapeDtypeStruct((INFO, extent), BF16),
            jax.ShapeDtypeStruct((extent, extent), F32),
            jax.ShapeDtypeStruct((8, extent, extent), BF16),
            jax.ShapeDtypeStruct(probe.shape, F32),
            jax.ShapeDtypeStruct((modes, 2, tile, extent), F32),
        ),
        [VMEM, HBM, HBM, HBM],
        [
            pltpu.VMEM(measured.shape, F32),
            pltpu.VMEM(tables.shape, BF16),
            pltpu.VMEM(probe.shape, F32),
            pltpu.VMEM((extent // 4, 8, extent), F32),
            dma((3,)),
        ],
        10**9, 2**22,
        band, probe, measured, tables,
    )
    full = (modes, 2, extent, extent)
    to_rows, mixed_back = call(
        frame_kernel, "frame",
        (part, jax.ShapeDtypeStruct(full, BF16)),
        [VMEM] * 7,
        [
            pltpu.VMEM((2, tile, extent), F32),
            pltpu.VMEM((modes, 2, half, extent), BF16),
            pltpu.VMEM(full, BF16),
            pltpu.VMEM(full, F32),
            pltpu.VMEM(full, BF16),
            pltpu.VMEM((2, tile, extent), F32),
        ],
        2 * 10**9, 2**22,
        first, second, *prepared,
    )
    from_first = lax.ppermute(to_rows, "row", swaps[0])
    from_second = lax.ppermute(to_rows, "row", swaps[1])
    partial, second_info = call(
        finish_kernel, "finish",
        (
            jax.ShapeDtypeStruct((columns, height, tile), F32),
            jax.ShapeDtypeStruct((8, tile), jnp.int32),
        ),
        [VMEM] * 7,
        [pltpu.VMEM((2, tile, extent), F32), pltpu.VMEM((height, extent), BF16)],
        5 * 10**8, 2**22,
        band, first, second, mixed_back, prepared[2], prepared[3], from_first,
    )
    summed = call(
        fold_kernel, "fold",
        jax.ShapeDtypeStruct((columns, height, tile), BF16),
        [VMEM] * 3,
        [],
        10**7, 2**20,
        partial, from_second, second_info,
    )
    shares = lax.all_to_all(summed, "col", split_axis=0, concat_axis=0, tiled=True)
    return jnp.sum(shares.astype(F32), axis=0).reshape(2, tile, tile)


def solution(mesh):
    return jax.shard_map(
        per_device,
        mesh=mesh,
        in_specs=(
            P(None, "row", "col"),
            P(),
            P("row", "col", None, None, None),
            P("row", "col", None, None),
            P("row", "col"),
            P("row", "col", None),
        ),
        out_specs=P(None, "row", "col"),
        check_vma=False,
    )
```

```python
import functools
import math

import jax
import jax.numpy as jnp
import numpy as np
from jax import lax
from jax.experimental import pallas as pl
from jax.experimental.pallas import tpu as pltpu
from jax.sharding import PartitionSpec as P

F32 = jnp.float32
BF16 = jnp.bfloat16
INFO = 16
STRIP = 16
VMEM = pl.BlockSpec(memory_space=pltpu.VMEM)
SMEM = pl.BlockSpec(memory_space=pltpu.SMEM)
HBM = pl.BlockSpec(memory_space=pltpu.HBM)


def dft_tables(extent):
    half = extent // 2
    steps = np.arange(extent, dtype=np.int32)
    angles = (steps[:, None] * steps[None, :] % extent).astype(np.float32)
    angles = angles * np.float32(2.0 * math.pi / extent)
    scaling = np.float32(1.0 / math.sqrt(extent))
    real = (np.cos(angles) * scaling).astype(BF16)
    imag = (-np.sin(angles) * scaling).astype(BF16)
    tables = []
    for parity in (0, 1):
        re, im = real[:half, parity::2], imag[:half, parity::2]
        right = np.concatenate(
            [np.concatenate([re, im], 1), np.concatenate([-im, re], 1)], 0
        )
        tables += [right, np.ascontiguousarray(right.T)]
    return jnp.asarray(np.stack(tables))


def dot(a, b):
    return jnp.dot(a, b, preferred_element_type=F32)


def quarters(tl, tr, bl, br):
    return jnp.concatenate(
        [jnp.concatenate([tl, tr], 1), jnp.concatenate([bl, br], 1)], 0
    )


def iota(shape, dim):
    return lax.broadcasted_iota(jnp.int32, shape, dim)


def fetch(pairs, sems):
    copies = [
        pltpu.make_async_copy(source, target, sems.at[i])
        for i, (source, target) in enumerate(pairs)
    ]
    for copy in copies:
        copy.start()
    return copies


def pack_kernel(specimen, centers, cnt, helpers, out, tile_v, cen, hlp, sems):
    copies = fetch(((specimen, tile_v), (centers, cen), (helpers, hlp)), sems)
    for copy in copies:
        copy.wait()
    tile = tile_v.shape[1]
    lanes = tile_v.shape[2]
    rows, cols = iota((INFO, lanes), 0), iota((INFO, lanes), 1)
    info = jnp.where(rows == 0, -1.0, 0.0)
    for j in range(centers.shape[2]):
        helper = jnp.where(j < cnt[0, 0], hlp[0, 0, j], -1)
        for r, value in enumerate((helper, cen[0, 0, j, 0], cen[0, 0, j, 1])):
            info = jnp.where((rows == r) & (cols == j), value.astype(F32), info)
    info = info.astype(BF16)
    for p in range(2):
        out[p * tile : (p + 1) * tile] = tile_v[p].astype(BF16)
    out[2 * tile :] = info


def gather_columns(get, source, col, columns, shape):
    lane = iota(shape, 1)
    beside = own = jnp.zeros(shape, F32)
    for c in range(columns):
        block = get(c)
        near = ((source == c + 1) & (lane >= col)) | ((source == c - 1) & (lane < col))
        beside = jnp.where(near, block, beside)
        own = jnp.where(source == c, block, own)
    return jnp.concatenate([beside, own], 1)


def first_product(probe, patch, tables):
    half = patch[0].shape[1] // 2
    wr = probe[0] * patch[0] - probe[1] * patch[1]
    wi = probe[0] * patch[1] + probe[1] * patch[0]
    out = []
    for sign, table in zip((1, -1), tables):
        folded = jnp.concatenate(
            [wr[:, :half] + sign * wr[:, half:], wi[:, :half] + sign * wi[:, half:]], 1
        )
        out.append(dot(folded.astype(BF16), table))
    return out


def frame_of(band):
    columns, height, lanes = band.shape
    me = lax.axis_index("col").astype(F32)
    code = jnp.zeros((1, lanes), F32)
    for c in range(columns):
        info = band[c, height - INFO :].astype(F32)
        hit = info[0:1] == me
        code += jnp.where(hit, c * 128.0 * 128.0 + info[1:2] * 128.0 + info[2:3], 0.0)
    code = jnp.sum(code).astype(jnp.int32)
    return code // (128 * 128), code // 128 % 128, code % 128


def prepare_kernel(
    band, probe, measured, tables,
    info_out, amplitude, tables_out, probe_out, half_out, raw, raw_tables, raw_probe, groups, sems,
):
    copies = fetch(
        ((measured, raw), (tables, raw_tables), (probe, raw_probe)), sems
    )
    columns = band.shape[0]
    tile = (band.shape[1] - INFO) // 2
    extent = raw.shape[-1]
    half = extent // 2
    modes = raw_probe.shape[0]
    source, row, col = frame_of(band)
    which = iota((INFO, extent), 0)
    info = jnp.where(which == 0, source, jnp.where(which == 1, col, row))
    info_out[...] = info.astype(F32).astype(BF16)

    shape = (extent, extent)

    def original(i):
        return jnp.where(i < half, 2 * i, 2 * (i - half) + 1)

    copies[0].wait()
    sort = (iota(shape, 1) == original(iota(shape, 0))).astype(F32).astype(BF16)
    sort_t = (iota(shape, 0) == original(iota(shape, 1))).astype(F32).astype(BF16)
    value = raw[0, 0, 0]
    coarse = value.astype(BF16)
    fine = (value - coarse.astype(F32)).astype(BF16)
    amplitude[...] = sum(
        dot(dot(sort, part).astype(BF16), sort_t) for part in (coarse, fine)
    )

    def roller(old, new, shift, parity):
        wrapped = new % half < shift
        hit = (old + shift - jnp.where(old % half + shift >= half, half, 0)) == new
        sign = jnp.where(wrapped, -1.0, 1.0) if parity else 1.0
        return jnp.where(hit, sign, 0.0).astype(BF16)

    copies[1].wait()
    i, j = iota(shape, 0), iota(shape, 1)
    for parity in range(2):
        right, left = raw_tables[2 * parity], raw_tables[2 * parity + 1]
        for axis, shift in enumerate((col, row)):
            rolled = dot(left, roller(i, j, shift, parity)).astype(BF16)
            rolled_t = dot(roller(j, i, shift, parity), right).astype(BF16)
            tables_out[4 * axis + parity] = rolled_t if axis == 0 else rolled
            tables_out[4 * axis + 2 + parity] = rolled if axis == 0 else rolled_t

    copies[2].wait()
    count = extent // 8
    base = row // 8
    step = row % 8
    lane = iota((extent, half), 1)
    sub = iota((count, 8, extent), 1)
    for k in range(modes):
        for p in range(2):
            lo = pltpu.roll(raw_probe[k, p, :, :half], col, 1)
            hi = pltpu.roll(raw_probe[k, p, :, half:], col, 1)
            turned = jnp.concatenate(
                [jnp.where(lane < col, hi, lo), jnp.where(lane < col, lo, hi)], 1
            )
            turned = pltpu.roll(turned.reshape(count, 8, extent), step, 1)
            turned = jnp.where(
                sub < step, jnp.concatenate([turned[-1:], turned[:-1]], 0), turned
            )
            groups[:count] = turned
            groups[count:] = turned
            probe_out[k, p] = groups[pl.ds(count - base, count)].reshape(extent, extent)

    patch = [
        gather_columns(
            lambda c: band[c, p * tile : (p + 1) * tile].astype(F32),
            source, col, columns, (tile, tile),
        )
        for p in range(2)
    ]
    for k in range(modes):
        products = first_product(
            [probe_out[k, p, half:] for p in range(2)], patch, (tables_out[0], tables_out[1])
        )
        for parity in range(2):
            half_out[k, parity] = products[parity]


def frame_kernel(
    first, second, info, amplitude, tables, probe, half_own,
    to_rows, turned, patch, folded, half_far, mixed, far, corrected, product, mixed_back,
):
    columns = first.shape[0]
    tile = (first.shape[1] - INFO) // 2
    extent = probe.shape[-1]
    half = extent // 2
    modes = probe.shape[0]
    odd = lax.axis_index("row") % 2
    source, col, row = (
        info[r : r + 1, :tile].astype(F32).astype(jnp.int32) for r in range(3)
    )
    strips = [pl.ds(r, STRIP) for r in range(0, half, STRIP)]
    lower = [pl.ds(half + r, STRIP) for r in range(0, half, STRIP)]

    def split(x):
        return x[:, :half], x[:, half:]

    def join(x, y):
        return jnp.concatenate([x, y], 1).astype(BF16)

    def gather(s):
        rows = iota((STRIP, tile), 0) + s.start
        from_first = (rows >= row).astype(jnp.int32) == odd
        for p in range(2):
            part = pl.ds(p * tile + s.start, STRIP)
            patch[p, s] = gather_columns(
                lambda c: jnp.where(
                    from_first, first[c, part].astype(F32), second[c, part].astype(F32)
                ),
                source, col, columns, (STRIP, tile),
            )

    def wave(k):
        for s in strips:
            pr, pi, xr, xi = probe[k, 0, s], probe[k, 1, s], patch[0, s], patch[1, s]
            re = split(pr * xr - pi * xi)
            im = split(pr * xi + pi * xr)
            folded[k, 0, s] = join(re[0] + re[1], im[0] + im[1])
            folded[k, 1, s] = join(re[0] - re[1], im[0] - im[1])

    def along_rows(k):
        for q in range(2):
            half_far[k, q] = dot(folded[k, q], tables[q])

    def mix(k):
        for s, t in zip(strips, lower):
            even, odds = half_far[k, 0, s], half_far[k, 1, s]
            even_own, odds_own = half_own[k, 0, s], half_own[k, 1, s]
            for q, (e, o) in enumerate(
                ((even + even_own, odds + odds_own), (even - even_own, odds - odds_own))
            ):
                (er, ei), (our, oui) = split(e), split(o)
                mixed[k, q, s] = join(er, our)
                mixed[k, q, t] = join(ei, oui)

    def along_columns(k, q):
        far[k, q] = dot(tables[4 + q], mixed[k, q])

    def correct(q, which):
        for s, t in list(zip(strips, lower))[which]:
            re = [far[k, q, s] for k in range(modes)]
            im = [far[k, q, t] for k in range(modes)]
            intensity = sum(x * x for x in re + im)
            size = amplitude[pl.ds(q * half + s.start, STRIP)]
            factor = 1.0 - size * lax.rsqrt(jnp.maximum(intensity, 0.25))
            out = pl.ds(q * half + s.start, STRIP)
            for k in range(modes):
                (re_even, re_odd), (im_even, im_odd) = split(re[k] * factor), split(im[k] * factor)
                corrected[k, 0, out] = join(re_even, im_even)
                corrected[k, 1, out] = join(re_odd, im_odd)

    def back_along_rows(k, q):
        part = pl.ds(q * half, half)
        for c in range(2):
            product[k, c, part] = dot(corrected[k, c, part], tables[2 + c])

    def mix_back(k, q):
        for s, t in zip(strips, lower):
            part = pl.ds(q * half + s.start, STRIP)
            x, y = product[k, 0, part], product[k, 1, part]
            (lr, li), (hr, hi) = split(x + y), split(x - y)
            mixed_back[k, q, s] = join(lr, hr)
            mixed_back[k, q, t] = join(li, hi)

    def back_along_columns(k, q):
        turned[k, q] = dot(tables[6 + q], mixed_back[k, q])

    for s in strips:
        gather(s)
    for k in range(modes + 1):
        if k < modes:
            wave(k)
            along_rows(k)
        if k > 0:
            mix(k - 1)
            along_columns(k - 1, 0)
    share = -(-len(strips) // modes)
    for k in range(modes):
        along_columns(k, 1)
        correct(0, slice(k * share, (k + 1) * share))
    for k in range(modes):
        back_along_rows(k, 0)
        correct(1, slice(k * share, (k + 1) * share))
    for k in range(modes):
        mix_back(k, 0)
        back_along_columns(k, 0)
        back_along_rows(k, 1)
    for k in range(modes):
        mix_back(k, 1)
        back_along_columns(k, 1)
    for s, t in zip(strips, lower):
        accumulate(to_rows, turned, probe, s, t, s, 1)


def accumulate(out, turned, probe, s, t, rows, sign):
    tile = out.shape[0] // 2
    re = im = 0.0
    for k in range(probe.shape[0]):
        pr, pi = probe[k, 0, rows], probe[k, 1, rows]
        cr = turned[k, 0, s] + sign * turned[k, 1, s]
        ci = turned[k, 0, t] + sign * turned[k, 1, t]
        re += pr * cr + pi * ci
        im += pr * ci - pi * cr
    out[s] = re.astype(BF16)
    out[pl.ds(tile + s.start, STRIP)] = im.astype(BF16)


def place(block, columns, source, col, taken):
    tile = block.shape[1] // 2
    beside, own = block[:, :tile], block[:, tile:]
    lane = iota(own.shape, 1)
    if taken is not None:
        beside, own = jnp.where(taken, beside, 0.0), jnp.where(taken, own, 0.0)
    out = []
    for c in range(columns):
        near = ((source == c + 1) & (lane >= col)) | ((source == c - 1) & (lane < col))
        out.append(jnp.where(near, beside, 0.0) + jnp.where(source == c, own, 0.0))
    return out


def finish_kernel(
    band, first_band, second_band, turned, probe, first, partial, second_info, centre,
):
    columns = band.shape[0]
    tile = (band.shape[1] - INFO) // 2
    odd = lax.axis_index("row") % 2
    own_frame, first_frame, second_frame = (
        frame_of(b) for b in (band, first_band, second_band)
    )
    which = iota(second_info.shape, 0)
    second_info[...] = jnp.where(
        which == 0, second_frame[0], jnp.where(which == 1, second_frame[1], second_frame[2])
    )
    for r in range(0, tile, STRIP):
        s, t = pl.ds(r, STRIP), pl.ds(tile + r, STRIP)
        accumulate(centre, turned, probe, s, t, t, -1)
        before = (iota((STRIP, tile), 0) + r < first_frame[1]).astype(jnp.int32)
        for part in (s, t):
            mine = place(centre[part].astype(F32), columns, own_frame[0], own_frame[2], None)
            other = place(
                first[part].astype(F32), columns, first_frame[0], first_frame[2], before == odd
            )
            for c in range(columns):
                partial[c, part] = mine[c] + other[c]


def fold_kernel(partial, second, second_info, out):
    columns, height, tile = out.shape
    odd = lax.axis_index("row") % 2
    source, row, col = (second_info[r : r + 1] for r in range(3))
    for r in range(0, height, STRIP):
        s = pl.ds(r, STRIP)
        before = (iota((STRIP, tile), 0) + r % tile < row).astype(jnp.int32)
        other = place(second[s].astype(F32), columns, source, col, before == 1 - odd)
        for c in range(columns):
            out[c, s] = (partial[c, s] + other[c]).astype(BF16)


def call(kernel, name, out_shape, in_specs, scratch, flops, moved, *args):
    args = [
        pltpu.with_memory_space_constraint(arg, pltpu.HBM) if spec is HBM else arg
        for arg, spec in zip(args, in_specs)
    ]
    return pl.pallas_call(
        kernel,
        out_shape=out_shape,
        in_specs=in_specs,
        out_specs=jax.tree.map(lambda _: VMEM, out_shape),
        scratch_shapes=scratch,
        compiler_params=pltpu.CompilerParams(vmem_limit_bytes=32 * 2**20),
        cost_estimate=pl.CostEstimate(flops=flops, bytes_accessed=moved, transcendentals=0),
        name=name,
    )(*args)


def per_device(specimen, probe, measured, centers, frame_counts, helper_cols):
    extent = probe.shape[-1]
    half = extent // 2
    tile = specimen.shape[1]
    modes = probe.shape[0]
    columns = lax.axis_size("col")
    height = 2 * tile
    part = jax.ShapeDtypeStruct((height, extent), BF16)
    dma = pltpu.SemaphoreType.DMA

    packed = call(
        pack_kernel, "pack",
        jax.ShapeDtypeStruct((height + INFO, tile), BF16),
        [HBM, HBM, SMEM, HBM],
        [
            pltpu.VMEM(specimen.shape, F32),
            pltpu.SMEM(centers.shape, jnp.int32),
            pltpu.SMEM(helper_cols.shape, jnp.int32),
            dma((3,)),
        ],
        10**5, 2**19,
        specimen, centers, frame_counts, helper_cols,
    )
    near = [[c, c + 1] for c in range(0, columns, 2)]
    far = [list(range(c, columns, 2)) for c in range(2)]
    band = lax.all_gather(packed, "col", axis_index_groups=near)
    band = lax.all_gather(band, "col", axis_index_groups=far, tiled=True)

    rows = lax.axis_size("row")
    swaps = []
    for start in (0, 1):
        pairs = [(i, i + 1) for i in range(start, rows - 1, 2)]
        swaps.append(pairs + [(b, a) for a, b in pairs])
    second = lax.ppermute(band, "row", swaps[1])
    first = lax.ppermute(band, "row", swaps[0])
    tables = dft_tables(extent)
    prepared = call(
        prepare_kernel, "prepare",
        (
            jax.ShapeDtypeStruct((INFO, extent), BF16),
            jax.ShapeDtypeStruct((extent, extent), F32),
            jax.ShapeDtypeStruct((8, extent, extent), BF16),
            jax.ShapeDtypeStruct(probe.shape, F32),
            jax.ShapeDtypeStruct((modes, 2, tile, extent), F32),
        ),
        [VMEM, HBM, HBM, HBM],
        [
            pltpu.VMEM(measured.shape, F32),
            pltpu.VMEM(tables.shape, BF16),
            pltpu.VMEM(probe.shape, F32),
            pltpu.VMEM((extent // 4, 8, extent), F32),
            dma((3,)),
        ],
        10**9, 2**22,
        band, probe, measured, tables,
    )
    full = (modes, 2, extent, extent)
    to_rows, turned = call(
        frame_kernel, "frame",
        (part, jax.ShapeDtypeStruct(full, F32)),
        [VMEM] * 7,
        [
            pltpu.VMEM((2, tile, extent), F32),
            pltpu.VMEM((modes, 2, half, extent), BF16),
            pltpu.VMEM((modes, 2, half, extent), F32),
            pltpu.VMEM(full, BF16),
            pltpu.VMEM(full, F32),
            pltpu.VMEM(full, BF16),
            pltpu.VMEM(full, F32),
            pltpu.VMEM(full, BF16),
        ],
        2 * 10**9, 2**22,
        first, second, *prepared,
    )
    from_first = lax.ppermute(to_rows, "row", swaps[0])
    from_second = lax.ppermute(to_rows, "row", swaps[1])
    partial, second_info = call(
        finish_kernel, "finish",
        (
            jax.ShapeDtypeStruct((columns, height, tile), F32),
            jax.ShapeDtypeStruct((8, tile), jnp.int32),
        ),
        [VMEM] * 6,
        [pltpu.VMEM((height, extent), BF16)],
        10**7, 2**22,
        band, first, second, turned, prepared[3], from_first,
    )
    summed = call(
        fold_kernel, "fold",
        jax.ShapeDtypeStruct((columns, height, tile), BF16),
        [VMEM] * 3,
        [],
        10**7, 2**20,
        partial, from_second, second_info,
    )
    shares = lax.all_to_all(summed, "col", split_axis=0, concat_axis=0, tiled=True)
    return jnp.sum(shares.astype(F32), axis=0).reshape(2, tile, tile)


def solution(mesh):
    return jax.shard_map(
        per_device,
        mesh=mesh,
        in_specs=(
            P(None, "row", "col"),
            P(),
            P("row", "col", None, None, None),
            P("row", "col", None, None),
            P("row", "col"),
            P("row", "col", None),
        ),
        out_specs=P(None, "row", "col"),
        check_vma=False,
    )
```

```python
import functools
import math

import jax
import jax.numpy as jnp
import numpy as np
from jax import lax
from jax.experimental import pallas as pl
from jax.experimental.pallas import tpu as pltpu
from jax.sharding import PartitionSpec as P

F32 = jnp.float32
BF16 = jnp.bfloat16
INFO = 16
STRIP = 16
VMEM = pl.BlockSpec(memory_space=pltpu.VMEM)
SMEM = pl.BlockSpec(memory_space=pltpu.SMEM)
HBM = pl.BlockSpec(memory_space=pltpu.HBM)


def dft_tables(extent):
    half = extent // 2
    steps = np.arange(extent, dtype=np.int32)
    angles = (steps[:, None] * steps[None, :] % extent).astype(np.float32)
    angles = angles * np.float32(2.0 * math.pi / extent)
    scaling = np.float32(1.0 / math.sqrt(extent))
    real = (np.cos(angles) * scaling).astype(BF16)
    imag = (-np.sin(angles) * scaling).astype(BF16)
    tables = []
    for parity in (0, 1):
        re, im = real[:half, parity::2], imag[:half, parity::2]
        right = np.concatenate(
            [np.concatenate([re, im], 1), np.concatenate([-im, re], 1)], 0
        )
        tables += [right, np.ascontiguousarray(right.T)]
    return jnp.asarray(np.stack(tables))


def dot(a, b):
    return jnp.dot(a, b, preferred_element_type=F32)


def quarters(tl, tr, bl, br):
    return jnp.concatenate(
        [jnp.concatenate([tl, tr], 1), jnp.concatenate([bl, br], 1)], 0
    )


def iota(shape, dim):
    return lax.broadcasted_iota(jnp.int32, shape, dim)


def fetch(pairs, sems):
    copies = [
        pltpu.make_async_copy(source, target, sems.at[i])
        for i, (source, target) in enumerate(pairs)
    ]
    for copy in copies:
        copy.start()
    return copies


def pack_kernel(specimen, centers, cnt, helpers, out, tile_v, cen, hlp, sems):
    copies = fetch(((specimen, tile_v), (centers, cen), (helpers, hlp)), sems)
    for copy in copies:
        copy.wait()
    tile = tile_v.shape[1]
    lanes = tile_v.shape[2]
    rows, cols = iota((INFO, lanes), 0), iota((INFO, lanes), 1)
    info = jnp.where(rows == 0, -1.0, 0.0)
    for j in range(centers.shape[2]):
        helper = jnp.where(j < cnt[0, 0], hlp[0, 0, j], -1)
        for r, value in enumerate((helper, cen[0, 0, j, 0], cen[0, 0, j, 1])):
            info = jnp.where((rows == r) & (cols == j), value.astype(F32), info)
    info = info.astype(BF16)
    for p in range(2):
        out[p * tile : (p + 1) * tile] = tile_v[p].astype(BF16)
    out[2 * tile :] = info


def gather_columns(get, source, col, columns, shape):
    lane = iota(shape, 1)
    beside = own = jnp.zeros(shape, F32)
    for c in range(columns):
        block = get(c)
        near = ((source == c + 1) & (lane >= col)) | ((source == c - 1) & (lane < col))
        beside = jnp.where(near, block, beside)
        own = jnp.where(source == c, block, own)
    return jnp.concatenate([beside, own], 1)


def first_product(probe, patch, tables):
    half = patch[0].shape[1] // 2
    wr = probe[0] * patch[0] - probe[1] * patch[1]
    wi = probe[0] * patch[1] + probe[1] * patch[0]
    out = []
    for sign, table in zip((1, -1), tables):
        folded = jnp.concatenate(
            [wr[:, :half] + sign * wr[:, half:], wi[:, :half] + sign * wi[:, half:]], 1
        )
        out.append(dot(folded.astype(BF16), table))
    return out


def frame_of(band):
    columns, height, lanes = band.shape
    me = lax.axis_index("col").astype(F32)
    code = jnp.zeros((1, lanes), F32)
    for c in range(columns):
        info = band[c, height - INFO :].astype(F32)
        hit = info[0:1] == me
        code += jnp.where(hit, c * 128.0 * 128.0 + info[1:2] * 128.0 + info[2:3], 0.0)
    code = jnp.sum(code).astype(jnp.int32)
    return code // (128 * 128), code // 128 % 128, code % 128


def prepare_kernel(
    band, probe, measured, tables,
    info_out, amplitude, tables_out, probe_out, half_out, raw, raw_tables, raw_probe, groups, sems,
):
    copies = fetch(
        ((measured, raw), (tables, raw_tables), (probe, raw_probe)), sems
    )
    columns = band.shape[0]
    tile = (band.shape[1] - INFO) // 2
    extent = raw.shape[-1]
    half = extent // 2
    modes = raw_probe.shape[0]
    source, row, col = frame_of(band)
    which = iota((INFO, extent), 0)
    info = jnp.where(which == 0, source, jnp.where(which == 1, col, row))
    info_out[...] = info.astype(F32).astype(BF16)

    shape = (extent, extent)

    def original(i):
        return jnp.where(i < half, 2 * i, 2 * (i - half) + 1)

    copies[0].wait()
    sort = (iota(shape, 1) == original(iota(shape, 0))).astype(F32).astype(BF16)
    sort_t = (iota(shape, 0) == original(iota(shape, 1))).astype(F32).astype(BF16)
    value = raw[0, 0, 0]
    coarse = value.astype(BF16)
    fine = (value - coarse.astype(F32)).astype(BF16)
    amplitude[...] = sum(
        dot(dot(sort, part).astype(BF16), sort_t) for part in (coarse, fine)
    )

    def roller(old, new, shift, parity):
        wrapped = new % half < shift
        hit = (old + shift - jnp.where(old % half + shift >= half, half, 0)) == new
        sign = jnp.where(wrapped, -1.0, 1.0) if parity else 1.0
        return jnp.where(hit, sign, 0.0).astype(BF16)

    copies[1].wait()
    i, j = iota(shape, 0), iota(shape, 1)
    for parity in range(2):
        right, left = raw_tables[2 * parity], raw_tables[2 * parity + 1]
        for axis, shift in enumerate((col, row)):
            rolled = dot(left, roller(i, j, shift, parity)).astype(BF16)
            rolled_t = dot(roller(j, i, shift, parity), right).astype(BF16)
            tables_out[4 * axis + parity] = rolled_t if axis == 0 else rolled
            tables_out[4 * axis + 2 + parity] = rolled if axis == 0 else rolled_t

    copies[2].wait()
    count = extent // 8
    base = row // 8
    step = row % 8
    lane = iota((extent, half), 1)
    sub = iota((count, 8, extent), 1)
    for k in range(modes):
        for p in range(2):
            lo = pltpu.roll(raw_probe[k, p, :, :half], col, 1)
            hi = pltpu.roll(raw_probe[k, p, :, half:], col, 1)
            turned = jnp.concatenate(
                [jnp.where(lane < col, hi, lo), jnp.where(lane < col, lo, hi)], 1
            )
            turned = pltpu.roll(turned.reshape(count, 8, extent), step, 1)
            turned = jnp.where(
                sub < step, jnp.concatenate([turned[-1:], turned[:-1]], 0), turned
            )
            groups[:count] = turned
            groups[count:] = turned
            probe_out[k, p] = groups[pl.ds(count - base, count)].reshape(extent, extent)

    patch = [
        gather_columns(
            lambda c: band[c, p * tile : (p + 1) * tile].astype(F32),
            source, col, columns, (tile, tile),
        )
        for p in range(2)
    ]
    for k in range(modes):
        products = first_product(
            [probe_out[k, p, half:] for p in range(2)], patch, (tables_out[0], tables_out[1])
        )
        for parity in range(2):
            half_out[k, parity] = products[parity]


def frame_kernel(
    first, second, info, amplitude, tables, probe, half_own,
    to_rows, turned, patch, folded, half_far, mixed, far, corrected, product, mixed_back,
):
    columns = first.shape[0]
    tile = (first.shape[1] - INFO) // 2
    extent = probe.shape[-1]
    half = extent // 2
    modes = probe.shape[0]
    odd = lax.axis_index("row") % 2
    source, col, row = (
        info[r : r + 1, :tile].astype(F32).astype(jnp.int32) for r in range(3)
    )
    strips = [pl.ds(r, STRIP) for r in range(0, half, STRIP)]
    lower = [pl.ds(half + r, STRIP) for r in range(0, half, STRIP)]

    def split(x):
        return x[:, :half], x[:, half:]

    def join(x, y):
        return jnp.concatenate([x, y], 1).astype(BF16)

    def gather(s):
        rows = iota((STRIP, tile), 0) + s.start
        from_first = (rows >= row).astype(jnp.int32) == odd
        for p in range(2):
            part = pl.ds(p * tile + s.start, STRIP)
            patch[p, s] = gather_columns(
                lambda c: jnp.where(
                    from_first, first[c, part].astype(F32), second[c, part].astype(F32)
                ),
                source, col, columns, (STRIP, tile),
            )

    def wave(k):
        for s in strips:
            pr, pi, xr, xi = probe[k, 0, s], probe[k, 1, s], patch[0, s], patch[1, s]
            re = split(pr * xr - pi * xi)
            im = split(pr * xi + pi * xr)
            folded[k, 0, s] = join(re[0] + re[1], im[0] + im[1])
            folded[k, 1, s] = join(re[0] - re[1], im[0] - im[1])

    def along_rows(k):
        for q in range(2):
            half_far[k, q] = dot(folded[k, q], tables[q])

    def mix(k):
        for s, t in zip(strips, lower):
            even, odds = half_far[k, 0, s], half_far[k, 1, s]
            even_own, odds_own = half_own[k, 0, s], half_own[k, 1, s]
            for q, (e, o) in enumerate(
                ((even + even_own, odds + odds_own), (even - even_own, odds - odds_own))
            ):
                (er, ei), (our, oui) = split(e), split(o)
                mixed[k, q, s] = join(er, our)
                mixed[k, q, t] = join(ei, oui)

    def along_columns(k, q):
        far[k, q] = dot(tables[4 + q], mixed[k, q])

    def correct(q, which):
        for s, t in list(zip(strips, lower))[which]:
            re = [far[k, q, s] for k in range(modes)]
            im = [far[k, q, t] for k in range(modes)]
            intensity = sum(x * x for x in re + im)
            size = amplitude[pl.ds(q * half + s.start, STRIP)]
            factor = 1.0 - size * lax.rsqrt(jnp.maximum(intensity, 0.25))
            out = pl.ds(q * half + s.start, STRIP)
            for k in range(modes):
                (re_even, re_odd), (im_even, im_odd) = split(re[k] * factor), split(im[k] * factor)
                corrected[k, 0, out] = join(re_even, im_even)
                corrected[k, 1, out] = join(re_odd, im_odd)

    def back_along_rows(k, q):
        part = pl.ds(q * half, half)
        for c in range(2):
            product[k, c, part] = dot(corrected[k, c, part], tables[2 + c])

    def mix_back(k, q):
        for s, t in zip(strips, lower):
            part = pl.ds(q * half + s.start, STRIP)
            x, y = product[k, 0, part], product[k, 1, part]
            (lr, li), (hr, hi) = split(x + y), split(x - y)
            mixed_back[k, q, s] = join(lr, hr)
            mixed_back[k, q, t] = join(li, hi)

    def back_along_columns(k, q):
        turned[k, q] = dot(tables[6 + q], mixed_back[k, q])

    for s in strips:
        gather(s)
    for k in range(modes + 1):
        if k < modes:
            wave(k)
            along_rows(k)
        if k > 0:
            mix(k - 1)
            along_columns(k - 1, 0)
    share = -(-len(strips) // modes)
    for k in range(modes):
        along_columns(k, 1)
        correct(0, slice(k * share, (k + 1) * share))
    for k in range(modes):
        back_along_rows(k, 0)
        correct(1, slice(k * share, (k + 1) * share))
    for k in range(modes):
        mix_back(k, 0)
        back_along_columns(k, 0)
        back_along_rows(k, 1)
    for k in range(modes):
        mix_back(k, 1)
        back_along_columns(k, 1)
    for s, t in zip(strips, lower):
        accumulate(to_rows, turned, probe, s, t, s, 1)


def accumulate(out, turned, probe, s, t, rows, sign):
    tile = out.shape[0] // 2
    re = im = 0.0
    for k in range(probe.shape[0]):
        pr, pi = probe[k, 0, rows], probe[k, 1, rows]
        cr = turned[k, 0, s] + sign * turned[k, 1, s]
        ci = turned[k, 0, t] + sign * turned[k, 1, t]
        re += pr * cr + pi * ci
        im += pr * ci - pi * cr
    out[s] = re.astype(BF16)
    out[pl.ds(tile + s.start, STRIP)] = im.astype(BF16)


def place(block, columns, source, col, taken):
    tile = block.shape[1] // 2
    beside, own = block[:, :tile], block[:, tile:]
    lane = iota(own.shape, 1)
    if taken is not None:
        beside, own = jnp.where(taken, beside, 0.0), jnp.where(taken, own, 0.0)
    out = []
    for c in range(columns):
        near = ((source == c + 1) & (lane >= col)) | ((source == c - 1) & (lane < col))
        out.append(jnp.where(near, beside, 0.0) + jnp.where(source == c, own, 0.0))
    return out


def finish_kernel(
    band, first_band, second_band, turned, probe, first, pair, out, centre,
):
    columns = band.shape[0]
    tile = (band.shape[1] - INFO) // 2
    me = lax.axis_index("row")
    odd = me % 2
    own_frame, first_frame, second_frame = (
        frame_of(b) for b in (band, first_band, second_band)
    )
    outer = ((me > 0) & (me < lax.axis_size("row") - 1)).astype(jnp.int32)
    for r in range(0, tile, STRIP):
        s, t = pl.ds(r, STRIP), pl.ds(tile + r, STRIP)
        accumulate(centre, turned, probe, s, t, t, -1)
        rows = iota((STRIP, tile), 0) + r
        from_first = (rows < first_frame[1]).astype(jnp.int32) == odd
        from_second = (rows < second_frame[1]).astype(jnp.int32) + 2 * (1 - outer) == 1 - odd
        for part in (s, t):
            own = place(centre[part].astype(F32), columns, own_frame[0], own_frame[2], None)
            near = place(
                first[part].astype(F32), columns, first_frame[0], first_frame[2], from_first
            )
            far = place(
                pair[odd, part].astype(F32), columns, second_frame[0], second_frame[2], from_second
            )
            for c in range(columns):
                out[c, part] = (own[c] + near[c] + far[c]).astype(BF16)


def call(kernel, name, out_shape, in_specs, scratch, flops, moved, *args):
    args = [
        pltpu.with_memory_space_constraint(arg, pltpu.HBM) if spec is HBM else arg
        for arg, spec in zip(args, in_specs)
    ]
    return pl.pallas_call(
        kernel,
        out_shape=out_shape,
        in_specs=in_specs,
        out_specs=jax.tree.map(lambda _: VMEM, out_shape),
        scratch_shapes=scratch,
        compiler_params=pltpu.CompilerParams(vmem_limit_bytes=32 * 2**20),
        cost_estimate=pl.CostEstimate(flops=flops, bytes_accessed=moved, transcendentals=0),
        name=name,
    )(*args)


def per_device(specimen, probe, measured, centers, frame_counts, helper_cols):
    extent = probe.shape[-1]
    half = extent // 2
    tile = specimen.shape[1]
    modes = probe.shape[0]
    columns = lax.axis_size("col")
    height = 2 * tile
    part = jax.ShapeDtypeStruct((height, extent), BF16)
    dma = pltpu.SemaphoreType.DMA

    packed = call(
        pack_kernel, "pack",
        jax.ShapeDtypeStruct((height + INFO, tile), BF16),
        [HBM, HBM, SMEM, HBM],
        [
            pltpu.VMEM(specimen.shape, F32),
            pltpu.SMEM(centers.shape, jnp.int32),
            pltpu.SMEM(helper_cols.shape, jnp.int32),
            dma((3,)),
        ],
        10**5, 2**19,
        specimen, centers, frame_counts, helper_cols,
    )
    band = lax.all_gather(packed, "col")

    rows = lax.axis_size("row")
    swaps = []
    for start in (0, 1):
        pairs = [(i, i + 1) for i in range(start, rows - 1, 2)]
        swaps.append(pairs + [(b, a) for a, b in pairs])
    second = lax.ppermute(band, "row", swaps[1])
    first = lax.ppermute(band, "row", swaps[0])
    tables = dft_tables(extent)
    prepared = call(
        prepare_kernel, "prepare",
        (
            jax.ShapeDtypeStruct((INFO, extent), BF16),
            jax.ShapeDtypeStruct((extent, extent), F32),
            jax.ShapeDtypeStruct((8, extent, extent), BF16),
            jax.ShapeDtypeStruct(probe.shape, F32),
            jax.ShapeDtypeStruct((modes, 2, tile, extent), F32),
        ),
        [VMEM, HBM, HBM, HBM],
        [
            pltpu.VMEM(measured.shape, F32),
            pltpu.VMEM(tables.shape, BF16),
            pltpu.VMEM(probe.shape, F32),
            pltpu.VMEM((extent // 4, 8, extent), F32),
            dma((3,)),
        ],
        10**9, 2**22,
        band, probe, measured, tables,
    )
    full = (modes, 2, extent, extent)
    to_rows, turned = call(
        frame_kernel, "frame",
        (part, jax.ShapeDtypeStruct(full, F32)),
        [VMEM] * 7,
        [
            pltpu.VMEM((2, tile, extent), F32),
            pltpu.VMEM((modes, 2, half, extent), BF16),
            pltpu.VMEM((modes, 2, half, extent), F32),
            pltpu.VMEM(full, BF16),
            pltpu.VMEM(full, F32),
            pltpu.VMEM(full, BF16),
            pltpu.VMEM(full, F32),
            pltpu.VMEM(full, BF16),
        ],
        2 * 10**9, 2**22,
        first, second, *prepared,
    )
    from_first = lax.ppermute(to_rows, "row", swaps[0])
    ends = [r * columns + c for r in (0, rows - 1) for c in range(columns)]
    pairs = [ends[i : i + 2] for i in range(0, 2 * columns, 2)]
    pairs += [
        [r * columns + c, (r + 1) * columns + c]
        for r in range(1, rows - 1, 2) for c in range(columns)
    ]
    pair = lax.all_gather(to_rows, ("row", "col"), axis_index_groups=pairs)
    summed = call(
        finish_kernel, "finish",
        jax.ShapeDtypeStruct((columns, height, tile), BF16),
        [VMEM] * 7,
        [pltpu.VMEM((height, extent), BF16)],
        10**7, 2**22,
        band, first, second, turned, prepared[3], from_first, pair,
    )
    shares = lax.all_to_all(summed, "col", split_axis=0, concat_axis=0, tiled=True)
    return jnp.sum(shares.astype(F32), axis=0).reshape(2, tile, tile)


def solution(mesh):
    return jax.shard_map(
        per_device,
        mesh=mesh,
        in_specs=(
            P(None, "row", "col"),
            P(),
            P("row", "col", None, None, None),
            P("row", "col", None, None),
            P("row", "col"),
            P("row", "col", None),
        ),
        out_specs=P(None, "row", "col"),
        check_vma=False,
    )
```

```python
import functools
import math

import jax
import jax.numpy as jnp
import numpy as np
from jax import lax
from jax.experimental import pallas as pl
from jax.experimental.pallas import tpu as pltpu
from jax.sharding import PartitionSpec as P

F32 = jnp.float32
BF16 = jnp.bfloat16
INFO = 16
STRIP = 16
VMEM = pl.BlockSpec(memory_space=pltpu.VMEM)
SMEM = pl.BlockSpec(memory_space=pltpu.SMEM)
HBM = pl.BlockSpec(memory_space=pltpu.HBM)


def dft_tables(extent):
    half = extent // 2
    steps = np.arange(extent, dtype=np.int32)
    angles = (steps[:, None] * steps[None, :] % extent).astype(np.float32)
    angles = angles * np.float32(2.0 * math.pi / extent)
    scaling = np.float32(1.0 / math.sqrt(extent))
    real = (np.cos(angles) * scaling).astype(BF16)
    imag = (-np.sin(angles) * scaling).astype(BF16)
    tables = []
    for parity in (0, 1):
        re, im = real[:half, parity::2], imag[:half, parity::2]
        right = np.concatenate(
            [np.concatenate([re, im], 1), np.concatenate([-im, re], 1)], 0
        )
        tables += [right, np.ascontiguousarray(right.T)]
    return jnp.asarray(np.stack(tables))


def dot(a, b):
    return jnp.dot(a, b, preferred_element_type=F32)


def quarters(tl, tr, bl, br):
    return jnp.concatenate(
        [jnp.concatenate([tl, tr], 1), jnp.concatenate([bl, br], 1)], 0
    )


def iota(shape, dim):
    return lax.broadcasted_iota(jnp.int32, shape, dim)


def fetch(pairs, sems):
    copies = [
        pltpu.make_async_copy(source, target, sems.at[i])
        for i, (source, target) in enumerate(pairs)
    ]
    for copy in copies:
        copy.start()
    return copies


def pack_kernel(specimen, centers, cnt, helpers, out, tile_v, cen, hlp, sems):
    copies = fetch(((specimen, tile_v), (centers, cen), (helpers, hlp)), sems)
    for copy in copies:
        copy.wait()
    tile = tile_v.shape[1]
    lanes = tile_v.shape[2]
    rows, cols = iota((INFO, lanes), 0), iota((INFO, lanes), 1)
    info = jnp.where(rows == 0, -1.0, 0.0)
    for j in range(centers.shape[2]):
        helper = jnp.where(j < cnt[0, 0], hlp[0, 0, j], -1)
        for r, value in enumerate((helper, cen[0, 0, j, 0], cen[0, 0, j, 1])):
            info = jnp.where((rows == r) & (cols == j), value.astype(F32), info)
    info = info.astype(BF16)
    for p in range(2):
        out[p * tile : (p + 1) * tile] = tile_v[p].astype(BF16)
    out[2 * tile :] = info


def gather_columns(get, source, col, columns, shape):
    lane = iota(shape, 1)
    beside = own = jnp.zeros(shape, F32)
    for c in range(columns):
        block = get(c)
        near = ((source == c + 1) & (lane >= col)) | ((source == c - 1) & (lane < col))
        beside = jnp.where(near, block, beside)
        own = jnp.where(source == c, block, own)
    return jnp.concatenate([beside, own], 1)


def first_product(probe, patch, tables):
    half = patch[0].shape[1] // 2
    wr = probe[0] * patch[0] - probe[1] * patch[1]
    wi = probe[0] * patch[1] + probe[1] * patch[0]
    out = []
    for sign, table in zip((1, -1), tables):
        folded = jnp.concatenate(
            [wr[:, :half] + sign * wr[:, half:], wi[:, :half] + sign * wi[:, half:]], 1
        )
        out.append(dot(folded.astype(BF16), table))
    return out


def frame_of(band):
    columns, height, lanes = band.shape
    me = lax.axis_index("col").astype(F32)
    code = jnp.zeros((1, lanes), F32)
    for c in range(columns):
        info = band[c, height - INFO :].astype(F32)
        hit = info[0:1] == me
        code += jnp.where(hit, c * 128.0 * 128.0 + info[1:2] * 128.0 + info[2:3], 0.0)
    code = jnp.sum(code).astype(jnp.int32)
    return code // (128 * 128), code // 128 % 128, code % 128


def prepare_kernel(
    band, probe, measured, tables,
    info_out, amplitude, tables_out, probe_out, half_out, raw, raw_tables, raw_probe, groups, sems,
):
    copies = fetch(
        ((measured, raw), (tables, raw_tables), (probe, raw_probe)), sems
    )
    columns = band.shape[0]
    tile = (band.shape[1] - INFO) // 2
    extent = raw.shape[-1]
    half = extent // 2
    modes = raw_probe.shape[0]
    source, row, col = frame_of(band)
    which = iota((INFO, extent), 0)
    info = jnp.where(which == 0, source, jnp.where(which == 1, col, row))
    info_out[...] = info.astype(F32).astype(BF16)

    shape = (extent, extent)

    def original(i):
        return jnp.where(i < half, 2 * i, 2 * (i - half) + 1)

    copies[0].wait()
    sort = (iota(shape, 1) == original(iota(shape, 0))).astype(F32).astype(BF16)
    sort_t = (iota(shape, 0) == original(iota(shape, 1))).astype(F32).astype(BF16)
    value = raw[0, 0, 0]
    coarse = value.astype(BF16)
    fine = (value - coarse.astype(F32)).astype(BF16)
    amplitude[...] = sum(
        dot(dot(sort, part).astype(BF16), sort_t) for part in (coarse, fine)
    )

    def roller(old, new, shift, parity):
        wrapped = new % half < shift
        hit = (old + shift - jnp.where(old % half + shift >= half, half, 0)) == new
        sign = jnp.where(wrapped, -1.0, 1.0) if parity else 1.0
        return jnp.where(hit, sign, 0.0).astype(BF16)

    copies[1].wait()
    i, j = iota(shape, 0), iota(shape, 1)
    for parity in range(2):
        right, left = raw_tables[2 * parity], raw_tables[2 * parity + 1]
        for axis, shift in enumerate((col, row)):
            rolled = dot(left, roller(i, j, shift, parity)).astype(BF16)
            rolled_t = dot(roller(j, i, shift, parity), right).astype(BF16)
            tables_out[4 * axis + parity] = rolled_t if axis == 0 else rolled
            tables_out[4 * axis + 2 + parity] = rolled if axis == 0 else rolled_t

    copies[2].wait()
    count = extent // 8
    base = row // 8
    step = row % 8
    lane = iota((extent, half), 1)
    sub = iota((count, 8, extent), 1)
    for k in range(modes):
        for p in range(2):
            lo = pltpu.roll(raw_probe[k, p, :, :half], col, 1)
            hi = pltpu.roll(raw_probe[k, p, :, half:], col, 1)
            turned = jnp.concatenate(
                [jnp.where(lane < col, hi, lo), jnp.where(lane < col, lo, hi)], 1
            )
            turned = pltpu.roll(turned.reshape(count, 8, extent), step, 1)
            turned = jnp.where(
                sub < step, jnp.concatenate([turned[-1:], turned[:-1]], 0), turned
            )
            groups[:count] = turned
            groups[count:] = turned
            probe_out[k, p] = groups[pl.ds(count - base, count)].reshape(extent, extent)

    patch = [
        gather_columns(
            lambda c: band[c, p * tile : (p + 1) * tile].astype(F32),
            source, col, columns, (tile, tile),
        )
        for p in range(2)
    ]
    for k in range(modes):
        products = first_product(
            [probe_out[k, p, half:] for p in range(2)], patch, (tables_out[0], tables_out[1])
        )
        for parity in range(2):
            half_out[k, parity] = products[parity]


def frame_kernel(
    first, second, info, amplitude, tables, probe, half_own,
    to_rows, turned, patch, folded, half_far, mixed, far, corrected, product, mixed_back,
):
    columns = first.shape[0]
    tile = (first.shape[1] - INFO) // 2
    extent = probe.shape[-1]
    half = extent // 2
    modes = probe.shape[0]
    odd = lax.axis_index("row") % 2
    source, col, row = (
        info[r : r + 1, :tile].astype(F32).astype(jnp.int32) for r in range(3)
    )
    strips = [pl.ds(r, STRIP) for r in range(0, half, STRIP)]
    lower = [pl.ds(half + r, STRIP) for r in range(0, half, STRIP)]

    def strip(i, offset=0):
        return pl.ds(pl.multiple_of(offset + i * STRIP, STRIP), STRIP)

    def split(x):
        return x[:, :half], x[:, half:]

    def join(x, y):
        return jnp.concatenate([x, y], 1).astype(BF16)

    def gather(i, carry):
        s = strip(i)
        rows = iota((STRIP, tile), 0) + s.start
        from_first = (rows >= row).astype(jnp.int32) == odd
        for p in range(2):
            part = strip(i, p * tile)
            patch[p, s] = gather_columns(
                lambda c: jnp.where(
                    from_first, first[c, part].astype(F32), second[c, part].astype(F32)
                ),
                source, col, columns, (STRIP, tile),
            )
        return carry

    def wave(k):
        for s in strips:
            pr, pi, xr, xi = probe[k, 0, s], probe[k, 1, s], patch[0, s], patch[1, s]
            re = split(pr * xr - pi * xi)
            im = split(pr * xi + pi * xr)
            folded[k, 0, s] = join(re[0] + re[1], im[0] + im[1])
            folded[k, 1, s] = join(re[0] - re[1], im[0] - im[1])

    def along_rows(k):
        for q in range(2):
            half_far[k, q] = dot(folded[k, q], tables[q])

    def mix(k):
        for s, t in zip(strips, lower):
            even, odds = half_far[k, 0, s], half_far[k, 1, s]
            even_own, odds_own = half_own[k, 0, s], half_own[k, 1, s]
            for q, (e, o) in enumerate(
                ((even + even_own, odds + odds_own), (even - even_own, odds - odds_own))
            ):
                (er, ei), (our, oui) = split(e), split(o)
                mixed[k, q, s] = join(er, our)
                mixed[k, q, t] = join(ei, oui)

    def along_columns(k):
        for q in range(2):
            far[k, q] = dot(tables[4 + q], mixed[k, q])

    def correct(i, carry):
        for q in range(2):
            s, t = strip(i), strip(i, half)
            out = strip(i, q * half)
            re = [far[k, q, s] for k in range(modes)]
            im = [far[k, q, t] for k in range(modes)]
            intensity = sum(x * x for x in re + im)
            factor = 1.0 - amplitude[out] * lax.rsqrt(jnp.maximum(intensity, 0.25))
            for k in range(modes):
                (re_even, re_odd), (im_even, im_odd) = split(re[k] * factor), split(im[k] * factor)
                corrected[k, 0, out] = join(re_even, im_even)
                corrected[k, 1, out] = join(re_odd, im_odd)
        return carry

    def back_along_rows(k):
        for c in range(2):
            product[k, c] = dot(corrected[k, c], tables[2 + c])

    def mix_back(k):
        for q in range(2):
            for s, t in zip(strips, lower):
                part = pl.ds(q * half + s.start, STRIP)
                x, y = product[k, 0, part], product[k, 1, part]
                (lr, li), (hr, hi) = split(x + y), split(x - y)
                mixed_back[k, q, s] = join(lr, hr)
                mixed_back[k, q, t] = join(li, hi)

    def back_along_columns(k):
        for q in range(2):
            turned[k, q] = dot(tables[6 + q], mixed_back[k, q])

    def forward(k, carry):
        wave(k + 1)
        along_rows(k + 1)
        mix(k)
        along_columns(k)
        return carry

    def backward(k, carry):
        back_along_rows(k + 1)
        mix_back(k)
        back_along_columns(k)
        return carry

    def finish(i, carry):
        accumulate(to_rows, turned, probe, strip(i), strip(i, half), strip(i), 1)
        return carry

    lax.fori_loop(0, len(strips), gather, 0)
    wave(0)
    along_rows(0)
    lax.fori_loop(0, modes - 1, forward, 0)
    mix(modes - 1)
    along_columns(modes - 1)
    lax.fori_loop(0, len(strips), correct, 0)
    back_along_rows(0)
    lax.fori_loop(0, modes - 1, backward, 0)
    mix_back(modes - 1)
    back_along_columns(modes - 1)
    lax.fori_loop(0, len(strips), finish, 0)


def accumulate(out, turned, probe, s, t, rows, sign):
    tile = out.shape[0] // 2
    re = im = 0.0
    for k in range(probe.shape[0]):
        pr, pi = probe[k, 0, rows], probe[k, 1, rows]
        cr = turned[k, 0, s] + sign * turned[k, 1, s]
        ci = turned[k, 0, t] + sign * turned[k, 1, t]
        re += pr * cr + pi * ci
        im += pr * ci - pi * cr
    out[s] = re.astype(BF16)
    out[pl.ds(pl.multiple_of(tile + s.start, STRIP), STRIP)] = im.astype(BF16)


def place(block, columns, source, col, taken):
    tile = block.shape[1] // 2
    beside, own = block[:, :tile], block[:, tile:]
    lane = iota(own.shape, 1)
    if taken is not None:
        beside, own = jnp.where(taken, beside, 0.0), jnp.where(taken, own, 0.0)
    out = []
    for c in range(columns):
        near = ((source == c + 1) & (lane >= col)) | ((source == c - 1) & (lane < col))
        out.append(jnp.where(near, beside, 0.0) + jnp.where(source == c, own, 0.0))
    return out


def finish_kernel(
    band, first_band, second_band, turned, probe, first, partial, second_info, centre,
):
    columns = band.shape[0]
    tile = (band.shape[1] - INFO) // 2
    odd = lax.axis_index("row") % 2
    own_frame, first_frame, second_frame = (
        frame_of(b) for b in (band, first_band, second_band)
    )
    which = iota(second_info.shape, 0)
    second_info[...] = jnp.where(
        which == 0, second_frame[0], jnp.where(which == 1, second_frame[1], second_frame[2])
    )
    for r in range(0, tile, STRIP):
        s, t = pl.ds(r, STRIP), pl.ds(tile + r, STRIP)
        accumulate(centre, turned, probe, s, t, t, -1)
        before = (iota((STRIP, tile), 0) + r < first_frame[1]).astype(jnp.int32)
        for part in (s, t):
            mine = place(centre[part].astype(F32), columns, own_frame[0], own_frame[2], None)
            other = place(
                first[part].astype(F32), columns, first_frame[0], first_frame[2], before == odd
            )
            for c in range(columns):
                partial[c, part] = mine[c] + other[c]


def fold_kernel(partial, second, second_info, out):
    columns, height, tile = out.shape
    odd = lax.axis_index("row") % 2
    source, row, col = (second_info[r : r + 1] for r in range(3))
    for r in range(0, height, STRIP):
        s = pl.ds(r, STRIP)
        before = (iota((STRIP, tile), 0) + r % tile < row).astype(jnp.int32)
        other = place(second[s].astype(F32), columns, source, col, before == 1 - odd)
        for c in range(columns):
            out[c, s] = (partial[c, s] + other[c]).astype(BF16)


def call(kernel, name, out_shape, in_specs, scratch, flops, moved, *args):
    args = [
        pltpu.with_memory_space_constraint(arg, pltpu.HBM) if spec is HBM else arg
        for arg, spec in zip(args, in_specs)
    ]
    return pl.pallas_call(
        kernel,
        out_shape=out_shape,
        in_specs=in_specs,
        out_specs=jax.tree.map(lambda _: VMEM, out_shape),
        scratch_shapes=scratch,
        compiler_params=pltpu.CompilerParams(vmem_limit_bytes=32 * 2**20),
        cost_estimate=pl.CostEstimate(flops=flops, bytes_accessed=moved, transcendentals=0),
        name=name,
    )(*args)


def per_device(specimen, probe, measured, centers, frame_counts, helper_cols):
    extent = probe.shape[-1]
    half = extent // 2
    tile = specimen.shape[1]
    modes = probe.shape[0]
    columns = lax.axis_size("col")
    height = 2 * tile
    part = jax.ShapeDtypeStruct((height, extent), BF16)
    dma = pltpu.SemaphoreType.DMA

    packed = call(
        pack_kernel, "pack",
        jax.ShapeDtypeStruct((height + INFO, tile), BF16),
        [HBM, HBM, SMEM, HBM],
        [
            pltpu.VMEM(specimen.shape, F32),
            pltpu.SMEM(centers.shape, jnp.int32),
            pltpu.SMEM(helper_cols.shape, jnp.int32),
            dma((3,)),
        ],
        10**5, 2**19,
        specimen, centers, frame_counts, helper_cols,
    )
    band = lax.all_gather(packed, "col")

    rows = lax.axis_size("row")
    swaps = []
    for start in (0, 1):
        pairs = [(i, i + 1) for i in range(start, rows - 1, 2)]
        swaps.append(pairs + [(b, a) for a, b in pairs])
    second = lax.ppermute(band, "row", swaps[1])
    first = lax.ppermute(band, "row", swaps[0])
    tables = dft_tables(extent)
    prepared = call(
        prepare_kernel, "prepare",
        (
            jax.ShapeDtypeStruct((INFO, extent), BF16),
            jax.ShapeDtypeStruct((extent, extent), F32),
            jax.ShapeDtypeStruct((8, extent, extent), BF16),
            jax.ShapeDtypeStruct(probe.shape, F32),
            jax.ShapeDtypeStruct((modes, 2, tile, extent), F32),
        ),
        [VMEM, HBM, HBM, HBM],
        [
            pltpu.VMEM(measured.shape, F32),
            pltpu.VMEM(tables.shape, BF16),
            pltpu.VMEM(probe.shape, F32),
            pltpu.VMEM((extent // 4, 8, extent), F32),
            dma((3,)),
        ],
        10**9, 2**22,
        band, probe, measured, tables,
    )
    full = (modes, 2, extent, extent)
    to_rows, turned = call(
        frame_kernel, "frame",
        (part, jax.ShapeDtypeStruct(full, F32)),
        [VMEM] * 7,
        [
            pltpu.VMEM((2, tile, extent), F32),
            pltpu.VMEM((modes, 2, half, extent), BF16),
            pltpu.VMEM((modes, 2, half, extent), F32),
            pltpu.VMEM(full, BF16),
            pltpu.VMEM(full, F32),
            pltpu.VMEM(full, BF16),
            pltpu.VMEM(full, F32),
            pltpu.VMEM(full, BF16),
        ],
        2 * 10**9, 2**22,
        first, second, *prepared,
    )
    from_first = lax.ppermute(to_rows, "row", swaps[0])
    from_second = lax.ppermute(to_rows, "row", swaps[1])
    partial, second_info = call(
        finish_kernel, "finish",
        (
            jax.ShapeDtypeStruct((columns, height, tile), F32),
            jax.ShapeDtypeStruct((8, tile), jnp.int32),
        ),
        [VMEM] * 6,
        [pltpu.VMEM((height, extent), BF16)],
        10**7, 2**22,
        band, first, second, turned, prepared[3], from_first,
    )
    summed = call(
        fold_kernel, "fold",
        jax.ShapeDtypeStruct((columns, height, tile), BF16),
        [VMEM] * 3,
        [],
        10**7, 2**20,
        partial, from_second, second_info,
    )
    shares = lax.all_to_all(summed, "col", split_axis=0, concat_axis=0, tiled=True)
    return jnp.sum(shares.astype(F32), axis=0).reshape(2, tile, tile)


def solution(mesh):
    return jax.shard_map(
        per_device,
        mesh=mesh,
        in_specs=(
            P(None, "row", "col"),
            P(),
            P("row", "col", None, None, None),
            P("row", "col", None, None),
            P("row", "col"),
            P("row", "col", None),
        ),
        out_specs=P(None, "row", "col"),
        check_vma=False,
    )
```

```python
import functools
import math

import jax
import jax.numpy as jnp
import numpy as np
from jax import lax
from jax.experimental import pallas as pl
from jax.experimental.pallas import tpu as pltpu
from jax.sharding import PartitionSpec as P

F32 = jnp.float32
BF16 = jnp.bfloat16
INFO = 16
STRIP = 16
VMEM = pl.BlockSpec(memory_space=pltpu.VMEM)
SMEM = pl.BlockSpec(memory_space=pltpu.SMEM)
HBM = pl.BlockSpec(memory_space=pltpu.HBM)


def dft_tables(extent):
    half = extent // 2
    steps = np.arange(extent, dtype=np.int32)
    angles = (steps[:, None] * steps[None, :] % extent).astype(np.float32)
    angles = angles * np.float32(2.0 * math.pi / extent)
    scaling = np.float32(1.0 / math.sqrt(extent))
    real = (np.cos(angles) * scaling).astype(BF16)
    imag = (-np.sin(angles) * scaling).astype(BF16)
    tables = []
    for parity in (0, 1):
        re, im = real[:half, parity::2], imag[:half, parity::2]
        right = np.concatenate(
            [np.concatenate([re, im], 1), np.concatenate([-im, re], 1)], 0
        )
        tables += [right, np.ascontiguousarray(right.T)]
    return jnp.asarray(np.stack(tables))


def dot(a, b):
    return jnp.dot(a, b, preferred_element_type=F32)


def quarters(tl, tr, bl, br):
    return jnp.concatenate(
        [jnp.concatenate([tl, tr], 1), jnp.concatenate([bl, br], 1)], 0
    )


def iota(shape, dim):
    return lax.broadcasted_iota(jnp.int32, shape, dim)


def fetch(pairs, sems):
    copies = [
        pltpu.make_async_copy(source, target, sems.at[i])
        for i, (source, target) in enumerate(pairs)
    ]
    for copy in copies:
        copy.start()
    return copies


def pack_kernel(specimen, centers, cnt, helpers, out, tile_v, cen, hlp, sems):
    copies = fetch(((specimen, tile_v), (centers, cen), (helpers, hlp)), sems)
    for copy in copies:
        copy.wait()
    tile = tile_v.shape[1]
    lanes = tile_v.shape[2]
    rows, cols = iota((INFO, lanes), 0), iota((INFO, lanes), 1)
    info = jnp.where(rows == 0, -1.0, 0.0)
    for j in range(centers.shape[2]):
        helper = jnp.where(j < cnt[0, 0], hlp[0, 0, j], -1)
        for r, value in enumerate((helper, cen[0, 0, j, 0], cen[0, 0, j, 1])):
            info = jnp.where((rows == r) & (cols == j), value.astype(F32), info)
    info = info.astype(BF16)
    for p in range(2):
        out[p * tile : (p + 1) * tile] = tile_v[p].astype(BF16)
    out[2 * tile :] = info


def gather_columns(get, source, col, columns, shape):
    lane = iota(shape, 1)
    beside = own = jnp.zeros(shape, F32)
    for c in range(columns):
        block = get(c)
        near = ((source == c + 1) & (lane >= col)) | ((source == c - 1) & (lane < col))
        beside = jnp.where(near, block, beside)
        own = jnp.where(source == c, block, own)
    return jnp.concatenate([beside, own], 1)


def first_product(probe, patch, tables):
    half = patch[0].shape[1] // 2
    wr = probe[0] * patch[0] - probe[1] * patch[1]
    wi = probe[0] * patch[1] + probe[1] * patch[0]
    out = []
    for sign, table in zip((1, -1), tables):
        folded = jnp.concatenate(
            [wr[:, :half] + sign * wr[:, half:], wi[:, :half] + sign * wi[:, half:]], 1
        )
        out.append(dot(folded.astype(BF16), table))
    return out


def frame_of(band):
    columns, height, lanes = band.shape
    me = lax.axis_index("col").astype(F32)
    code = jnp.zeros((1, lanes), F32)
    for c in range(columns):
        info = band[c, height - INFO :].astype(F32)
        hit = info[0:1] == me
        code += jnp.where(hit, (c * lanes + info[1:2]) * lanes + info[2:3], 0.0)
    code = jnp.sum(code).astype(jnp.int32)
    return code // (lanes * lanes), code // lanes % lanes, code % lanes


def prepare_kernel(
    band, probe, measured, tables,
    info_out, amplitude, tables_out, probe_out, half_out, raw, raw_tables, raw_probe, groups, sems,
):
    copies = fetch(
        ((measured, raw), (tables, raw_tables), (probe, raw_probe)), sems
    )
    columns = band.shape[0]
    tile = (band.shape[1] - INFO) // 2
    extent = raw.shape[-1]
    half = extent // 2
    modes = raw_probe.shape[0]
    source, row, col = frame_of(band)
    which = iota((INFO, extent), 0)
    info = jnp.where(which == 0, source, jnp.where(which == 1, col, row))
    info_out[...] = info.astype(F32).astype(BF16)

    shape = (extent, extent)

    def original(i):
        return jnp.where(i < half, 2 * i, 2 * (i - half) + 1)

    copies[0].wait()
    sort = (iota(shape, 1) == original(iota(shape, 0))).astype(F32).astype(BF16)
    sort_t = (iota(shape, 0) == original(iota(shape, 1))).astype(F32).astype(BF16)
    value = raw[0, 0, 0]
    coarse = value.astype(BF16)
    fine = (value - coarse.astype(F32)).astype(BF16)
    amplitude[...] = sum(
        dot(dot(sort, part).astype(BF16), sort_t) for part in (coarse, fine)
    )

    def roller(old, new, shift, parity):
        wrapped = new % half < shift
        hit = (old + shift - jnp.where(old % half + shift >= half, half, 0)) == new
        sign = jnp.where(wrapped, -1.0, 1.0) if parity else 1.0
        return jnp.where(hit, sign, 0.0).astype(BF16)

    copies[1].wait()
    i, j = iota(shape, 0), iota(shape, 1)
    for parity in range(2):
        right, left = raw_tables[2 * parity], raw_tables[2 * parity + 1]
        for axis, shift in enumerate((col, row)):
            rolled = dot(left, roller(i, j, shift, parity)).astype(BF16)
            rolled_t = dot(roller(j, i, shift, parity), right).astype(BF16)
            tables_out[4 * axis + parity] = rolled_t if axis == 0 else rolled
            tables_out[4 * axis + 2 + parity] = rolled if axis == 0 else rolled_t

    copies[2].wait()
    count = extent // 8
    base = row // 8
    step = row % 8
    lane = iota((extent, half), 1)
    sub = iota((count, 8, extent), 1)
    for k in range(modes):
        for p in range(2):
            lo = pltpu.roll(raw_probe[k, p, :, :half], col, 1)
            hi = pltpu.roll(raw_probe[k, p, :, half:], col, 1)
            turned = jnp.concatenate(
                [jnp.where(lane < col, hi, lo), jnp.where(lane < col, lo, hi)], 1
            )
            turned = pltpu.roll(turned.reshape(count, 8, extent), step, 1)
            turned = jnp.where(
                sub < step, jnp.concatenate([turned[-1:], turned[:-1]], 0), turned
            )
            groups[:count] = turned
            groups[count:] = turned
            probe_out[k, p] = groups[pl.ds(count - base, count)].reshape(extent, extent)

    patch = [
        gather_columns(
            lambda c: band[c, p * tile : (p + 1) * tile].astype(F32),
            source, col, columns, (tile, tile),
        )
        for p in range(2)
    ]
    for k in range(modes):
        products = first_product(
            [probe_out[k, p, half:] for p in range(2)], patch, (tables_out[0], tables_out[1])
        )
        for parity in range(2):
            half_out[k, parity] = products[parity]


def frame_kernel(
    first, second, info, amplitude, tables, probe, half_own,
    to_rows, mixed_back, patch, folded, half_far, mixed, far, corrected, product, chi,
):
    columns = first.shape[0]
    tile = (first.shape[1] - INFO) // 2
    extent = probe.shape[-1]
    half = extent // 2
    modes = probe.shape[0]
    odd = lax.axis_index("row") % 2
    source, col, row = (
        info[r : r + 1, :tile].astype(F32).astype(jnp.int32) for r in range(3)
    )
    strips = [pl.ds(r, STRIP) for r in range(0, half, STRIP)]
    lower = [pl.ds(half + r, STRIP) for r in range(0, half, STRIP)]

    def split(x):
        return x[:, :half], x[:, half:]

    def join(x, y):
        return jnp.concatenate([x, y], 1).astype(BF16)

    def gather(s):
        rows = iota((STRIP, tile), 0) + s.start
        from_first = (rows >= row).astype(jnp.int32) == odd
        for p in range(2):
            part = pl.ds(p * tile + s.start, STRIP)
            patch[p, s] = gather_columns(
                lambda c: jnp.where(
                    from_first, first[c, part].astype(F32), second[c, part].astype(F32)
                ),
                source, col, columns, (STRIP, tile),
            )

    def wave(k):
        for s in strips:
            pr, pi, xr, xi = probe[k, 0, s], probe[k, 1, s], patch[0, s], patch[1, s]
            re = split(pr * xr - pi * xi)
            im = split(pr * xi + pi * xr)
            folded[k, 0, s] = join(re[0] + re[1], im[0] + im[1])
            folded[k, 1, s] = join(re[0] - re[1], im[0] - im[1])

    def along_rows(k):
        for q in range(2):
            half_far[k, q] = dot(folded[k, q], tables[q])

    def mix(k):
        for s, t in zip(strips, lower):
            even, odds = half_far[k, 0, s], half_far[k, 1, s]
            even_own, odds_own = half_own[k, 0, s], half_own[k, 1, s]
            for q, (e, o) in enumerate(
                ((even + even_own, odds + odds_own), (even - even_own, odds - odds_own))
            ):
                (er, ei), (our, oui) = split(e), split(o)
                mixed[k, q, s] = join(er, our)
                mixed[k, q, t] = join(ei, oui)

    def along_columns(k, q):
        far[k, q] = dot(tables[4 + q], mixed[k, q])

    def correct(q, which):
        for s, t in list(zip(strips, lower))[which]:
            re = [far[k, q, s] for k in range(modes)]
            im = [far[k, q, t] for k in range(modes)]
            intensity = sum(x * x for x in re + im)
            size = amplitude[pl.ds(q * half + s.start, STRIP)]
            factor = 1.0 - size * lax.rsqrt(jnp.maximum(intensity, 0.25))
            out = pl.ds(q * half + s.start, STRIP)
            for k in range(modes):
                (re_even, re_odd), (im_even, im_odd) = split(re[k] * factor), split(im[k] * factor)
                corrected[k, 0, out] = join(re_even, im_even)
                corrected[k, 1, out] = join(re_odd, im_odd)

    def back_along_rows(k, q):
        part = pl.ds(q * half, half)
        for c in range(2):
            product[k, c, part] = dot(corrected[k, c, part], tables[2 + c])

    def mix_back(k, q):
        for s, t in zip(strips, lower):
            part = pl.ds(q * half + s.start, STRIP)
            x, y = product[k, 0, part], product[k, 1, part]
            (lr, li), (hr, hi) = split(x + y), split(x - y)
            mixed_back[k, q, s] = join(lr, hr)
            mixed_back[k, q, t] = join(li, hi)

    both_back = jnp.concatenate([tables[6], tables[7]], 1)

    def back_along_columns(k):
        chi[k] = dot(both_back, mixed_back[k].reshape(2 * extent, extent))

    for s in strips:
        gather(s)
    for k in range(modes + 1):
        if k < modes:
            wave(k)
            along_rows(k)
        if k > 0:
            mix(k - 1)
            along_columns(k - 1, 0)
    share = -(-len(strips) // modes)
    for k in range(modes):
        along_columns(k, 1)
        correct(0, slice(k * share, (k + 1) * share))
    for k in range(modes):
        back_along_rows(k, 0)
        correct(1, slice(k * share, (k + 1) * share))
    for k in range(modes):
        mix_back(k, 0)
        back_along_rows(k, 1)
    for k in range(modes):
        mix_back(k, 1)
        back_along_columns(k)
    for s, t in zip(strips, lower):
        accumulate(to_rows, chi, probe, s, t, s)


def accumulate(out, chi, probe, s, t, rows):
    tile = out.shape[0] // 2
    re = im = 0.0
    for k in range(probe.shape[0]):
        pr, pi = probe[k, 0, rows], probe[k, 1, rows]
        cr, ci = chi[k, s], chi[k, t]
        re += pr * cr + pi * ci
        im += pr * ci - pi * cr
    out[s] = re.astype(BF16)
    out[pl.ds(tile + s.start, STRIP)] = im.astype(BF16)


def place(block, columns, source, col, taken):
    tile = block.shape[1] // 2
    beside, own = block[:, :tile], block[:, tile:]
    lane = iota(own.shape, 1)
    if taken is not None:
        beside, own = jnp.where(taken, beside, 0.0), jnp.where(taken, own, 0.0)
    out = []
    for c in range(columns):
        near = ((source == c + 1) & (lane >= col)) | ((source == c - 1) & (lane < col))
        out.append(jnp.where(near, beside, 0.0) + jnp.where(source == c, own, 0.0))
    return out


def finish_kernel(
    band, first_band, second_band, mixed_back, tables, probe, first,
    partial, second_info, chi, centre,
):
    columns = band.shape[0]
    extent = probe.shape[-1]
    tile = (band.shape[1] - INFO) // 2
    odd = lax.axis_index("row") % 2
    own_frame, first_frame, second_frame = (
        frame_of(b) for b in (band, first_band, second_band)
    )
    which = iota(second_info.shape, 0)
    second_info[...] = jnp.where(
        which == 0, second_frame[0], jnp.where(which == 1, second_frame[1], second_frame[2])
    )
    both_back = jnp.concatenate([tables[6], -tables[7]], 1)
    for k in range(probe.shape[0]):
        chi[k] = dot(both_back, mixed_back[k].reshape(2 * extent, extent))
    for r in range(0, tile, STRIP):
        s, t = pl.ds(r, STRIP), pl.ds(tile + r, STRIP)
        accumulate(centre, chi, probe, s, t, t)
        before = (iota((STRIP, tile), 0) + r < first_frame[1]).astype(jnp.int32)
        for part in (s, t):
            mine = place(centre[part].astype(F32), columns, own_frame[0], own_frame[2], None)
            other = place(
                first[part].astype(F32), columns, first_frame[0], first_frame[2], before == odd
            )
            for c in range(columns):
                partial[c, part] = mine[c] + other[c]


def fold_kernel(partial, second, second_info, out):
    columns, height, tile = out.shape
    odd = lax.axis_index("row") % 2
    source, row, col = (second_info[r : r + 1] for r in range(3))
    for r in range(0, height, STRIP):
        s = pl.ds(r, STRIP)
        before = (iota((STRIP, tile), 0) + r % tile < row).astype(jnp.int32)
        other = place(second[s].astype(F32), columns, source, col, before == 1 - odd)
        for c in range(columns):
            out[c, s] = (partial[c, s] + other[c]).astype(BF16)


def call(kernel, name, out_shape, in_specs, scratch, flops, moved, *args):
    args = [
        pltpu.with_memory_space_constraint(arg, pltpu.HBM) if spec is HBM else arg
        for arg, spec in zip(args, in_specs)
    ]
    return pl.pallas_call(
        kernel,
        out_shape=out_shape,
        in_specs=in_specs,
        out_specs=jax.tree.map(lambda _: VMEM, out_shape),
        scratch_shapes=scratch,
        compiler_params=pltpu.CompilerParams(vmem_limit_bytes=32 * 2**20),
        cost_estimate=pl.CostEstimate(flops=flops, bytes_accessed=moved, transcendentals=0),
        name=name,
    )(*args)


def per_device(specimen, probe, measured, centers, frame_counts, helper_cols):
    extent = probe.shape[-1]
    half = extent // 2
    tile = specimen.shape[1]
    modes = probe.shape[0]
    columns = lax.axis_size("col")
    height = 2 * tile
    part = jax.ShapeDtypeStruct((height, extent), BF16)
    dma = pltpu.SemaphoreType.DMA

    packed = call(
        pack_kernel, "pack",
        jax.ShapeDtypeStruct((height + INFO, tile), BF16),
        [HBM, HBM, SMEM, HBM],
        [
            pltpu.VMEM(specimen.shape, F32),
            pltpu.SMEM(centers.shape, jnp.int32),
            pltpu.SMEM(helper_cols.shape, jnp.int32),
            dma((3,)),
        ],
        10**5, 2**19,
        specimen, centers, frame_counts, helper_cols,
    )
    band = lax.all_gather(packed, "col")

    rows = lax.axis_size("row")
    swaps = []
    for start in (0, 1):
        pairs = [(i, i + 1) for i in range(start, rows - 1, 2)]
        swaps.append(pairs + [(b, a) for a, b in pairs])
    second = lax.ppermute(band, "row", swaps[1])
    first = lax.ppermute(band, "row", swaps[0])
    tables = dft_tables(extent)
    prepared = call(
        prepare_kernel, "prepare",
        (
            jax.ShapeDtypeStruct((INFO, extent), BF16),
            jax.ShapeDtypeStruct((extent, extent), F32),
            jax.ShapeDtypeStruct((8, extent, extent), BF16),
            jax.ShapeDtypeStruct(probe.shape, F32),
            jax.ShapeDtypeStruct((modes, 2, tile, extent), F32),
        ),
        [VMEM, HBM, HBM, HBM],
        [
            pltpu.VMEM(measured.shape, F32),
            pltpu.VMEM(tables.shape, BF16),
            pltpu.VMEM(probe.shape, F32),
            pltpu.VMEM((extent // 4, 8, extent), F32),
            dma((3,)),
        ],
        10**9, 2**22,
        band, probe, measured, tables,
    )
    full = (modes, 2, extent, extent)
    to_rows, mixed_back = call(
        frame_kernel, "frame",
        (part, jax.ShapeDtypeStruct(full, BF16)),
        [VMEM] * 7,
        [
            pltpu.VMEM((2, tile, extent), F32),
            pltpu.VMEM((modes, 2, half, extent), BF16),
            pltpu.VMEM((modes, 2, half, extent), F32),
            pltpu.VMEM(full, BF16),
            pltpu.VMEM(full, F32),
            pltpu.VMEM(full, BF16),
            pltpu.VMEM(full, F32),
            pltpu.VMEM((modes, extent, extent), F32),
        ],
        2 * 10**9, 2**22,
        first, second, *prepared,
    )
    from_first = lax.ppermute(to_rows, "row", swaps[0])
    from_second = lax.ppermute(to_rows, "row", swaps[1])
    partial, second_info = call(
        finish_kernel, "finish",
        (
            jax.ShapeDtypeStruct((columns, height, tile), F32),
            jax.ShapeDtypeStruct((8, tile), jnp.int32),
        ),
        [VMEM] * 7,
        [pltpu.VMEM((modes, extent, extent), F32), pltpu.VMEM((height, extent), BF16)],
        5 * 10**8, 2**22,
        band, first, second, mixed_back, prepared[2], prepared[3], from_first,
    )
    summed = call(
        fold_kernel, "fold",
        jax.ShapeDtypeStruct((columns, height, tile), BF16),
        [VMEM] * 3,
        [],
        10**7, 2**20,
        partial, from_second, second_info,
    )
    shares = lax.all_to_all(summed, "col", split_axis=0, concat_axis=0, tiled=True)
    return jnp.sum(shares.astype(F32), axis=0).reshape(2, tile, tile)


def solution(mesh):
    return jax.shard_map(
        per_device,
        mesh=mesh,
        in_specs=(
            P(None, "row", "col"),
            P(),
            P("row", "col", None, None, None),
            P("row", "col", None, None),
            P("row", "col"),
            P("row", "col", None),
        ),
        out_specs=P(None, "row", "col"),
        check_vma=False,
    )
```

```python
import functools
import math

import jax
import jax.numpy as jnp
import numpy as np
from jax import lax
from jax.experimental import pallas as pl
from jax.experimental.pallas import tpu as pltpu
from jax.sharding import PartitionSpec as P

F32 = jnp.float32
BF16 = jnp.bfloat16
INFO = 16
STRIP = 16
VMEM = pl.BlockSpec(memory_space=pltpu.VMEM)
SMEM = pl.BlockSpec(memory_space=pltpu.SMEM)
HBM = pl.BlockSpec(memory_space=pltpu.HBM)


def dft_tables(extent):
    half = extent // 2
    steps = np.arange(extent, dtype=np.int32)
    angles = (steps[:, None] * steps[None, :] % extent).astype(np.float32)
    angles = angles * np.float32(2.0 * math.pi / extent)
    scaling = np.float32(1.0 / math.sqrt(extent))
    real = (np.cos(angles) * scaling).astype(BF16)
    imag = (-np.sin(angles) * scaling).astype(BF16)
    tables = []
    for parity in (0, 1):
        re, im = real[:half, parity::2], imag[:half, parity::2]
        right = np.concatenate(
            [np.concatenate([re, im], 1), np.concatenate([-im, re], 1)], 0
        )
        tables += [right, np.ascontiguousarray(right.T)]
    return jnp.asarray(np.stack(tables))


def dot(a, b):
    return jnp.dot(a, b, preferred_element_type=F32)


def quarters(tl, tr, bl, br):
    return jnp.concatenate(
        [jnp.concatenate([tl, tr], 1), jnp.concatenate([bl, br], 1)], 0
    )


def iota(shape, dim):
    return lax.broadcasted_iota(jnp.int32, shape, dim)


def fetch(pairs, sems):
    copies = [
        pltpu.make_async_copy(source, target, sems.at[i])
        for i, (source, target) in enumerate(pairs)
    ]
    for copy in copies:
        copy.start()
    return copies


def pack_kernel(specimen, centers, cnt, helpers, out, tile_v, cen, hlp, sems):
    copies = fetch(((specimen, tile_v), (centers, cen), (helpers, hlp)), sems)
    for copy in copies:
        copy.wait()
    tile = tile_v.shape[1]
    lanes = tile_v.shape[2]
    rows, cols = iota((INFO, lanes), 0), iota((INFO, lanes), 1)
    info = jnp.where(rows == 0, -1.0, 0.0)
    for j in range(centers.shape[2]):
        helper = jnp.where(j < cnt[0, 0], hlp[0, 0, j], -1)
        for r, value in enumerate((helper, cen[0, 0, j, 0], cen[0, 0, j, 1])):
            info = jnp.where((rows == r) & (cols == j), value.astype(F32), info)
    info = info.astype(BF16)
    for p in range(2):
        out[p * tile : (p + 1) * tile] = tile_v[p].astype(BF16)
    out[2 * tile :] = info


def gather_columns(get, source, col, columns, shape):
    lane = iota(shape, 1)
    beside = own = jnp.zeros(shape, F32)
    for c in range(columns):
        block = get(c)
        near = ((source == c + 1) & (lane >= col)) | ((source == c - 1) & (lane < col))
        beside = jnp.where(near, block, beside)
        own = jnp.where(source == c, block, own)
    return jnp.concatenate([beside, own], 1)


def first_product(probe, patch, tables):
    half = patch[0].shape[1] // 2
    wr = probe[0] * patch[0] - probe[1] * patch[1]
    wi = probe[0] * patch[1] + probe[1] * patch[0]
    out = []
    for sign, table in zip((1, -1), tables):
        folded = jnp.concatenate(
            [wr[:, :half] + sign * wr[:, half:], wi[:, :half] + sign * wi[:, half:]], 1
        )
        out.append(dot(folded.astype(BF16), table))
    return out


def ring(columns):
    if columns & (columns - 1):
        return list(range(columns))
    return [i ^ (i >> 1) for i in range(columns)]


def frame_of(band):
    columns, height, lanes = band.shape
    me = lax.axis_index("col").astype(F32)
    code = jnp.zeros((1, lanes), F32)
    for place, c in enumerate(ring(columns)):
        info = band[place, height - INFO :].astype(F32)
        hit = info[0:1] == me
        code += jnp.where(hit, (c * lanes + info[1:2]) * lanes + info[2:3], 0.0)
    code = jnp.sum(code).astype(jnp.int32)
    return code // (lanes * lanes), code // lanes % lanes, code % lanes


def prepare_kernel(
    band, probe, measured, tables,
    info_out, amplitude, tables_out, probe_out, half_out, raw, raw_tables, raw_probe, groups, sems,
):
    copies = fetch(
        ((measured, raw), (tables, raw_tables), (probe, raw_probe)), sems
    )
    columns = band.shape[0]
    tile = (band.shape[1] - INFO) // 2
    extent = raw.shape[-1]
    half = extent // 2
    modes = raw_probe.shape[0]
    source, row, col = frame_of(band)
    which = iota((INFO, extent), 0)
    info = jnp.where(which == 0, source, jnp.where(which == 1, col, row))
    info_out[...] = info.astype(F32).astype(BF16)

    shape = (extent, extent)

    def original(i):
        return jnp.where(i < half, 2 * i, 2 * (i - half) + 1)

    copies[0].wait()
    sort = (iota(shape, 1) == original(iota(shape, 0))).astype(F32).astype(BF16)
    sort_t = (iota(shape, 0) == original(iota(shape, 1))).astype(F32).astype(BF16)
    value = raw[0, 0, 0]
    coarse = value.astype(BF16)
    fine = (value - coarse.astype(F32)).astype(BF16)
    amplitude[...] = sum(
        dot(dot(sort, part).astype(BF16), sort_t) for part in (coarse, fine)
    )

    def roller(old, new, shift, parity):
        wrapped = new % half < shift
        hit = (old + shift - jnp.where(old % half + shift >= half, half, 0)) == new
        sign = jnp.where(wrapped, -1.0, 1.0) if parity else 1.0
        return jnp.where(hit, sign, 0.0).astype(BF16)

    copies[1].wait()
    i, j = iota(shape, 0), iota(shape, 1)
    for parity in range(2):
        right, left = raw_tables[2 * parity], raw_tables[2 * parity + 1]
        for axis, shift in enumerate((col, row)):
            rolled = dot(left, roller(i, j, shift, parity)).astype(BF16)
            rolled_t = dot(roller(j, i, shift, parity), right).astype(BF16)
            tables_out[4 * axis + parity] = rolled_t if axis == 0 else rolled
            tables_out[4 * axis + 2 + parity] = rolled if axis == 0 else rolled_t

    copies[2].wait()
    count = extent // 8
    base = row // 8
    step = row % 8
    lane = iota((extent, half), 1)
    sub = iota((count, 8, extent), 1)
    for k in range(modes):
        for p in range(2):
            lo = pltpu.roll(raw_probe[k, p, :, :half], col, 1)
            hi = pltpu.roll(raw_probe[k, p, :, half:], col, 1)
            turned = jnp.concatenate(
                [jnp.where(lane < col, hi, lo), jnp.where(lane < col, lo, hi)], 1
            )
            turned = pltpu.roll(turned.reshape(count, 8, extent), step, 1)
            turned = jnp.where(
                sub < step, jnp.concatenate([turned[-1:], turned[:-1]], 0), turned
            )
            groups[:count] = turned
            groups[count:] = turned
            probe_out[k, p] = groups[pl.ds(count - base, count)].reshape(extent, extent)

    order = ring(columns)
    patch = [
        gather_columns(
            lambda c: band[order.index(c), p * tile : (p + 1) * tile].astype(F32),
            source, col, columns, (tile, tile),
        )
        for p in range(2)
    ]
    for k in range(modes):
        products = first_product(
            [probe_out[k, p, half:] for p in range(2)], patch, (tables_out[0], tables_out[1])
        )
        for parity in range(2):
            half_out[k, parity] = products[parity]


def frame_kernel(
    first, second, info, amplitude, tables, probe, half_own,
    to_rows, mixed_back, patch, folded, half_far, mixed, far, corrected, product, chi,
):
    columns = first.shape[0]
    tile = (first.shape[1] - INFO) // 2
    extent = probe.shape[-1]
    half = extent // 2
    modes = probe.shape[0]
    order = ring(columns)
    odd = lax.axis_index("row") % 2
    source, col, row = (
        info[r : r + 1, :tile].astype(F32).astype(jnp.int32) for r in range(3)
    )
    strips = [pl.ds(r, STRIP) for r in range(0, half, STRIP)]
    lower = [pl.ds(half + r, STRIP) for r in range(0, half, STRIP)]

    def split(x):
        return x[:, :half], x[:, half:]

    def join(x, y):
        return jnp.concatenate([x, y], 1).astype(BF16)

    def gather(s):
        rows = iota((STRIP, tile), 0) + s.start
        from_first = (rows >= row).astype(jnp.int32) == odd
        for p in range(2):
            part = pl.ds(p * tile + s.start, STRIP)
            patch[p, s] = gather_columns(
                lambda c: jnp.where(
                    from_first,
                    first[order.index(c), part].astype(F32),
                    second[order.index(c), part].astype(F32),
                ),
                source, col, columns, (STRIP, tile),
            )

    def wave(k):
        for s in strips:
            pr, pi, xr, xi = probe[k, 0, s], probe[k, 1, s], patch[0, s], patch[1, s]
            re = split(pr * xr - pi * xi)
            im = split(pr * xi + pi * xr)
            folded[k, 0, s] = join(re[0] + re[1], im[0] + im[1])
            folded[k, 1, s] = join(re[0] - re[1], im[0] - im[1])

    def along_rows(k):
        for q in range(2):
            half_far[k, q] = dot(folded[k, q], tables[q])

    def mix(k):
        for s, t in zip(strips, lower):
            even, odds = half_far[k, 0, s], half_far[k, 1, s]
            even_own, odds_own = half_own[k, 0, s], half_own[k, 1, s]
            for q, (e, o) in enumerate(
                ((even + even_own, odds + odds_own), (even - even_own, odds - odds_own))
            ):
                (er, ei), (our, oui) = split(e), split(o)
                mixed[k, q, s] = join(er, our)
                mixed[k, q, t] = join(ei, oui)

    def along_columns(k, q):
        far[k, q] = dot(tables[4 + q], mixed[k, q])

    def correct(q, which):
        for s, t in list(zip(strips, lower))[which]:
            re = [far[k, q, s] for k in range(modes)]
            im = [far[k, q, t] for k in range(modes)]
            intensity = sum(x * x for x in re + im)
            size = amplitude[pl.ds(q * half + s.start, STRIP)]
            factor = 1.0 - size * lax.rsqrt(jnp.maximum(intensity, 0.25))
            out = pl.ds(q * half + s.start, STRIP)
            for k in range(modes):
                (re_even, re_odd), (im_even, im_odd) = split(re[k] * factor), split(im[k] * factor)
                corrected[k, 0, out] = join(re_even, im_even)
                corrected[k, 1, out] = join(re_odd, im_odd)

    def back_along_rows(k, q):
        part = pl.ds(q * half, half)
        for c in range(2):
            product[k, c, part] = dot(corrected[k, c, part], tables[2 + c])

    def mix_back(k, q):
        for s, t in zip(strips, lower):
            part = pl.ds(q * half + s.start, STRIP)
            x, y = product[k, 0, part], product[k, 1, part]
            (lr, li), (hr, hi) = split(x + y), split(x - y)
            mixed_back[k, q, s] = join(lr, hr)
            mixed_back[k, q, t] = join(li, hi)

    both_back = jnp.concatenate([tables[6], tables[7]], 1)

    def back_along_columns(k):
        chi[k] = dot(both_back, mixed_back[k].reshape(2 * extent, extent))

    for s in strips:
        gather(s)
    for k in range(modes + 1):
        if k < modes:
            wave(k)
            along_rows(k)
        if k > 0:
            mix(k - 1)
            along_columns(k - 1, 0)
    share = -(-len(strips) // modes)
    for k in range(modes):
        along_columns(k, 1)
        correct(0, slice(k * share, (k + 1) * share))
    for k in range(modes):
        back_along_rows(k, 0)
        correct(1, slice(k * share, (k + 1) * share))
    for k in range(modes):
        mix_back(k, 0)
        back_along_rows(k, 1)
    for k in range(modes):
        mix_back(k, 1)
        back_along_columns(k)
    for s, t in zip(strips, lower):
        accumulate(to_rows, chi, probe, s, t, s)


def accumulate(out, chi, probe, s, t, rows):
    tile = out.shape[0] // 2
    re = im = 0.0
    for k in range(probe.shape[0]):
        pr, pi = probe[k, 0, rows], probe[k, 1, rows]
        cr, ci = chi[k, s], chi[k, t]
        re += pr * cr + pi * ci
        im += pr * ci - pi * cr
    out[s] = re.astype(BF16)
    out[pl.ds(tile + s.start, STRIP)] = im.astype(BF16)


def place(block, columns, source, col, taken):
    tile = block.shape[1] // 2
    beside, own = block[:, :tile], block[:, tile:]
    lane = iota(own.shape, 1)
    if taken is not None:
        beside, own = jnp.where(taken, beside, 0.0), jnp.where(taken, own, 0.0)
    out = []
    for c in range(columns):
        near = ((source == c + 1) & (lane >= col)) | ((source == c - 1) & (lane < col))
        out.append(jnp.where(near, beside, 0.0) + jnp.where(source == c, own, 0.0))
    return out


def finish_kernel(
    band, first_band, second_band, mixed_back, tables, probe, first,
    partial, second_info, chi, centre,
):
    columns = band.shape[0]
    extent = probe.shape[-1]
    tile = (band.shape[1] - INFO) // 2
    odd = lax.axis_index("row") % 2
    own_frame, first_frame, second_frame = (
        frame_of(b) for b in (band, first_band, second_band)
    )
    which = iota(second_info.shape, 0)
    second_info[...] = jnp.where(
        which == 0, second_frame[0], jnp.where(which == 1, second_frame[1], second_frame[2])
    )
    both_back = jnp.concatenate([tables[6], -tables[7]], 1)
    for k in range(probe.shape[0]):
        chi[k] = dot(both_back, mixed_back[k].reshape(2 * extent, extent))
    for r in range(0, tile, STRIP):
        s, t = pl.ds(r, STRIP), pl.ds(tile + r, STRIP)
        accumulate(centre, chi, probe, s, t, t)
        before = (iota((STRIP, tile), 0) + r < first_frame[1]).astype(jnp.int32)
        for part in (s, t):
            mine = place(centre[part].astype(F32), columns, own_frame[0], own_frame[2], None)
            other = place(
                first[part].astype(F32), columns, first_frame[0], first_frame[2], before == odd
            )
            for c in range(columns):
                partial[c, part] = mine[c] + other[c]


def fold_kernel(partial, second, second_info, out):
    columns, height, tile = out.shape
    odd = lax.axis_index("row") % 2
    source, row, col = (second_info[r : r + 1] for r in range(3))
    for r in range(0, height, STRIP):
        s = pl.ds(r, STRIP)
        before = (iota((STRIP, tile), 0) + r % tile < row).astype(jnp.int32)
        other = place(second[s].astype(F32), columns, source, col, before == 1 - odd)
        for c in range(columns):
            out[c, s] = (partial[c, s] + other[c]).astype(BF16)


def call(kernel, name, out_shape, in_specs, scratch, flops, moved, *args):
    args = [
        pltpu.with_memory_space_constraint(arg, pltpu.HBM) if spec is HBM else arg
        for arg, spec in zip(args, in_specs)
    ]
    return pl.pallas_call(
        kernel,
        out_shape=out_shape,
        in_specs=in_specs,
        out_specs=jax.tree.map(lambda _: VMEM, out_shape),
        scratch_shapes=scratch,
        compiler_params=pltpu.CompilerParams(vmem_limit_bytes=32 * 2**20),
        cost_estimate=pl.CostEstimate(flops=flops, bytes_accessed=moved, transcendentals=0),
        name=name,
    )(*args)


def per_device(specimen, probe, measured, centers, frame_counts, helper_cols):
    extent = probe.shape[-1]
    half = extent // 2
    tile = specimen.shape[1]
    modes = probe.shape[0]
    columns = lax.axis_size("col")
    height = 2 * tile
    part = jax.ShapeDtypeStruct((height, extent), BF16)
    dma = pltpu.SemaphoreType.DMA

    packed = call(
        pack_kernel, "pack",
        jax.ShapeDtypeStruct((height + INFO, tile), BF16),
        [HBM, HBM, SMEM, HBM],
        [
            pltpu.VMEM(specimen.shape, F32),
            pltpu.SMEM(centers.shape, jnp.int32),
            pltpu.SMEM(helper_cols.shape, jnp.int32),
            dma((3,)),
        ],
        10**5, 2**19,
        specimen, centers, frame_counts, helper_cols,
    )
    band = lax.all_gather(packed, "col", axis_index_groups=[ring(columns)])

    rows = lax.axis_size("row")
    swaps = []
    for start in (0, 1):
        pairs = [(i, i + 1) for i in range(start, rows - 1, 2)]
        swaps.append(pairs + [(b, a) for a, b in pairs])
    second = lax.ppermute(band, "row", swaps[1])
    first = lax.ppermute(band, "row", swaps[0])
    tables = dft_tables(extent)
    prepared = call(
        prepare_kernel, "prepare",
        (
            jax.ShapeDtypeStruct((INFO, extent), BF16),
            jax.ShapeDtypeStruct((extent, extent), F32),
            jax.ShapeDtypeStruct((8, extent, extent), BF16),
            jax.ShapeDtypeStruct(probe.shape, F32),
            jax.ShapeDtypeStruct((modes, 2, tile, extent), F32),
        ),
        [VMEM, HBM, HBM, HBM],
        [
            pltpu.VMEM(measured.shape, F32),
            pltpu.VMEM(tables.shape, BF16),
            pltpu.VMEM(probe.shape, F32),
            pltpu.VMEM((extent // 4, 8, extent), F32),
            dma((3,)),
        ],
        10**9, 2**22,
        band, probe, measured, tables,
    )
    full = (modes, 2, extent, extent)
    to_rows, mixed_back = call(
        frame_kernel, "frame",
        (part, jax.ShapeDtypeStruct(full, BF16)),
        [VMEM] * 7,
        [
            pltpu.VMEM((2, tile, extent), F32),
            pltpu.VMEM((modes, 2, half, extent), BF16),
            pltpu.VMEM((modes, 2, half, extent), F32),
            pltpu.VMEM(full, BF16),
            pltpu.VMEM(full, F32),
            pltpu.VMEM(full, BF16),
            pltpu.VMEM(full, F32),
            pltpu.VMEM((modes, extent, extent), F32),
        ],
        2 * 10**9, 2**22,
        first, second, *prepared,
    )
    from_first = lax.ppermute(to_rows, "row", swaps[0])
    from_second = lax.ppermute(to_rows, "row", swaps[1])
    partial, second_info = call(
        finish_kernel, "finish",
        (
            jax.ShapeDtypeStruct((columns, height, tile), F32),
            jax.ShapeDtypeStruct((8, tile), jnp.int32),
        ),
        [VMEM] * 7,
        [pltpu.VMEM((modes, extent, extent), F32), pltpu.VMEM((height, extent), BF16)],
        5 * 10**8, 2**22,
        band, first, second, mixed_back, prepared[2], prepared[3], from_first,
    )
    summed = call(
        fold_kernel, "fold",
        jax.ShapeDtypeStruct((columns, height, tile), BF16),
        [VMEM] * 3,
        [],
        10**7, 2**20,
        partial, from_second, second_info,
    )
    shares = lax.all_to_all(summed, "col", split_axis=0, concat_axis=0, tiled=True)
    return jnp.sum(shares.astype(F32), axis=0).reshape(2, tile, tile)


def solution(mesh):
    return jax.shard_map(
        per_device,
        mesh=mesh,
        in_specs=(
            P(None, "row", "col"),
            P(),
            P("row", "col", None, None, None),
            P("row", "col", None, None),
            P("row", "col"),
            P("row", "col", None),
        ),
        out_specs=P(None, "row", "col"),
        check_vma=False,
    )
```

```python
import functools
import math

import jax
import jax.numpy as jnp
import numpy as np
from jax import lax
from jax.experimental import pallas as pl
from jax.experimental.pallas import tpu as pltpu
from jax.sharding import PartitionSpec as P

F32 = jnp.float32
BF16 = jnp.bfloat16
INFO = 16
ROW = ("pair", "core")
STRIP = 16
VMEM = pl.BlockSpec(memory_space=pltpu.VMEM)
SMEM = pl.BlockSpec(memory_space=pltpu.SMEM)
HBM = pl.BlockSpec(memory_space=pltpu.HBM)


def dft_tables(extent):
    half = extent // 2
    steps = np.arange(extent, dtype=np.int32)
    angles = (steps[:, None] * steps[None, :] % extent).astype(np.float32)
    angles = angles * np.float32(2.0 * math.pi / extent)
    scaling = np.float32(1.0 / math.sqrt(extent))
    real = (np.cos(angles) * scaling).astype(BF16)
    imag = (-np.sin(angles) * scaling).astype(BF16)
    tables = []
    for parity in (0, 1):
        re, im = real[:half, parity::2], imag[:half, parity::2]
        right = np.concatenate(
            [np.concatenate([re, im], 1), np.concatenate([-im, re], 1)], 0
        )
        tables += [right, np.ascontiguousarray(right.T)]
    return jnp.asarray(np.stack(tables))


def dot(a, b):
    return jnp.dot(a, b, preferred_element_type=F32)


def quarters(tl, tr, bl, br):
    return jnp.concatenate(
        [jnp.concatenate([tl, tr], 1), jnp.concatenate([bl, br], 1)], 0
    )


def iota(shape, dim):
    return lax.broadcasted_iota(jnp.int32, shape, dim)


def fetch(pairs, sems):
    copies = [
        pltpu.make_async_copy(source, target, sems.at[i])
        for i, (source, target) in enumerate(pairs)
    ]
    for copy in copies:
        copy.start()
    return copies


def pack_kernel(specimen, centers, cnt, helpers, out, tile_v, cen, hlp, sems):
    copies = fetch(((specimen, tile_v), (centers, cen), (helpers, hlp)), sems)
    for copy in copies:
        copy.wait()
    tile = tile_v.shape[1]
    lanes = tile_v.shape[2]
    rows, cols = iota((INFO, lanes), 0), iota((INFO, lanes), 1)
    info = jnp.where(rows == 0, -1.0, 0.0)
    for j in range(centers.shape[2]):
        helper = jnp.where(j < cnt[0, 0], hlp[0, 0, j], -1)
        for r, value in enumerate((helper, cen[0, 0, j, 0], cen[0, 0, j, 1])):
            info = jnp.where((rows == r) & (cols == j), value.astype(F32), info)
    info = info.astype(BF16)
    for p in range(2):
        out[p * tile : (p + 1) * tile] = tile_v[p].astype(BF16)
    out[2 * tile :] = info


def gather_columns(get, source, col, columns, shape):
    lane = iota(shape, 1)
    beside = own = jnp.zeros(shape, F32)
    for c in range(columns):
        block = get(c)
        near = ((source == c + 1) & (lane >= col)) | ((source == c - 1) & (lane < col))
        beside = jnp.where(near, block, beside)
        own = jnp.where(source == c, block, own)
    return jnp.concatenate([beside, own], 1)


def first_product(probe, patch, tables):
    half = patch[0].shape[1] // 2
    wr = probe[0] * patch[0] - probe[1] * patch[1]
    wi = probe[0] * patch[1] + probe[1] * patch[0]
    out = []
    for sign, table in zip((1, -1), tables):
        folded = jnp.concatenate(
            [wr[:, :half] + sign * wr[:, half:], wi[:, :half] + sign * wi[:, half:]], 1
        )
        out.append(dot(folded.astype(BF16), table))
    return out


def frame_of(band, base, columns):
    _, height, lanes = band.shape
    me = lax.axis_index("col").astype(F32)
    code = jnp.zeros((1, lanes), F32)
    for c in range(columns):
        info = band[base + c, height - INFO :].astype(F32)
        hit = info[0:1] == me
        code += jnp.where(hit, c * 128.0 * 128.0 + info[1:2] * 128.0 + info[2:3], 0.0)
    code = jnp.sum(code).astype(jnp.int32)
    return code // (128 * 128), code // 128 % 128, code % 128


def halves(bands):
    columns = bands.shape[0] // 2
    odd = lax.axis_index(ROW) % 2
    return odd * columns, (1 - odd) * columns, columns


def prepare_kernel(
    bands, probe, measured, tables,
    info_out, amplitude, tables_out, probe_out, half_out, raw, raw_tables, raw_probe, groups, sems,
):
    copies = fetch(
        ((measured, raw), (tables, raw_tables), (probe, raw_probe)), sems
    )
    mine, _, columns = halves(bands)
    tile = (bands.shape[1] - INFO) // 2
    extent = raw.shape[-1]
    half = extent // 2
    modes = raw_probe.shape[0]
    source, row, col = frame_of(bands, mine, columns)
    which = iota((INFO, extent), 0)
    info = jnp.where(which == 0, source, jnp.where(which == 1, col, row))
    info_out[...] = info.astype(F32).astype(BF16)

    shape = (extent, extent)

    def original(i):
        return jnp.where(i < half, 2 * i, 2 * (i - half) + 1)

    copies[0].wait()
    sort = (iota(shape, 1) == original(iota(shape, 0))).astype(F32).astype(BF16)
    sort_t = (iota(shape, 0) == original(iota(shape, 1))).astype(F32).astype(BF16)
    value = raw[0, 0, 0]
    coarse = value.astype(BF16)
    fine = (value - coarse.astype(F32)).astype(BF16)
    amplitude[...] = sum(
        dot(dot(sort, part).astype(BF16), sort_t) for part in (coarse, fine)
    )

    def roller(old, new, shift, parity):
        wrapped = new % half < shift
        hit = (old + shift - jnp.where(old % half + shift >= half, half, 0)) == new
        sign = jnp.where(wrapped, -1.0, 1.0) if parity else 1.0
        return jnp.where(hit, sign, 0.0).astype(BF16)

    copies[1].wait()
    i, j = iota(shape, 0), iota(shape, 1)
    for parity in range(2):
        right, left = raw_tables[2 * parity], raw_tables[2 * parity + 1]
        for axis, shift in enumerate((col, row)):
            rolled = dot(left, roller(i, j, shift, parity)).astype(BF16)
            rolled_t = dot(roller(j, i, shift, parity), right).astype(BF16)
            tables_out[4 * axis + parity] = rolled_t if axis == 0 else rolled
            tables_out[4 * axis + 2 + parity] = rolled if axis == 0 else rolled_t

    copies[2].wait()
    count = extent // 8
    base = row // 8
    step = row % 8
    lane = iota((extent, half), 1)
    sub = iota((count, 8, extent), 1)
    for k in range(modes):
        for p in range(2):
            lo = pltpu.roll(raw_probe[k, p, :, :half], col, 1)
            hi = pltpu.roll(raw_probe[k, p, :, half:], col, 1)
            turned = jnp.concatenate(
                [jnp.where(lane < col, hi, lo), jnp.where(lane < col, lo, hi)], 1
            )
            turned = pltpu.roll(turned.reshape(count, 8, extent), step, 1)
            turned = jnp.where(
                sub < step, jnp.concatenate([turned[-1:], turned[:-1]], 0), turned
            )
            groups[:count] = turned
            groups[count:] = turned
            probe_out[k, p] = groups[pl.ds(count - base, count)].reshape(extent, extent)

    patch = [
        gather_columns(
            lambda c: bands[mine + c, p * tile : (p + 1) * tile].astype(F32),
            source, col, columns, (tile, tile),
        )
        for p in range(2)
    ]
    for k in range(modes):
        products = first_product(
            [probe_out[k, p, half:] for p in range(2)], patch, (tables_out[0], tables_out[1])
        )
        for parity in range(2):
            half_out[k, parity] = products[parity]


def frame_kernel(
    bands, second, info, amplitude, tables, probe, half_own,
    to_rows, turned, patch, folded, half_far, mixed, far, corrected, product, mixed_back,
):
    _, theirs, columns = halves(bands)
    tile = (bands.shape[1] - INFO) // 2
    extent = probe.shape[-1]
    half = extent // 2
    modes = probe.shape[0]
    odd = lax.axis_index(ROW) % 2
    source, col, row = (
        info[r : r + 1, :tile].astype(F32).astype(jnp.int32) for r in range(3)
    )
    strips = [pl.ds(r, STRIP) for r in range(0, half, STRIP)]
    lower = [pl.ds(half + r, STRIP) for r in range(0, half, STRIP)]

    def split(x):
        return x[:, :half], x[:, half:]

    def join(x, y):
        return jnp.concatenate([x, y], 1).astype(BF16)

    def gather(s):
        rows = iota((STRIP, tile), 0) + s.start
        from_first = (rows >= row).astype(jnp.int32) == odd
        for p in range(2):
            part = pl.ds(p * tile + s.start, STRIP)
            patch[p, s] = gather_columns(
                lambda c: jnp.where(
                    from_first, bands[theirs + c, part].astype(F32), second[c, part].astype(F32)
                ),
                source, col, columns, (STRIP, tile),
            )

    def wave(k):
        for s in strips:
            pr, pi, xr, xi = probe[k, 0, s], probe[k, 1, s], patch[0, s], patch[1, s]
            re = split(pr * xr - pi * xi)
            im = split(pr * xi + pi * xr)
            folded[k, 0, s] = join(re[0] + re[1], im[0] + im[1])
            folded[k, 1, s] = join(re[0] - re[1], im[0] - im[1])

    def along_rows(k):
        for q in range(2):
            half_far[k, q] = dot(folded[k, q], tables[q])

    def mix(k):
        for s, t in zip(strips, lower):
            even, odds = half_far[k, 0, s], half_far[k, 1, s]
            even_own, odds_own = half_own[k, 0, s], half_own[k, 1, s]
            for q, (e, o) in enumerate(
                ((even + even_own, odds + odds_own), (even - even_own, odds - odds_own))
            ):
                (er, ei), (our, oui) = split(e), split(o)
                mixed[k, q, s] = join(er, our)
                mixed[k, q, t] = join(ei, oui)

    def along_columns(k, q):
        far[k, q] = dot(tables[4 + q], mixed[k, q])

    def correct(q, which):
        for s, t in list(zip(strips, lower))[which]:
            re = [far[k, q, s] for k in range(modes)]
            im = [far[k, q, t] for k in range(modes)]
            intensity = sum(x * x for x in re + im)
            size = amplitude[pl.ds(q * half + s.start, STRIP)]
            factor = 1.0 - size * lax.rsqrt(jnp.maximum(intensity, 0.25))
            out = pl.ds(q * half + s.start, STRIP)
            for k in range(modes):
                (re_even, re_odd), (im_even, im_odd) = split(re[k] * factor), split(im[k] * factor)
                corrected[k, 0, out] = join(re_even, im_even)
                corrected[k, 1, out] = join(re_odd, im_odd)

    def back_along_rows(k, q):
        part = pl.ds(q * half, half)
        for c in range(2):
            product[k, c, part] = dot(corrected[k, c, part], tables[2 + c])

    def mix_back(k, q):
        for s, t in zip(strips, lower):
            part = pl.ds(q * half + s.start, STRIP)
            x, y = product[k, 0, part], product[k, 1, part]
            (lr, li), (hr, hi) = split(x + y), split(x - y)
            mixed_back[k, q, s] = join(lr, hr)
            mixed_back[k, q, t] = join(li, hi)

    def back_along_columns(k, q):
        turned[k, q] = dot(tables[6 + q], mixed_back[k, q])

    for s in strips:
        gather(s)
    for k in range(modes + 1):
        if k < modes:
            wave(k)
            along_rows(k)
        if k > 0:
            mix(k - 1)
            along_columns(k - 1, 0)
    share = -(-len(strips) // modes)
    for k in range(modes):
        along_columns(k, 1)
        correct(0, slice(k * share, (k + 1) * share))
    for k in range(modes):
        back_along_rows(k, 0)
        correct(1, slice(k * share, (k + 1) * share))
    for k in range(modes):
        mix_back(k, 0)
        back_along_columns(k, 0)
        back_along_rows(k, 1)
    for k in range(modes):
        mix_back(k, 1)
        back_along_columns(k, 1)
    for s, t in zip(strips, lower):
        accumulate(to_rows, turned, probe, s, t, s, 1)


def accumulate(out, turned, probe, s, t, rows, sign):
    tile = out.shape[0] // 2
    re = im = 0.0
    for k in range(probe.shape[0]):
        pr, pi = probe[k, 0, rows], probe[k, 1, rows]
        cr = turned[k, 0, s] + sign * turned[k, 1, s]
        ci = turned[k, 0, t] + sign * turned[k, 1, t]
        re += pr * cr + pi * ci
        im += pr * ci - pi * cr
    out[s] = re.astype(BF16)
    out[pl.ds(tile + s.start, STRIP)] = im.astype(BF16)


def place(block, columns, source, col, taken):
    tile = block.shape[1] // 2
    beside, own = block[:, :tile], block[:, tile:]
    lane = iota(own.shape, 1)
    if taken is not None:
        beside, own = jnp.where(taken, beside, 0.0), jnp.where(taken, own, 0.0)
    out = []
    for c in range(columns):
        near = ((source == c + 1) & (lane >= col)) | ((source == c - 1) & (lane < col))
        out.append(jnp.where(near, beside, 0.0) + jnp.where(source == c, own, 0.0))
    return out


def finish_kernel(
    bands, second_band, turned, probe, first, partial, second_info, centre,
):
    mine, theirs, columns = halves(bands)
    tile = (bands.shape[1] - INFO) // 2
    odd = lax.axis_index(ROW) % 2
    own_frame, first_frame, second_frame = (
        frame_of(ref, base, columns)
        for ref, base in ((bands, mine), (bands, theirs), (second_band, 0))
    )
    which = iota(second_info.shape, 0)
    second_info[...] = jnp.where(
        which == 0, second_frame[0], jnp.where(which == 1, second_frame[1], second_frame[2])
    )
    for r in range(0, tile, STRIP):
        s, t = pl.ds(r, STRIP), pl.ds(tile + r, STRIP)
        accumulate(centre, turned, probe, s, t, t, -1)
        before = (iota((STRIP, tile), 0) + r < first_frame[1]).astype(jnp.int32)
        for part in (s, t):
            own = place(centre[part].astype(F32), columns, own_frame[0], own_frame[2], None)
            other = place(
                first[part].astype(F32), columns, first_frame[0], first_frame[2], before == odd
            )
            for c in range(columns):
                partial[c, part] = own[c] + other[c]


def fold_kernel(partial, second, second_info, out):
    columns, height, tile = out.shape
    odd = lax.axis_index(ROW) % 2
    source, row, col = (second_info[r : r + 1] for r in range(3))
    for r in range(0, height, STRIP):
        s = pl.ds(r, STRIP)
        before = (iota((STRIP, tile), 0) + r % tile < row).astype(jnp.int32)
        other = place(second[s].astype(F32), columns, source, col, before == 1 - odd)
        for c in range(columns):
            out[c, s] = (partial[c, s] + other[c]).astype(BF16)


def call(kernel, name, out_shape, in_specs, scratch, flops, moved, *args):
    args = [
        pltpu.with_memory_space_constraint(arg, pltpu.HBM) if spec is HBM else arg
        for arg, spec in zip(args, in_specs)
    ]
    return pl.pallas_call(
        kernel,
        out_shape=out_shape,
        in_specs=in_specs,
        out_specs=jax.tree.map(lambda _: VMEM, out_shape),
        scratch_shapes=scratch,
        compiler_params=pltpu.CompilerParams(vmem_limit_bytes=32 * 2**20),
        cost_estimate=pl.CostEstimate(flops=flops, bytes_accessed=moved, transcendentals=0),
        name=name,
    )(*args)


def per_device(specimen, probe, measured, centers, frame_counts, helper_cols):
    extent = probe.shape[-1]
    half = extent // 2
    tile = specimen.shape[1]
    modes = probe.shape[0]
    columns = lax.axis_size("col")
    height = 2 * tile
    part = jax.ShapeDtypeStruct((height, extent), BF16)
    dma = pltpu.SemaphoreType.DMA

    packed = call(
        pack_kernel, "pack",
        jax.ShapeDtypeStruct((height + INFO, tile), BF16),
        [HBM, HBM, SMEM, HBM],
        [
            pltpu.VMEM(specimen.shape, F32),
            pltpu.SMEM(centers.shape, jnp.int32),
            pltpu.SMEM(helper_cols.shape, jnp.int32),
            dma((3,)),
        ],
        10**5, 2**19,
        specimen, centers, frame_counts, helper_cols,
    )
    rows = (lax.axis_size("pair") * lax.axis_size("core"))
    swaps = []
    for start in (0, 1):
        pairs = [(i, i + 1) for i in range(start, rows - 1, 2)]
        swaps.append(pairs + [(b, a) for a, b in pairs])
    bands = lax.all_gather(packed, ("core", "col"))
    band = lax.dynamic_slice_in_dim(bands, lax.axis_index(ROW) % 2 * columns, columns)
    second = lax.ppermute(band, ROW, swaps[1])
    tables = dft_tables(extent)
    prepared = call(
        prepare_kernel, "prepare",
        (
            jax.ShapeDtypeStruct((INFO, extent), BF16),
            jax.ShapeDtypeStruct((extent, extent), F32),
            jax.ShapeDtypeStruct((8, extent, extent), BF16),
            jax.ShapeDtypeStruct(probe.shape, F32),
            jax.ShapeDtypeStruct((modes, 2, tile, extent), F32),
        ),
        [VMEM, HBM, HBM, HBM],
        [
            pltpu.VMEM(measured.shape, F32),
            pltpu.VMEM(tables.shape, BF16),
            pltpu.VMEM(probe.shape, F32),
            pltpu.VMEM((extent // 4, 8, extent), F32),
            dma((3,)),
        ],
        10**9, 2**22,
        bands, probe, measured, tables,
    )
    full = (modes, 2, extent, extent)
    to_rows, turned = call(
        frame_kernel, "frame",
        (part, jax.ShapeDtypeStruct(full, F32)),
        [VMEM] * 7,
        [
            pltpu.VMEM((2, tile, extent), F32),
            pltpu.VMEM((modes, 2, half, extent), BF16),
            pltpu.VMEM((modes, 2, half, extent), F32),
            pltpu.VMEM(full, BF16),
            pltpu.VMEM(full, F32),
            pltpu.VMEM(full, BF16),
            pltpu.VMEM(full, F32),
            pltpu.VMEM(full, BF16),
        ],
        2 * 10**9, 2**22,
        bands, second, *prepared,
    )
    from_first = lax.ppermute(to_rows, ROW, swaps[0])
    from_second = lax.ppermute(to_rows, ROW, swaps[1])
    partial, second_info = call(
        finish_kernel, "finish",
        (
            jax.ShapeDtypeStruct((columns, height, tile), F32),
            jax.ShapeDtypeStruct((8, tile), jnp.int32),
        ),
        [VMEM] * 5,
        [pltpu.VMEM((height, extent), BF16)],
        10**7, 2**22,
        bands, second, turned, prepared[3], from_first,
    )
    summed = call(
        fold_kernel, "fold",
        jax.ShapeDtypeStruct((columns, height, tile), BF16),
        [VMEM] * 3,
        [],
        10**7, 2**20,
        partial, from_second, second_info,
    )
    shares = lax.all_to_all(summed, "col", split_axis=0, concat_axis=0, tiled=True)
    return jnp.sum(shares.astype(F32), axis=0).reshape(2, tile, tile)


def solution(mesh):
    rows, columns = mesh.devices.shape
    split = jax.sharding.Mesh(mesh.devices.reshape(rows // 2, 2, columns), ROW + ("col",))
    return jax.shard_map(
        per_device,
        mesh=split,
        in_specs=(
            P(None, ROW, "col"),
            P(),
            P(ROW, "col", None, None, None),
            P(ROW, "col", None, None),
            P(ROW, "col"),
            P(ROW, "col", None),
        ),
        out_specs=P(None, ROW, "col"),
        check_vma=False,
    )
```

```python
import functools
import itertools
import math

import jax
import jax.numpy as jnp
import numpy as np
from jax import lax
from jax.experimental import pallas as pl
from jax.experimental.pallas import tpu as pltpu
from jax.sharding import PartitionSpec as P

F32 = jnp.float32
BF16 = jnp.bfloat16
INFO = 16
STRIP = 16
VMEM = pl.BlockSpec(memory_space=pltpu.VMEM)
SMEM = pl.BlockSpec(memory_space=pltpu.SMEM)
HBM = pl.BlockSpec(memory_space=pltpu.HBM)


def dft_tables(extent):
    half = extent // 2
    steps = np.arange(extent, dtype=np.int32)
    angles = (steps[:, None] * steps[None, :] % extent).astype(np.float32)
    angles = angles * np.float32(2.0 * math.pi / extent)
    scaling = np.float32(1.0 / math.sqrt(extent))
    real = (np.cos(angles) * scaling).astype(BF16)
    imag = (-np.sin(angles) * scaling).astype(BF16)
    tables = []
    for parity in (0, 1):
        re, im = real[:half, parity::2], imag[:half, parity::2]
        right = np.concatenate(
            [np.concatenate([re, im], 1), np.concatenate([-im, re], 1)], 0
        )
        tables += [right, np.ascontiguousarray(right.T)]
    return jnp.asarray(np.stack(tables))


def dot(a, b):
    return jnp.dot(a, b, preferred_element_type=F32)


def quarters(tl, tr, bl, br):
    return jnp.concatenate(
        [jnp.concatenate([tl, tr], 1), jnp.concatenate([bl, br], 1)], 0
    )


def iota(shape, dim):
    return lax.broadcasted_iota(jnp.int32, shape, dim)


def fetch(pairs, sems):
    copies = [
        pltpu.make_async_copy(source, target, sems.at[i])
        for i, (source, target) in enumerate(pairs)
    ]
    for copy in copies:
        copy.start()
    return copies


def pack_kernel(specimen, centers, cnt, helpers, out, tile_v, cen, hlp, sems):
    copies = fetch(((specimen, tile_v), (centers, cen), (helpers, hlp)), sems)
    for copy in copies:
        copy.wait()
    tile = tile_v.shape[1]
    lanes = tile_v.shape[2]
    rows, cols = iota((INFO, lanes), 0), iota((INFO, lanes), 1)
    info = jnp.where(rows == 0, -1.0, 0.0)
    for j in range(centers.shape[2]):
        helper = jnp.where(j < cnt[0, 0], hlp[0, 0, j], -1)
        for r, value in enumerate((helper, cen[0, 0, j, 0], cen[0, 0, j, 1])):
            info = jnp.where((rows == r) & (cols == j), value.astype(F32), info)
    info = info.astype(BF16)
    for p in range(2):
        out[p * tile : (p + 1) * tile] = tile_v[p].astype(BF16)
    out[2 * tile :] = info


def gather_columns(get, source, col, columns, shape):
    lane = iota(shape, 1)
    beside = own = jnp.zeros(shape, F32)
    for c in range(columns):
        block = get(c)
        near = ((source == c + 1) & (lane >= col)) | ((source == c - 1) & (lane < col))
        beside = jnp.where(near, block, beside)
        own = jnp.where(source == c, block, own)
    return jnp.concatenate([beside, own], 1)


def first_product(probe, patch, tables):
    half = patch[0].shape[1] // 2
    wr = probe[0] * patch[0] - probe[1] * patch[1]
    wi = probe[0] * patch[1] + probe[1] * patch[0]
    out = []
    for sign, table in zip((1, -1), tables):
        folded = jnp.concatenate(
            [wr[:, :half] + sign * wr[:, half:], wi[:, :half] + sign * wi[:, half:]], 1
        )
        out.append(dot(folded.astype(BF16), table))
    return out


def frame_of(band):
    columns, height, lanes = band.shape
    me = lax.axis_index("col").astype(F32)
    code = jnp.zeros((1, lanes), F32)
    for c in range(columns):
        info = band[c, height - INFO :].astype(F32)
        hit = info[0:1] == me
        code += jnp.where(hit, (c * lanes + info[1:2]) * lanes + info[2:3], 0.0)
    code = jnp.sum(code).astype(jnp.int32)
    return code // (lanes * lanes), code // lanes % lanes, code % lanes


def prepare_kernel(
    band, probe, measured, tables,
    info_out, amplitude, tables_out, probe_out, half_out, raw, raw_tables, raw_probe, groups, sems,
):
    copies = fetch(
        ((measured, raw), (tables, raw_tables), (probe, raw_probe)), sems
    )
    columns = band.shape[0]
    tile = (band.shape[1] - INFO) // 2
    extent = raw.shape[-1]
    half = extent // 2
    modes = raw_probe.shape[0]
    source, row, col = frame_of(band)
    which = iota((INFO, extent), 0)
    info = jnp.where(which == 0, source, jnp.where(which == 1, col, row))
    info_out[...] = info.astype(F32).astype(BF16)

    shape = (extent, extent)

    def original(i):
        return jnp.where(i < half, 2 * i, 2 * (i - half) + 1)

    copies[0].wait()
    sort = (iota(shape, 1) == original(iota(shape, 0))).astype(F32).astype(BF16)
    sort_t = (iota(shape, 0) == original(iota(shape, 1))).astype(F32).astype(BF16)
    value = raw[0, 0, 0]
    coarse = value.astype(BF16)
    fine = (value - coarse.astype(F32)).astype(BF16)
    amplitude[...] = sum(
        dot(dot(sort, part).astype(BF16), sort_t) for part in (coarse, fine)
    )

    def roller(old, new, shift, parity):
        wrapped = new % half < shift
        hit = (old + shift - jnp.where(old % half + shift >= half, half, 0)) == new
        sign = jnp.where(wrapped, -1.0, 1.0) if parity else 1.0
        return jnp.where(hit, sign, 0.0).astype(BF16)

    copies[1].wait()
    i, j = iota(shape, 0), iota(shape, 1)
    for parity in range(2):
        right, left = raw_tables[2 * parity], raw_tables[2 * parity + 1]
        for axis, shift in enumerate((col, row)):
            rolled = dot(left, roller(i, j, shift, parity)).astype(BF16)
            rolled_t = dot(roller(j, i, shift, parity), right).astype(BF16)
            tables_out[4 * axis + parity] = rolled_t if axis == 0 else rolled
            tables_out[4 * axis + 2 + parity] = rolled if axis == 0 else rolled_t

    copies[2].wait()
    count = extent // 8
    base = row // 8
    step = row % 8
    lane = iota((extent, half), 1)
    sub = iota((count, 8, extent), 1)
    for k in range(modes):
        for p in range(2):
            lo = pltpu.roll(raw_probe[k, p, :, :half], col, 1)
            hi = pltpu.roll(raw_probe[k, p, :, half:], col, 1)
            turned = jnp.concatenate(
                [jnp.where(lane < col, hi, lo), jnp.where(lane < col, lo, hi)], 1
            )
            turned = pltpu.roll(turned.reshape(count, 8, extent), step, 1)
            turned = jnp.where(
                sub < step, jnp.concatenate([turned[-1:], turned[:-1]], 0), turned
            )
            groups[:count] = turned
            groups[count:] = turned
            probe_out[k, p] = groups[pl.ds(count - base, count)].reshape(extent, extent)

    patch = [
        gather_columns(
            lambda c: band[c, p * tile : (p + 1) * tile].astype(F32),
            source, col, columns, (tile, tile),
        )
        for p in range(2)
    ]
    for k in range(modes):
        products = first_product(
            [probe_out[k, p, half:] for p in range(2)], patch, (tables_out[0], tables_out[1])
        )
        for parity in range(2):
            half_out[k, parity] = products[parity]


def frame_kernel(
    first, second, info, amplitude, tables, probe, half_own,
    to_rows, mixed_back, patch, folded, half_far, mixed, far, corrected, product, chi,
):
    columns = first.shape[0]
    tile = (first.shape[1] - INFO) // 2
    extent = probe.shape[-1]
    half = extent // 2
    modes = probe.shape[0]
    odd = lax.axis_index("row") % 2
    source, col, row = (
        info[r : r + 1, :tile].astype(F32).astype(jnp.int32) for r in range(3)
    )
    strips = [pl.ds(r, STRIP) for r in range(0, half, STRIP)]
    lower = [pl.ds(half + r, STRIP) for r in range(0, half, STRIP)]

    def split(x):
        return x[:, :half], x[:, half:]

    def join(x, y):
        return jnp.concatenate([x, y], 1).astype(BF16)

    def gather(s):
        rows = iota((STRIP, tile), 0) + s.start
        from_first = (rows >= row).astype(jnp.int32) == odd
        for p in range(2):
            part = pl.ds(p * tile + s.start, STRIP)
            patch[p, s] = gather_columns(
                lambda c: jnp.where(
                    from_first, first[c, part].astype(F32), second[c, part].astype(F32)
                ),
                source, col, columns, (STRIP, tile),
            )

    def wave(k, s):
        pr, pi, xr, xi = probe[k, 0, s], probe[k, 1, s], patch[0, s], patch[1, s]
        re = split(pr * xr - pi * xi)
        im = split(pr * xi + pi * xr)
        folded[k, 0, s] = join(re[0] + re[1], im[0] + im[1])
        folded[k, 1, s] = join(re[0] - re[1], im[0] - im[1])

    def along_rows(k, q):
        half_far[k, q] = dot(folded[k, q], tables[q])

    def mix(k, s, t):
        even, odds = half_far[k, 0, s], half_far[k, 1, s]
        even_own, odds_own = half_own[k, 0, s], half_own[k, 1, s]
        for q, (e, o) in enumerate(
            ((even + even_own, odds + odds_own), (even - even_own, odds - odds_own))
        ):
            (er, ei), (our, oui) = split(e), split(o)
            mixed[k, q, s] = join(er, our)
            mixed[k, q, t] = join(ei, oui)

    def along_columns(k, q, part):
        far[k, q, part] = dot(tables[4 + q, part], mixed[k, q])

    def correct(q, s, t):
        re = [far[k, q, s] for k in range(modes)]
        im = [far[k, q, t] for k in range(modes)]
        intensity = sum(x * x for x in re + im)
        out = pl.ds(q * half + s.start, STRIP)
        factor = 1.0 - amplitude[out] * lax.rsqrt(jnp.maximum(intensity, 0.25))
        for k in range(modes):
            (re_even, re_odd), (im_even, im_odd) = split(re[k] * factor), split(im[k] * factor)
            corrected[k, 0, out] = join(re_even, im_even)
            corrected[k, 1, out] = join(re_odd, im_odd)

    def back_along_rows(k, q, c):
        part = pl.ds(q * half, half)
        product[k, c, part] = dot(corrected[k, c, part], tables[2 + c])

    def mix_back(k, q, s, t):
        part = pl.ds(q * half + s.start, STRIP)
        x, y = product[k, 0, part], product[k, 1, part]
        (lr, li), (hr, hi) = split(x + y), split(x - y)
        mixed_back[k, q, s] = join(lr, hr)
        mixed_back[k, q, t] = join(li, hi)

    both_back = jnp.concatenate([tables[6], tables[7]], 1)

    def back_along_columns(k, part):
        rows = both_back[part.start : part.start + half]
        chi[k, part] = dot(rows, mixed_back[k].reshape(2 * extent, extent))

    parts = [pl.ds(0, half), pl.ds(half, half)]
    pairs = list(zip(strips, lower))
    every = range(modes)

    def steps(function, *lists):
        return [functools.partial(function, *args) for args in itertools.product(*lists)]

    def on_strips(function, *lists):
        return [
            functools.partial(function, *args, s, t)
            for args in itertools.product(*lists) for s, t in pairs
        ]

    def run(products, strip_work):
        count = len(products)
        share = -(-len(strip_work) // max(count, 1))
        for i in range(max(count, 1)):
            if i < count:
                products[i]()
            for work in strip_work[i * share : (i + 1) * share]:
                work()

    for s in strips:
        gather(s)
    run([], steps(wave, [0], strips))
    for k in range(modes + 1):
        run(
            (steps(along_rows, [k], range(2)) if k < modes else [])
            + (steps(along_columns, [k - 2], [0], parts) if k > 1 else []),
            (on_strips(mix, [k - 1]) if k > 0 else [])
            + (steps(wave, [k + 1], strips) if k + 1 < modes else []),
        )
    run(steps(along_columns, [modes - 1], [0], parts), [])
    run(steps(along_columns, every, [1], parts), on_strips(correct, [0]))
    run(steps(back_along_rows, every, [0], range(2)), on_strips(correct, [1]))
    run(steps(back_along_rows, every, [1], range(2)), on_strips(mix_back, every, [0]))
    for k in range(modes + 1):
        run(
            steps(back_along_columns, [k - 1], parts) if k > 0 else [],
            on_strips(mix_back, [k], [1]) if k < modes else [],
        )
    for s, t in pairs:
        accumulate(to_rows, chi, probe, s, t, s)


def accumulate(out, chi, probe, s, t, rows):
    tile = out.shape[0] // 2
    re = im = 0.0
    for k in range(probe.shape[0]):
        pr, pi = probe[k, 0, rows], probe[k, 1, rows]
        cr, ci = chi[k, s], chi[k, t]
        re += pr * cr + pi * ci
        im += pr * ci - pi * cr
    out[s] = re.astype(BF16)
    out[pl.ds(tile + s.start, STRIP)] = im.astype(BF16)


def place(block, columns, source, col, taken):
    tile = block.shape[1] // 2
    beside, own = block[:, :tile], block[:, tile:]
    lane = iota(own.shape, 1)
    if taken is not None:
        beside, own = jnp.where(taken, beside, 0.0), jnp.where(taken, own, 0.0)
    out = []
    for c in range(columns):
        near = ((source == c + 1) & (lane >= col)) | ((source == c - 1) & (lane < col))
        out.append(jnp.where(near, beside, 0.0) + jnp.where(source == c, own, 0.0))
    return out


def finish_kernel(
    band, first_band, second_band, mixed_back, tables, probe, first,
    partial, second_info, chi, centre,
):
    columns = band.shape[0]
    extent = probe.shape[-1]
    tile = (band.shape[1] - INFO) // 2
    odd = lax.axis_index("row") % 2
    own_frame, first_frame, second_frame = (
        frame_of(b) for b in (band, first_band, second_band)
    )
    which = iota(second_info.shape, 0)
    second_info[...] = jnp.where(
        which == 0, second_frame[0], jnp.where(which == 1, second_frame[1], second_frame[2])
    )
    both_back = jnp.concatenate([tables[6], -tables[7]], 1)
    for k in range(probe.shape[0]):
        chi[k] = dot(both_back, mixed_back[k].reshape(2 * extent, extent))
    for r in range(0, tile, STRIP):
        s, t = pl.ds(r, STRIP), pl.ds(tile + r, STRIP)
        accumulate(centre, chi, probe, s, t, t)
        before = (iota((STRIP, tile), 0) + r < first_frame[1]).astype(jnp.int32)
        for part in (s, t):
            mine = place(centre[part].astype(F32), columns, own_frame[0], own_frame[2], None)
            other = place(
                first[part].astype(F32), columns, first_frame[0], first_frame[2], before == odd
            )
            for c in range(columns):
                partial[c, part] = mine[c] + other[c]


def fold_kernel(partial, second, second_info, out):
    columns, height, tile = out.shape
    odd = lax.axis_index("row") % 2
    source, row, col = (second_info[r : r + 1] for r in range(3))
    for r in range(0, height, STRIP):
        s = pl.ds(r, STRIP)
        before = (iota((STRIP, tile), 0) + r % tile < row).astype(jnp.int32)
        other = place(second[s].astype(F32), columns, source, col, before == 1 - odd)
        for c in range(columns):
            out[c, s] = (partial[c, s] + other[c]).astype(BF16)


def call(kernel, name, out_shape, in_specs, scratch, flops, moved, *args):
    args = [
        pltpu.with_memory_space_constraint(arg, pltpu.HBM) if spec is HBM else arg
        for arg, spec in zip(args, in_specs)
    ]
    return pl.pallas_call(
        kernel,
        out_shape=out_shape,
        in_specs=in_specs,
        out_specs=jax.tree.map(lambda _: VMEM, out_shape),
        scratch_shapes=scratch,
        compiler_params=pltpu.CompilerParams(vmem_limit_bytes=32 * 2**20),
        cost_estimate=pl.CostEstimate(flops=flops, bytes_accessed=moved, transcendentals=0),
        name=name,
    )(*args)


def per_device(specimen, probe, measured, centers, frame_counts, helper_cols):
    extent = probe.shape[-1]
    half = extent // 2
    tile = specimen.shape[1]
    modes = probe.shape[0]
    columns = lax.axis_size("col")
    height = 2 * tile
    part = jax.ShapeDtypeStruct((height, extent), BF16)
    dma = pltpu.SemaphoreType.DMA

    packed = call(
        pack_kernel, "pack",
        jax.ShapeDtypeStruct((height + INFO, tile), BF16),
        [HBM, HBM, SMEM, HBM],
        [
            pltpu.VMEM(specimen.shape, F32),
            pltpu.SMEM(centers.shape, jnp.int32),
            pltpu.SMEM(helper_cols.shape, jnp.int32),
            dma((3,)),
        ],
        10**5, 2**19,
        specimen, centers, frame_counts, helper_cols,
    )
    band = lax.all_gather(packed, "col")

    rows = lax.axis_size("row")
    swaps = []
    for start in (0, 1):
        pairs = [(i, i + 1) for i in range(start, rows - 1, 2)]
        swaps.append(pairs + [(b, a) for a, b in pairs])
    second = lax.ppermute(band, "row", swaps[1])
    first = lax.ppermute(band, "row", swaps[0])
    tables = dft_tables(extent)
    prepared = call(
        prepare_kernel, "prepare",
        (
            jax.ShapeDtypeStruct((INFO, extent), BF16),
            jax.ShapeDtypeStruct((extent, extent), F32),
            jax.ShapeDtypeStruct((8, extent, extent), BF16),
            jax.ShapeDtypeStruct(probe.shape, F32),
            jax.ShapeDtypeStruct((modes, 2, tile, extent), F32),
        ),
        [VMEM, HBM, HBM, HBM],
        [
            pltpu.VMEM(measured.shape, F32),
            pltpu.VMEM(tables.shape, BF16),
            pltpu.VMEM(probe.shape, F32),
            pltpu.VMEM((extent // 4, 8, extent), F32),
            dma((3,)),
        ],
        10**9, 2**22,
        band, probe, measured, tables,
    )
    full = (modes, 2, extent, extent)
    to_rows, mixed_back = call(
        frame_kernel, "frame",
        (part, jax.ShapeDtypeStruct(full, BF16)),
        [VMEM] * 7,
        [
            pltpu.VMEM((2, tile, extent), F32),
            pltpu.VMEM((modes, 2, half, extent), BF16),
            pltpu.VMEM((modes, 2, half, extent), F32),
            pltpu.VMEM(full, BF16),
            pltpu.VMEM(full, F32),
            pltpu.VMEM(full, BF16),
            pltpu.VMEM(full, F32),
            pltpu.VMEM((modes, extent, extent), F32),
        ],
        2 * 10**9, 2**22,
        first, second, *prepared,
    )
    from_first = lax.ppermute(to_rows, "row", swaps[0])
    from_second = lax.ppermute(to_rows, "row", swaps[1])
    partial, second_info = call(
        finish_kernel, "finish",
        (
            jax.ShapeDtypeStruct((columns, height, tile), F32),
            jax.ShapeDtypeStruct((8, tile), jnp.int32),
        ),
        [VMEM] * 7,
        [pltpu.VMEM((modes, extent, extent), F32), pltpu.VMEM((height, extent), BF16)],
        5 * 10**8, 2**22,
        band, first, second, mixed_back, prepared[2], prepared[3], from_first,
    )
    summed = call(
        fold_kernel, "fold",
        jax.ShapeDtypeStruct((columns, height, tile), BF16),
        [VMEM] * 3,
        [],
        10**7, 2**20,
        partial, from_second, second_info,
    )
    shares = lax.all_to_all(summed, "col", split_axis=0, concat_axis=0, tiled=True)
    return jnp.sum(shares.astype(F32), axis=0).reshape(2, tile, tile)


def solution(mesh):
    return jax.shard_map(
        per_device,
        mesh=mesh,
        in_specs=(
            P(None, "row", "col"),
            P(),
            P("row", "col", None, None, None),
            P("row", "col", None, None),
            P("row", "col"),
            P("row", "col", None),
        ),
        out_specs=P(None, "row", "col"),
        check_vma=False,
    )
```

```python
import functools
import math

import jax
import jax.numpy as jnp
import numpy as np
from jax import lax
from jax.experimental import pallas as pl
from jax.experimental.pallas import tpu as pltpu
from jax.sharding import PartitionSpec as P

F32 = jnp.float32
BF16 = jnp.bfloat16
INFO = 16
STRIP = 16
VMEM = pl.BlockSpec(memory_space=pltpu.VMEM)
SMEM = pl.BlockSpec(memory_space=pltpu.SMEM)
HBM = pl.BlockSpec(memory_space=pltpu.HBM)


def dft_tables(extent):
    half = extent // 2
    steps = np.arange(extent, dtype=np.int32)
    angles = (steps[:, None] * steps[None, :] % extent).astype(np.float32)
    angles = angles * np.float32(2.0 * math.pi / extent)
    scaling = np.float32(1.0 / math.sqrt(extent))
    real = (np.cos(angles) * scaling).astype(BF16)
    imag = (-np.sin(angles) * scaling).astype(BF16)
    tables = []
    for parity in (0, 1):
        re, im = real[:half, parity::2], imag[:half, parity::2]
        right = np.concatenate(
            [np.concatenate([re, im], 1), np.concatenate([-im, re], 1)], 0
        )
        tables += [right, np.ascontiguousarray(right.T)]
    return jnp.asarray(np.stack(tables))


def dot(a, b):
    return jnp.dot(a, b, preferred_element_type=F32)


def quarters(tl, tr, bl, br):
    return jnp.concatenate(
        [jnp.concatenate([tl, tr], 1), jnp.concatenate([bl, br], 1)], 0
    )


def iota(shape, dim):
    return lax.broadcasted_iota(jnp.int32, shape, dim)


def fetch(pairs, sems):
    copies = [
        pltpu.make_async_copy(source, target, sems.at[i])
        for i, (source, target) in enumerate(pairs)
    ]
    for copy in copies:
        copy.start()
    return copies


def pack_kernel(specimen, centers, cnt, helpers, out, tile_v, cen, hlp, sems):
    copies = fetch(((specimen, tile_v), (centers, cen), (helpers, hlp)), sems)
    for copy in copies:
        copy.wait()
    tile = tile_v.shape[1]
    lanes = tile_v.shape[2]
    rows, cols = iota((INFO, lanes), 0), iota((INFO, lanes), 1)
    info = jnp.where(rows == 0, -1.0, 0.0)
    for j in range(centers.shape[2]):
        helper = jnp.where(j < cnt[0, 0], hlp[0, 0, j], -1)
        for r, value in enumerate((helper, cen[0, 0, j, 0], cen[0, 0, j, 1])):
            info = jnp.where((rows == r) & (cols == j), value.astype(F32), info)
    info = info.astype(BF16)
    for p in range(2):
        out[p * tile : (p + 1) * tile] = tile_v[p].astype(BF16)
    out[2 * tile :] = info


def gather_columns(get, source, col, columns, shape):
    lane = iota(shape, 1)
    beside = own = jnp.zeros(shape, F32)
    for c in range(columns):
        block = get(c)
        near = ((source == c + 1) & (lane >= col)) | ((source == c - 1) & (lane < col))
        beside = jnp.where(near, block, beside)
        own = jnp.where(source == c, block, own)
    return jnp.concatenate([beside, own], 1)


def first_product(probe, patch, tables):
    half = patch[0].shape[1] // 2
    wr = probe[0] * patch[0] - probe[1] * patch[1]
    wi = probe[0] * patch[1] + probe[1] * patch[0]
    out = []
    for sign, table in zip((1, -1), tables):
        folded = jnp.concatenate(
            [wr[:, :half] + sign * wr[:, half:], wi[:, :half] + sign * wi[:, half:]], 1
        )
        out.append(dot(folded.astype(BF16), table))
    return out


def frame_of(band):
    columns, height, lanes = band.shape
    me = lax.axis_index("col").astype(F32)
    code = jnp.zeros((1, lanes), F32)
    for c in range(columns):
        info = band[c, height - INFO :].astype(F32)
        hit = info[0:1] == me
        code += jnp.where(hit, (c * lanes + info[1:2]) * lanes + info[2:3], 0.0)
    code = jnp.sum(code).astype(jnp.int32)
    return code // (lanes * lanes), code // lanes % lanes, code % lanes


def prepare_kernel(
    band, probe, measured, tables,
    info_out, amplitude, tables_out, probe_out, half_out, raw, raw_tables, raw_probe, groups, sems,
):
    copies = fetch(
        ((measured, raw), (tables, raw_tables), (probe, raw_probe)), sems
    )
    columns = band.shape[0]
    tile = (band.shape[1] - INFO) // 2
    extent = raw.shape[-1]
    half = extent // 2
    modes = raw_probe.shape[0]
    source, row, col = frame_of(band)
    which = iota((INFO, extent), 0)
    info = jnp.where(which == 0, source, jnp.where(which == 1, col, row))
    info_out[...] = info.astype(F32).astype(BF16)

    shape = (extent, extent)

    def original(i):
        return jnp.where(i < half, 2 * i, 2 * (i - half) + 1)

    copies[0].wait()
    sort = (iota(shape, 1) == original(iota(shape, 0))).astype(F32).astype(BF16)
    sort_t = (iota(shape, 0) == original(iota(shape, 1))).astype(F32).astype(BF16)
    value = raw[0, 0, 0]
    coarse = value.astype(BF16)
    fine = (value - coarse.astype(F32)).astype(BF16)
    amplitude[...] = sum(
        dot(dot(sort, part).astype(BF16), sort_t) for part in (coarse, fine)
    )

    def roller(old, new, shift, parity):
        wrapped = new % half < shift
        hit = (old + shift - jnp.where(old % half + shift >= half, half, 0)) == new
        sign = jnp.where(wrapped, -1.0, 1.0) if parity else 1.0
        return jnp.where(hit, sign, 0.0).astype(BF16)

    copies[1].wait()
    i, j = iota(shape, 0), iota(shape, 1)
    for parity in range(2):
        right, left = raw_tables[2 * parity], raw_tables[2 * parity + 1]
        for axis, shift in enumerate((col, row)):
            rolled = dot(left, roller(i, j, shift, parity)).astype(BF16)
            rolled_t = dot(roller(j, i, shift, parity), right).astype(BF16)
            tables_out[4 * axis + parity] = rolled_t if axis == 0 else rolled
            tables_out[4 * axis + 2 + parity] = rolled if axis == 0 else rolled_t

    copies[2].wait()
    count = extent // 8
    base = row // 8
    step = row % 8
    lane = iota((extent, half), 1)
    sub = iota((count, 8, extent), 1)
    for k in range(modes):
        for p in range(2):
            lo = pltpu.roll(raw_probe[k, p, :, :half], col, 1)
            hi = pltpu.roll(raw_probe[k, p, :, half:], col, 1)
            turned = jnp.concatenate(
                [jnp.where(lane < col, hi, lo), jnp.where(lane < col, lo, hi)], 1
            )
            turned = pltpu.roll(turned.reshape(count, 8, extent), step, 1)
            turned = jnp.where(
                sub < step, jnp.concatenate([turned[-1:], turned[:-1]], 0), turned
            )
            groups[:count] = turned
            groups[count:] = turned
            probe_out[k, p] = groups[pl.ds(count - base, count)].reshape(extent, extent)

    patch = [
        gather_columns(
            lambda c: band[c, p * tile : (p + 1) * tile].astype(F32),
            source, col, columns, (tile, tile),
        )
        for p in range(2)
    ]
    for k in range(modes):
        products = first_product(
            [probe_out[k, p, half:] for p in range(2)], patch, (tables_out[0], tables_out[1])
        )
        for parity in range(2):
            half_out[k, parity] = products[parity]


def frame_kernel(
    first, second, info, amplitude, tables, probe, half_own,
    to_rows, mixed_back, patch, folded, half_far, mixed, far, corrected, product, chi,
):
    columns = first.shape[0]
    tile = (first.shape[1] - INFO) // 2
    extent = probe.shape[-1]
    half = extent // 2
    modes = probe.shape[0]
    odd = lax.axis_index("row") % 2
    me = lax.axis_index("row")
    outer = ((me > 0) & (me < lax.axis_size("row") - 1)).astype(jnp.int32)
    source, col, row = (
        info[r : r + 1, :tile].astype(F32).astype(jnp.int32) for r in range(3)
    )
    strips = [pl.ds(r, STRIP) for r in range(0, half, STRIP)]
    lower = [pl.ds(half + r, STRIP) for r in range(0, half, STRIP)]

    def split(x):
        return x[:, :half], x[:, half:]

    def join(x, y):
        return jnp.concatenate([x, y], 1).astype(BF16)

    def gather(s):
        rows = iota((STRIP, tile), 0) + s.start
        from_above = (rows >= row).astype(jnp.int32)
        from_first = from_above == odd
        from_second = from_above + 2 * (1 - outer) == 1 - odd
        for p in range(2):
            part = pl.ds(p * tile + s.start, STRIP)
            patch[p, s] = gather_columns(
                lambda c: jnp.where(
                    from_first,
                    first[c, part].astype(F32),
                    jnp.where(from_second, second[odd, c, part].astype(F32), 0.0),
                ),
                source, col, columns, (STRIP, tile),
            )

    def wave(k):
        for s in strips:
            pr, pi, xr, xi = probe[k, 0, s], probe[k, 1, s], patch[0, s], patch[1, s]
            re = split(pr * xr - pi * xi)
            im = split(pr * xi + pi * xr)
            folded[k, 0, s] = join(re[0] + re[1], im[0] + im[1])
            folded[k, 1, s] = join(re[0] - re[1], im[0] - im[1])

    def along_rows(k):
        for q in range(2):
            half_far[k, q] = dot(folded[k, q], tables[q])

    def mix(k):
        for s, t in zip(strips, lower):
            even, odds = half_far[k, 0, s], half_far[k, 1, s]
            even_own, odds_own = half_own[k, 0, s], half_own[k, 1, s]
            for q, (e, o) in enumerate(
                ((even + even_own, odds + odds_own), (even - even_own, odds - odds_own))
            ):
                (er, ei), (our, oui) = split(e), split(o)
                mixed[k, q, s] = join(er, our)
                mixed[k, q, t] = join(ei, oui)

    def along_columns(k, q):
        far[k, q] = dot(tables[4 + q], mixed[k, q])

    def correct(q, which):
        for s, t in list(zip(strips, lower))[which]:
            re = [far[k, q, s] for k in range(modes)]
            im = [far[k, q, t] for k in range(modes)]
            intensity = sum(x * x for x in re + im)
            size = amplitude[pl.ds(q * half + s.start, STRIP)]
            factor = 1.0 - size * lax.rsqrt(jnp.maximum(intensity, 0.25))
            out = pl.ds(q * half + s.start, STRIP)
            for k in range(modes):
                (re_even, re_odd), (im_even, im_odd) = split(re[k] * factor), split(im[k] * factor)
                corrected[k, 0, out] = join(re_even, im_even)
                corrected[k, 1, out] = join(re_odd, im_odd)

    def back_along_rows(k, q):
        part = pl.ds(q * half, half)
        for c in range(2):
            product[k, c, part] = dot(corrected[k, c, part], tables[2 + c])

    def mix_back(k, q):
        for s, t in zip(strips, lower):
            part = pl.ds(q * half + s.start, STRIP)
            x, y = product[k, 0, part], product[k, 1, part]
            (lr, li), (hr, hi) = split(x + y), split(x - y)
            mixed_back[k, q, s] = join(lr, hr)
            mixed_back[k, q, t] = join(li, hi)

    both_back = jnp.concatenate([tables[6], tables[7]], 1)

    def back_along_columns(k):
        chi[k] = dot(both_back, mixed_back[k].reshape(2 * extent, extent))

    for s in strips:
        gather(s)
    for k in range(modes + 1):
        if k < modes:
            wave(k)
            along_rows(k)
        if k > 0:
            mix(k - 1)
            along_columns(k - 1, 0)
    share = -(-len(strips) // modes)
    for k in range(modes):
        along_columns(k, 1)
        correct(0, slice(k * share, (k + 1) * share))
    for k in range(modes):
        back_along_rows(k, 0)
        correct(1, slice(k * share, (k + 1) * share))
    for k in range(modes):
        mix_back(k, 0)
        back_along_rows(k, 1)
    for k in range(modes):
        mix_back(k, 1)
        back_along_columns(k)
    for s, t in zip(strips, lower):
        accumulate(to_rows, chi, probe, s, t, s)


def accumulate(out, chi, probe, s, t, rows):
    tile = out.shape[0] // 2
    re = im = 0.0
    for k in range(probe.shape[0]):
        pr, pi = probe[k, 0, rows], probe[k, 1, rows]
        cr, ci = chi[k, s], chi[k, t]
        re += pr * cr + pi * ci
        im += pr * ci - pi * cr
    out[s] = re.astype(BF16)
    out[pl.ds(tile + s.start, STRIP)] = im.astype(BF16)


def place(block, columns, source, col, taken):
    tile = block.shape[1] // 2
    beside, own = block[:, :tile], block[:, tile:]
    lane = iota(own.shape, 1)
    if taken is not None:
        beside, own = jnp.where(taken, beside, 0.0), jnp.where(taken, own, 0.0)
    out = []
    for c in range(columns):
        near = ((source == c + 1) & (lane >= col)) | ((source == c - 1) & (lane < col))
        out.append(jnp.where(near, beside, 0.0) + jnp.where(source == c, own, 0.0))
    return out


def finish_kernel(
    band, first_band, second_band, mixed_back, tables, probe, first,
    partial, second_info, chi, centre,
):
    columns = band.shape[0]
    extent = probe.shape[-1]
    tile = (band.shape[1] - INFO) // 2
    odd = lax.axis_index("row") % 2
    own_frame, first_frame, second_frame = (
        frame_of(b) for b in (band, first_band, second_band.at[odd])
    )
    which = iota(second_info.shape, 0)
    second_info[...] = jnp.where(
        which == 0, second_frame[0], jnp.where(which == 1, second_frame[1], second_frame[2])
    )
    both_back = jnp.concatenate([tables[6], -tables[7]], 1)
    for k in range(probe.shape[0]):
        chi[k] = dot(both_back, mixed_back[k].reshape(2 * extent, extent))
    for r in range(0, tile, STRIP):
        s, t = pl.ds(r, STRIP), pl.ds(tile + r, STRIP)
        accumulate(centre, chi, probe, s, t, t)
        before = (iota((STRIP, tile), 0) + r < first_frame[1]).astype(jnp.int32)
        for part in (s, t):
            mine = place(centre[part].astype(F32), columns, own_frame[0], own_frame[2], None)
            other = place(
                first[part].astype(F32), columns, first_frame[0], first_frame[2], before == odd
            )
            for c in range(columns):
                partial[c, part] = mine[c] + other[c]


def fold_kernel(partial, second, second_info, out):
    columns, height, tile = out.shape
    odd = lax.axis_index("row") % 2
    source, row, col = (second_info[r : r + 1] for r in range(3))
    for r in range(0, height, STRIP):
        s = pl.ds(r, STRIP)
        before = (iota((STRIP, tile), 0) + r % tile < row).astype(jnp.int32)
        other = place(second[s].astype(F32), columns, source, col, before == 1 - odd)
        for c in range(columns):
            out[c, s] = (partial[c, s] + other[c]).astype(BF16)


def call(kernel, name, out_shape, in_specs, scratch, flops, moved, *args):
    args = [
        pltpu.with_memory_space_constraint(arg, pltpu.HBM) if spec is HBM else arg
        for arg, spec in zip(args, in_specs)
    ]
    return pl.pallas_call(
        kernel,
        out_shape=out_shape,
        in_specs=in_specs,
        out_specs=jax.tree.map(lambda _: VMEM, out_shape),
        scratch_shapes=scratch,
        compiler_params=pltpu.CompilerParams(vmem_limit_bytes=32 * 2**20),
        cost_estimate=pl.CostEstimate(flops=flops, bytes_accessed=moved, transcendentals=0),
        name=name,
    )(*args)


def per_device(specimen, probe, measured, centers, frame_counts, helper_cols):
    extent = probe.shape[-1]
    half = extent // 2
    tile = specimen.shape[1]
    modes = probe.shape[0]
    columns = lax.axis_size("col")
    height = 2 * tile
    part = jax.ShapeDtypeStruct((height, extent), BF16)
    dma = pltpu.SemaphoreType.DMA

    packed = call(
        pack_kernel, "pack",
        jax.ShapeDtypeStruct((height + INFO, tile), BF16),
        [HBM, HBM, SMEM, HBM],
        [
            pltpu.VMEM(specimen.shape, F32),
            pltpu.SMEM(centers.shape, jnp.int32),
            pltpu.SMEM(helper_cols.shape, jnp.int32),
            dma((3,)),
        ],
        10**5, 2**19,
        specimen, centers, frame_counts, helper_cols,
    )
    band = lax.all_gather(packed, "col")

    rows = lax.axis_size("row")
    swaps = []
    for start in (0, 1):
        pairs = [(i, i + 1) for i in range(start, rows - 1, 2)]
        swaps.append(pairs + [(b, a) for a, b in pairs])
    ends = [r * columns + c for r in (0, rows - 1) for c in range(columns)]
    pairs = [ends[i : i + 2] for i in range(0, 2 * columns, 2)]
    pairs += [
        [r * columns + c, (r + 1) * columns + c]
        for r in range(1, rows - 1, 2) for c in range(columns)
    ]
    second = lax.all_to_all(
        jnp.broadcast_to(band, (2,) + band.shape), ("row", "col"),
        split_axis=0, concat_axis=0, axis_index_groups=pairs, tiled=True,
    )
    first = lax.ppermute(band, "row", swaps[0])
    tables = dft_tables(extent)
    prepared = call(
        prepare_kernel, "prepare",
        (
            jax.ShapeDtypeStruct((INFO, extent), BF16),
            jax.ShapeDtypeStruct((extent, extent), F32),
            jax.ShapeDtypeStruct((8, extent, extent), BF16),
            jax.ShapeDtypeStruct(probe.shape, F32),
            jax.ShapeDtypeStruct((modes, 2, tile, extent), F32),
        ),
        [VMEM, HBM, HBM, HBM],
        [
            pltpu.VMEM(measured.shape, F32),
            pltpu.VMEM(tables.shape, BF16),
            pltpu.VMEM(probe.shape, F32),
            pltpu.VMEM((extent // 4, 8, extent), F32),
            dma((3,)),
        ],
        10**9, 2**22,
        band, probe, measured, tables,
    )
    full = (modes, 2, extent, extent)
    to_rows, mixed_back = call(
        frame_kernel, "frame",
        (part, jax.ShapeDtypeStruct(full, BF16)),
        [VMEM] * 7,
        [
            pltpu.VMEM((2, tile, extent), F32),
            pltpu.VMEM((modes, 2, half, extent), BF16),
            pltpu.VMEM((modes, 2, half, extent), F32),
            pltpu.VMEM(full, BF16),
            pltpu.VMEM(full, F32),
            pltpu.VMEM(full, BF16),
            pltpu.VMEM(full, F32),
            pltpu.VMEM((modes, extent, extent), F32),
        ],
        2 * 10**9, 2**22,
        first, second, *prepared,
    )
    from_first = lax.ppermute(to_rows, "row", swaps[0])
    from_second = lax.ppermute(to_rows, "row", swaps[1])
    partial, second_info = call(
        finish_kernel, "finish",
        (
            jax.ShapeDtypeStruct((columns, height, tile), F32),
            jax.ShapeDtypeStruct((8, tile), jnp.int32),
        ),
        [VMEM] * 7,
        [pltpu.VMEM((modes, extent, extent), F32), pltpu.VMEM((height, extent), BF16)],
        5 * 10**8, 2**22,
        band, first, second, mixed_back, prepared[2], prepared[3], from_first,
    )
    summed = call(
        fold_kernel, "fold",
        jax.ShapeDtypeStruct((columns, height, tile), BF16),
        [VMEM] * 3,
        [],
        10**7, 2**20,
        partial, from_second, second_info,
    )
    shares = lax.all_to_all(summed, "col", split_axis=0, concat_axis=0, tiled=True)
    return jnp.sum(shares.astype(F32), axis=0).reshape(2, tile, tile)


def solution(mesh):
    return jax.shard_map(
        per_device,
        mesh=mesh,
        in_specs=(
            P(None, "row", "col"),
            P(),
            P("row", "col", None, None, None),
            P("row", "col", None, None),
            P("row", "col"),
            P("row", "col", None),
        ),
        out_specs=P(None, "row", "col"),
        check_vma=False,
    )
```

```python
import functools
import math

import jax
import jax.numpy as jnp
import numpy as np
from jax import lax
from jax.experimental import pallas as pl
from jax.experimental.pallas import tpu as pltpu
from jax.sharding import PartitionSpec as P

F32 = jnp.float32
BF16 = jnp.bfloat16
INFO = 16
STRIP = 16
VMEM = pl.BlockSpec(memory_space=pltpu.VMEM)
SMEM = pl.BlockSpec(memory_space=pltpu.SMEM)
HBM = pl.BlockSpec(memory_space=pltpu.HBM)


def dft_tables(extent):
    half = extent // 2
    steps = np.arange(extent, dtype=np.int32)
    angles = (steps[:, None] * steps[None, :] % extent).astype(np.float32)
    angles = angles * np.float32(2.0 * math.pi / extent)
    scaling = np.float32(1.0 / math.sqrt(extent))
    real = (np.cos(angles) * scaling).astype(BF16)
    imag = (-np.sin(angles) * scaling).astype(BF16)
    tables = []
    for parity in (0, 1):
        re, im = real[:half, parity::2], imag[:half, parity::2]
        right = np.concatenate(
            [np.concatenate([re, im], 1), np.concatenate([-im, re], 1)], 0
        )
        tables += [right, np.ascontiguousarray(right.T)]
    return jnp.asarray(np.stack(tables))


def dot(a, b):
    return jnp.dot(a, b, preferred_element_type=F32)


def quarters(tl, tr, bl, br):
    return jnp.concatenate(
        [jnp.concatenate([tl, tr], 1), jnp.concatenate([bl, br], 1)], 0
    )


def iota(shape, dim):
    return lax.broadcasted_iota(jnp.int32, shape, dim)


def fetch(pairs, sems):
    copies = [
        pltpu.make_async_copy(source, target, sems.at[i])
        for i, (source, target) in enumerate(pairs)
    ]
    for copy in copies:
        copy.start()
    return copies


def pack_kernel(specimen, centers, cnt, helpers, out, tile_v, cen, hlp, sems):
    copies = fetch(((specimen, tile_v), (centers, cen), (helpers, hlp)), sems)
    for copy in copies:
        copy.wait()
    tile = tile_v.shape[1]
    lanes = tile_v.shape[2]
    rows, cols = iota((INFO, lanes), 0), iota((INFO, lanes), 1)
    info = jnp.where(rows == 0, -1.0, 0.0)
    for j in range(centers.shape[2]):
        helper = jnp.where(j < cnt[0, 0], hlp[0, 0, j], -1)
        for r, value in enumerate((helper, cen[0, 0, j, 0], cen[0, 0, j, 1])):
            info = jnp.where((rows == r) & (cols == j), value.astype(F32), info)
    info = info.astype(BF16)
    for p in range(2):
        out[p * tile : (p + 1) * tile] = tile_v[p].astype(BF16)
    out[2 * tile :] = info


def gather_columns(get, source, col, columns, shape):
    lane = iota(shape, 1)
    beside = own = jnp.zeros(shape, F32)
    for c in range(columns):
        block = get(c)
        near = ((source == c + 1) & (lane >= col)) | ((source == c - 1) & (lane < col))
        beside = jnp.where(near, block, beside)
        own = jnp.where(source == c, block, own)
    return jnp.concatenate([beside, own], 1)


def first_product(probe, patch, tables):
    half = patch[0].shape[1] // 2
    wr = probe[0] * patch[0] - probe[1] * patch[1]
    wi = probe[0] * patch[1] + probe[1] * patch[0]
    out = []
    for sign, table in zip((1, -1), tables):
        folded = jnp.concatenate(
            [wr[:, :half] + sign * wr[:, half:], wi[:, :half] + sign * wi[:, half:]], 1
        )
        out.append(dot(folded.astype(BF16), table))
    return out


def frame_of(band):
    columns, height, lanes = band.shape
    me = lax.axis_index("col").astype(F32)
    code = jnp.zeros((1, lanes), F32)
    for c in range(columns):
        info = band[c, height - INFO :].astype(F32)
        hit = info[0:1] == me
        code += jnp.where(hit, (c * lanes + info[1:2]) * lanes + info[2:3], 0.0)
    code = jnp.sum(code).astype(jnp.int32)
    return code // (lanes * lanes), code // lanes % lanes, code % lanes


def prepare_kernel(
    band, probe, measured, tables,
    info_out, amplitude, tables_out, probe_out, half_out, raw, raw_tables, raw_probe, groups, sems,
):
    copies = fetch(
        ((measured, raw), (tables, raw_tables), (probe, raw_probe)), sems
    )
    columns = band.shape[0]
    tile = (band.shape[1] - INFO) // 2
    extent = raw.shape[-1]
    half = extent // 2
    modes = raw_probe.shape[0]
    source, row, col = frame_of(band)
    which = iota((INFO, extent), 0)
    info = jnp.where(which == 0, source, jnp.where(which == 1, col, row))
    info_out[...] = info.astype(F32).astype(BF16)

    shape = (extent, extent)

    def original(i):
        return jnp.where(i < half, 2 * i, 2 * (i - half) + 1)

    copies[0].wait()
    sort = (iota(shape, 1) == original(iota(shape, 0))).astype(F32).astype(BF16)
    sort_t = (iota(shape, 0) == original(iota(shape, 1))).astype(F32).astype(BF16)
    value = raw[0, 0, 0]
    coarse = value.astype(BF16)
    fine = (value - coarse.astype(F32)).astype(BF16)
    amplitude[...] = sum(
        dot(dot(sort, part).astype(BF16), sort_t) for part in (coarse, fine)
    )

    def roller(old, new, shift, parity):
        wrapped = new % half < shift
        hit = (old + shift - jnp.where(old % half + shift >= half, half, 0)) == new
        sign = jnp.where(wrapped, -1.0, 1.0) if parity else 1.0
        return jnp.where(hit, sign, 0.0).astype(BF16)

    copies[1].wait()
    i, j = iota(shape, 0), iota(shape, 1)
    for parity in range(2):
        right, left = raw_tables[2 * parity], raw_tables[2 * parity + 1]
        for axis, shift in enumerate((col, row)):
            rolled = dot(left, roller(i, j, shift, parity)).astype(BF16)
            rolled_t = dot(roller(j, i, shift, parity), right).astype(BF16)
            tables_out[4 * axis + parity] = rolled_t if axis == 0 else rolled
            tables_out[4 * axis + 2 + parity] = rolled if axis == 0 else rolled_t

    copies[2].wait()
    count = extent // 8
    base = row // 8
    step = row % 8
    lane = iota((extent, half), 1)
    sub = iota((count, 8, extent), 1)
    for k in range(modes):
        for p in range(2):
            lo = pltpu.roll(raw_probe[k, p, :, :half], col, 1)
            hi = pltpu.roll(raw_probe[k, p, :, half:], col, 1)
            turned = jnp.concatenate(
                [jnp.where(lane < col, hi, lo), jnp.where(lane < col, lo, hi)], 1
            )
            turned = pltpu.roll(turned.reshape(count, 8, extent), step, 1)
            turned = jnp.where(
                sub < step, jnp.concatenate([turned[-1:], turned[:-1]], 0), turned
            )
            groups[:count] = turned
            groups[count:] = turned
            probe_out[k, p] = groups[pl.ds(count - base, count)].reshape(extent, extent)

    patch = [
        gather_columns(
            lambda c: band[c, p * tile : (p + 1) * tile].astype(F32),
            source, col, columns, (tile, tile),
        )
        for p in range(2)
    ]
    for k in range(modes):
        products = first_product(
            [probe_out[k, p, half:] for p in range(2)], patch, (tables_out[0], tables_out[1])
        )
        for parity in range(2):
            half_out[k, parity] = products[parity]


def frame_kernel(
    first, second, info, amplitude, tables, probe, half_own,
    to_rows, mixed_back, patch, folded, half_far, mixed, far, corrected, product, chi,
):
    columns = first.shape[0]
    tile = (first.shape[1] - INFO) // 2
    extent = probe.shape[-1]
    half = extent // 2
    modes = probe.shape[0]
    odd = lax.axis_index("row") % 2
    source, col, row = (
        info[r : r + 1, :tile].astype(F32).astype(jnp.int32) for r in range(3)
    )
    strips = [pl.ds(r, STRIP) for r in range(0, half, STRIP)]
    lower = [pl.ds(half + r, STRIP) for r in range(0, half, STRIP)]

    def split(x):
        return x[:, :half], x[:, half:]

    def join(x, y):
        return jnp.concatenate([x, y], 1).astype(BF16)

    def gather(s):
        rows = iota((STRIP, tile), 0) + s.start
        from_first = (rows >= row).astype(jnp.int32) == odd
        for p in range(2):
            part = pl.ds(p * tile + s.start, STRIP)
            patch[p, s] = gather_columns(
                lambda c: jnp.where(
                    from_first, first[c, part].astype(F32), second[c, part].astype(F32)
                ),
                source, col, columns, (STRIP, tile),
            )

    def wave(k):
        for s in strips:
            pr, pi, xr, xi = probe[k, 0, s], probe[k, 1, s], patch[0, s], patch[1, s]
            re = split(pr * xr - pi * xi)
            im = split(pr * xi + pi * xr)
            folded[k, 0, s] = join(re[0] + re[1], im[0] + im[1])
            folded[k, 1, s] = join(re[0] - re[1], im[0] - im[1])

    def along_rows(k):
        for q in range(2):
            half_far[k, q] = dot(folded[k, q], tables[q])

    def mix(k):
        for s, t in zip(strips, lower):
            even, odds = half_far[k, 0, s], half_far[k, 1, s]
            even_own, odds_own = half_own[k, 0, s], half_own[k, 1, s]
            for q, (e, o) in enumerate(
                ((even + even_own, odds + odds_own), (even - even_own, odds - odds_own))
            ):
                (er, ei), (our, oui) = split(e), split(o)
                mixed[k, q, s] = join(er, our)
                mixed[k, q, t] = join(ei, oui)

    def along_columns(k, q):
        far[k, q] = dot(tables[4 + q], mixed[k, q])

    def correct(q, which):
        for s, t in list(zip(strips, lower))[which]:
            re = [far[k, q, s] for k in range(modes)]
            im = [far[k, q, t] for k in range(modes)]
            intensity = sum(x * x for x in re + im)
            size = amplitude[pl.ds(q * half + s.start, STRIP)]
            factor = 1.0 - size * lax.rsqrt(jnp.maximum(intensity, 0.25))
            out = pl.ds(q * half + s.start, STRIP)
            for k in range(modes):
                (re_even, re_odd), (im_even, im_odd) = split(re[k] * factor), split(im[k] * factor)
                corrected[k, 0, out] = join(re_even, im_even)
                corrected[k, 1, out] = join(re_odd, im_odd)

    def back_along_rows(k, q):
        part = pl.ds(q * half, half)
        for c in range(2):
            product[k, c, part] = dot(corrected[k, c, part], tables[2 + c])

    def mix_back(k, q):
        for s, t in zip(strips, lower):
            part = pl.ds(q * half + s.start, STRIP)
            x, y = product[k, 0, part], product[k, 1, part]
            (lr, li), (hr, hi) = split(x + y), split(x - y)
            mixed_back[k, q, s] = join(lr, hr)
            mixed_back[k, q, t] = join(li, hi)

    both_back = jnp.concatenate([tables[6], tables[7]], 1)

    def back_along_columns(k):
        chi[k] = dot(both_back, mixed_back[k].reshape(2 * extent, extent))

    for s in strips:
        gather(s)
    for k in range(modes + 1):
        if k < modes:
            wave(k)
            along_rows(k)
        if k > 0:
            mix(k - 1)
            along_columns(k - 1, 0)
    share = -(-len(strips) // modes)
    for k in range(modes):
        along_columns(k, 1)
        correct(0, slice(k * share, (k + 1) * share))
    for k in range(modes):
        back_along_rows(k, 0)
        correct(1, slice(k * share, (k + 1) * share))
    for k in range(modes):
        mix_back(k, 0)
        back_along_rows(k, 1)
    for k in range(modes):
        mix_back(k, 1)
        back_along_columns(k)
    for s, t in zip(strips, lower):
        accumulate(to_rows, chi, probe, s, t, s)


def accumulate(out, chi, probe, s, t, rows):
    tile = out.shape[0] // 2
    re = im = 0.0
    for k in range(probe.shape[0]):
        pr, pi = probe[k, 0, rows], probe[k, 1, rows]
        cr, ci = chi[k, s], chi[k, t]
        re += pr * cr + pi * ci
        im += pr * ci - pi * cr
    out[s] = re.astype(BF16)
    out[pl.ds(tile + s.start, STRIP)] = im.astype(BF16)


def place(block, columns, source, col, taken):
    tile = block.shape[1] // 2
    beside, own = block[:, :tile], block[:, tile:]
    lane = iota(own.shape, 1)
    if taken is not None:
        beside, own = jnp.where(taken, beside, 0.0), jnp.where(taken, own, 0.0)
    out = []
    for c in range(columns):
        near = ((source == c + 1) & (lane >= col)) | ((source == c - 1) & (lane < col))
        out.append(jnp.where(near, beside, 0.0) + jnp.where(source == c, own, 0.0))
    return out


def finish_kernel(
    band, first_band, second_band, mixed_back, tables, probe, first,
    partial, second_info, chi, centre,
):
    columns = band.shape[0]
    extent = probe.shape[-1]
    tile = (band.shape[1] - INFO) // 2
    odd = lax.axis_index("row") % 2
    own_frame, first_frame, second_frame = (
        frame_of(b) for b in (band, first_band, second_band)
    )
    which = iota(second_info.shape, 0)
    second_info[...] = jnp.where(
        which == 0, second_frame[0], jnp.where(which == 1, second_frame[1], second_frame[2])
    )
    both_back = jnp.concatenate([tables[6], -tables[7]], 1)
    for k in range(probe.shape[0]):
        chi[k] = dot(both_back, mixed_back[k].reshape(2 * extent, extent))
    for r in range(0, tile, STRIP):
        s, t = pl.ds(r, STRIP), pl.ds(tile + r, STRIP)
        accumulate(centre, chi, probe, s, t, t)
        before = (iota((STRIP, tile), 0) + r < first_frame[1]).astype(jnp.int32)
        for part in (s, t):
            mine = place(centre[part].astype(F32), columns, own_frame[0], own_frame[2], None)
            other = place(
                first[part].astype(F32), columns, first_frame[0], first_frame[2], before == odd
            )
            for c in range(columns):
                partial[c, part] = mine[c] + other[c]


def fold_kernel(partial, second, second_info, out):
    columns, height, tile = out.shape
    odd = lax.axis_index("row") % 2
    source, row, col = (second_info[r : r + 1] for r in range(3))
    for r in range(0, height, STRIP):
        s = pl.ds(r, STRIP)
        before = (iota((STRIP, tile), 0) + r % tile < row).astype(jnp.int32)
        other = place(second[s].astype(F32), columns, source, col, before == 1 - odd)
        for c in range(columns):
            out[c, s] = (partial[c, s] + other[c]).astype(BF16)


def total_kernel(shares, out, total, sems):
    planes, tile, _ = out.shape
    pieces = sems.shape[0]
    rows = planes * tile // pieces
    copies = []
    for i in range(pieces):
        plane, start = i * rows // tile, i * rows % tile
        part = pl.ds(i * rows, rows)
        total[part] = sum(shares[c, part].astype(F32) for c in range(shares.shape[0]))
        copies.append(
            pltpu.make_async_copy(total.at[part], out.at[plane, pl.ds(start, rows)], sems.at[i])
        )
        copies[-1].start()
    for copy in copies:
        copy.wait()


def call(kernel, name, out_shape, in_specs, scratch, flops, moved, *args, out_specs=None):
    args = [
        pltpu.with_memory_space_constraint(arg, pltpu.HBM) if spec is HBM else arg
        for arg, spec in zip(args, in_specs)
    ]
    return pl.pallas_call(
        kernel,
        out_shape=out_shape,
        in_specs=in_specs,
        out_specs=out_specs or jax.tree.map(lambda _: VMEM, out_shape),
        scratch_shapes=scratch,
        compiler_params=pltpu.CompilerParams(vmem_limit_bytes=32 * 2**20),
        cost_estimate=pl.CostEstimate(flops=flops, bytes_accessed=moved, transcendentals=0),
        name=name,
    )(*args)


def per_device(specimen, probe, measured, centers, frame_counts, helper_cols):
    extent = probe.shape[-1]
    half = extent // 2
    tile = specimen.shape[1]
    modes = probe.shape[0]
    columns = lax.axis_size("col")
    height = 2 * tile
    part = jax.ShapeDtypeStruct((height, extent), BF16)
    dma = pltpu.SemaphoreType.DMA

    packed = call(
        pack_kernel, "pack",
        jax.ShapeDtypeStruct((height + INFO, tile), BF16),
        [HBM, HBM, SMEM, HBM],
        [
            pltpu.VMEM(specimen.shape, F32),
            pltpu.SMEM(centers.shape, jnp.int32),
            pltpu.SMEM(helper_cols.shape, jnp.int32),
            dma((3,)),
        ],
        10**5, 2**19,
        specimen, centers, frame_counts, helper_cols,
    )
    band = lax.all_gather(packed, "col")

    rows = lax.axis_size("row")
    swaps = []
    for start in (0, 1):
        pairs = [(i, i + 1) for i in range(start, rows - 1, 2)]
        swaps.append(pairs + [(b, a) for a, b in pairs])
    second = lax.ppermute(band, "row", swaps[1])
    first = lax.ppermute(band, "row", swaps[0])
    tables = dft_tables(extent)
    prepared = call(
        prepare_kernel, "prepare",
        (
            jax.ShapeDtypeStruct((INFO, extent), BF16),
            jax.ShapeDtypeStruct((extent, extent), F32),
            jax.ShapeDtypeStruct((8, extent, extent), BF16),
            jax.ShapeDtypeStruct(probe.shape, F32),
            jax.ShapeDtypeStruct((modes, 2, tile, extent), F32),
        ),
        [VMEM, HBM, HBM, HBM],
        [
            pltpu.VMEM(measured.shape, F32),
            pltpu.VMEM(tables.shape, BF16),
            pltpu.VMEM(probe.shape, F32),
            pltpu.VMEM((extent // 4, 8, extent), F32),
            dma((3,)),
        ],
        10**9, 2**22,
        band, probe, measured, tables,
    )
    full = (modes, 2, extent, extent)
    to_rows, mixed_back = call(
        frame_kernel, "frame",
        (part, jax.ShapeDtypeStruct(full, BF16)),
        [VMEM] * 7,
        [
            pltpu.VMEM((2, tile, extent), F32),
            pltpu.VMEM((modes, 2, half, extent), BF16),
            pltpu.VMEM((modes, 2, half, extent), F32),
            pltpu.VMEM(full, BF16),
            pltpu.VMEM(full, F32),
            pltpu.VMEM(full, BF16),
            pltpu.VMEM(full, F32),
            pltpu.VMEM((modes, extent, extent), F32),
        ],
        2 * 10**9, 2**22,
        first, second, *prepared,
    )
    from_first = lax.ppermute(to_rows, "row", swaps[0])
    from_second = lax.ppermute(to_rows, "row", swaps[1])
    partial, second_info = call(
        finish_kernel, "finish",
        (
            jax.ShapeDtypeStruct((columns, height, tile), F32),
            jax.ShapeDtypeStruct((8, tile), jnp.int32),
        ),
        [VMEM] * 7,
        [pltpu.VMEM((modes, extent, extent), F32), pltpu.VMEM((height, extent), BF16)],
        5 * 10**8, 2**22,
        band, first, second, mixed_back, prepared[2], prepared[3], from_first,
    )
    summed = call(
        fold_kernel, "fold",
        jax.ShapeDtypeStruct((columns, height, tile), BF16),
        [VMEM] * 3,
        [],
        10**7, 2**20,
        partial, from_second, second_info,
    )
    shares = lax.all_to_all(summed, "col", split_axis=0, concat_axis=0, tiled=True)
    return call(
        total_kernel, "total",
        jax.ShapeDtypeStruct(specimen.shape, F32),
        [VMEM],
        [pltpu.VMEM((height, tile), F32), dma((4,))],
        10**6, 2**18,
        shares,
        out_specs=HBM,
    )


def solution(mesh):
    return jax.shard_map(
        per_device,
        mesh=mesh,
        in_specs=(
            P(None, "row", "col"),
            P(),
            P("row", "col", None, None, None),
            P("row", "col", None, None),
            P("row", "col"),
            P("row", "col", None),
        ),
        out_specs=P(None, "row", "col"),
        check_vma=False,
    )
```

```python
import functools
import math

import jax
import jax.numpy as jnp
import numpy as np
from jax import lax
from jax.experimental import pallas as pl
from jax.experimental.pallas import tpu as pltpu
from jax.sharding import PartitionSpec as P

F32 = jnp.float32
BF16 = jnp.bfloat16
INFO = 16
COL = ("high", "low")
STRIP = 16
VMEM = pl.BlockSpec(memory_space=pltpu.VMEM)
SMEM = pl.BlockSpec(memory_space=pltpu.SMEM)
HBM = pl.BlockSpec(memory_space=pltpu.HBM)


def dft_tables(extent):
    half = extent // 2
    steps = np.arange(extent, dtype=np.int32)
    angles = (steps[:, None] * steps[None, :] % extent).astype(np.float32)
    angles = angles * np.float32(2.0 * math.pi / extent)
    scaling = np.float32(1.0 / math.sqrt(extent))
    real = (np.cos(angles) * scaling).astype(BF16)
    imag = (-np.sin(angles) * scaling).astype(BF16)
    tables = []
    for parity in (0, 1):
        re, im = real[:half, parity::2], imag[:half, parity::2]
        right = np.concatenate(
            [np.concatenate([re, im], 1), np.concatenate([-im, re], 1)], 0
        )
        tables += [right, np.ascontiguousarray(right.T)]
    return jnp.asarray(np.stack(tables))


def dot(a, b):
    return jnp.dot(a, b, preferred_element_type=F32)


def quarters(tl, tr, bl, br):
    return jnp.concatenate(
        [jnp.concatenate([tl, tr], 1), jnp.concatenate([bl, br], 1)], 0
    )


def iota(shape, dim):
    return lax.broadcasted_iota(jnp.int32, shape, dim)


def fetch(pairs, sems):
    copies = [
        pltpu.make_async_copy(source, target, sems.at[i])
        for i, (source, target) in enumerate(pairs)
    ]
    for copy in copies:
        copy.start()
    return copies


def pack_kernel(specimen, centers, cnt, helpers, out, tile_v, cen, hlp, sems):
    copies = fetch(((specimen, tile_v), (centers, cen), (helpers, hlp)), sems)
    for copy in copies:
        copy.wait()
    tile = tile_v.shape[1]
    lanes = tile_v.shape[2]
    rows, cols = iota((INFO, lanes), 0), iota((INFO, lanes), 1)
    info = jnp.where(rows == 0, -1.0, 0.0)
    for j in range(centers.shape[2]):
        helper = jnp.where(j < cnt[0, 0], hlp[0, 0, j], -1)
        for r, value in enumerate((helper, cen[0, 0, j, 0], cen[0, 0, j, 1])):
            info = jnp.where((rows == r) & (cols == j), value.astype(F32), info)
    info = info.astype(BF16)
    for p in range(2):
        out[p * tile : (p + 1) * tile] = tile_v[p].astype(BF16)
    out[2 * tile :] = info


def gather_columns(get, source, col, columns, shape):
    lane = iota(shape, 1)
    beside = own = jnp.zeros(shape, F32)
    for c in range(columns):
        block = get(c)
        near = ((source == c + 1) & (lane >= col)) | ((source == c - 1) & (lane < col))
        beside = jnp.where(near, block, beside)
        own = jnp.where(source == c, block, own)
    return jnp.concatenate([beside, own], 1)


def first_product(probe, patch, tables):
    half = patch[0].shape[1] // 2
    wr = probe[0] * patch[0] - probe[1] * patch[1]
    wi = probe[0] * patch[1] + probe[1] * patch[0]
    out = []
    for sign, table in zip((1, -1), tables):
        folded = jnp.concatenate(
            [wr[:, :half] + sign * wr[:, half:], wi[:, :half] + sign * wi[:, half:]], 1
        )
        out.append(dot(folded.astype(BF16), table))
    return out


def frame_of(band):
    columns, height, lanes = band.shape
    me = lax.axis_index(COL).astype(F32)
    code = jnp.zeros((1, lanes), F32)
    for c in range(columns):
        info = band[c, height - INFO :].astype(F32)
        hit = info[0:1] == me
        code += jnp.where(hit, (c * lanes + info[1:2]) * lanes + info[2:3], 0.0)
    code = jnp.sum(code).astype(jnp.int32)
    return code // (lanes * lanes), code // lanes % lanes, code % lanes


def prepare_kernel(
    band, probe, measured, tables,
    info_out, amplitude, tables_out, probe_out, half_out, raw, raw_tables, raw_probe, groups, sems,
):
    copies = fetch(
        ((measured, raw), (tables, raw_tables), (probe, raw_probe)), sems
    )
    columns = band.shape[0]
    tile = (band.shape[1] - INFO) // 2
    extent = raw.shape[-1]
    half = extent // 2
    modes = raw_probe.shape[0]
    source, row, col = frame_of(band)
    which = iota((INFO, extent), 0)
    info = jnp.where(which == 0, source, jnp.where(which == 1, col, row))
    info_out[...] = info.astype(F32).astype(BF16)

    shape = (extent, extent)

    def original(i):
        return jnp.where(i < half, 2 * i, 2 * (i - half) + 1)

    copies[0].wait()
    sort = (iota(shape, 1) == original(iota(shape, 0))).astype(F32).astype(BF16)
    sort_t = (iota(shape, 0) == original(iota(shape, 1))).astype(F32).astype(BF16)
    value = raw[0, 0, 0]
    coarse = value.astype(BF16)
    fine = (value - coarse.astype(F32)).astype(BF16)
    amplitude[...] = sum(
        dot(dot(sort, part).astype(BF16), sort_t) for part in (coarse, fine)
    )

    def roller(old, new, shift, parity):
        wrapped = new % half < shift
        hit = (old + shift - jnp.where(old % half + shift >= half, half, 0)) == new
        sign = jnp.where(wrapped, -1.0, 1.0) if parity else 1.0
        return jnp.where(hit, sign, 0.0).astype(BF16)

    copies[1].wait()
    i, j = iota(shape, 0), iota(shape, 1)
    for parity in range(2):
        right, left = raw_tables[2 * parity], raw_tables[2 * parity + 1]
        for axis, shift in enumerate((col, row)):
            rolled = dot(left, roller(i, j, shift, parity)).astype(BF16)
            rolled_t = dot(roller(j, i, shift, parity), right).astype(BF16)
            tables_out[4 * axis + parity] = rolled_t if axis == 0 else rolled
            tables_out[4 * axis + 2 + parity] = rolled if axis == 0 else rolled_t

    copies[2].wait()
    count = extent // 8
    base = row // 8
    step = row % 8
    lane = iota((extent, half), 1)
    sub = iota((count, 8, extent), 1)
    for k in range(modes):
        for p in range(2):
            lo = pltpu.roll(raw_probe[k, p, :, :half], col, 1)
            hi = pltpu.roll(raw_probe[k, p, :, half:], col, 1)
            turned = jnp.concatenate(
                [jnp.where(lane < col, hi, lo), jnp.where(lane < col, lo, hi)], 1
            )
            turned = pltpu.roll(turned.reshape(count, 8, extent), step, 1)
            turned = jnp.where(
                sub < step, jnp.concatenate([turned[-1:], turned[:-1]], 0), turned
            )
            groups[:count] = turned
            groups[count:] = turned
            probe_out[k, p] = groups[pl.ds(count - base, count)].reshape(extent, extent)

    patch = [
        gather_columns(
            lambda c: band[c, p * tile : (p + 1) * tile].astype(F32),
            source, col, columns, (tile, tile),
        )
        for p in range(2)
    ]
    for k in range(modes):
        products = first_product(
            [probe_out[k, p, half:] for p in range(2)], patch, (tables_out[0], tables_out[1])
        )
        for parity in range(2):
            half_out[k, parity] = products[parity]


def frame_kernel(
    first, second, info, amplitude, tables, probe, half_own,
    to_rows, mixed_back, patch, folded, half_far, mixed, far, corrected, product, chi,
):
    columns = first.shape[0]
    tile = (first.shape[1] - INFO) // 2
    extent = probe.shape[-1]
    half = extent // 2
    modes = probe.shape[0]
    odd = lax.axis_index("row") % 2
    source, col, row = (
        info[r : r + 1, :tile].astype(F32).astype(jnp.int32) for r in range(3)
    )
    strips = [pl.ds(r, STRIP) for r in range(0, half, STRIP)]
    lower = [pl.ds(half + r, STRIP) for r in range(0, half, STRIP)]

    def split(x):
        return x[:, :half], x[:, half:]

    def join(x, y):
        return jnp.concatenate([x, y], 1).astype(BF16)

    def gather(s):
        rows = iota((STRIP, tile), 0) + s.start
        from_first = (rows >= row).astype(jnp.int32) == odd
        for p in range(2):
            part = pl.ds(p * tile + s.start, STRIP)
            patch[p, s] = gather_columns(
                lambda c: jnp.where(
                    from_first, first[c, part].astype(F32), second[c, part].astype(F32)
                ),
                source, col, columns, (STRIP, tile),
            )

    def wave(k):
        for s in strips:
            pr, pi, xr, xi = probe[k, 0, s], probe[k, 1, s], patch[0, s], patch[1, s]
            re = split(pr * xr - pi * xi)
            im = split(pr * xi + pi * xr)
            folded[k, 0, s] = join(re[0] + re[1], im[0] + im[1])
            folded[k, 1, s] = join(re[0] - re[1], im[0] - im[1])

    def along_rows(k):
        for q in range(2):
            half_far[k, q] = dot(folded[k, q], tables[q])

    def mix(k):
        for s, t in zip(strips, lower):
            even, odds = half_far[k, 0, s], half_far[k, 1, s]
            even_own, odds_own = half_own[k, 0, s], half_own[k, 1, s]
            for q, (e, o) in enumerate(
                ((even + even_own, odds + odds_own), (even - even_own, odds - odds_own))
            ):
                (er, ei), (our, oui) = split(e), split(o)
                mixed[k, q, s] = join(er, our)
                mixed[k, q, t] = join(ei, oui)

    def along_columns(k, q):
        far[k, q] = dot(tables[4 + q], mixed[k, q])

    def correct(q, which):
        for s, t in list(zip(strips, lower))[which]:
            re = [far[k, q, s] for k in range(modes)]
            im = [far[k, q, t] for k in range(modes)]
            intensity = sum(x * x for x in re + im)
            size = amplitude[pl.ds(q * half + s.start, STRIP)]
            factor = 1.0 - size * lax.rsqrt(jnp.maximum(intensity, 0.25))
            out = pl.ds(q * half + s.start, STRIP)
            for k in range(modes):
                (re_even, re_odd), (im_even, im_odd) = split(re[k] * factor), split(im[k] * factor)
                corrected[k, 0, out] = join(re_even, im_even)
                corrected[k, 1, out] = join(re_odd, im_odd)

    def back_along_rows(k, q):
        part = pl.ds(q * half, half)
        for c in range(2):
            product[k, c, part] = dot(corrected[k, c, part], tables[2 + c])

    def mix_back(k, q):
        for s, t in zip(strips, lower):
            part = pl.ds(q * half + s.start, STRIP)
            x, y = product[k, 0, part], product[k, 1, part]
            (lr, li), (hr, hi) = split(x + y), split(x - y)
            mixed_back[k, q, s] = join(lr, hr)
            mixed_back[k, q, t] = join(li, hi)

    both_back = jnp.concatenate([tables[6], tables[7]], 1)

    def back_along_columns(k):
        chi[k] = dot(both_back, mixed_back[k].reshape(2 * extent, extent))

    for s in strips:
        gather(s)
    for k in range(modes + 1):
        if k < modes:
            wave(k)
            along_rows(k)
        if k > 0:
            mix(k - 1)
            along_columns(k - 1, 0)
    share = -(-len(strips) // modes)
    for k in range(modes):
        along_columns(k, 1)
        correct(0, slice(k * share, (k + 1) * share))
    for k in range(modes):
        back_along_rows(k, 0)
        correct(1, slice(k * share, (k + 1) * share))
    for k in range(modes):
        mix_back(k, 0)
        back_along_rows(k, 1)
    for k in range(modes):
        mix_back(k, 1)
        back_along_columns(k)
    for s, t in zip(strips, lower):
        accumulate(to_rows, chi, probe, s, t, s)


def accumulate(out, chi, probe, s, t, rows):
    tile = out.shape[0] // 2
    re = im = 0.0
    for k in range(probe.shape[0]):
        pr, pi = probe[k, 0, rows], probe[k, 1, rows]
        cr, ci = chi[k, s], chi[k, t]
        re += pr * cr + pi * ci
        im += pr * ci - pi * cr
    out[s] = re.astype(BF16)
    out[pl.ds(tile + s.start, STRIP)] = im.astype(BF16)


def place(block, columns, source, col, taken):
    tile = block.shape[1] // 2
    beside, own = block[:, :tile], block[:, tile:]
    lane = iota(own.shape, 1)
    if taken is not None:
        beside, own = jnp.where(taken, beside, 0.0), jnp.where(taken, own, 0.0)
    out = []
    for c in range(columns):
        near = ((source == c + 1) & (lane >= col)) | ((source == c - 1) & (lane < col))
        out.append(jnp.where(near, beside, 0.0) + jnp.where(source == c, own, 0.0))
    return out


def finish_kernel(
    band, first_band, second_band, mixed_back, tables, probe, first,
    partial, second_info, chi, centre,
):
    columns = band.shape[0]
    extent = probe.shape[-1]
    tile = (band.shape[1] - INFO) // 2
    odd = lax.axis_index("row") % 2
    own_frame, first_frame, second_frame = (
        frame_of(b) for b in (band, first_band, second_band)
    )
    which = iota(second_info.shape, 0)
    second_info[...] = jnp.where(
        which == 0, second_frame[0], jnp.where(which == 1, second_frame[1], second_frame[2])
    )
    both_back = jnp.concatenate([tables[6], -tables[7]], 1)
    for k in range(probe.shape[0]):
        chi[k] = dot(both_back, mixed_back[k].reshape(2 * extent, extent))
    for r in range(0, tile, STRIP):
        s, t = pl.ds(r, STRIP), pl.ds(tile + r, STRIP)
        accumulate(centre, chi, probe, s, t, t)
        before = (iota((STRIP, tile), 0) + r < first_frame[1]).astype(jnp.int32)
        for part in (s, t):
            mine = place(centre[part].astype(F32), columns, own_frame[0], own_frame[2], None)
            other = place(
                first[part].astype(F32), columns, first_frame[0], first_frame[2], before == odd
            )
            for c in range(columns):
                partial[c, part] = mine[c] + other[c]


def fold_kernel(partial, second, second_info, out):
    columns, height, tile = out.shape
    odd = lax.axis_index("row") % 2
    source, row, col = (second_info[r : r + 1] for r in range(3))
    for r in range(0, height, STRIP):
        s = pl.ds(r, STRIP)
        before = (iota((STRIP, tile), 0) + r % tile < row).astype(jnp.int32)
        other = place(second[s].astype(F32), columns, source, col, before == 1 - odd)
        for c in range(columns):
            out[c, s] = (partial[c, s] + other[c]).astype(BF16)


def call(kernel, name, out_shape, in_specs, scratch, flops, moved, *args):
    args = [
        pltpu.with_memory_space_constraint(arg, pltpu.HBM) if spec is HBM else arg
        for arg, spec in zip(args, in_specs)
    ]
    return pl.pallas_call(
        kernel,
        out_shape=out_shape,
        in_specs=in_specs,
        out_specs=jax.tree.map(lambda _: VMEM, out_shape),
        scratch_shapes=scratch,
        compiler_params=pltpu.CompilerParams(vmem_limit_bytes=32 * 2**20),
        cost_estimate=pl.CostEstimate(flops=flops, bytes_accessed=moved, transcendentals=0),
        name=name,
    )(*args)


def per_device(specimen, probe, measured, centers, frame_counts, helper_cols):
    extent = probe.shape[-1]
    half = extent // 2
    tile = specimen.shape[1]
    modes = probe.shape[0]
    columns = (lax.axis_size("high") * lax.axis_size("low"))
    height = 2 * tile
    part = jax.ShapeDtypeStruct((height, extent), BF16)
    dma = pltpu.SemaphoreType.DMA

    packed = call(
        pack_kernel, "pack",
        jax.ShapeDtypeStruct((height + INFO, tile), BF16),
        [HBM, HBM, SMEM, HBM],
        [
            pltpu.VMEM(specimen.shape, F32),
            pltpu.SMEM(centers.shape, jnp.int32),
            pltpu.SMEM(helper_cols.shape, jnp.int32),
            dma((3,)),
        ],
        10**5, 2**19,
        specimen, centers, frame_counts, helper_cols,
    )
    band = lax.all_gather(packed, COL)

    rows = lax.axis_size("row")
    swaps = []
    for start in (0, 1):
        pairs = [(i, i + 1) for i in range(start, rows - 1, 2)]
        swaps.append(pairs + [(b, a) for a, b in pairs])
    second = lax.ppermute(band, "row", swaps[1])
    first = lax.ppermute(band, "row", swaps[0])
    tables = dft_tables(extent)
    prepared = call(
        prepare_kernel, "prepare",
        (
            jax.ShapeDtypeStruct((INFO, extent), BF16),
            jax.ShapeDtypeStruct((extent, extent), F32),
            jax.ShapeDtypeStruct((8, extent, extent), BF16),
            jax.ShapeDtypeStruct(probe.shape, F32),
            jax.ShapeDtypeStruct((modes, 2, tile, extent), F32),
        ),
        [VMEM, HBM, HBM, HBM],
        [
            pltpu.VMEM(measured.shape, F32),
            pltpu.VMEM(tables.shape, BF16),
            pltpu.VMEM(probe.shape, F32),
            pltpu.VMEM((extent // 4, 8, extent), F32),
            dma((3,)),
        ],
        10**9, 2**22,
        band, probe, measured, tables,
    )
    full = (modes, 2, extent, extent)
    to_rows, mixed_back = call(
        frame_kernel, "frame",
        (part, jax.ShapeDtypeStruct(full, BF16)),
        [VMEM] * 7,
        [
            pltpu.VMEM((2, tile, extent), F32),
            pltpu.VMEM((modes, 2, half, extent), BF16),
            pltpu.VMEM((modes, 2, half, extent), F32),
            pltpu.VMEM(full, BF16),
            pltpu.VMEM(full, F32),
            pltpu.VMEM(full, BF16),
            pltpu.VMEM(full, F32),
            pltpu.VMEM((modes, extent, extent), F32),
        ],
        2 * 10**9, 2**22,
        first, second, *prepared,
    )
    from_first = lax.ppermute(to_rows, "row", swaps[0])
    from_second = lax.ppermute(to_rows, "row", swaps[1])
    partial, second_info = call(
        finish_kernel, "finish",
        (
            jax.ShapeDtypeStruct((columns, height, tile), F32),
            jax.ShapeDtypeStruct((8, tile), jnp.int32),
        ),
        [VMEM] * 7,
        [pltpu.VMEM((modes, extent, extent), F32), pltpu.VMEM((height, extent), BF16)],
        5 * 10**8, 2**22,
        band, first, second, mixed_back, prepared[2], prepared[3], from_first,
    )
    summed = call(
        fold_kernel, "fold",
        jax.ShapeDtypeStruct((columns, height, tile), BF16),
        [VMEM] * 3,
        [],
        10**7, 2**20,
        partial, from_second, second_info,
    )
    shares = lax.all_to_all(summed, COL, split_axis=0, concat_axis=0, tiled=True)
    return jnp.sum(shares.astype(F32), axis=0).reshape(2, tile, tile)


def solution(mesh):
    rows, columns = mesh.devices.shape
    low = math.gcd(columns, 2)
    split = jax.sharding.Mesh(
        mesh.devices.reshape(rows, columns // low, low), ("row",) + COL
    )
    return jax.shard_map(
        per_device,
        mesh=split,
        in_specs=(
            P(None, "row", COL),
            P(),
            P("row", COL, None, None, None),
            P("row", COL, None, None),
            P("row", COL),
            P("row", COL, None),
        ),
        out_specs=P(None, "row", COL),
        check_vma=False,
    )
```

```python
import functools
import math

import jax
import jax.numpy as jnp
import numpy as np
from jax import lax
from jax.experimental import pallas as pl
from jax.experimental.pallas import tpu as pltpu
from jax.sharding import PartitionSpec as P

F32 = jnp.float32
BF16 = jnp.bfloat16
INFO = 16
STRIP = 16
VMEM = pl.BlockSpec(memory_space=pltpu.VMEM)
SMEM = pl.BlockSpec(memory_space=pltpu.SMEM)
HBM = pl.BlockSpec(memory_space=pltpu.HBM)


def dft_tables(extent):
    half = extent // 2
    steps = np.arange(extent, dtype=np.int32)
    angles = (steps[:, None] * steps[None, :] % extent).astype(np.float32)
    angles = angles * np.float32(2.0 * math.pi / extent)
    scaling = np.float32(1.0 / math.sqrt(extent))
    real = (np.cos(angles) * scaling).astype(BF16)
    imag = (-np.sin(angles) * scaling).astype(BF16)
    tables = []
    for parity in (0, 1):
        re, im = real[:half, parity::2], imag[:half, parity::2]
        right = np.concatenate(
            [np.concatenate([re, im], 1), np.concatenate([-im, re], 1)], 0
        )
        tables += [right, np.ascontiguousarray(right.T)]
    return jnp.asarray(np.stack(tables))


def dot(a, b):
    return jnp.dot(a, b, preferred_element_type=F32)


def quarters(tl, tr, bl, br):
    return jnp.concatenate(
        [jnp.concatenate([tl, tr], 1), jnp.concatenate([bl, br], 1)], 0
    )


def iota(shape, dim):
    return lax.broadcasted_iota(jnp.int32, shape, dim)


def fetch(pairs, sems):
    copies = [
        pltpu.make_async_copy(source, target, sems.at[i])
        for i, (source, target) in enumerate(pairs)
    ]
    for copy in copies:
        copy.start()
    return copies


def pack_kernel(specimen, centers, cnt, helpers, out, tile_v, cen, hlp, sems):
    copies = fetch(((specimen, tile_v), (centers, cen), (helpers, hlp)), sems)
    for copy in copies:
        copy.wait()
    tile = tile_v.shape[1]
    lanes = tile_v.shape[2]
    rows, cols = iota((INFO, lanes), 0), iota((INFO, lanes), 1)
    info = jnp.where(rows == 0, -1.0, 0.0)
    for j in range(centers.shape[2]):
        helper = jnp.where(j < cnt[0, 0], hlp[0, 0, j], -1)
        for r, value in enumerate((helper, cen[0, 0, j, 0], cen[0, 0, j, 1])):
            info = jnp.where((rows == r) & (cols == j), value.astype(F32), info)
    info = info.astype(BF16)
    for p in range(2):
        out[p * tile : (p + 1) * tile] = tile_v[p].astype(BF16)
    out[2 * tile :] = info


def gather_columns(get, source, col, columns, shape):
    lane = iota(shape, 1)
    beside = own = jnp.zeros(shape, F32)
    for c in range(columns):
        block = get(c)
        near = ((source == c + 1) & (lane >= col)) | ((source == c - 1) & (lane < col))
        beside = jnp.where(near, block, beside)
        own = jnp.where(source == c, block, own)
    return jnp.concatenate([beside, own], 1)


def first_product(probe, patch, tables):
    half = patch[0].shape[1] // 2
    wr = probe[0] * patch[0] - probe[1] * patch[1]
    wi = probe[0] * patch[1] + probe[1] * patch[0]
    out = []
    for sign, table in zip((1, -1), tables):
        folded = jnp.concatenate(
            [wr[:, :half] + sign * wr[:, half:], wi[:, :half] + sign * wi[:, half:]], 1
        )
        out.append(dot(folded.astype(BF16), table))
    return out


def ring(columns):
    return list(range(0, columns, 2)) + list(range(1, columns, 2))


def frame_of(band):
    columns, height, lanes = band.shape
    me = lax.axis_index("col").astype(F32)
    code = jnp.zeros((1, lanes), F32)
    for place, c in enumerate(ring(columns)):
        info = band[place, height - INFO :].astype(F32)
        hit = info[0:1] == me
        code += jnp.where(hit, (c * lanes + info[1:2]) * lanes + info[2:3], 0.0)
    code = jnp.sum(code).astype(jnp.int32)
    return code // (lanes * lanes), code // lanes % lanes, code % lanes


def prepare_kernel(
    band, probe, measured, tables,
    info_out, amplitude, tables_out, probe_out, half_out, raw, raw_tables, raw_probe, groups, sems,
):
    copies = fetch(
        ((measured, raw), (tables, raw_tables), (probe, raw_probe)), sems
    )
    columns = band.shape[0]
    tile = (band.shape[1] - INFO) // 2
    extent = raw.shape[-1]
    half = extent // 2
    modes = raw_probe.shape[0]
    source, row, col = frame_of(band)
    which = iota((INFO, extent), 0)
    info = jnp.where(which == 0, source, jnp.where(which == 1, col, row))
    info_out[...] = info.astype(F32).astype(BF16)

    shape = (extent, extent)

    def original(i):
        return jnp.where(i < half, 2 * i, 2 * (i - half) + 1)

    copies[0].wait()
    sort = (iota(shape, 1) == original(iota(shape, 0))).astype(F32).astype(BF16)
    sort_t = (iota(shape, 0) == original(iota(shape, 1))).astype(F32).astype(BF16)
    value = raw[0, 0, 0]
    coarse = value.astype(BF16)
    fine = (value - coarse.astype(F32)).astype(BF16)
    amplitude[...] = sum(
        dot(dot(sort, part).astype(BF16), sort_t) for part in (coarse, fine)
    )

    def roller(old, new, shift, parity):
        wrapped = new % half < shift
        hit = (old + shift - jnp.where(old % half + shift >= half, half, 0)) == new
        sign = jnp.where(wrapped, -1.0, 1.0) if parity else 1.0
        return jnp.where(hit, sign, 0.0).astype(BF16)

    copies[1].wait()
    i, j = iota(shape, 0), iota(shape, 1)
    for parity in range(2):
        right, left = raw_tables[2 * parity], raw_tables[2 * parity + 1]
        for axis, shift in enumerate((col, row)):
            rolled = dot(left, roller(i, j, shift, parity)).astype(BF16)
            rolled_t = dot(roller(j, i, shift, parity), right).astype(BF16)
            tables_out[4 * axis + parity] = rolled_t if axis == 0 else rolled
            tables_out[4 * axis + 2 + parity] = rolled if axis == 0 else rolled_t

    copies[2].wait()
    count = extent // 8
    base = row // 8
    step = row % 8
    lane = iota((extent, half), 1)
    sub = iota((count, 8, extent), 1)
    for k in range(modes):
        for p in range(2):
            lo = pltpu.roll(raw_probe[k, p, :, :half], col, 1)
            hi = pltpu.roll(raw_probe[k, p, :, half:], col, 1)
            turned = jnp.concatenate(
                [jnp.where(lane < col, hi, lo), jnp.where(lane < col, lo, hi)], 1
            )
            turned = pltpu.roll(turned.reshape(count, 8, extent), step, 1)
            turned = jnp.where(
                sub < step, jnp.concatenate([turned[-1:], turned[:-1]], 0), turned
            )
            groups[:count] = turned
            groups[count:] = turned
            probe_out[k, p] = groups[pl.ds(count - base, count)].reshape(extent, extent)

    order = ring(columns)
    patch = [
        gather_columns(
            lambda c: band[order.index(c), p * tile : (p + 1) * tile].astype(F32),
            source, col, columns, (tile, tile),
        )
        for p in range(2)
    ]
    for k in range(modes):
        products = first_product(
            [probe_out[k, p, half:] for p in range(2)], patch, (tables_out[0], tables_out[1])
        )
        for parity in range(2):
            half_out[k, parity] = products[parity]


def frame_kernel(
    first, second, info, amplitude, tables, probe, half_own,
    to_rows, mixed_back, patch, folded, half_far, mixed, far, corrected, product, chi,
):
    columns = first.shape[0]
    tile = (first.shape[1] - INFO) // 2
    extent = probe.shape[-1]
    half = extent // 2
    modes = probe.shape[0]
    order = ring(columns)
    odd = lax.axis_index("row") % 2
    source, col, row = (
        info[r : r + 1, :tile].astype(F32).astype(jnp.int32) for r in range(3)
    )
    strips = [pl.ds(r, STRIP) for r in range(0, half, STRIP)]
    lower = [pl.ds(half + r, STRIP) for r in range(0, half, STRIP)]

    def split(x):
        return x[:, :half], x[:, half:]

    def join(x, y):
        return jnp.concatenate([x, y], 1).astype(BF16)

    def gather(s):
        rows = iota((STRIP, tile), 0) + s.start
        from_first = (rows >= row).astype(jnp.int32) == odd
        for p in range(2):
            part = pl.ds(p * tile + s.start, STRIP)
            patch[p, s] = gather_columns(
                lambda c: jnp.where(
                    from_first,
                    first[order.index(c), part].astype(F32),
                    second[order.index(c), part].astype(F32),
                ),
                source, col, columns, (STRIP, tile),
            )

    def wave(k):
        for s in strips:
            pr, pi, xr, xi = probe[k, 0, s], probe[k, 1, s], patch[0, s], patch[1, s]
            re = split(pr * xr - pi * xi)
            im = split(pr * xi + pi * xr)
            folded[k, 0, s] = join(re[0] + re[1], im[0] + im[1])
            folded[k, 1, s] = join(re[0] - re[1], im[0] - im[1])

    def along_rows(k):
        for q in range(2):
            half_far[k, q] = dot(folded[k, q], tables[q])

    def mix(k):
        for s, t in zip(strips, lower):
            even, odds = half_far[k, 0, s], half_far[k, 1, s]
            even_own, odds_own = half_own[k, 0, s], half_own[k, 1, s]
            for q, (e, o) in enumerate(
                ((even + even_own, odds + odds_own), (even - even_own, odds - odds_own))
            ):
                (er, ei), (our, oui) = split(e), split(o)
                mixed[k, q, s] = join(er, our)
                mixed[k, q, t] = join(ei, oui)

    def along_columns(k, q):
        far[k, q] = dot(tables[4 + q], mixed[k, q])

    def correct(q, which):
        for s, t in list(zip(strips, lower))[which]:
            re = [far[k, q, s] for k in range(modes)]
            im = [far[k, q, t] for k in range(modes)]
            intensity = sum(x * x for x in re + im)
            size = amplitude[pl.ds(q * half + s.start, STRIP)]
            factor = 1.0 - size * lax.rsqrt(jnp.maximum(intensity, 0.25))
            out = pl.ds(q * half + s.start, STRIP)
            for k in range(modes):
                (re_even, re_odd), (im_even, im_odd) = split(re[k] * factor), split(im[k] * factor)
                corrected[k, 0, out] = join(re_even, im_even)
                corrected[k, 1, out] = join(re_odd, im_odd)

    def back_along_rows(k, q):
        part = pl.ds(q * half, half)
        for c in range(2):
            product[k, c, part] = dot(corrected[k, c, part], tables[2 + c])

    def mix_back(k, q):
        for s, t in zip(strips, lower):
            part = pl.ds(q * half + s.start, STRIP)
            x, y = product[k, 0, part], product[k, 1, part]
            (lr, li), (hr, hi) = split(x + y), split(x - y)
            mixed_back[k, q, s] = join(lr, hr)
            mixed_back[k, q, t] = join(li, hi)

    both_back = jnp.concatenate([tables[6], tables[7]], 1)

    def back_along_columns(k):
        chi[k] = dot(both_back, mixed_back[k].reshape(2 * extent, extent))

    for s in strips:
        gather(s)
    for k in range(modes + 1):
        if k < modes:
            wave(k)
            along_rows(k)
        if k > 0:
            mix(k - 1)
            along_columns(k - 1, 0)
    share = -(-len(strips) // modes)
    for k in range(modes):
        along_columns(k, 1)
        correct(0, slice(k * share, (k + 1) * share))
    for k in range(modes):
        back_along_rows(k, 0)
        correct(1, slice(k * share, (k + 1) * share))
    for k in range(modes):
        mix_back(k, 0)
        back_along_rows(k, 1)
    for k in range(modes):
        mix_back(k, 1)
        back_along_columns(k)
    for s, t in zip(strips, lower):
        accumulate(to_rows, chi, probe, s, t, s)


def accumulate(out, chi, probe, s, t, rows):
    tile = out.shape[0] // 2
    re = im = 0.0
    for k in range(probe.shape[0]):
        pr, pi = probe[k, 0, rows], probe[k, 1, rows]
        cr, ci = chi[k, s], chi[k, t]
        re += pr * cr + pi * ci
        im += pr * ci - pi * cr
    out[s] = re.astype(BF16)
    out[pl.ds(tile + s.start, STRIP)] = im.astype(BF16)


def place(block, columns, source, col, taken):
    tile = block.shape[1] // 2
    beside, own = block[:, :tile], block[:, tile:]
    lane = iota(own.shape, 1)
    if taken is not None:
        beside, own = jnp.where(taken, beside, 0.0), jnp.where(taken, own, 0.0)
    out = []
    for c in range(columns):
        near = ((source == c + 1) & (lane >= col)) | ((source == c - 1) & (lane < col))
        out.append(jnp.where(near, beside, 0.0) + jnp.where(source == c, own, 0.0))
    return out


def finish_kernel(
    band, first_band, second_band, mixed_back, tables, probe, first,
    partial, second_info, chi, centre,
):
    columns = band.shape[0]
    extent = probe.shape[-1]
    tile = (band.shape[1] - INFO) // 2
    odd = lax.axis_index("row") % 2
    own_frame, first_frame, second_frame = (
        frame_of(b) for b in (band, first_band, second_band)
    )
    which = iota(second_info.shape, 0)
    second_info[...] = jnp.where(
        which == 0, second_frame[0], jnp.where(which == 1, second_frame[1], second_frame[2])
    )
    both_back = jnp.concatenate([tables[6], -tables[7]], 1)
    for k in range(probe.shape[0]):
        chi[k] = dot(both_back, mixed_back[k].reshape(2 * extent, extent))
    for r in range(0, tile, STRIP):
        s, t = pl.ds(r, STRIP), pl.ds(tile + r, STRIP)
        accumulate(centre, chi, probe, s, t, t)
        before = (iota((STRIP, tile), 0) + r < first_frame[1]).astype(jnp.int32)
        for part in (s, t):
            mine = place(centre[part].astype(F32), columns, own_frame[0], own_frame[2], None)
            other = place(
                first[part].astype(F32), columns, first_frame[0], first_frame[2], before == odd
            )
            for c in range(columns):
                partial[c, part] = mine[c] + other[c]


def fold_kernel(partial, second, second_info, out):
    columns, height, tile = out.shape
    odd = lax.axis_index("row") % 2
    source, row, col = (second_info[r : r + 1] for r in range(3))
    for r in range(0, height, STRIP):
        s = pl.ds(r, STRIP)
        before = (iota((STRIP, tile), 0) + r % tile < row).astype(jnp.int32)
        other = place(second[s].astype(F32), columns, source, col, before == 1 - odd)
        for c in range(columns):
            out[c, s] = (partial[c, s] + other[c]).astype(BF16)


def call(kernel, name, out_shape, in_specs, scratch, flops, moved, *args):
    args = [
        pltpu.with_memory_space_constraint(arg, pltpu.HBM) if spec is HBM else arg
        for arg, spec in zip(args, in_specs)
    ]
    return pl.pallas_call(
        kernel,
        out_shape=out_shape,
        in_specs=in_specs,
        out_specs=jax.tree.map(lambda _: VMEM, out_shape),
        scratch_shapes=scratch,
        compiler_params=pltpu.CompilerParams(vmem_limit_bytes=32 * 2**20),
        cost_estimate=pl.CostEstimate(flops=flops, bytes_accessed=moved, transcendentals=0),
        name=name,
    )(*args)


def per_device(specimen, probe, measured, centers, frame_counts, helper_cols):
    extent = probe.shape[-1]
    half = extent // 2
    tile = specimen.shape[1]
    modes = probe.shape[0]
    columns = lax.axis_size("col")
    height = 2 * tile
    part = jax.ShapeDtypeStruct((height, extent), BF16)
    dma = pltpu.SemaphoreType.DMA

    packed = call(
        pack_kernel, "pack",
        jax.ShapeDtypeStruct((height + INFO, tile), BF16),
        [HBM, HBM, SMEM, HBM],
        [
            pltpu.VMEM(specimen.shape, F32),
            pltpu.SMEM(centers.shape, jnp.int32),
            pltpu.SMEM(helper_cols.shape, jnp.int32),
            dma((3,)),
        ],
        10**5, 2**19,
        specimen, centers, frame_counts, helper_cols,
    )
    band = lax.all_gather(packed, "col", axis_index_groups=[ring(columns)])

    rows = lax.axis_size("row")
    swaps = []
    for start in (0, 1):
        pairs = [(i, i + 1) for i in range(start, rows - 1, 2)]
        swaps.append(pairs + [(b, a) for a, b in pairs])
    second = lax.ppermute(band, "row", swaps[1])
    first = lax.ppermute(band, "row", swaps[0])
    tables = dft_tables(extent)
    prepared = call(
        prepare_kernel, "prepare",
        (
            jax.ShapeDtypeStruct((INFO, extent), BF16),
            jax.ShapeDtypeStruct((extent, extent), F32),
            jax.ShapeDtypeStruct((8, extent, extent), BF16),
            jax.ShapeDtypeStruct(probe.shape, F32),
            jax.ShapeDtypeStruct((modes, 2, tile, extent), F32),
        ),
        [VMEM, HBM, HBM, HBM],
        [
            pltpu.VMEM(measured.shape, F32),
            pltpu.VMEM(tables.shape, BF16),
            pltpu.VMEM(probe.shape, F32),
            pltpu.VMEM((extent // 4, 8, extent), F32),
            dma((3,)),
        ],
        10**9, 2**22,
        band, probe, measured, tables,
    )
    full = (modes, 2, extent, extent)
    to_rows, mixed_back = call(
        frame_kernel, "frame",
        (part, jax.ShapeDtypeStruct(full, BF16)),
        [VMEM] * 7,
        [
            pltpu.VMEM((2, tile, extent), F32),
            pltpu.VMEM((modes, 2, half, extent), BF16),
            pltpu.VMEM((modes, 2, half, extent), F32),
            pltpu.VMEM(full, BF16),
            pltpu.VMEM(full, F32),
            pltpu.VMEM(full, BF16),
            pltpu.VMEM(full, F32),
            pltpu.VMEM((modes, extent, extent), F32),
        ],
        2 * 10**9, 2**22,
        first, second, *prepared,
    )
    from_first = lax.ppermute(to_rows, "row", swaps[0])
    from_second = lax.ppermute(to_rows, "row", swaps[1])
    partial, second_info = call(
        finish_kernel, "finish",
        (
            jax.ShapeDtypeStruct((columns, height, tile), F32),
            jax.ShapeDtypeStruct((8, tile), jnp.int32),
        ),
        [VMEM] * 7,
        [pltpu.VMEM((modes, extent, extent), F32), pltpu.VMEM((height, extent), BF16)],
        5 * 10**8, 2**22,
        band, first, second, mixed_back, prepared[2], prepared[3], from_first,
    )
    summed = call(
        fold_kernel, "fold",
        jax.ShapeDtypeStruct((columns, height, tile), BF16),
        [VMEM] * 3,
        [],
        10**7, 2**20,
        partial, from_second, second_info,
    )
    shares = lax.all_to_all(summed, "col", split_axis=0, concat_axis=0, tiled=True)
    return jnp.sum(shares.astype(F32), axis=0).reshape(2, tile, tile)


def solution(mesh):
    return jax.shard_map(
        per_device,
        mesh=mesh,
        in_specs=(
            P(None, "row", "col"),
            P(),
            P("row", "col", None, None, None),
            P("row", "col", None, None),
            P("row", "col"),
            P("row", "col", None),
        ),
        out_specs=P(None, "row", "col"),
        check_vma=False,
    )
```

```python
import functools
import math

import jax
import jax.numpy as jnp
import numpy as np
from jax import lax
from jax.experimental import pallas as pl
from jax.experimental.pallas import tpu as pltpu
from jax.sharding import PartitionSpec as P

F32 = jnp.float32
BF16 = jnp.bfloat16
INFO = 16
STRIP = 16
VMEM = pl.BlockSpec(memory_space=pltpu.VMEM)
SMEM = pl.BlockSpec(memory_space=pltpu.SMEM)
HBM = pl.BlockSpec(memory_space=pltpu.HBM)


def dft_tables(extent):
    half = extent // 2
    steps = np.arange(extent, dtype=np.int32)
    angles = (steps[:, None] * steps[None, :] % extent).astype(np.float32)
    angles = angles * np.float32(2.0 * math.pi / extent)
    scaling = np.float32(1.0 / math.sqrt(extent))
    real = (np.cos(angles) * scaling).astype(BF16)
    imag = (-np.sin(angles) * scaling).astype(BF16)
    tables = []
    for parity in (0, 1):
        re, im = real[:half, parity::2], imag[:half, parity::2]
        right = np.concatenate(
            [np.concatenate([re, im], 1), np.concatenate([-im, re], 1)], 0
        )
        tables += [right, np.ascontiguousarray(right.T)]
    return jnp.asarray(np.stack(tables))


def dot(a, b):
    return jnp.dot(a, b, preferred_element_type=F32)


def quarters(tl, tr, bl, br):
    return jnp.concatenate(
        [jnp.concatenate([tl, tr], 1), jnp.concatenate([bl, br], 1)], 0
    )


def iota(shape, dim):
    return lax.broadcasted_iota(jnp.int32, shape, dim)


def fetch(pairs, sems):
    copies = [
        pltpu.make_async_copy(source, target, sems.at[i])
        for i, (source, target) in enumerate(pairs)
    ]
    for copy in copies:
        copy.start()
    return copies


def pack_kernel(specimen, centers, cnt, helpers, out, tile_v, cen, hlp, sems):
    copies = fetch(((specimen, tile_v), (centers, cen), (helpers, hlp)), sems)
    for copy in copies:
        copy.wait()
    tile = tile_v.shape[1]
    lanes = tile_v.shape[2]
    rows, cols = iota((INFO, lanes), 0), iota((INFO, lanes), 1)
    info = jnp.where(rows == 0, -1.0, 0.0)
    for j in range(centers.shape[2]):
        helper = jnp.where(j < cnt[0, 0], hlp[0, 0, j], -1)
        for r, value in enumerate((helper, cen[0, 0, j, 0], cen[0, 0, j, 1])):
            info = jnp.where((rows == r) & (cols == j), value.astype(F32), info)
    info = info.astype(BF16)
    for p in range(2):
        out[p * tile : (p + 1) * tile] = tile_v[p].astype(BF16)
    out[2 * tile :] = info


def gather_columns(get, source, col, columns, shape):
    lane = iota(shape, 1)
    beside = own = jnp.zeros(shape, F32)
    for c in range(columns):
        block = get(c)
        near = ((source == c + 1) & (lane >= col)) | ((source == c - 1) & (lane < col))
        beside = jnp.where(near, block, beside)
        own = jnp.where(source == c, block, own)
    return jnp.concatenate([beside, own], 1)


def first_product(probe, patch, tables):
    half = patch[0].shape[1] // 2
    wr = probe[0] * patch[0] - probe[1] * patch[1]
    wi = probe[0] * patch[1] + probe[1] * patch[0]
    out = []
    for sign, table in zip((1, -1), tables):
        folded = jnp.concatenate(
            [wr[:, :half] + sign * wr[:, half:], wi[:, :half] + sign * wi[:, half:]], 1
        )
        out.append(dot(folded.astype(BF16), table))
    return out


def frame_of(band):
    columns, height, lanes = band.shape
    me = lax.axis_index("col").astype(F32)
    code = jnp.zeros((1, lanes), F32)
    for c in range(columns):
        info = band[c, height - INFO :].astype(F32)
        hit = info[0:1] == me
        code += jnp.where(hit, (c * lanes + info[1:2]) * lanes + info[2:3], 0.0)
    code = jnp.sum(code).astype(jnp.int32)
    return code // (lanes * lanes), code // lanes % lanes, code % lanes


def prepare_kernel(
    band, probe, measured, tables,
    info_out, amplitude, tables_out, probe_out, half_out, raw, raw_tables, raw_probe, groups, sems,
):
    copies = fetch(
        ((measured, raw), (tables, raw_tables), (probe, raw_probe)), sems
    )
    columns = band.shape[0]
    tile = (band.shape[1] - INFO) // 2
    extent = raw.shape[-1]
    half = extent // 2
    modes = raw_probe.shape[0]
    source, row, col = frame_of(band)
    which = iota((INFO, extent), 0)
    info = jnp.where(which == 0, source, jnp.where(which == 1, col, row))
    info_out[...] = info.astype(F32).astype(BF16)

    shape = (extent, extent)

    def original(i):
        return jnp.where(i < half, 2 * i, 2 * (i - half) + 1)

    copies[0].wait()
    sort = (iota(shape, 1) == original(iota(shape, 0))).astype(F32).astype(BF16)
    sort_t = (iota(shape, 0) == original(iota(shape, 1))).astype(F32).astype(BF16)
    value = raw[0, 0, 0]
    coarse = value.astype(BF16)
    fine = (value - coarse.astype(F32)).astype(BF16)
    amplitude[...] = sum(
        dot(dot(sort, part).astype(BF16), sort_t) for part in (coarse, fine)
    )

    def roller(old, new, shift, parity):
        wrapped = new % half < shift
        hit = (old + shift - jnp.where(old % half + shift >= half, half, 0)) == new
        sign = jnp.where(wrapped, -1.0, 1.0) if parity else 1.0
        return jnp.where(hit, sign, 0.0).astype(BF16)

    copies[1].wait()
    i, j = iota(shape, 0), iota(shape, 1)
    for parity in range(2):
        right, left = raw_tables[2 * parity], raw_tables[2 * parity + 1]
        for axis, shift in enumerate((col, row)):
            rolled = dot(left, roller(i, j, shift, parity)).astype(BF16)
            rolled_t = dot(roller(j, i, shift, parity), right).astype(BF16)
            tables_out[4 * axis + parity] = rolled_t if axis == 0 else rolled
            tables_out[4 * axis + 2 + parity] = rolled if axis == 0 else rolled_t

    copies[2].wait()
    count = extent // 8
    base = row // 8
    step = row % 8
    lane = iota((extent, half), 1)
    sub = iota((count, 8, extent), 1)
    for k in range(modes):
        for p in range(2):
            lo = pltpu.roll(raw_probe[k, p, :, :half], col, 1)
            hi = pltpu.roll(raw_probe[k, p, :, half:], col, 1)
            turned = jnp.concatenate(
                [jnp.where(lane < col, hi, lo), jnp.where(lane < col, lo, hi)], 1
            )
            turned = pltpu.roll(turned.reshape(count, 8, extent), step, 1)
            turned = jnp.where(
                sub < step, jnp.concatenate([turned[-1:], turned[:-1]], 0), turned
            )
            groups[:count] = turned
            groups[count:] = turned
            probe_out[k, p] = groups[pl.ds(count - base, count)].reshape(extent, extent)

    patch = [
        gather_columns(
            lambda c: band[c, p * tile : (p + 1) * tile].astype(F32),
            source, col, columns, (tile, tile),
        )
        for p in range(2)
    ]
    for k in range(modes):
        products = first_product(
            [probe_out[k, p, half:] for p in range(2)], patch, (tables_out[0], tables_out[1])
        )
        for parity in range(2):
            half_out[k, parity] = products[parity]


def frame_kernel(
    first, second, info, amplitude, tables, probe, half_own,
    to_second, to_first, mixed_back, patch, folded, half_far, mixed, far, corrected, product, chi,
):
    columns = first.shape[0]
    tile = (first.shape[1] - INFO) // 2
    extent = probe.shape[-1]
    half = extent // 2
    modes = probe.shape[0]
    odd = lax.axis_index("row") % 2
    source, col, row = (
        info[r : r + 1, :tile].astype(F32).astype(jnp.int32) for r in range(3)
    )
    strips = [pl.ds(r, STRIP) for r in range(0, half, STRIP)]
    lower = [pl.ds(half + r, STRIP) for r in range(0, half, STRIP)]

    def split(x):
        return x[:, :half], x[:, half:]

    def join(x, y):
        return jnp.concatenate([x, y], 1).astype(BF16)

    def gather(s):
        rows = iota((STRIP, tile), 0) + s.start
        from_first = (rows >= row).astype(jnp.int32) == odd
        for p in range(2):
            part = pl.ds(p * tile + s.start, STRIP)
            patch[p, s] = gather_columns(
                lambda c: jnp.where(
                    from_first, first[c, part].astype(F32), second[c, part].astype(F32)
                ),
                source, col, columns, (STRIP, tile),
            )

    def wave(k):
        for s in strips:
            pr, pi, xr, xi = probe[k, 0, s], probe[k, 1, s], patch[0, s], patch[1, s]
            re = split(pr * xr - pi * xi)
            im = split(pr * xi + pi * xr)
            folded[k, 0, s] = join(re[0] + re[1], im[0] + im[1])
            folded[k, 1, s] = join(re[0] - re[1], im[0] - im[1])

    def along_rows(k):
        for q in range(2):
            half_far[k, q] = dot(folded[k, q], tables[q])

    def mix(k):
        for s, t in zip(strips, lower):
            even, odds = half_far[k, 0, s], half_far[k, 1, s]
            even_own, odds_own = half_own[k, 0, s], half_own[k, 1, s]
            for q, (e, o) in enumerate(
                ((even + even_own, odds + odds_own), (even - even_own, odds - odds_own))
            ):
                (er, ei), (our, oui) = split(e), split(o)
                mixed[k, q, s] = join(er, our)
                mixed[k, q, t] = join(ei, oui)

    def along_columns(k, q):
        far[k, q] = dot(tables[4 + q], mixed[k, q])

    def correct(q, which):
        for s, t in list(zip(strips, lower))[which]:
            re = [far[k, q, s] for k in range(modes)]
            im = [far[k, q, t] for k in range(modes)]
            intensity = sum(x * x for x in re + im)
            size = amplitude[pl.ds(q * half + s.start, STRIP)]
            factor = 1.0 - size * lax.rsqrt(jnp.maximum(intensity, 0.25))
            out = pl.ds(q * half + s.start, STRIP)
            for k in range(modes):
                (re_even, re_odd), (im_even, im_odd) = split(re[k] * factor), split(im[k] * factor)
                corrected[k, 0, out] = join(re_even, im_even)
                corrected[k, 1, out] = join(re_odd, im_odd)

    def back_along_rows(k, q):
        part = pl.ds(q * half, half)
        for c in range(2):
            product[k, c, part] = dot(corrected[k, c, part], tables[2 + c])

    def mix_back(k, q):
        for s, t in zip(strips, lower):
            part = pl.ds(q * half + s.start, STRIP)
            x, y = product[k, 0, part], product[k, 1, part]
            (lr, li), (hr, hi) = split(x + y), split(x - y)
            mixed_back[k, q, s] = join(lr, hr)
            mixed_back[k, q, t] = join(li, hi)

    both_back = jnp.concatenate([tables[6], tables[7]], 1)

    def back_along_columns(k):
        chi[k] = dot(both_back, mixed_back[k].reshape(2 * extent, extent))

    for s in strips:
        gather(s)
    for k in range(modes + 1):
        if k < modes:
            wave(k)
            along_rows(k)
        if k > 0:
            mix(k - 1)
            along_columns(k - 1, 0)
    share = -(-len(strips) // modes)
    for k in range(modes):
        along_columns(k, 1)
        correct(0, slice(k * share, (k + 1) * share))
    for k in range(modes):
        back_along_rows(k, 0)
        correct(1, slice(k * share, (k + 1) * share))
    for k in range(modes):
        mix_back(k, 0)
        back_along_rows(k, 1)
    for k in range(modes):
        mix_back(k, 1)
        back_along_columns(k)
    for s, t in zip(strips, lower):
        accumulate((to_second, to_first), chi, probe, s, t, s)


def accumulate(outs, chi, probe, s, t, rows):
    tile = outs[0].shape[0] // 2
    re = im = 0.0
    for k in range(probe.shape[0]):
        pr, pi = probe[k, 0, rows], probe[k, 1, rows]
        cr, ci = chi[k, s], chi[k, t]
        re += pr * cr + pi * ci
        im += pr * ci - pi * cr
    for out in outs:
        out[s] = re.astype(BF16)
        out[pl.ds(tile + s.start, STRIP)] = im.astype(BF16)


def place(block, columns, source, col, taken):
    tile = block.shape[1] // 2
    beside, own = block[:, :tile], block[:, tile:]
    lane = iota(own.shape, 1)
    if taken is not None:
        beside, own = jnp.where(taken, beside, 0.0), jnp.where(taken, own, 0.0)
    out = []
    for c in range(columns):
        near = ((source == c + 1) & (lane >= col)) | ((source == c - 1) & (lane < col))
        out.append(jnp.where(near, beside, 0.0) + jnp.where(source == c, own, 0.0))
    return out


def finish_kernel(
    band, first_band, second_band, mixed_back, tables, probe, first,
    partial, second_info, chi, centre,
):
    columns = band.shape[0]
    extent = probe.shape[-1]
    tile = (band.shape[1] - INFO) // 2
    odd = lax.axis_index("row") % 2
    own_frame, first_frame, second_frame = (
        frame_of(b) for b in (band, first_band, second_band)
    )
    which = iota(second_info.shape, 0)
    second_info[...] = jnp.where(
        which == 0, second_frame[0], jnp.where(which == 1, second_frame[1], second_frame[2])
    )
    both_back = jnp.concatenate([tables[6], -tables[7]], 1)
    for k in range(probe.shape[0]):
        chi[k] = dot(both_back, mixed_back[k].reshape(2 * extent, extent))
    for r in range(0, tile, STRIP):
        s, t = pl.ds(r, STRIP), pl.ds(tile + r, STRIP)
        accumulate((centre,), chi, probe, s, t, t)
        before = (iota((STRIP, tile), 0) + r < first_frame[1]).astype(jnp.int32)
        for part in (s, t):
            mine = place(centre[part].astype(F32), columns, own_frame[0], own_frame[2], None)
            other = place(
                first[part].astype(F32), columns, first_frame[0], first_frame[2], before == odd
            )
            for c in range(columns):
                partial[c, part] = mine[c] + other[c]


def fold_kernel(partial, second, second_info, out):
    columns, height, tile = out.shape
    odd = lax.axis_index("row") % 2
    source, row, col = (second_info[r : r + 1] for r in range(3))
    for r in range(0, height, STRIP):
        s = pl.ds(r, STRIP)
        before = (iota((STRIP, tile), 0) + r % tile < row).astype(jnp.int32)
        other = place(second[s].astype(F32), columns, source, col, before == 1 - odd)
        for c in range(columns):
            out[c, s] = (partial[c, s] + other[c]).astype(BF16)


def call(kernel, name, out_shape, in_specs, scratch, flops, moved, *args):
    args = [
        pltpu.with_memory_space_constraint(arg, pltpu.HBM) if spec is HBM else arg
        for arg, spec in zip(args, in_specs)
    ]
    return pl.pallas_call(
        kernel,
        out_shape=out_shape,
        in_specs=in_specs,
        out_specs=jax.tree.map(lambda _: VMEM, out_shape),
        scratch_shapes=scratch,
        compiler_params=pltpu.CompilerParams(vmem_limit_bytes=32 * 2**20),
        cost_estimate=pl.CostEstimate(flops=flops, bytes_accessed=moved, transcendentals=0),
        name=name,
    )(*args)


def per_device(specimen, probe, measured, centers, frame_counts, helper_cols):
    extent = probe.shape[-1]
    half = extent // 2
    tile = specimen.shape[1]
    modes = probe.shape[0]
    columns = lax.axis_size("col")
    height = 2 * tile
    part = jax.ShapeDtypeStruct((height, extent), BF16)
    dma = pltpu.SemaphoreType.DMA

    packed = call(
        pack_kernel, "pack",
        jax.ShapeDtypeStruct((height + INFO, tile), BF16),
        [HBM, HBM, SMEM, HBM],
        [
            pltpu.VMEM(specimen.shape, F32),
            pltpu.SMEM(centers.shape, jnp.int32),
            pltpu.SMEM(helper_cols.shape, jnp.int32),
            dma((3,)),
        ],
        10**5, 2**19,
        specimen, centers, frame_counts, helper_cols,
    )
    band = lax.all_gather(packed, "col")

    rows = lax.axis_size("row")
    swaps = []
    for start in (0, 1):
        pairs = [(i, i + 1) for i in range(start, rows - 1, 2)]
        swaps.append(pairs + [(b, a) for a, b in pairs])
    second = lax.ppermute(band, "row", swaps[1])
    first = lax.ppermute(band, "row", swaps[0])
    tables = dft_tables(extent)
    prepared = call(
        prepare_kernel, "prepare",
        (
            jax.ShapeDtypeStruct((INFO, extent), BF16),
            jax.ShapeDtypeStruct((extent, extent), F32),
            jax.ShapeDtypeStruct((8, extent, extent), BF16),
            jax.ShapeDtypeStruct(probe.shape, F32),
            jax.ShapeDtypeStruct((modes, 2, tile, extent), F32),
        ),
        [VMEM, HBM, HBM, HBM],
        [
            pltpu.VMEM(measured.shape, F32),
            pltpu.VMEM(tables.shape, BF16),
            pltpu.VMEM(probe.shape, F32),
            pltpu.VMEM((extent // 4, 8, extent), F32),
            dma((3,)),
        ],
        10**9, 2**22,
        band, probe, measured, tables,
    )
    full = (modes, 2, extent, extent)
    to_second, to_first, mixed_back = call(
        frame_kernel, "frame",
        (part, part, jax.ShapeDtypeStruct(full, BF16)),
        [VMEM] * 7,
        [
            pltpu.VMEM((2, tile, extent), F32),
            pltpu.VMEM((modes, 2, half, extent), BF16),
            pltpu.VMEM((modes, 2, half, extent), F32),
            pltpu.VMEM(full, BF16),
            pltpu.VMEM(full, F32),
            pltpu.VMEM(full, BF16),
            pltpu.VMEM(full, F32),
            pltpu.VMEM((modes, extent, extent), F32),
        ],
        2 * 10**9, 2**22,
        first, second, *prepared,
    )
    from_second = lax.ppermute(to_second, "row", swaps[1])
    from_first = lax.ppermute(to_first, "row", swaps[0])
    partial, second_info = call(
        finish_kernel, "finish",
        (
            jax.ShapeDtypeStruct((columns, height, tile), F32),
            jax.ShapeDtypeStruct((8, tile), jnp.int32),
        ),
        [VMEM] * 7,
        [pltpu.VMEM((modes, extent, extent), F32), pltpu.VMEM((height, extent), BF16)],
        5 * 10**8, 2**22,
        band, first, second, mixed_back, prepared[2], prepared[3], from_first,
    )
    summed = call(
        fold_kernel, "fold",
        jax.ShapeDtypeStruct((columns, height, tile), BF16),
        [VMEM] * 3,
        [],
        10**7, 2**20,
        partial, from_second, second_info,
    )
    shares = lax.all_to_all(summed, "col", split_axis=0, concat_axis=0, tiled=True)
    return jnp.sum(shares.astype(F32), axis=0).reshape(2, tile, tile)


def solution(mesh):
    return jax.shard_map(
        per_device,
        mesh=mesh,
        in_specs=(
            P(None, "row", "col"),
            P(),
            P("row", "col", None, None, None),
            P("row", "col", None, None),
            P("row", "col"),
            P("row", "col", None),
        ),
        out_specs=P(None, "row", "col"),
        check_vma=False,
    )
```

```python
import functools
import math

import jax
import jax.numpy as jnp
import numpy as np
from jax import lax
from jax.experimental import pallas as pl
from jax.experimental.pallas import tpu as pltpu
from jax.sharding import PartitionSpec as P

F32 = jnp.float32
BF16 = jnp.bfloat16
INFO = 16
STRIP = 32
VMEM = pl.BlockSpec(memory_space=pltpu.VMEM)
SMEM = pl.BlockSpec(memory_space=pltpu.SMEM)
HBM = pl.BlockSpec(memory_space=pltpu.HBM)


def dft_tables(extent):
    half = extent // 2
    steps = np.arange(extent, dtype=np.int32)
    angles = (steps[:, None] * steps[None, :] % extent).astype(np.float32)
    angles = angles * np.float32(2.0 * math.pi / extent)
    scaling = np.float32(1.0 / math.sqrt(extent))
    real = (np.cos(angles) * scaling).astype(BF16)
    imag = (-np.sin(angles) * scaling).astype(BF16)
    tables = []
    for parity in (0, 1):
        re, im = real[:half, parity::2], imag[:half, parity::2]
        right = np.concatenate(
            [np.concatenate([re, im], 1), np.concatenate([-im, re], 1)], 0
        )
        tables += [right, np.ascontiguousarray(right.T)]
    return jnp.asarray(np.stack(tables))


def dot(a, b):
    return jnp.dot(a, b, preferred_element_type=F32)


def quarters(tl, tr, bl, br):
    return jnp.concatenate(
        [jnp.concatenate([tl, tr], 1), jnp.concatenate([bl, br], 1)], 0
    )


def iota(shape, dim):
    return lax.broadcasted_iota(jnp.int32, shape, dim)


def fetch(pairs, sems):
    copies = [
        pltpu.make_async_copy(source, target, sems.at[i])
        for i, (source, target) in enumerate(pairs)
    ]
    for copy in copies:
        copy.start()
    return copies


def pack_kernel(specimen, centers, cnt, helpers, out, tile_v, cen, hlp, sems):
    copies = fetch(((specimen, tile_v), (centers, cen), (helpers, hlp)), sems)
    for copy in copies:
        copy.wait()
    tile = tile_v.shape[1]
    lanes = tile_v.shape[2]
    rows, cols = iota((INFO, lanes), 0), iota((INFO, lanes), 1)
    info = jnp.where(rows == 0, -1.0, 0.0)
    for j in range(centers.shape[2]):
        helper = jnp.where(j < cnt[0, 0], hlp[0, 0, j], -1)
        for r, value in enumerate((helper, cen[0, 0, j, 0], cen[0, 0, j, 1])):
            info = jnp.where((rows == r) & (cols == j), value.astype(F32), info)
    info = info.astype(BF16)
    for p in range(2):
        out[p * tile : (p + 1) * tile] = tile_v[p].astype(BF16)
    out[2 * tile :] = info


def gather_columns(get, source, col, columns, shape):
    lane = iota(shape, 1)
    beside = own = jnp.zeros(shape, F32)
    for c in range(columns):
        block = get(c)
        near = ((source == c + 1) & (lane >= col)) | ((source == c - 1) & (lane < col))
        beside = jnp.where(near, block, beside)
        own = jnp.where(source == c, block, own)
    return jnp.concatenate([beside, own], 1)


def first_product(probe, patch, tables):
    half = patch[0].shape[1] // 2
    wr = probe[0] * patch[0] - probe[1] * patch[1]
    wi = probe[0] * patch[1] + probe[1] * patch[0]
    out = []
    for sign, table in zip((1, -1), tables):
        folded = jnp.concatenate(
            [wr[:, :half] + sign * wr[:, half:], wi[:, :half] + sign * wi[:, half:]], 1
        )
        out.append(dot(folded.astype(BF16), table))
    return out


def frame_of(band):
    columns, height, lanes = band.shape
    me = lax.axis_index("col").astype(F32)
    code = jnp.zeros((1, lanes), F32)
    for c in range(columns):
        info = band[c, height - INFO :].astype(F32)
        hit = info[0:1] == me
        code += jnp.where(hit, (c * lanes + info[1:2]) * lanes + info[2:3], 0.0)
    code = jnp.sum(code).astype(jnp.int32)
    return code // (lanes * lanes), code // lanes % lanes, code % lanes


def prepare_kernel(
    band, probe, measured, tables,
    info_out, amplitude, tables_out, probe_out, half_out, raw, raw_tables, raw_probe, groups, sems,
):
    copies = fetch(
        ((measured, raw), (tables, raw_tables), (probe, raw_probe)), sems
    )
    columns = band.shape[0]
    tile = (band.shape[1] - INFO) // 2
    extent = raw.shape[-1]
    half = extent // 2
    modes = raw_probe.shape[0]
    source, row, col = frame_of(band)
    which = iota((INFO, extent), 0)
    info = jnp.where(which == 0, source, jnp.where(which == 1, col, row))
    info_out[...] = info.astype(F32).astype(BF16)

    shape = (extent, extent)

    def original(i):
        return jnp.where(i < half, 2 * i, 2 * (i - half) + 1)

    copies[0].wait()
    sort = (iota(shape, 1) == original(iota(shape, 0))).astype(F32).astype(BF16)
    sort_t = (iota(shape, 0) == original(iota(shape, 1))).astype(F32).astype(BF16)
    value = raw[0, 0, 0]
    coarse = value.astype(BF16)
    fine = (value - coarse.astype(F32)).astype(BF16)
    amplitude[...] = sum(
        dot(dot(sort, part).astype(BF16), sort_t) for part in (coarse, fine)
    )

    def roller(old, new, shift, parity):
        wrapped = new % half < shift
        hit = (old + shift - jnp.where(old % half + shift >= half, half, 0)) == new
        sign = jnp.where(wrapped, -1.0, 1.0) if parity else 1.0
        return jnp.where(hit, sign, 0.0).astype(BF16)

    copies[1].wait()
    i, j = iota(shape, 0), iota(shape, 1)
    for parity in range(2):
        right, left = raw_tables[2 * parity], raw_tables[2 * parity + 1]
        for axis, shift in enumerate((col, row)):
            rolled = dot(left, roller(i, j, shift, parity)).astype(BF16)
            rolled_t = dot(roller(j, i, shift, parity), right).astype(BF16)
            tables_out[4 * axis + parity] = rolled_t if axis == 0 else rolled
            tables_out[4 * axis + 2 + parity] = rolled if axis == 0 else rolled_t

    copies[2].wait()
    count = extent // 8
    base = row // 8
    step = row % 8
    lane = iota((extent, half), 1)
    sub = iota((count, 8, extent), 1)
    for k in range(modes):
        for p in range(2):
            lo = pltpu.roll(raw_probe[k, p, :, :half], col, 1)
            hi = pltpu.roll(raw_probe[k, p, :, half:], col, 1)
            turned = jnp.concatenate(
                [jnp.where(lane < col, hi, lo), jnp.where(lane < col, lo, hi)], 1
            )
            turned = pltpu.roll(turned.reshape(count, 8, extent), step, 1)
            turned = jnp.where(
                sub < step, jnp.concatenate([turned[-1:], turned[:-1]], 0), turned
            )
            groups[:count] = turned
            groups[count:] = turned
            probe_out[k, p] = groups[pl.ds(count - base, count)].reshape(extent, extent)

    patch = [
        gather_columns(
            lambda c: band[c, p * tile : (p + 1) * tile].astype(F32),
            source, col, columns, (tile, tile),
        )
        for p in range(2)
    ]
    for k in range(modes):
        products = first_product(
            [probe_out[k, p, half:] for p in range(2)], patch, (tables_out[0], tables_out[1])
        )
        for parity in range(2):
            half_out[k, parity] = products[parity]


def frame_kernel(
    first, second, info, amplitude, tables, probe, half_own,
    to_rows, mixed_back, patch, folded, half_far, mixed, far, corrected, product, chi,
):
    columns = first.shape[0]
    tile = (first.shape[1] - INFO) // 2
    extent = probe.shape[-1]
    half = extent // 2
    modes = probe.shape[0]
    odd = lax.axis_index("row") % 2
    source, col, row = (
        info[r : r + 1, :tile].astype(F32).astype(jnp.int32) for r in range(3)
    )
    strips = [pl.ds(r, STRIP) for r in range(0, half, STRIP)]
    lower = [pl.ds(half + r, STRIP) for r in range(0, half, STRIP)]

    def split(x):
        return x[:, :half], x[:, half:]

    def join(x, y):
        return jnp.concatenate([x, y], 1).astype(BF16)

    def gather(s):
        rows = iota((STRIP, tile), 0) + s.start
        from_first = (rows >= row).astype(jnp.int32) == odd
        for p in range(2):
            part = pl.ds(p * tile + s.start, STRIP)
            patch[p, s] = gather_columns(
                lambda c: jnp.where(
                    from_first, first[c, part].astype(F32), second[c, part].astype(F32)
                ),
                source, col, columns, (STRIP, tile),
            )

    def wave(k):
        for s in strips:
            pr, pi, xr, xi = probe[k, 0, s], probe[k, 1, s], patch[0, s], patch[1, s]
            re = split(pr * xr - pi * xi)
            im = split(pr * xi + pi * xr)
            folded[k, 0, s] = join(re[0] + re[1], im[0] + im[1])
            folded[k, 1, s] = join(re[0] - re[1], im[0] - im[1])

    def along_rows(k):
        for q in range(2):
            half_far[k, q] = dot(folded[k, q], tables[q])

    def mix(k):
        for s, t in zip(strips, lower):
            even, odds = half_far[k, 0, s], half_far[k, 1, s]
            even_own, odds_own = half_own[k, 0, s], half_own[k, 1, s]
            for q, (e, o) in enumerate(
                ((even + even_own, odds + odds_own), (even - even_own, odds - odds_own))
            ):
                (er, ei), (our, oui) = split(e), split(o)
                mixed[k, q, s] = join(er, our)
                mixed[k, q, t] = join(ei, oui)

    def along_columns(k, q):
        far[k, q] = dot(tables[4 + q], mixed[k, q])

    def correct(q, which):
        for s, t in list(zip(strips, lower))[which]:
            re = [far[k, q, s] for k in range(modes)]
            im = [far[k, q, t] for k in range(modes)]
            intensity = sum(x * x for x in re + im)
            size = amplitude[pl.ds(q * half + s.start, STRIP)]
            factor = 1.0 - size * lax.rsqrt(jnp.maximum(intensity, 0.25))
            out = pl.ds(q * half + s.start, STRIP)
            for k in range(modes):
                (re_even, re_odd), (im_even, im_odd) = split(re[k] * factor), split(im[k] * factor)
                corrected[k, 0, out] = join(re_even, im_even)
                corrected[k, 1, out] = join(re_odd, im_odd)

    def back_along_rows(k, q):
        part = pl.ds(q * half, half)
        for c in range(2):
            product[k, c, part] = dot(corrected[k, c, part], tables[2 + c])

    def mix_back(k, q):
        for s, t in zip(strips, lower):
            part = pl.ds(q * half + s.start, STRIP)
            x, y = product[k, 0, part], product[k, 1, part]
            (lr, li), (hr, hi) = split(x + y), split(x - y)
            mixed_back[k, q, s] = join(lr, hr)
            mixed_back[k, q, t] = join(li, hi)

    both_back = jnp.concatenate([tables[6], tables[7]], 1)

    def back_along_columns(k):
        chi[k] = dot(both_back, mixed_back[k].reshape(2 * extent, extent))

    for s in strips:
        gather(s)
    for k in range(modes + 1):
        if k < modes:
            wave(k)
            along_rows(k)
        if k > 0:
            mix(k - 1)
            along_columns(k - 1, 0)
    share = -(-len(strips) // modes)
    for k in range(modes):
        along_columns(k, 1)
        correct(0, slice(k * share, (k + 1) * share))
    for k in range(modes):
        back_along_rows(k, 0)
        correct(1, slice(k * share, (k + 1) * share))
    for k in range(modes):
        mix_back(k, 0)
        back_along_rows(k, 1)
    for k in range(modes):
        mix_back(k, 1)
        back_along_columns(k)
    for s, t in zip(strips, lower):
        accumulate(to_rows, chi, probe, s, t, s)


def accumulate(out, chi, probe, s, t, rows):
    tile = out.shape[0] // 2
    re = im = 0.0
    for k in range(probe.shape[0]):
        pr, pi = probe[k, 0, rows], probe[k, 1, rows]
        cr, ci = chi[k, s], chi[k, t]
        re += pr * cr + pi * ci
        im += pr * ci - pi * cr
    out[s] = re.astype(BF16)
    out[pl.ds(tile + s.start, STRIP)] = im.astype(BF16)


def place(block, columns, source, col, taken):
    tile = block.shape[1] // 2
    beside, own = block[:, :tile], block[:, tile:]
    lane = iota(own.shape, 1)
    if taken is not None:
        beside, own = jnp.where(taken, beside, 0.0), jnp.where(taken, own, 0.0)
    out = []
    for c in range(columns):
        near = ((source == c + 1) & (lane >= col)) | ((source == c - 1) & (lane < col))
        out.append(jnp.where(near, beside, 0.0) + jnp.where(source == c, own, 0.0))
    return out


def finish_kernel(
    band, first_band, second_band, mixed_back, tables, probe, first,
    partial, second_info, chi, centre,
):
    columns = band.shape[0]
    extent = probe.shape[-1]
    tile = (band.shape[1] - INFO) // 2
    odd = lax.axis_index("row") % 2
    own_frame, first_frame, second_frame = (
        frame_of(b) for b in (band, first_band, second_band)
    )
    which = iota(second_info.shape, 0)
    second_info[...] = jnp.where(
        which == 0, second_frame[0], jnp.where(which == 1, second_frame[1], second_frame[2])
    )
    both_back = jnp.concatenate([tables[6], -tables[7]], 1)
    for k in range(probe.shape[0]):
        chi[k] = dot(both_back, mixed_back[k].reshape(2 * extent, extent))
    for r in range(0, tile, STRIP):
        s, t = pl.ds(r, STRIP), pl.ds(tile + r, STRIP)
        accumulate(centre, chi, probe, s, t, t)
        before = (iota((STRIP, tile), 0) + r < first_frame[1]).astype(jnp.int32)
        for part in (s, t):
            mine = place(centre[part].astype(F32), columns, own_frame[0], own_frame[2], None)
            other = place(
                first[part].astype(F32), columns, first_frame[0], first_frame[2], before == odd
            )
            for c in range(columns):
                partial[c, part] = mine[c] + other[c]


def fold_kernel(partial, second, second_info, out):
    columns, height, tile = out.shape
    odd = lax.axis_index("row") % 2
    source, row, col = (second_info[r : r + 1] for r in range(3))
    for r in range(0, height, STRIP):
        s = pl.ds(r, STRIP)
        before = (iota((STRIP, tile), 0) + r % tile < row).astype(jnp.int32)
        other = place(second[s].astype(F32), columns, source, col, before == 1 - odd)
        for c in range(columns):
            out[c, s] = (partial[c, s] + other[c]).astype(BF16)


def call(kernel, name, out_shape, in_specs, scratch, flops, moved, *args):
    args = [
        pltpu.with_memory_space_constraint(arg, pltpu.HBM) if spec is HBM else arg
        for arg, spec in zip(args, in_specs)
    ]
    return pl.pallas_call(
        kernel,
        out_shape=out_shape,
        in_specs=in_specs,
        out_specs=jax.tree.map(lambda _: VMEM, out_shape),
        scratch_shapes=scratch,
        compiler_params=pltpu.CompilerParams(vmem_limit_bytes=32 * 2**20),
        cost_estimate=pl.CostEstimate(flops=flops, bytes_accessed=moved, transcendentals=0),
        name=name,
    )(*args)


def per_device(specimen, probe, measured, centers, frame_counts, helper_cols):
    extent = probe.shape[-1]
    half = extent // 2
    tile = specimen.shape[1]
    modes = probe.shape[0]
    columns = lax.axis_size("col")
    height = 2 * tile
    part = jax.ShapeDtypeStruct((height, extent), BF16)
    dma = pltpu.SemaphoreType.DMA

    packed = call(
        pack_kernel, "pack",
        jax.ShapeDtypeStruct((height + INFO, tile), BF16),
        [HBM, HBM, SMEM, HBM],
        [
            pltpu.VMEM(specimen.shape, F32),
            pltpu.SMEM(centers.shape, jnp.int32),
            pltpu.SMEM(helper_cols.shape, jnp.int32),
            dma((3,)),
        ],
        10**5, 2**19,
        specimen, centers, frame_counts, helper_cols,
    )
    band = lax.all_gather(packed, "col")

    rows = lax.axis_size("row")
    swaps = []
    for start in (0, 1):
        pairs = [(i, i + 1) for i in range(start, rows - 1, 2)]
        swaps.append(pairs + [(b, a) for a, b in pairs])
    second = lax.ppermute(band, "row", swaps[1])
    first = lax.ppermute(band, "row", swaps[0])
    tables = dft_tables(extent)
    prepared = call(
        prepare_kernel, "prepare",
        (
            jax.ShapeDtypeStruct((INFO, extent), BF16),
            jax.ShapeDtypeStruct((extent, extent), F32),
            jax.ShapeDtypeStruct((8, extent, extent), BF16),
            jax.ShapeDtypeStruct(probe.shape, F32),
            jax.ShapeDtypeStruct((modes, 2, tile, extent), F32),
        ),
        [VMEM, HBM, HBM, HBM],
        [
            pltpu.VMEM(measured.shape, F32),
            pltpu.VMEM(tables.shape, BF16),
            pltpu.VMEM(probe.shape, F32),
            pltpu.VMEM((extent // 4, 8, extent), F32),
            dma((3,)),
        ],
        10**9, 2**22,
        band, probe, measured, tables,
    )
    full = (modes, 2, extent, extent)
    to_rows, mixed_back = call(
        frame_kernel, "frame",
        (part, jax.ShapeDtypeStruct(full, BF16)),
        [VMEM] * 7,
        [
            pltpu.VMEM((2, tile, extent), F32),
            pltpu.VMEM((modes, 2, half, extent), BF16),
            pltpu.VMEM((modes, 2, half, extent), F32),
            pltpu.VMEM(full, BF16),
            pltpu.VMEM(full, F32),
            pltpu.VMEM(full, BF16),
            pltpu.VMEM(full, F32),
            pltpu.VMEM((modes, extent, extent), F32),
        ],
        2 * 10**9, 2**22,
        first, second, *prepared,
    )
    from_first = lax.ppermute(to_rows, "row", swaps[0])
    from_second = lax.ppermute(to_rows, "row", swaps[1])
    partial, second_info = call(
        finish_kernel, "finish",
        (
            jax.ShapeDtypeStruct((columns, height, tile), F32),
            jax.ShapeDtypeStruct((8, tile), jnp.int32),
        ),
        [VMEM] * 7,
        [pltpu.VMEM((modes, extent, extent), F32), pltpu.VMEM((height, extent), BF16)],
        5 * 10**8, 2**22,
        band, first, second, mixed_back, prepared[2], prepared[3], from_first,
    )
    summed = call(
        fold_kernel, "fold",
        jax.ShapeDtypeStruct((columns, height, tile), BF16),
        [VMEM] * 3,
        [],
        10**7, 2**20,
        partial, from_second, second_info,
    )
    shares = lax.all_to_all(summed, "col", split_axis=0, concat_axis=0, tiled=True)
    return jnp.sum(shares.astype(F32), axis=0).reshape(2, tile, tile)


def solution(mesh):
    return jax.shard_map(
        per_device,
        mesh=mesh,
        in_specs=(
            P(None, "row", "col"),
            P(),
            P("row", "col", None, None, None),
            P("row", "col", None, None),
            P("row", "col"),
            P("row", "col", None),
        ),
        out_specs=P(None, "row", "col"),
        check_vma=False,
    )
```

```python
import functools
import math

import jax
import jax.numpy as jnp
import numpy as np
from jax import lax
from jax.experimental import pallas as pl
from jax.experimental.pallas import tpu as pltpu
from jax.sharding import PartitionSpec as P

F32 = jnp.float32
BF16 = jnp.bfloat16
INFO = 16
STRIP = 16
VMEM = pl.BlockSpec(memory_space=pltpu.VMEM)
SMEM = pl.BlockSpec(memory_space=pltpu.SMEM)
HBM = pl.BlockSpec(memory_space=pltpu.HBM)


def dft_tables(extent):
    half = extent // 2
    steps = np.arange(extent, dtype=np.int32)
    angles = (steps[:, None] * steps[None, :] % extent).astype(np.float32)
    angles = angles * np.float32(2.0 * math.pi / extent)
    scaling = np.float32(1.0 / math.sqrt(extent))
    real = (np.cos(angles) * scaling).astype(BF16)
    imag = (-np.sin(angles) * scaling).astype(BF16)
    tables = []
    for parity in (0, 1):
        re, im = real[:half, parity::2], imag[:half, parity::2]
        right = np.concatenate(
            [np.concatenate([re, im], 1), np.concatenate([-im, re], 1)], 0
        )
        tables += [right, np.ascontiguousarray(right.T)]
    return jnp.asarray(np.stack(tables))


def dot(a, b):
    return jnp.dot(a, b, preferred_element_type=F32)


def quarters(tl, tr, bl, br):
    return jnp.concatenate(
        [jnp.concatenate([tl, tr], 1), jnp.concatenate([bl, br], 1)], 0
    )


def iota(shape, dim):
    return lax.broadcasted_iota(jnp.int32, shape, dim)


def fetch(pairs, sems):
    copies = [
        pltpu.make_async_copy(source, target, sems.at[i])
        for i, (source, target) in enumerate(pairs)
    ]
    for copy in copies:
        copy.start()
    return copies


def pack_kernel(specimen, centers, cnt, helpers, out, tile_v, cen, hlp, sems):
    copies = fetch(((specimen, tile_v), (centers, cen), (helpers, hlp)), sems)
    for copy in copies:
        copy.wait()
    tile = tile_v.shape[1]
    lanes = tile_v.shape[2]
    rows, cols = iota((INFO, lanes), 0), iota((INFO, lanes), 1)
    info = jnp.where(rows == 0, -1.0, 0.0)
    for j in range(centers.shape[2]):
        helper = jnp.where(j < cnt[0, 0], hlp[0, 0, j], -1)
        for r, value in enumerate((helper, cen[0, 0, j, 0], cen[0, 0, j, 1])):
            info = jnp.where((rows == r) & (cols == j), value.astype(F32), info)
    info = info.astype(BF16)
    for p in range(2):
        out[p * tile : (p + 1) * tile] = tile_v[p].astype(BF16)
    out[2 * tile :] = info


def gather_columns(get, source, col, columns, shape):
    lane = iota(shape, 1)
    beside = own = jnp.zeros(shape, F32)
    for c in range(columns):
        block = get(c)
        near = ((source == c + 1) & (lane >= col)) | ((source == c - 1) & (lane < col))
        beside = jnp.where(near, block, beside)
        own = jnp.where(source == c, block, own)
    return jnp.concatenate([beside, own], 1)


def first_product(probe, patch, tables):
    half = patch[0].shape[1] // 2
    wr = probe[0] * patch[0] - probe[1] * patch[1]
    wi = probe[0] * patch[1] + probe[1] * patch[0]
    out = []
    for sign, table in zip((1, -1), tables):
        folded = jnp.concatenate(
            [wr[:, :half] + sign * wr[:, half:], wi[:, :half] + sign * wi[:, half:]], 1
        )
        out.append(dot(folded.astype(BF16), table))
    return out


def frame_of(band):
    columns, height, lanes = band.shape
    me = lax.axis_index("col").astype(F32)
    code = jnp.zeros((1, lanes), F32)
    for c in range(columns):
        info = band[c, height - INFO :].astype(F32)
        hit = info[0:1] == me
        code += jnp.where(hit, (c * lanes + info[1:2]) * lanes + info[2:3], 0.0)
    code = jnp.sum(code).astype(jnp.int32)
    return code // (lanes * lanes), code // lanes % lanes, code % lanes


def prepare_kernel(
    band, probe, measured, tables,
    info_out, amplitude, tables_out, probe_out, half_out, raw, raw_tables, raw_probe, groups, sems,
):
    copies = fetch(
        ((measured, raw), (tables, raw_tables), (probe, raw_probe)), sems
    )
    columns = band.shape[0]
    tile = (band.shape[1] - INFO) // 2
    extent = raw.shape[-1]
    half = extent // 2
    modes = raw_probe.shape[0]
    source, row, col = frame_of(band)
    which = iota((INFO, extent), 0)
    info = jnp.where(which == 0, source, jnp.where(which == 1, col, row))
    info_out[...] = info.astype(F32).astype(BF16)

    shape = (extent, extent)

    def original(i):
        return jnp.where(i < half, 2 * i, 2 * (i - half) + 1)

    copies[0].wait()
    sort = (iota(shape, 1) == original(iota(shape, 0))).astype(F32).astype(BF16)
    sort_t = (iota(shape, 0) == original(iota(shape, 1))).astype(F32).astype(BF16)
    value = raw[0, 0, 0]
    coarse = value.astype(BF16)
    fine = (value - coarse.astype(F32)).astype(BF16)
    amplitude[...] = sum(
        dot(dot(sort, part).astype(BF16), sort_t) for part in (coarse, fine)
    )

    def roller(old, new, shift, parity):
        wrapped = new % half < shift
        hit = (old + shift - jnp.where(old % half + shift >= half, half, 0)) == new
        sign = jnp.where(wrapped, -1.0, 1.0) if parity else 1.0
        return jnp.where(hit, sign, 0.0).astype(BF16)

    copies[1].wait()
    i, j = iota(shape, 0), iota(shape, 1)
    for parity in range(2):
        right, left = raw_tables[2 * parity], raw_tables[2 * parity + 1]
        for axis, shift in enumerate((col, row)):
            rolled = dot(left, roller(i, j, shift, parity)).astype(BF16)
            rolled_t = dot(roller(j, i, shift, parity), right).astype(BF16)
            tables_out[4 * axis + parity] = rolled_t if axis == 0 else rolled
            tables_out[4 * axis + 2 + parity] = rolled if axis == 0 else rolled_t

    copies[2].wait()
    count = extent // 8
    base = row // 8
    step = row % 8
    lane = iota((extent, half), 1)
    sub = iota((count, 8, extent), 1)
    for k in range(modes):
        for p in range(2):
            lo = pltpu.roll(raw_probe[k, p, :, :half], col, 1)
            hi = pltpu.roll(raw_probe[k, p, :, half:], col, 1)
            turned = jnp.concatenate(
                [jnp.where(lane < col, hi, lo), jnp.where(lane < col, lo, hi)], 1
            )
            turned = pltpu.roll(turned.reshape(count, 8, extent), step, 1)
            turned = jnp.where(
                sub < step, jnp.concatenate([turned[-1:], turned[:-1]], 0), turned
            )
            groups[:count] = turned
            groups[count:] = turned
            probe_out[k, p] = groups[pl.ds(count - base, count)].reshape(extent, extent)

    patch = [
        gather_columns(
            lambda c: band[c, p * tile : (p + 1) * tile].astype(F32),
            source, col, columns, (tile, tile),
        )
        for p in range(2)
    ]
    for k in range(modes):
        products = first_product(
            [probe_out[k, p, half:] for p in range(2)], patch, (tables_out[0], tables_out[1])
        )
        for parity in range(2):
            half_out[k, parity] = products[parity]


def near_kernel(first, info, near):
    columns = first.shape[0]
    _, tile, _ = near.shape
    source, col = (info[r : r + 1, :tile].astype(F32).astype(jnp.int32) for r in range(2))
    for p in range(2):
        for r in range(0, tile, STRIP):
            part = pl.ds(p * tile + r, STRIP)
            near[p, pl.ds(r, STRIP)] = gather_columns(
                lambda c: first[c, part].astype(F32), source, col, columns, (STRIP, tile)
            )


def frame_kernel(
    near, second, info, amplitude, tables, probe, half_own,
    to_rows, mixed_back, patch, folded, half_far, mixed, far, corrected, product, chi,
):
    columns = second.shape[0]
    tile = (second.shape[1] - INFO) // 2
    extent = probe.shape[-1]
    half = extent // 2
    modes = probe.shape[0]
    odd = lax.axis_index("row") % 2
    source, col = (info[r : r + 1, :tile].astype(F32).astype(jnp.int32) for r in range(2))
    center_row = info[2:3].astype(F32).astype(jnp.int32)
    strips = [pl.ds(r, STRIP) for r in range(0, half, STRIP)]
    lower = [pl.ds(half + r, STRIP) for r in range(0, half, STRIP)]

    def split(x):
        return x[:, :half], x[:, half:]

    def join(x, y):
        return jnp.concatenate([x, y], 1).astype(BF16)

    def gather(s):
        rows = iota((STRIP, extent), 0) + s.start
        from_first = (rows >= center_row).astype(jnp.int32) == odd
        for p in range(2):
            part = pl.ds(p * tile + s.start, STRIP)
            far_rows = gather_columns(
                lambda c: second[c, part].astype(F32),
                source, col, columns, (STRIP, tile),
            )
            patch[p, s] = jnp.where(from_first, near[p, s], far_rows)

    def wave(k):
        for s in strips:
            pr, pi, xr, xi = probe[k, 0, s], probe[k, 1, s], patch[0, s], patch[1, s]
            re = split(pr * xr - pi * xi)
            im = split(pr * xi + pi * xr)
            folded[k, 0, s] = join(re[0] + re[1], im[0] + im[1])
            folded[k, 1, s] = join(re[0] - re[1], im[0] - im[1])

    def along_rows(k):
        for q in range(2):
            half_far[k, q] = dot(folded[k, q], tables[q])

    def mix(k):
        for s, t in zip(strips, lower):
            even, odds = half_far[k, 0, s], half_far[k, 1, s]
            even_own, odds_own = half_own[k, 0, s], half_own[k, 1, s]
            for q, (e, o) in enumerate(
                ((even + even_own, odds + odds_own), (even - even_own, odds - odds_own))
            ):
                (er, ei), (our, oui) = split(e), split(o)
                mixed[k, q, s] = join(er, our)
                mixed[k, q, t] = join(ei, oui)

    def along_columns(k, q):
        far[k, q] = dot(tables[4 + q], mixed[k, q])

    def correct(q, which):
        for s, t in list(zip(strips, lower))[which]:
            re = [far[k, q, s] for k in range(modes)]
            im = [far[k, q, t] for k in range(modes)]
            intensity = sum(x * x for x in re + im)
            size = amplitude[pl.ds(q * half + s.start, STRIP)]
            factor = 1.0 - size * lax.rsqrt(jnp.maximum(intensity, 0.25))
            out = pl.ds(q * half + s.start, STRIP)
            for k in range(modes):
                (re_even, re_odd), (im_even, im_odd) = split(re[k] * factor), split(im[k] * factor)
                corrected[k, 0, out] = join(re_even, im_even)
                corrected[k, 1, out] = join(re_odd, im_odd)

    def back_along_rows(k, q):
        part = pl.ds(q * half, half)
        for c in range(2):
            product[k, c, part] = dot(corrected[k, c, part], tables[2 + c])

    def mix_back(k, q):
        for s, t in zip(strips, lower):
            part = pl.ds(q * half + s.start, STRIP)
            x, y = product[k, 0, part], product[k, 1, part]
            (lr, li), (hr, hi) = split(x + y), split(x - y)
            mixed_back[k, q, s] = join(lr, hr)
            mixed_back[k, q, t] = join(li, hi)

    both_back = jnp.concatenate([tables[6], tables[7]], 1)

    def back_along_columns(k):
        chi[k] = dot(both_back, mixed_back[k].reshape(2 * extent, extent))

    for s in strips:
        gather(s)
    for k in range(modes + 1):
        if k < modes:
            wave(k)
            along_rows(k)
        if k > 0:
            mix(k - 1)
            along_columns(k - 1, 0)
    share = -(-len(strips) // modes)
    for k in range(modes):
        along_columns(k, 1)
        correct(0, slice(k * share, (k + 1) * share))
    for k in range(modes):
        back_along_rows(k, 0)
        correct(1, slice(k * share, (k + 1) * share))
    for k in range(modes):
        mix_back(k, 0)
        back_along_rows(k, 1)
    for k in range(modes):
        mix_back(k, 1)
        back_along_columns(k)
    for s, t in zip(strips, lower):
        accumulate(to_rows, chi, probe, s, t, s)


def accumulate(out, chi, probe, s, t, rows):
    tile = out.shape[0] // 2
    re = im = 0.0
    for k in range(probe.shape[0]):
        pr, pi = probe[k, 0, rows], probe[k, 1, rows]
        cr, ci = chi[k, s], chi[k, t]
        re += pr * cr + pi * ci
        im += pr * ci - pi * cr
    out[s] = re.astype(BF16)
    out[pl.ds(tile + s.start, STRIP)] = im.astype(BF16)


def place(block, columns, source, col, taken):
    tile = block.shape[1] // 2
    beside, own = block[:, :tile], block[:, tile:]
    lane = iota(own.shape, 1)
    if taken is not None:
        beside, own = jnp.where(taken, beside, 0.0), jnp.where(taken, own, 0.0)
    out = []
    for c in range(columns):
        near = ((source == c + 1) & (lane >= col)) | ((source == c - 1) & (lane < col))
        out.append(jnp.where(near, beside, 0.0) + jnp.where(source == c, own, 0.0))
    return out


def finish_kernel(
    band, first_band, second_band, mixed_back, tables, probe, first,
    partial, second_info, chi, centre,
):
    columns = band.shape[0]
    extent = probe.shape[-1]
    tile = (band.shape[1] - INFO) // 2
    odd = lax.axis_index("row") % 2
    own_frame, first_frame, second_frame = (
        frame_of(b) for b in (band, first_band, second_band)
    )
    which = iota(second_info.shape, 0)
    second_info[...] = jnp.where(
        which == 0, second_frame[0], jnp.where(which == 1, second_frame[1], second_frame[2])
    )
    both_back = jnp.concatenate([tables[6], -tables[7]], 1)
    for k in range(probe.shape[0]):
        chi[k] = dot(both_back, mixed_back[k].reshape(2 * extent, extent))
    for r in range(0, tile, STRIP):
        s, t = pl.ds(r, STRIP), pl.ds(tile + r, STRIP)
        accumulate(centre, chi, probe, s, t, t)
        before = (iota((STRIP, tile), 0) + r < first_frame[1]).astype(jnp.int32)
        for part in (s, t):
            mine = place(centre[part].astype(F32), columns, own_frame[0], own_frame[2], None)
            other = place(
                first[part].astype(F32), columns, first_frame[0], first_frame[2], before == odd
            )
            for c in range(columns):
                partial[c, part] = mine[c] + other[c]


def fold_kernel(partial, second, second_info, out):
    columns, height, tile = out.shape
    odd = lax.axis_index("row") % 2
    source, row, col = (second_info[r : r + 1] for r in range(3))
    for r in range(0, height, STRIP):
        s = pl.ds(r, STRIP)
        before = (iota((STRIP, tile), 0) + r % tile < row).astype(jnp.int32)
        other = place(second[s].astype(F32), columns, source, col, before == 1 - odd)
        for c in range(columns):
            out[c, s] = (partial[c, s] + other[c]).astype(BF16)


def call(kernel, name, out_shape, in_specs, scratch, flops, moved, *args):
    args = [
        pltpu.with_memory_space_constraint(arg, pltpu.HBM) if spec is HBM else arg
        for arg, spec in zip(args, in_specs)
    ]
    return pl.pallas_call(
        kernel,
        out_shape=out_shape,
        in_specs=in_specs,
        out_specs=jax.tree.map(lambda _: VMEM, out_shape),
        scratch_shapes=scratch,
        compiler_params=pltpu.CompilerParams(vmem_limit_bytes=32 * 2**20),
        cost_estimate=pl.CostEstimate(flops=flops, bytes_accessed=moved, transcendentals=0),
        name=name,
    )(*args)


def per_device(specimen, probe, measured, centers, frame_counts, helper_cols):
    extent = probe.shape[-1]
    half = extent // 2
    tile = specimen.shape[1]
    modes = probe.shape[0]
    columns = lax.axis_size("col")
    height = 2 * tile
    part = jax.ShapeDtypeStruct((height, extent), BF16)
    dma = pltpu.SemaphoreType.DMA

    packed = call(
        pack_kernel, "pack",
        jax.ShapeDtypeStruct((height + INFO, tile), BF16),
        [HBM, HBM, SMEM, HBM],
        [
            pltpu.VMEM(specimen.shape, F32),
            pltpu.SMEM(centers.shape, jnp.int32),
            pltpu.SMEM(helper_cols.shape, jnp.int32),
            dma((3,)),
        ],
        10**5, 2**19,
        specimen, centers, frame_counts, helper_cols,
    )
    band = lax.all_gather(packed, "col")

    rows = lax.axis_size("row")
    swaps = []
    for start in (0, 1):
        pairs = [(i, i + 1) for i in range(start, rows - 1, 2)]
        swaps.append(pairs + [(b, a) for a, b in pairs])
    second = lax.ppermute(band, "row", swaps[1])
    first = lax.ppermute(band, "row", swaps[0])
    tables = dft_tables(extent)
    prepared = call(
        prepare_kernel, "prepare",
        (
            jax.ShapeDtypeStruct((INFO, extent), BF16),
            jax.ShapeDtypeStruct((extent, extent), F32),
            jax.ShapeDtypeStruct((8, extent, extent), BF16),
            jax.ShapeDtypeStruct(probe.shape, F32),
            jax.ShapeDtypeStruct((modes, 2, tile, extent), F32),
        ),
        [VMEM, HBM, HBM, HBM],
        [
            pltpu.VMEM(measured.shape, F32),
            pltpu.VMEM(tables.shape, BF16),
            pltpu.VMEM(probe.shape, F32),
            pltpu.VMEM((extent // 4, 8, extent), F32),
            dma((3,)),
        ],
        10**9, 2**22,
        band, probe, measured, tables,
    )
    near = call(
        near_kernel, "near",
        jax.ShapeDtypeStruct((2, tile, extent), F32),
        [VMEM] * 2,
        [],
        10**6, 2**19,
        first, prepared[0],
    )
    full = (modes, 2, extent, extent)
    to_rows, mixed_back = call(
        frame_kernel, "frame",
        (part, jax.ShapeDtypeStruct(full, BF16)),
        [VMEM] * 7,
        [
            pltpu.VMEM((2, tile, extent), F32),
            pltpu.VMEM((modes, 2, half, extent), BF16),
            pltpu.VMEM((modes, 2, half, extent), F32),
            pltpu.VMEM(full, BF16),
            pltpu.VMEM(full, F32),
            pltpu.VMEM(full, BF16),
            pltpu.VMEM(full, F32),
            pltpu.VMEM((modes, extent, extent), F32),
        ],
        2 * 10**9, 2**22,
        near, second, *prepared,
    )
    from_first = lax.ppermute(to_rows, "row", swaps[0])
    from_second = lax.ppermute(to_rows, "row", swaps[1])
    partial, second_info = call(
        finish_kernel, "finish",
        (
            jax.ShapeDtypeStruct((columns, height, tile), F32),
            jax.ShapeDtypeStruct((8, tile), jnp.int32),
        ),
        [VMEM] * 7,
        [pltpu.VMEM((modes, extent, extent), F32), pltpu.VMEM((height, extent), BF16)],
        5 * 10**8, 2**22,
        band, first, second, mixed_back, prepared[2], prepared[3], from_first,
    )
    summed = call(
        fold_kernel, "fold",
        jax.ShapeDtypeStruct((columns, height, tile), BF16),
        [VMEM] * 3,
        [],
        10**7, 2**20,
        partial, from_second, second_info,
    )
    shares = lax.all_to_all(summed, "col", split_axis=0, concat_axis=0, tiled=True)
    return jnp.sum(shares.astype(F32), axis=0).reshape(2, tile, tile)


def solution(mesh):
    return jax.shard_map(
        per_device,
        mesh=mesh,
        in_specs=(
            P(None, "row", "col"),
            P(),
            P("row", "col", None, None, None),
            P("row", "col", None, None),
            P("row", "col"),
            P("row", "col", None),
        ),
        out_specs=P(None, "row", "col"),
        check_vma=False,
    )
```

```python
import functools
import math

import jax
import jax.numpy as jnp
import numpy as np
from jax import lax
from jax.experimental import pallas as pl
from jax.experimental.pallas import tpu as pltpu
from jax.sharding import PartitionSpec as P

F32 = jnp.float32
BF16 = jnp.bfloat16
INFO = 16
STRIP = 16
VMEM = pl.BlockSpec(memory_space=pltpu.VMEM)
SMEM = pl.BlockSpec(memory_space=pltpu.SMEM)
HBM = pl.BlockSpec(memory_space=pltpu.HBM)


def dft_tables(extent):
    half = extent // 2
    steps = np.arange(extent, dtype=np.int32)
    angles = (steps[:, None] * steps[None, :] % extent).astype(np.float32)
    angles = angles * np.float32(2.0 * math.pi / extent)
    scaling = np.float32(1.0 / math.sqrt(extent))
    real = (np.cos(angles) * scaling).astype(BF16)
    imag = (-np.sin(angles) * scaling).astype(BF16)
    tables = []
    for parity in (0, 1):
        re, im = real[:half, parity::2], imag[:half, parity::2]
        right = np.concatenate(
            [np.concatenate([re, im], 1), np.concatenate([-im, re], 1)], 0
        )
        tables += [right, np.ascontiguousarray(right.T)]
    return jnp.asarray(np.stack(tables))


def dot(a, b):
    return jnp.dot(a, b, preferred_element_type=F32)


def quarters(tl, tr, bl, br):
    return jnp.concatenate(
        [jnp.concatenate([tl, tr], 1), jnp.concatenate([bl, br], 1)], 0
    )


def iota(shape, dim):
    return lax.broadcasted_iota(jnp.int32, shape, dim)


def fetch(pairs, sems):
    copies = [
        pltpu.make_async_copy(source, target, sems.at[i])
        for i, (source, target) in enumerate(pairs)
    ]
    for copy in copies:
        copy.start()
    return copies


def pack_kernel(specimen, centers, cnt, helpers, out, tile_v, cen, hlp, sems):
    copies = fetch(((specimen, tile_v), (centers, cen), (helpers, hlp)), sems)
    for copy in copies:
        copy.wait()
    tile = tile_v.shape[1]
    lanes = tile_v.shape[2]
    rows, cols = iota((INFO, lanes), 0), iota((INFO, lanes), 1)
    info = jnp.where(rows == 0, -1.0, 0.0)
    for j in range(centers.shape[2]):
        helper = jnp.where(j < cnt[0, 0], hlp[0, 0, j], -1)
        for r, value in enumerate((helper, cen[0, 0, j, 0], cen[0, 0, j, 1])):
            info = jnp.where((rows == r) & (cols == j), value.astype(F32), info)
    info = info.astype(BF16)
    for p in range(2):
        out[p * tile : (p + 1) * tile] = tile_v[p].astype(BF16)
    out[2 * tile :] = info


def gather_columns(get, source, col, columns, shape):
    lane = iota(shape, 1)
    beside = own = jnp.zeros(shape, F32)
    for c in range(columns):
        block = get(c)
        near = ((source == c + 1) & (lane >= col)) | ((source == c - 1) & (lane < col))
        beside = jnp.where(near, block, beside)
        own = jnp.where(source == c, block, own)
    return jnp.concatenate([beside, own], 1)


def first_product(probe, patch, tables):
    half = patch[0].shape[1] // 2
    wr = probe[0] * patch[0] - probe[1] * patch[1]
    wi = probe[0] * patch[1] + probe[1] * patch[0]
    out = []
    for sign, table in zip((1, -1), tables):
        folded = jnp.concatenate(
            [wr[:, :half] + sign * wr[:, half:], wi[:, :half] + sign * wi[:, half:]], 1
        )
        out.append(dot(folded.astype(BF16), table))
    return out


def frame_of(band):
    columns, height, lanes = band.shape
    me = lax.axis_index("col").astype(F32)
    code = jnp.zeros((1, lanes), F32)
    for c in range(columns):
        info = band[c, height - INFO :].astype(F32)
        hit = info[0:1] == me
        code += jnp.where(hit, (c * lanes + info[1:2]) * lanes + info[2:3], 0.0)
    code = jnp.sum(code).astype(jnp.int32)
    return code // (lanes * lanes), code // lanes % lanes, code % lanes


def prepare_kernel(
    band, probe, measured, tables,
    info_out, amplitude, tables_out, probe_out, half_out, raw, raw_tables, raw_probe, groups, sems,
):
    copies = fetch(
        ((measured, raw), (tables, raw_tables), (probe, raw_probe)), sems
    )
    columns = band.shape[0]
    tile = (band.shape[1] - INFO) // 2
    extent = raw.shape[-1]
    half = extent // 2
    modes = raw_probe.shape[0]
    source, row, col = frame_of(band)
    which = iota((INFO, extent), 0)
    info = jnp.where(which == 0, source, jnp.where(which == 1, col, row))
    info_out[...] = info.astype(F32).astype(BF16)

    shape = (extent, extent)

    def original(i):
        return jnp.where(i < half, 2 * i, 2 * (i - half) + 1)

    copies[0].wait()
    sort = (iota(shape, 1) == original(iota(shape, 0))).astype(F32).astype(BF16)
    sort_t = (iota(shape, 0) == original(iota(shape, 1))).astype(F32).astype(BF16)
    value = raw[0, 0, 0]
    coarse = value.astype(BF16)
    fine = (value - coarse.astype(F32)).astype(BF16)
    amplitude[...] = sum(
        dot(dot(sort, part).astype(BF16), sort_t) for part in (coarse, fine)
    )

    def roller(old, new, shift, parity):
        wrapped = new % half < shift
        hit = (old + shift - jnp.where(old % half + shift >= half, half, 0)) == new
        sign = jnp.where(wrapped, -1.0, 1.0) if parity else 1.0
        return jnp.where(hit, sign, 0.0).astype(BF16)

    copies[1].wait()
    i, j = iota(shape, 0), iota(shape, 1)
    for parity in range(2):
        right, left = raw_tables[2 * parity], raw_tables[2 * parity + 1]
        for axis, shift in enumerate((col, row)):
            rolled = dot(left, roller(i, j, shift, parity)).astype(BF16)
            rolled_t = dot(roller(j, i, shift, parity), right).astype(BF16)
            tables_out[4 * axis + parity] = rolled_t if axis == 0 else rolled
            tables_out[4 * axis + 2 + parity] = rolled if axis == 0 else rolled_t

    copies[2].wait()
    count = extent // 8
    base = row // 8
    step = row % 8
    lane = iota((extent, half), 1)
    sub = iota((count, 8, extent), 1)
    for k in range(modes):
        for p in range(2):
            lo = pltpu.roll(raw_probe[k, p, :, :half], col, 1)
            hi = pltpu.roll(raw_probe[k, p, :, half:], col, 1)
            turned = jnp.concatenate(
                [jnp.where(lane < col, hi, lo), jnp.where(lane < col, lo, hi)], 1
            )
            turned = pltpu.roll(turned.reshape(count, 8, extent), step, 1)
            turned = jnp.where(
                sub < step, jnp.concatenate([turned[-1:], turned[:-1]], 0), turned
            )
            groups[:count] = turned
            groups[count:] = turned
            probe_out[k, p] = groups[pl.ds(count - base, count)].reshape(extent, extent)

    patch = [
        gather_columns(
            lambda c: band[c, p * tile : (p + 1) * tile].astype(F32),
            source, col, columns, (tile, tile),
        )
        for p in range(2)
    ]
    for k in range(modes):
        products = first_product(
            [probe_out[k, p, half:] for p in range(2)], patch, (tables_out[0], tables_out[1])
        )
        for parity in range(2):
            half_out[k, parity] = products[parity]


def near_kernel(first, info, near):
    columns = first.shape[0]
    _, tile, _ = near.shape
    source, col = (info[r : r + 1, :tile].astype(F32).astype(jnp.int32) for r in range(2))
    for p in range(2):
        for r in range(0, tile, STRIP):
            part = pl.ds(p * tile + r, STRIP)
            near[p, pl.ds(r, STRIP)] = gather_columns(
                lambda c: first[c, part].astype(F32), source, col, columns, (STRIP, tile)
            )


def frame_kernel(
    near, second, info, amplitude, tables, probe, half_own,
    to_rows, mixed_back, patch, folded, half_far, mixed, far, corrected, product, chi,
):
    columns = second.shape[0]
    tile = (second.shape[1] - INFO) // 2
    extent = probe.shape[-1]
    half = extent // 2
    modes = probe.shape[0]
    odd = lax.axis_index("row") % 2
    source, col = (info[r : r + 1, :tile].astype(F32).astype(jnp.int32) for r in range(2))
    center_row = info[2:3].astype(F32).astype(jnp.int32)
    strips = [pl.ds(r, STRIP) for r in range(0, half, STRIP)]
    lower = [pl.ds(half + r, STRIP) for r in range(0, half, STRIP)]

    def split(x):
        return x[:, :half], x[:, half:]

    def join(x, y):
        return jnp.concatenate([x, y], 1).astype(BF16)

    def gather(s):
        rows = iota((STRIP, extent), 0) + s.start
        from_first = (rows >= center_row).astype(jnp.int32) == odd
        for p in range(2):
            part = pl.ds(p * tile + s.start, STRIP)
            far_rows = gather_columns(
                lambda c: second[c, part].astype(F32),
                source, col, columns, (STRIP, tile),
            )
            patch[p, s] = jnp.where(from_first, near[p, s], far_rows)

    def wave(k):
        for s in strips:
            pr, pi, xr, xi = probe[k, 0, s], probe[k, 1, s], patch[0, s], patch[1, s]
            re = split(pr * xr - pi * xi)
            im = split(pr * xi + pi * xr)
            folded[k, 0, s] = join(re[0] + re[1], im[0] + im[1])
            folded[k, 1, s] = join(re[0] - re[1], im[0] - im[1])

    def along_rows(k):
        for q in range(2):
            half_far[k, q] = dot(folded[k, q], tables[q])

    def mix(k):
        for s, t in zip(strips, lower):
            even, odds = half_far[k, 0, s], half_far[k, 1, s]
            even_own, odds_own = half_own[k, 0, s], half_own[k, 1, s]
            for q, (e, o) in enumerate(
                ((even + even_own, odds + odds_own), (even - even_own, odds - odds_own))
            ):
                (er, ei), (our, oui) = split(e), split(o)
                mixed[k, q, s] = join(er, our)
                mixed[k, q, t] = join(ei, oui)

    def along_columns(k, q):
        far[k, q] = dot(tables[4 + q], mixed[k, q])

    def correct(q, which):
        for s, t in list(zip(strips, lower))[which]:
            re = [far[k, q, s] for k in range(modes)]
            im = [far[k, q, t] for k in range(modes)]
            intensity = sum(x * x for x in re + im)
            size = amplitude[pl.ds(q * half + s.start, STRIP)]
            factor = 1.0 - size * lax.rsqrt(jnp.maximum(intensity, 0.25))
            out = pl.ds(q * half + s.start, STRIP)
            for k in range(modes):
                (re_even, re_odd), (im_even, im_odd) = split(re[k] * factor), split(im[k] * factor)
                corrected[k, 0, out] = join(re_even, im_even)
                corrected[k, 1, out] = join(re_odd, im_odd)

    def back_along_rows(k, q):
        part = pl.ds(q * half, half)
        for c in range(2):
            product[k, c, part] = dot(corrected[k, c, part], tables[2 + c])

    def mix_back(k, q):
        for s, t in zip(strips, lower):
            part = pl.ds(q * half + s.start, STRIP)
            x, y = product[k, 0, part], product[k, 1, part]
            (lr, li), (hr, hi) = split(x + y), split(x - y)
            mixed_back[k, q, s] = join(lr, hr)
            mixed_back[k, q, t] = join(li, hi)

    both_back = jnp.concatenate([tables[6], tables[7]], 1)

    def back_along_columns(k):
        chi[k] = dot(both_back, mixed_back[k].reshape(2 * extent, extent))

    for s in strips:
        gather(s)
    for k in range(modes + 1):
        if k < modes:
            wave(k)
            along_rows(k)
        if k > 0:
            mix(k - 1)
            along_columns(k - 1, 0)
    share = -(-len(strips) // modes)
    for k in range(modes):
        along_columns(k, 1)
        correct(0, slice(k * share, (k + 1) * share))
    for k in range(modes):
        back_along_rows(k, 0)
        correct(1, slice(k * share, (k + 1) * share))
    for k in range(modes):
        mix_back(k, 0)
        back_along_rows(k, 1)
    for k in range(modes):
        mix_back(k, 1)
        back_along_columns(k)
    for s, t in zip(strips, lower):
        accumulate(to_rows, chi, probe, s, t, s)


def accumulate(out, chi, probe, s, t, rows):
    tile = out.shape[0] // 2
    re = im = 0.0
    for k in range(probe.shape[0]):
        pr, pi = probe[k, 0, rows], probe[k, 1, rows]
        cr, ci = chi[k, s], chi[k, t]
        re += pr * cr + pi * ci
        im += pr * ci - pi * cr
    out[s] = re.astype(BF16)
    out[pl.ds(tile + s.start, STRIP)] = im.astype(BF16)


def place(block, columns, source, col, taken):
    tile = block.shape[1] // 2
    beside, own = block[:, :tile], block[:, tile:]
    lane = iota(own.shape, 1)
    if taken is not None:
        beside, own = jnp.where(taken, beside, 0.0), jnp.where(taken, own, 0.0)
    out = []
    for c in range(columns):
        near = ((source == c + 1) & (lane >= col)) | ((source == c - 1) & (lane < col))
        out.append(jnp.where(near, beside, 0.0) + jnp.where(source == c, own, 0.0))
    return out


def finish_kernel(
    band, first_band, second_band, mixed_back, tables, probe, first, pair,
    out, chi, centre,
):
    columns = band.shape[0]
    extent = probe.shape[-1]
    tile = (band.shape[1] - INFO) // 2
    odd = lax.axis_index("row") % 2
    own_frame, first_frame, second_frame = (
        frame_of(b) for b in (band, first_band, second_band)
    )
    me = lax.axis_index("row")
    outer = ((me > 0) & (me < lax.axis_size("row") - 1)).astype(jnp.int32)
    both_back = jnp.concatenate([tables[6], -tables[7]], 1)
    for k in range(probe.shape[0]):
        chi[k] = dot(both_back, mixed_back[k].reshape(2 * extent, extent))
    for r in range(0, tile, STRIP):
        s, t = pl.ds(r, STRIP), pl.ds(tile + r, STRIP)
        accumulate(centre, chi, probe, s, t, t)
        rows = iota((STRIP, tile), 0) + r
        from_first = (rows < first_frame[1]).astype(jnp.int32) == odd
        from_second = (rows < second_frame[1]).astype(jnp.int32) + 2 * (1 - outer) == 1 - odd
        for part in (s, t):
            own = place(centre[part].astype(F32), columns, own_frame[0], own_frame[2], None)
            close = place(
                first[part].astype(F32), columns, first_frame[0], first_frame[2], from_first
            )
            other = place(
                pair[odd, part].astype(F32), columns, second_frame[0], second_frame[2], from_second
            )
            for c in range(columns):
                out[c, part] = (own[c] + close[c] + other[c]).astype(BF16)


def call(kernel, name, out_shape, in_specs, scratch, flops, moved, *args):
    args = [
        pltpu.with_memory_space_constraint(arg, pltpu.HBM) if spec is HBM else arg
        for arg, spec in zip(args, in_specs)
    ]
    return pl.pallas_call(
        kernel,
        out_shape=out_shape,
        in_specs=in_specs,
        out_specs=jax.tree.map(lambda _: VMEM, out_shape),
        scratch_shapes=scratch,
        compiler_params=pltpu.CompilerParams(vmem_limit_bytes=32 * 2**20),
        cost_estimate=pl.CostEstimate(flops=flops, bytes_accessed=moved, transcendentals=0),
        name=name,
    )(*args)


def per_device(specimen, probe, measured, centers, frame_counts, helper_cols):
    extent = probe.shape[-1]
    half = extent // 2
    tile = specimen.shape[1]
    modes = probe.shape[0]
    columns = lax.axis_size("col")
    height = 2 * tile
    part = jax.ShapeDtypeStruct((height, extent), BF16)
    dma = pltpu.SemaphoreType.DMA

    packed = call(
        pack_kernel, "pack",
        jax.ShapeDtypeStruct((height + INFO, tile), BF16),
        [HBM, HBM, SMEM, HBM],
        [
            pltpu.VMEM(specimen.shape, F32),
            pltpu.SMEM(centers.shape, jnp.int32),
            pltpu.SMEM(helper_cols.shape, jnp.int32),
            dma((3,)),
        ],
        10**5, 2**19,
        specimen, centers, frame_counts, helper_cols,
    )
    band = lax.all_gather(packed, "col")

    rows = lax.axis_size("row")
    swaps = []
    for start in (0, 1):
        pairs = [(i, i + 1) for i in range(start, rows - 1, 2)]
        swaps.append(pairs + [(b, a) for a, b in pairs])
    second = lax.ppermute(band, "row", swaps[1])
    first = lax.ppermute(band, "row", swaps[0])
    tables = dft_tables(extent)
    prepared = call(
        prepare_kernel, "prepare",
        (
            jax.ShapeDtypeStruct((INFO, extent), BF16),
            jax.ShapeDtypeStruct((extent, extent), F32),
            jax.ShapeDtypeStruct((8, extent, extent), BF16),
            jax.ShapeDtypeStruct(probe.shape, F32),
            jax.ShapeDtypeStruct((modes, 2, tile, extent), F32),
        ),
        [VMEM, HBM, HBM, HBM],
        [
            pltpu.VMEM(measured.shape, F32),
            pltpu.VMEM(tables.shape, BF16),
            pltpu.VMEM(probe.shape, F32),
            pltpu.VMEM((extent // 4, 8, extent), F32),
            dma((3,)),
        ],
        10**9, 2**22,
        band, probe, measured, tables,
    )
    near = call(
        near_kernel, "near",
        jax.ShapeDtypeStruct((2, tile, extent), F32),
        [VMEM] * 2,
        [],
        10**6, 2**19,
        first, prepared[0],
    )
    full = (modes, 2, extent, extent)
    to_rows, mixed_back = call(
        frame_kernel, "frame",
        (part, jax.ShapeDtypeStruct(full, BF16)),
        [VMEM] * 7,
        [
            pltpu.VMEM((2, tile, extent), F32),
            pltpu.VMEM((modes, 2, half, extent), BF16),
            pltpu.VMEM((modes, 2, half, extent), F32),
            pltpu.VMEM(full, BF16),
            pltpu.VMEM(full, F32),
            pltpu.VMEM(full, BF16),
            pltpu.VMEM(full, F32),
            pltpu.VMEM((modes, extent, extent), F32),
        ],
        2 * 10**9, 2**22,
        near, second, *prepared,
    )
    from_first = lax.ppermute(to_rows, "row", swaps[0])
    ends = [r * columns + c for r in (0, rows - 1) for c in range(columns)]
    pairs = [ends[i : i + 2] for i in range(0, 2 * columns, 2)]
    pairs += [
        [r * columns + c, (r + 1) * columns + c]
        for r in range(1, rows - 1, 2) for c in range(columns)
    ]
    pair = lax.all_gather(to_rows, ("row", "col"), axis_index_groups=pairs)
    summed = call(
        finish_kernel, "finish",
        jax.ShapeDtypeStruct((columns, height, tile), BF16),
        [VMEM] * 8,
        [pltpu.VMEM((modes, extent, extent), F32), pltpu.VMEM((height, extent), BF16)],
        5 * 10**8, 2**22,
        band, first, second, mixed_back, prepared[2], prepared[3], from_first, pair,
    )
    shares = lax.all_to_all(summed, "col", split_axis=0, concat_axis=0, tiled=True)
    return jnp.sum(shares.astype(F32), axis=0).reshape(2, tile, tile)


def solution(mesh):
    return jax.shard_map(
        per_device,
        mesh=mesh,
        in_specs=(
            P(None, "row", "col"),
            P(),
            P("row", "col", None, None, None),
            P("row", "col", None, None),
            P("row", "col"),
            P("row", "col", None),
        ),
        out_specs=P(None, "row", "col"),
        check_vma=False,
    )
```

```python
import functools
import math

import jax
import jax.numpy as jnp
import numpy as np
from jax import lax
from jax.experimental import pallas as pl
from jax.experimental.pallas import tpu as pltpu
from jax.sharding import PartitionSpec as P

F32 = jnp.float32
BF16 = jnp.bfloat16
INFO = 16
STRIP = 32
VMEM = pl.BlockSpec(memory_space=pltpu.VMEM)
SMEM = pl.BlockSpec(memory_space=pltpu.SMEM)
HBM = pl.BlockSpec(memory_space=pltpu.HBM)


def dft_tables(extent):
    half = extent // 2
    steps = np.arange(extent, dtype=np.int32)
    angles = (steps[:, None] * steps[None, :] % extent).astype(np.float32)
    angles = angles * np.float32(2.0 * math.pi / extent)
    scaling = np.float32(1.0 / math.sqrt(extent))
    real = (np.cos(angles) * scaling).astype(BF16)
    imag = (-np.sin(angles) * scaling).astype(BF16)
    tables = []
    for parity in (0, 1):
        re, im = real[:half, parity::2], imag[:half, parity::2]
        right = np.concatenate(
            [np.concatenate([re, im], 1), np.concatenate([-im, re], 1)], 0
        )
        tables += [right, np.ascontiguousarray(right.T)]
    return jnp.asarray(np.stack(tables))


def dot(a, b):
    return jnp.dot(a, b, preferred_element_type=F32)


def quarters(tl, tr, bl, br):
    return jnp.concatenate(
        [jnp.concatenate([tl, tr], 1), jnp.concatenate([bl, br], 1)], 0
    )


def iota(shape, dim):
    return lax.broadcasted_iota(jnp.int32, shape, dim)


def fetch(pairs, sems):
    copies = [
        pltpu.make_async_copy(source, target, sems.at[i])
        for i, (source, target) in enumerate(pairs)
    ]
    for copy in copies:
        copy.start()
    return copies


def pack_kernel(specimen, centers, cnt, helpers, out, tile_v, cen, hlp, sems):
    copies = fetch(((specimen, tile_v), (centers, cen), (helpers, hlp)), sems)
    for copy in copies:
        copy.wait()
    tile = tile_v.shape[1]
    lanes = tile_v.shape[2]
    rows, cols = iota((INFO, lanes), 0), iota((INFO, lanes), 1)
    info = jnp.where(rows == 0, -1.0, 0.0)
    for j in range(centers.shape[2]):
        helper = jnp.where(j < cnt[0, 0], hlp[0, 0, j], -1)
        for r, value in enumerate((helper, cen[0, 0, j, 0], cen[0, 0, j, 1])):
            info = jnp.where((rows == r) & (cols == j), value.astype(F32), info)
    info = info.astype(BF16)
    for p in range(2):
        out[p * tile : (p + 1) * tile] = tile_v[p].astype(BF16)
    out[2 * tile :] = info


def gather_columns(get, source, col, columns, shape):
    lane = iota(shape, 1)
    beside = own = jnp.zeros(shape, F32)
    for c in range(columns):
        block = get(c)
        near = ((source == c + 1) & (lane >= col)) | ((source == c - 1) & (lane < col))
        beside = jnp.where(near, block, beside)
        own = jnp.where(source == c, block, own)
    return jnp.concatenate([beside, own], 1)


def first_product(probe, patch, tables):
    half = patch[0].shape[1] // 2
    wr = probe[0] * patch[0] - probe[1] * patch[1]
    wi = probe[0] * patch[1] + probe[1] * patch[0]
    out = []
    for sign, table in zip((1, -1), tables):
        folded = jnp.concatenate(
            [wr[:, :half] + sign * wr[:, half:], wi[:, :half] + sign * wi[:, half:]], 1
        )
        out.append(dot(folded.astype(BF16), table))
    return out


def frame_of(band):
    columns, height, lanes = band.shape
    me = lax.axis_index("col").astype(F32)
    code = jnp.zeros((1, lanes), F32)
    for c in range(columns):
        info = band[c, height - INFO :].astype(F32)
        hit = info[0:1] == me
        code += jnp.where(hit, (c * lanes + info[1:2]) * lanes + info[2:3], 0.0)
    code = jnp.sum(code).astype(jnp.int32)
    return code // (lanes * lanes), code // lanes % lanes, code % lanes


def prepare_kernel(
    band, probe, measured, tables,
    info_out, amplitude, tables_out, probe_out, half_out, raw, raw_tables, raw_probe, groups, sems,
):
    copies = fetch(
        ((measured, raw), (tables, raw_tables), (probe, raw_probe)), sems
    )
    columns = band.shape[0]
    tile = (band.shape[1] - INFO) // 2
    extent = raw.shape[-1]
    half = extent // 2
    modes = raw_probe.shape[0]
    source, row, col = frame_of(band)
    which = iota((INFO, extent), 0)
    info = jnp.where(which == 0, source, jnp.where(which == 1, col, row))
    info_out[...] = info.astype(F32).astype(BF16)

    shape = (extent, extent)

    def original(i):
        return jnp.where(i < half, 2 * i, 2 * (i - half) + 1)

    copies[0].wait()
    sort = (iota(shape, 1) == original(iota(shape, 0))).astype(F32).astype(BF16)
    sort_t = (iota(shape, 0) == original(iota(shape, 1))).astype(F32).astype(BF16)
    value = raw[0, 0, 0]
    coarse = value.astype(BF16)
    fine = (value - coarse.astype(F32)).astype(BF16)
    amplitude[...] = sum(
        dot(dot(sort, part).astype(BF16), sort_t) for part in (coarse, fine)
    )

    def roller(old, new, shift, parity):
        wrapped = new % half < shift
        hit = (old + shift - jnp.where(old % half + shift >= half, half, 0)) == new
        sign = jnp.where(wrapped, -1.0, 1.0) if parity else 1.0
        return jnp.where(hit, sign, 0.0).astype(BF16)

    copies[1].wait()
    i, j = iota(shape, 0), iota(shape, 1)
    for parity in range(2):
        right, left = raw_tables[2 * parity], raw_tables[2 * parity + 1]
        for axis, shift in enumerate((col, row)):
            rolled = dot(left, roller(i, j, shift, parity)).astype(BF16)
            rolled_t = dot(roller(j, i, shift, parity), right).astype(BF16)
            tables_out[4 * axis + parity] = rolled_t if axis == 0 else rolled
            tables_out[4 * axis + 2 + parity] = rolled if axis == 0 else rolled_t

    copies[2].wait()
    count = extent // 8
    base = row // 8
    step = row % 8
    lane = iota((extent, half), 1)
    sub = iota((count, 8, extent), 1)
    for k in range(modes):
        for p in range(2):
            lo = pltpu.roll(raw_probe[k, p, :, :half], col, 1)
            hi = pltpu.roll(raw_probe[k, p, :, half:], col, 1)
            turned = jnp.concatenate(
                [jnp.where(lane < col, hi, lo), jnp.where(lane < col, lo, hi)], 1
            )
            turned = pltpu.roll(turned.reshape(count, 8, extent), step, 1)
            turned = jnp.where(
                sub < step, jnp.concatenate([turned[-1:], turned[:-1]], 0), turned
            )
            groups[:count] = turned
            groups[count:] = turned
            probe_out[k, p] = groups[pl.ds(count - base, count)].reshape(extent, extent)

    patch = [
        gather_columns(
            lambda c: band[c, p * tile : (p + 1) * tile].astype(F32),
            source, col, columns, (tile, tile),
        )
        for p in range(2)
    ]
    for k in range(modes):
        products = first_product(
            [probe_out[k, p, half:] for p in range(2)], patch, (tables_out[0], tables_out[1])
        )
        for parity in range(2):
            half_out[k, parity] = products[parity]


def near_kernel(first, info, near):
    columns = first.shape[0]
    _, tile, _ = near.shape
    source, col = (info[r : r + 1, :tile].astype(F32).astype(jnp.int32) for r in range(2))
    for p in range(2):
        for r in range(0, tile, STRIP):
            part = pl.ds(p * tile + r, STRIP)
            near[p, pl.ds(r, STRIP)] = gather_columns(
                lambda c: first[c, part].astype(F32), source, col, columns, (STRIP, tile)
            )


def frame_kernel(
    near, second, info, amplitude, tables, probe, half_own,
    to_rows, mixed_back, patch, folded, half_far, mixed, far, corrected, product, chi,
):
    columns = second.shape[0]
    tile = (second.shape[1] - INFO) // 2
    extent = probe.shape[-1]
    half = extent // 2
    modes = probe.shape[0]
    odd = lax.axis_index("row") % 2
    source, col = (info[r : r + 1, :tile].astype(F32).astype(jnp.int32) for r in range(2))
    center_row = info[2:3].astype(F32).astype(jnp.int32)
    strips = [pl.ds(r, STRIP) for r in range(0, half, STRIP)]
    lower = [pl.ds(half + r, STRIP) for r in range(0, half, STRIP)]

    def split(x):
        return x[:, :half], x[:, half:]

    def join(x, y):
        return jnp.concatenate([x, y], 1).astype(BF16)

    def gather(s):
        rows = iota((STRIP, extent), 0) + s.start
        from_first = (rows >= center_row).astype(jnp.int32) == odd
        for p in range(2):
            part = pl.ds(p * tile + s.start, STRIP)
            far_rows = gather_columns(
                lambda c: second[c, part].astype(F32),
                source, col, columns, (STRIP, tile),
            )
            patch[p, s] = jnp.where(from_first, near[p, s], far_rows)

    def wave(k):
        for s in strips:
            pr, pi, xr, xi = probe[k, 0, s], probe[k, 1, s], patch[0, s], patch[1, s]
            re = split(pr * xr - pi * xi)
            im = split(pr * xi + pi * xr)
            folded[k, 0, s] = join(re[0] + re[1], im[0] + im[1])
            folded[k, 1, s] = join(re[0] - re[1], im[0] - im[1])

    def along_rows(k):
        for q in range(2):
            half_far[k, q] = dot(folded[k, q], tables[q])

    def mix(k):
        for s, t in zip(strips, lower):
            even, odds = half_far[k, 0, s], half_far[k, 1, s]
            even_own, odds_own = half_own[k, 0, s], half_own[k, 1, s]
            for q, (e, o) in enumerate(
                ((even + even_own, odds + odds_own), (even - even_own, odds - odds_own))
            ):
                (er, ei), (our, oui) = split(e), split(o)
                mixed[k, q, s] = join(er, our)
                mixed[k, q, t] = join(ei, oui)

    def along_columns(k, q):
        far[k, q] = dot(tables[4 + q], mixed[k, q])

    def correct(q, which):
        for s, t in list(zip(strips, lower))[which]:
            re = [far[k, q, s] for k in range(modes)]
            im = [far[k, q, t] for k in range(modes)]
            intensity = sum(x * x for x in re + im)
            size = amplitude[pl.ds(q * half + s.start, STRIP)]
            factor = 1.0 - size * lax.rsqrt(jnp.maximum(intensity, 0.25))
            out = pl.ds(q * half + s.start, STRIP)
            for k in range(modes):
                (re_even, re_odd), (im_even, im_odd) = split(re[k] * factor), split(im[k] * factor)
                corrected[k, 0, out] = join(re_even, im_even)
                corrected[k, 1, out] = join(re_odd, im_odd)

    def back_along_rows(k, q):
        part = pl.ds(q * half, half)
        for c in range(2):
            product[k, c, part] = dot(corrected[k, c, part], tables[2 + c])

    def mix_back(k, q):
        for s, t in zip(strips, lower):
            part = pl.ds(q * half + s.start, STRIP)
            x, y = product[k, 0, part], product[k, 1, part]
            (lr, li), (hr, hi) = split(x + y), split(x - y)
            mixed_back[k, q, s] = join(lr, hr)
            mixed_back[k, q, t] = join(li, hi)

    both_back = jnp.concatenate([tables[6], tables[7]], 1)

    def back_along_columns(k):
        chi[k] = dot(both_back, mixed_back[k].reshape(2 * extent, extent))

    for s in strips:
        gather(s)
    for k in range(modes + 1):
        if k < modes:
            wave(k)
            along_rows(k)
        if k > 0:
            mix(k - 1)
            along_columns(k - 1, 0)
    share = -(-len(strips) // modes)
    for k in range(modes):
        along_columns(k, 1)
        correct(0, slice(k * share, (k + 1) * share))
    for k in range(modes):
        back_along_rows(k, 0)
        correct(1, slice(k * share, (k + 1) * share))
    for k in range(modes):
        mix_back(k, 0)
        back_along_rows(k, 1)
    for k in range(modes):
        mix_back(k, 1)
        back_along_columns(k)
    for s, t in zip(strips, lower):
        accumulate(to_rows, chi, probe, s, t, s)


def accumulate(out, chi, probe, s, t, rows):
    tile = out.shape[0] // 2
    re = im = 0.0
    for k in range(probe.shape[0]):
        pr, pi = probe[k, 0, rows], probe[k, 1, rows]
        cr, ci = chi[k, s], chi[k, t]
        re += pr * cr + pi * ci
        im += pr * ci - pi * cr
    out[s] = re.astype(BF16)
    out[pl.ds(tile + s.start, STRIP)] = im.astype(BF16)


def place(block, columns, source, col, taken):
    tile = block.shape[1] // 2
    beside, own = block[:, :tile], block[:, tile:]
    lane = iota(own.shape, 1)
    if taken is not None:
        beside, own = jnp.where(taken, beside, 0.0), jnp.where(taken, own, 0.0)
    out = []
    for c in range(columns):
        near = ((source == c + 1) & (lane >= col)) | ((source == c - 1) & (lane < col))
        out.append(jnp.where(near, beside, 0.0) + jnp.where(source == c, own, 0.0))
    return out


def finish_kernel(
    band, first_band, second_band, mixed_back, tables, probe, first,
    partial, second_info, chi, centre,
):
    columns = band.shape[0]
    extent = probe.shape[-1]
    tile = (band.shape[1] - INFO) // 2
    odd = lax.axis_index("row") % 2
    own_frame, first_frame, second_frame = (
        frame_of(b) for b in (band, first_band, second_band)
    )
    which = iota(second_info.shape, 0)
    second_info[...] = jnp.where(
        which == 0, second_frame[0], jnp.where(which == 1, second_frame[1], second_frame[2])
    )
    both_back = jnp.concatenate([tables[6], -tables[7]], 1)
    for k in range(probe.shape[0]):
        chi[k] = dot(both_back, mixed_back[k].reshape(2 * extent, extent))
    for r in range(0, tile, STRIP):
        s, t = pl.ds(r, STRIP), pl.ds(tile + r, STRIP)
        accumulate(centre, chi, probe, s, t, t)
        before = (iota((STRIP, tile), 0) + r < first_frame[1]).astype(jnp.int32)
        for part in (s, t):
            mine = place(centre[part].astype(F32), columns, own_frame[0], own_frame[2], None)
            other = place(
                first[part].astype(F32), columns, first_frame[0], first_frame[2], before == odd
            )
            for c in range(columns):
                partial[c, part] = mine[c] + other[c]


def fold_kernel(partial, second, second_info, out):
    columns, height, tile = out.shape
    odd = lax.axis_index("row") % 2
    source, row, col = (second_info[r : r + 1] for r in range(3))
    for r in range(0, height, STRIP):
        s = pl.ds(r, STRIP)
        before = (iota((STRIP, tile), 0) + r % tile < row).astype(jnp.int32)
        other = place(second[s].astype(F32), columns, source, col, before == 1 - odd)
        for c in range(columns):
            out[c, s] = (partial[c, s] + other[c]).astype(BF16)


def call(kernel, name, out_shape, in_specs, scratch, flops, moved, *args):
    args = [
        pltpu.with_memory_space_constraint(arg, pltpu.HBM) if spec is HBM else arg
        for arg, spec in zip(args, in_specs)
    ]
    return pl.pallas_call(
        kernel,
        out_shape=out_shape,
        in_specs=in_specs,
        out_specs=jax.tree.map(lambda _: VMEM, out_shape),
        scratch_shapes=scratch,
        compiler_params=pltpu.CompilerParams(vmem_limit_bytes=32 * 2**20),
        cost_estimate=pl.CostEstimate(flops=flops, bytes_accessed=moved, transcendentals=0),
        name=name,
    )(*args)


def per_device(specimen, probe, measured, centers, frame_counts, helper_cols):
    extent = probe.shape[-1]
    half = extent // 2
    tile = specimen.shape[1]
    modes = probe.shape[0]
    columns = lax.axis_size("col")
    height = 2 * tile
    part = jax.ShapeDtypeStruct((height, extent), BF16)
    dma = pltpu.SemaphoreType.DMA

    packed = call(
        pack_kernel, "pack",
        jax.ShapeDtypeStruct((height + INFO, tile), BF16),
        [HBM, HBM, SMEM, HBM],
        [
            pltpu.VMEM(specimen.shape, F32),
            pltpu.SMEM(centers.shape, jnp.int32),
            pltpu.SMEM(helper_cols.shape, jnp.int32),
            dma((3,)),
        ],
        10**5, 2**19,
        specimen, centers, frame_counts, helper_cols,
    )
    band = lax.all_gather(packed, "col")

    rows = lax.axis_size("row")
    swaps = []
    for start in (0, 1):
        pairs = [(i, i + 1) for i in range(start, rows - 1, 2)]
        swaps.append(pairs + [(b, a) for a, b in pairs])
    second = lax.ppermute(band, "row", swaps[1])
    first = lax.ppermute(band, "row", swaps[0])
    tables = dft_tables(extent)
    prepared = call(
        prepare_kernel, "prepare",
        (
            jax.ShapeDtypeStruct((INFO, extent), BF16),
            jax.ShapeDtypeStruct((extent, extent), F32),
            jax.ShapeDtypeStruct((8, extent, extent), BF16),
            jax.ShapeDtypeStruct(probe.shape, F32),
            jax.ShapeDtypeStruct((modes, 2, tile, extent), F32),
        ),
        [VMEM, HBM, HBM, HBM],
        [
            pltpu.VMEM(measured.shape, F32),
            pltpu.VMEM(tables.shape, BF16),
            pltpu.VMEM(probe.shape, F32),
            pltpu.VMEM((extent // 4, 8, extent), F32),
            dma((3,)),
        ],
        10**9, 2**22,
        band, probe, measured, tables,
    )
    near = call(
        near_kernel, "near",
        jax.ShapeDtypeStruct((2, tile, extent), F32),
        [VMEM] * 2,
        [],
        10**6, 2**19,
        first, prepared[0],
    )
    full = (modes, 2, extent, extent)
    to_rows, mixed_back = call(
        frame_kernel, "frame",
        (part, jax.ShapeDtypeStruct(full, BF16)),
        [VMEM] * 7,
        [
            pltpu.VMEM((2, tile, extent), F32),
            pltpu.VMEM((modes, 2, half, extent), BF16),
            pltpu.VMEM((modes, 2, half, extent), F32),
            pltpu.VMEM(full, BF16),
            pltpu.VMEM(full, F32),
            pltpu.VMEM(full, BF16),
            pltpu.VMEM(full, F32),
            pltpu.VMEM((modes, extent, extent), F32),
        ],
        2 * 10**9, 2**22,
        near, second, *prepared,
    )
    from_first = lax.ppermute(to_rows, "row", swaps[0])
    from_second = lax.ppermute(to_rows, "row", swaps[1])
    partial, second_info = call(
        finish_kernel, "finish",
        (
            jax.ShapeDtypeStruct((columns, height, tile), F32),
            jax.ShapeDtypeStruct((8, tile), jnp.int32),
        ),
        [VMEM] * 7,
        [pltpu.VMEM((modes, extent, extent), F32), pltpu.VMEM((height, extent), BF16)],
        5 * 10**8, 2**22,
        band, first, second, mixed_back, prepared[2], prepared[3], from_first,
    )
    summed = call(
        fold_kernel, "fold",
        jax.ShapeDtypeStruct((columns, height, tile), BF16),
        [VMEM] * 3,
        [],
        10**7, 2**20,
        partial, from_second, second_info,
    )
    shares = lax.all_to_all(summed, "col", split_axis=0, concat_axis=0, tiled=True)
    return jnp.sum(shares.astype(F32), axis=0).reshape(2, tile, tile)


def solution(mesh):
    return jax.shard_map(
        per_device,
        mesh=mesh,
        in_specs=(
            P(None, "row", "col"),
            P(),
            P("row", "col", None, None, None),
            P("row", "col", None, None),
            P("row", "col"),
            P("row", "col", None),
        ),
        out_specs=P(None, "row", "col"),
        check_vma=False,
    )
```
